32 devices in a mesh: role: 2 (over core), dp: 8 (over z, x), head: 2 (over y).
Axes of the slice: x: 2, y: 2, z: 4, core: 2. Of those that a mesh axis runs over, the one named last changes fastest.
Arguments:
- layer_in: bfloat16 [2, 24576, 512], P('role', ('dp', 'head')), may hold values from -6 to 6
- lengths: int32 [2, 16, 24], P('role', 'dp'), may hold values from 1 to 100, 1536 in all within a row
- cotangent: bfloat16 [24576, 512], P(('dp', 'head')), may hold values from -6 to 6
- targets: int32 [24576], P(('dp', 'head')), may hold values 0 or 1
- self_qkv: bfloat16 [512, 3, 512], P(None, None, 'head'), may hold values from -0.25 to 0.25
- self_out: bfloat16 [512, 512], P('head'), may hold values from -1 to 1
- cross_q: bfloat16 [512, 512], P(None, 'head'), may hold values from -0.25 to 0.25
- cross_kv: bfloat16 [512, 2, 512], P(None, None, 'head'), may hold values from -0.25 to 0.25
- cross_out: bfloat16 [512, 512], P('head'), may hold values from -1 to 1
- ffn_in: bfloat16 [512, 2048], P(None, 'head'), may hold values from -0.25 to 0.25
- ffn_out: bfloat16 [2048, 512], P('head'), may hold values from -0.1875 to 0.1875
- norm_gain: float32 [3, 512], replicated, may hold values from 0.5 to 1.5
- norm_bias: float32 [3, 512], replicated, may hold values from -3 to 3
- halt_weight: float32 [512], replicated, may hold values from -0.25 to 0.25
- halt_bias: float32 [1], replicated, may hold values from -4 to 4
Outputs:
- layer_out: bfloat16 [2, 24576, 512], P('role', ('dp', 'head'))
- input_grads: float32 [2, 24576, 512], P('role', ('dp', 'head'))
- self_qkv_grad: float32 [512, 3, 512], P(None, None, 'head')
- self_out_grad: float32 [512, 512], P('head')
- cross_q_grad: float32 [512, 512], P(None, 'head')
- cross_kv_grad: float32 [512, 2, 512], P(None, None, 'head')
- cross_out_grad: float32 [512, 512], P('head')
- ffn_in_grad: float32 [512, 2048], P(None, 'head')
- ffn_out_grad: float32 [2048, 512], P('head')
- norm_gain_grad: float32 [3, 512], replicated
- norm_bias_grad: float32 [3, 512], replicated
- halt_weight_grad: float32 [512], replicated
- halt_bias_grad: float32 [1], replicated
The draws below stay inside these ranges and needn't reach their ends.
Inputs may be any that keep to these rules, and one draw needn't show every extreme that they name: Row r of lengths[0] holds the 24 sentence lengths of source row r and row r of lengths[1] those of target row r; each row sums to 1536; target sentence c reads source sentence c of the same row. `targets`: 1 where the token halts.
All inputs are finite; a program needn't handle non-finite values. No bound on the sum of `targets` on one device may be relied on, other than what follows from the above.
Results may differ from the reference program's by a relative error of at most 0.017.
The reference program's roundings to bfloat16 on the way (of `self_mix`, `cross_mix` and `activated`) count: a program that leaves them out, or rounds other values in their place, can miss the bound.
Values may be sent and summed in bfloat16 or wider, within the bound.
No kernel may reach another device: no remote copies, remote signals or barrier semaphores. Data moves between devices by JAX's collectives and lax.ppermute only.
A program may use at most 192 MiB of HBM per device.

```python
import math
import jax
import jax.numpy as jnp
import numpy as np
from jax import lax

D = 512
HEAD_DIM = 64
FF = 2048
ROW_LEN = 1536
SENTS = 24
MOST = 100
ROWS = 16
TOKENS = 24576


def plant(values, key, low, high):
    longest = values.shape.index(max(values.shape))
    spots = []
    for shift in (0, 1):
        where = [jax.random.randint(jax.random.fold_in(key, axis), (), 0, length) for axis, length in enumerate(values.shape)]
        where[longest] = (where[longest] + shift) % values.shape[longest]
        spots.append(tuple(where))
    return values.at[spots[0]].set(low).at[spots[1]].set(high)


def shard_levels(rng, dims, cuts, least, top_value):
    loudness, own = 1.0, jax.random.fold_in(rng, 6)
    for axis_at, parts in cuts:
        heights = jnp.exp(jax.random.uniform(jax.random.fold_in(own, axis_at), (parts,), jnp.float32, least / len(cuts), top_value / len(cuts)))
        loudness = loudness * jnp.repeat(heights, dims[axis_at] // parts).reshape([-1 if axis == axis_at else 1 for axis in range(len(dims))])
    return loudness


def split_up(count, total, bound, lean):
    loads = [(1 << 20) // math.isqrt(rank ** lean) + 1 for rank in range(2, count + 1)]
    rest, holding = total - bound - (count - 1), [1] * (count - 1)
    while rest > 0:
        movable = [i for i in range(count - 1) if holding[i] < bound]
        mass, left = sum([loads[i] for i in movable]), rest
        for i in movable:
            extra = min(bound - holding[i], max(1, left * loads[i] // mass), rest)
            holding[i] = holding[i] + extra
            rest = rest - extra
    return np.array([bound] + holding)


def uneven_parts(key, number_of, total, reach, skew):
    if number_of == 2:
        one = jax.random.randint(key, (), max(1, total - reach), min(reach, total - 1) + 1)
        return jnp.stack([one, total - one])
    sizes = jnp.asarray(split_up(number_of, total, reach, skew), jnp.int32)
    couples = (number_of - 1) // 2
    source_of, receiver = sizes[1:1 + 2 * couples:2], sizes[2:2 + 2 * couples:2]
    room = jnp.minimum(source_of - 1, reach - receiver)
    passed = jax.random.randint(jax.random.fold_in(key, 1), (couples,), 0, 1 << 20) % (room + 1)
    sizes = sizes.at[1:1 + 2 * couples:2].set(source_of - passed).at[2:2 + 2 * couples:2].set(receiver + passed)
    return sizes[jax.random.permutation(jax.random.fold_in(key, 2), number_of)]


def scatter_about(stream_key, dims, deviation, reach, split=(), kind=jnp.bfloat16):
    values = deviation * jax.random.normal(stream_key, dims, jnp.float32)
    if split:
        values = values * shard_levels(stream_key, dims, split, -0.22, 0.18)
    return jnp.clip(values, -reach, reach).astype(kind)


def setup_inputs(seed: int = 0) -> dict:
    splits = jax.random.split(jax.random.key(seed), 16)
    layer_in = scatter_about(splits[0], (2, TOKENS, D), 1.0, 6.0, ((0, 2), (1, 16)))
    lengths = jax.vmap(lambda own: uneven_parts(own, SENTS, ROW_LEN, MOST, 1))(jax.random.split(splits[1], 2 * ROWS)).reshape((2, ROWS, SENTS)).astype(jnp.int32)
    cotangent = scatter_about(splits[2], (TOKENS, D), 1.0, 6.0, ((0, 16),))
    targets = plant((jax.random.randint(splits[3], (TOKENS,), 0, 2) < 1).astype(jnp.int32), jax.random.fold_in(splits[3], 1), 0, 1)
    self_qkv = scatter_about(splits[4], (D, 3, D), D ** -0.5, 0.25, ((2, 2),))
    self_out = scatter_about(splits[5], (D, D), (D // 16) ** -0.5, 1.0, ((0, 2),))
    cross_q = scatter_about(splits[6], (D, D), D ** -0.5, 0.25, ((1, 2),))
    cross_kv = scatter_about(splits[7], (D, 2, D), D ** -0.5, 0.25, ((2, 2),))
    cross_out = scatter_about(splits[8], (D, D), (D // 16) ** -0.5, 1.0, ((0, 2),))
    ffn_in = scatter_about(splits[9], (D, FF), D ** -0.5, 0.25, ((1, 2),))
    ffn_out = scatter_about(splits[10], (FF, D), (FF // 2) ** -0.5, 0.1875, ((0, 2),))
    norm_gain = jnp.clip(1.0 + 0.1 * jax.random.normal(splits[11], (3, D), jnp.float32), 0.5, 1.5)
    norm_bias = scatter_about(splits[12], (3, D), 0.5, 3.0, (), jnp.float32)
    halt_weight = scatter_about(splits[13], (D,), D ** -0.5, 0.25, (), jnp.float32)
    halt_bias = scatter_about(splits[14], (1,), 1.0, 4.0, (), jnp.float32)
    return dict(layer_in=layer_in, lengths=lengths, cotangent=cotangent, targets=targets, self_qkv=self_qkv, self_out=self_out, cross_q=cross_q, cross_kv=cross_kv, cross_out=cross_out, ffn_in=ffn_in, ffn_out=ffn_out, norm_gain=norm_gain, norm_bias=norm_bias, halt_weight=halt_weight, halt_bias=halt_bias)


highest = lax.Precision.HIGHEST
masked_score = -1e+30

@jax.custom_vjp
def low(v):
    return lax.optimization_barrier(v.astype(jnp.bfloat16)).astype(jnp.float32)

@jax.custom_vjp
def low_back(v):
    return v

def low_keep(v):
    return (low(v), None)

def low_pass(kept, grad):
    return (grad,)

def back_keep(v):
    return (v, None)

def back_low(kept, grad):
    return (low(grad),)
low.defvjp(low_keep, low_pass)
low_back.defvjp(back_keep, back_low)

def norm_rows(values, norm_scale, shift_bias):
    center = values - lax.optimization_barrier(jnp.mean(values, axis=-1, keepdims=True))
    spread = lax.optimization_barrier(jnp.mean(center * center, axis=-1, keepdims=True))
    return center * lax.rsqrt(spread + 1e-05) * norm_scale + shift_bias

def segments(lengths_rows, row_len):
    sentence_ends = jnp.cumsum(lengths_rows, axis=-1)
    positions = jnp.arange(row_len, dtype=jnp.int32)
    return lax.optimization_barrier(jnp.sum((positions[None, :, None] >= sentence_ends[:, None, :]).astype(jnp.int32), axis=-1))

def allowed_keys(query_seg, key_seg, query_pos, causal):
    matches = query_seg[:, None] == key_seg[None, :]
    if causal:
        key_pos = jnp.arange(key_seg.shape[0], dtype=jnp.int32)
        matches = matches & (key_pos[None, :] <= query_pos[:, None])
    return matches

def attend(queries, key_rows, values, query_seg, key_seg, causal):
    row_len = queries.shape[0]
    block_rows = min(512, row_len)
    blocks = row_len // block_rows
    scaling = queries.shape[-1] ** (-0.5)
    positions = jnp.arange(row_len, dtype=jnp.int32).reshape(blocks, block_rows)

    def one_block(pieces):
        query_block, seg_block, pos_block = pieces
        scores = low_back(jnp.einsum('qhe,khe->hqk', query_block, key_rows, precision=highest) * scaling)
        allowed = allowed_keys(seg_block, key_seg, pos_block, causal)
        scores = jnp.where(allowed[None], scores, masked_score)
        row_max = lax.optimization_barrier(jnp.max(scores, axis=-1, keepdims=True))
        weights = jnp.exp(scores - row_max)
        probabilities = low(weights / lax.optimization_barrier(jnp.sum(weights, axis=-1, keepdims=True)))
        return jnp.einsum('hqk,khe->qhe', probabilities, values, precision=highest)
    shaped = queries.reshape((blocks, block_rows) + queries.shape[1:])
    mixture = lax.map(jax.checkpoint(one_block), (shaped, query_seg.reshape(blocks, block_rows), positions))
    return mixture.reshape(queries.shape)

def layer_row(params, states, memory, target_seg, source_seg):
    self_qkv, self_out, cross_q, cross_kv, cross_out, ffn_in, ffn_out, norm_gain, norm_bias, halt_weight, halt_bias = params
    row_len, width = states.shape
    heads = width // HEAD_DIM
    normed_one = low(norm_rows(states, norm_gain[0], norm_bias[0]))
    triple = low_back(low(jnp.einsum('td,dcf->tcf', normed_one, self_qkv, precision=highest)))
    triple = triple.reshape(row_len, 3, heads, HEAD_DIM)
    self_mix = attend(triple[:, 0], triple[:, 1], triple[:, 2], target_seg, target_seg, True)
    self_mix = low_back(low(self_mix.reshape(row_len, width)))
    hidden = states + low_back(jnp.dot(self_mix, self_out, precision=highest))
    normed_two = low(norm_rows(hidden, norm_gain[1], norm_bias[1]))
    cross_query = low_back(low(jnp.dot(normed_two, cross_q, precision=highest))).reshape(row_len, heads, HEAD_DIM)
    pair = low_back(low(jnp.einsum('td,dcf->tcf', memory, cross_kv, precision=highest)))
    pair = pair.reshape(row_len, 2, heads, HEAD_DIM)
    cross_mix = attend(cross_query, pair[:, 0], pair[:, 1], target_seg, source_seg, False)
    cross_mix = low_back(low(cross_mix.reshape(row_len, width)))
    hidden_two = hidden + low_back(jnp.dot(cross_mix, cross_out, precision=highest))
    normed_three = low(norm_rows(hidden_two, norm_gain[2], norm_bias[2]))
    inner = low_back(jnp.dot(normed_three, ffn_in, precision=highest))
    activated = low(jax.nn.gelu(inner))
    result = hidden_two + low_back(jnp.dot(activated, ffn_out, precision=highest))
    logits = jnp.dot(result, halt_weight, precision=highest) + halt_bias[0]
    return (result, logits)

def reference(layer_in, lengths, cotangent, targets, self_qkv, self_out, cross_q, cross_kv, cross_out, ffn_in, ffn_out, norm_gain, norm_bias, halt_weight, halt_bias):
    memory = layer_in[0].astype(jnp.float32).reshape(ROWS, ROW_LEN, D)
    states = layer_in[1].astype(jnp.float32).reshape(ROWS, ROW_LEN, D)
    source_seg = segments(lengths[0], ROW_LEN)
    target_seg = segments(lengths[1], ROW_LEN)
    params = tuple((weight.astype(jnp.float32) for weight in (self_qkv, self_out, cross_q, cross_kv, cross_out, ffn_in, ffn_out, norm_gain, norm_bias, halt_weight, halt_bias)))

    def forward(params, states, memory):

        def one_row(carry, pieces):
            return (carry, layer_row(params, pieces[0], pieces[1], pieces[2], pieces[3]))
        _, outputs = lax.scan(one_row, jnp.zeros((), jnp.float32), (states, memory, target_seg, source_seg))
        return outputs
    (result, logits), pullback = jax.vjp(forward, params, states, memory)
    logit_grad = jax.nn.sigmoid(logits) - targets.reshape(ROWS, ROW_LEN).astype(jnp.float32)
    out_grad = cotangent.astype(jnp.float32).reshape(ROWS, ROW_LEN, D)
    param_grads, state_grad, memory_grad = pullback((out_grad, logit_grad))
    layer_out = jnp.stack([layer_in[0], result.reshape(TOKENS, D).astype(jnp.bfloat16)])
    input_grads = jnp.stack([memory_grad.reshape(TOKENS, D), state_grad.reshape(TOKENS, D)])
    return (layer_out, input_grads, param_grads[0], param_grads[1], param_grads[2], param_grads[3], param_grads[4], param_grads[5], param_grads[6], param_grads[7], param_grads[8], param_grads[9], param_grads[10])
```

```python
import functools

import jax
import jax.numpy as jnp
from jax import lax
from jax.experimental import pallas as pl
from jax.experimental.pallas import tpu as pltpu
from jax.sharding import PartitionSpec as P

F32 = jnp.float32
BF16 = jnp.bfloat16

HEAD_DIM = 64
HALF = 256
HEADS = HALF // HEAD_DIM
HALO = 128
WINDOW = 128
MASKED = -1e30
VMEM_LIMIT = 56 * 1024 * 1024
ANY = pl.BlockSpec(memory_space=pl.ANY)
VMEM = pl.BlockSpec(memory_space=pltpu.VMEM)
SMEM = pl.BlockSpec(memory_space=pltpu.SMEM)
ARRIVALS = (0, 2, 1, 3)


def dot(a, b):
    return jnp.dot(a, b, preferred_element_type=F32)


def dot_nt(a, b):
    return lax.dot_general(a, b, (((1,), (1,)), ((), ())), preferred_element_type=F32)


def dot_tn(a, b):
    return lax.dot_general(a, b, (((0,), (0,)), ((), ())), preferred_element_type=F32)


def norm_parts(values):
    center = values - jnp.mean(values, axis=-1, keepdims=True)
    spread = jnp.mean(center * center, axis=-1, keepdims=True)
    scale = lax.rsqrt(spread + 1e-05)
    return center * scale, scale


def norm_back(grad, hat, scale, gain):
    grad_hat = grad * gain
    first = jnp.mean(grad_hat, axis=-1, keepdims=True)
    second = jnp.mean(grad_hat * hat, axis=-1, keepdims=True)
    return scale * (grad_hat - first - hat * second)


def start_weights(meta, own, arrived, held, sem):
    copies = [pltpu.make_async_copy(own, held.at[pl.ds(0, 4)], sem.at[0])]
    for at, (ref, flip) in enumerate(zip(arrived, ARRIVALS)):
        copies.append(pltpu.make_async_copy(ref, held.at[4 + (meta[1] ^ flip)], sem.at[1 + at]))
    for copy in copies:
        copy.start()
    return copies


def put_grads(meta, grads, keep, send, sem):
    rows = keep.shape[3]
    copies = []
    for half in range(2):
        for rel in range(4):
            at = 4 * half + (rel ^ meta[1])
            for z in range(4):
                first = pl.multiple_of((z ^ meta[2]) * rows, rows)
                target = (send if rel & 1 else keep).at[half, rel >> 1, z]
                copy = pltpu.make_async_copy(grads.at[at, pl.ds(first, rows)], target, sem.at[0])
                copy.start()
                copies.append(copy)
    return copies


def sentence_range(meta, segs, rows_here):
    first_row = meta[0] * rows_here

    def step(c, carry):
        target, source, low, high = carry
        target_end = target + segs[1, c]
        source_end = source + segs[0, c]
        mine = (target_end > first_row) & (target < first_row + rows_here)
        low = jnp.where(mine, jnp.minimum(low, source), low)
        high = jnp.where(mine, jnp.maximum(high, source_end), high)
        return target_end, source_end, low, high

    zero = jnp.int32(0)
    _, _, low, high = lax.fori_loop(0, segs.shape[1], step, (zero, zero, jnp.int32(1 << 20), zero))
    return low, high


def each_sentence(meta, segs, rows_here, body):
    first_row = meta[0] * rows_here

    def step(c, carry):
        target, source = carry
        target_end = target + segs[1, c]
        source_end = source + segs[0, c]

        @pl.when((target_end > first_row) & (target < first_row + rows_here))
        def _():
            shift = HALO - first_row
            body(target + shift, target_end + shift, source, source_end)

        return target_end, source_end

    lax.fori_loop(0, segs.shape[1], step, (jnp.int32(0), jnp.int32(0)))


def window_of(start):
    return pl.multiple_of((start // 16) * 16, 16)


def head_lanes():
    return lax.broadcasted_iota(jnp.int32, (1, HALF), 1) // HEAD_DIM


def spread_heads(block):
    lanes = head_lanes()
    return jnp.concatenate(
        [jnp.where(lanes == h, block, jnp.zeros_like(block)) for h in range(HEADS)], axis=0
    )


def join_heads(stacked):
    lanes = head_lanes()
    rows = stacked.shape[0] // HEADS
    total = jnp.zeros((rows, HALF), F32)
    for h in range(HEADS):
        total = jnp.where(lanes == h, stacked[h * rows : (h + 1) * rows], total)
    return total


def allowed_window(query_axis, q_first, q_low, q_high, k_first, k_low, k_high, causal):
    shape = (WINDOW, WINDOW)
    q = lax.broadcasted_iota(jnp.int32, shape, query_axis) + q_first
    k = lax.broadcasted_iota(jnp.int32, shape, 1 - query_axis) + k_first
    ok = (q >= q_low) & (q < q_high) & (k >= k_low) & (k < k_high)
    if causal:
        ok = ok & (k <= q)
    return ok


def attend_window(q, k, v, allowed):
    scale = jnp.asarray(HEAD_DIM**-0.5, BF16)
    scores = dot_nt(spread_heads(q * scale), k)
    allowed = jnp.concatenate([allowed] * HEADS, axis=0)
    scores = jnp.where(allowed, scores, MASKED)
    weights = jnp.exp(scores - jnp.max(scores, axis=-1, keepdims=True))
    inverse = 1.0 / jnp.sum(weights, axis=-1, keepdims=True)
    probabilities = jnp.where(allowed, weights * inverse, 0.0).astype(BF16)
    return join_heads(dot(probabilities, v))


def attend_window_back(q, k, v, grad, allowed):
    scale = HEAD_DIM**-0.5
    q_heads = spread_heads(q * jnp.asarray(scale, BF16))
    grad_heads = spread_heads(grad)
    allowed = jnp.concatenate([allowed] * HEADS, axis=1)
    scores = jnp.where(allowed, dot_nt(k, q_heads), MASKED)
    weights = jnp.exp(scores - jnp.max(scores, axis=0, keepdims=True))
    inverse = 1.0 / jnp.sum(weights, axis=0, keepdims=True)
    probabilities = jnp.where(allowed, weights * inverse, 0.0)
    prob_grad = dot_nt(v, grad_heads)
    inner = jnp.sum(probabilities * prob_grad, axis=0, keepdims=True)
    score_grad = (probabilities * (prob_grad - inner)).astype(BF16)
    q_grad = join_heads(dot_tn(score_grad, k)) * scale
    k_grad = dot(score_grad, q_heads)
    v_grad = dot(probabilities.astype(BF16), grad_heads)
    return q_grad, k_grad, v_grad


def out_product(mixes, held):
    left = sum(dot(mix, held[4 * half + 3, 0:HALF]) for half, mix in enumerate(mixes))
    right = sum(dot(mix, held[4 * half + 3, HALF:]) for half, mix in enumerate(mixes))
    return jnp.concatenate([left, right], axis=1)


def out_grads(grad_low, held, mixes, mix_grads, grads, first):
    rows = grad_low.shape[0]
    for half in range(2):
        at = 4 * half + 3
        for lo in range(0, rows, HALF):
            block = grad_low[lo : lo + HALF]
            mix_grad = dot_nt(block[:, :HALF], held[at, 0:HALF]) + dot_nt(
                block[:, HALF:], held[at, HALF:]
            )
            mix_grads[half, first + lo : first + lo + HALF] = mix_grad.astype(BF16)
        mix = mixes[half]
        grads[at, 0:HALF] = dot_tn(mix, grad_low[:, :HALF]).astype(BF16)
        grads[at, HALF:] = dot_tn(mix, grad_low[:, HALF:]).astype(BF16)


def copy_by_role(meta, pairs_zero, pairs_one, sem):
    @pl.when(meta[0] == 0)
    def _():
        for source, target in pairs_zero:
            pltpu.make_async_copy(source, target, sem).start()

    @pl.when(meta[0] == 1)
    def _():
        for source, target in pairs_one:
            pltpu.make_async_copy(source, target, sem).start()


def wait_by_role(meta, pairs_zero, pairs_one, sem):
    @pl.when(meta[0] == 0)
    def _():
        for source, target in pairs_zero:
            pltpu.make_async_copy(source, target, sem).wait()

    @pl.when(meta[0] == 1)
    def _():
        for source, target in pairs_one:
            pltpu.make_async_copy(source, target, sem).wait()


def states_copies(rows_ref, other_ref, held, here):
    zero = [(other_ref.at[pl.ds(0, here)], held.at[pl.ds(HALO, here)])]
    one = [(rows_ref.at[pl.ds(here - HALO, here + HALO)], held.at[pl.ds(0, here + HALO)])]
    return zero, one


def self_forward(
    meta, segs, rows_ref, other_ref, gain, bias, own, w1, w2, w3, w4,
    hidden, mix, qkv, held, states, mixed, sem_w, sem_x,
):
    here = hidden.shape[0]
    full = here + HALO
    state_copies = states_copies(rows_ref, other_ref, states, here)
    copy_by_role(meta, *state_copies, sem_x)
    weights = start_weights(meta, own, (w1, w2, w3, w4), held, sem_w)
    qkv[:, :, full:] = jnp.zeros((2, 3, WINDOW, HALF), BF16)
    mixed[...] = jnp.zeros(mixed.shape, F32)
    wait_by_role(meta, *state_copies, sem_x)

    @pl.when(meta[0] == 0)
    def _():
        states[0:HALO] = jnp.zeros((HALO, states.shape[1]), BF16)

    for copy in weights:
        copy.wait()
    step = full // 2
    for lo in range(0, full, step):
        hat, _ = norm_parts(states[lo : lo + step].astype(F32))
        normed = (hat * gain[0:1] + bias[0:1]).astype(BF16)
        for half in range(2):
            for c in range(3):
                qkv[half, c, lo : lo + step] = dot(normed, held[4 * half + c]).astype(BF16)

    def sentence(low, high, _low, _high):
        first = window_of(low)
        allowed = allowed_window(
            0, first, jnp.maximum(low, HALO), jnp.minimum(high, full), first, low, high, True
        )
        at = pl.ds(first, WINDOW)
        for half in range(2):
            mixed[half, at] += attend_window(qkv[half, 0, at], qkv[half, 1, at], qkv[half, 2, at], allowed)

    each_sentence(meta, segs, here, sentence)
    mix[...] = mixed[:, HALO:full].astype(BF16)
    for lo in range(0, here, HALF):
        at = slice(lo, lo + HALF)
        hidden[at] = states[HALO + lo : HALO + lo + HALF].astype(F32) + out_product(
            [mix[0, at], mix[1, at]], held
        )


def memory_copies(rows_ref, other_ref, held):
    return [(rows_ref, held)], [(other_ref, held)]


def cross_forward(
    meta, segs, rows_ref, other_ref, hidden, gain, bias, own, w1, w2, w3, w4,
    hidden_two, mix, queries, pairs, held, memory, mixed, sem_w, sem_x,
):
    here = hidden.shape[0]
    full = here + HALO
    copies = memory_copies(rows_ref, other_ref, memory)
    copy_by_role(meta, *copies, sem_x)
    weights = start_weights(meta, own, (w1, w2, w3, w4), held, sem_w)
    queries[:, 0:HALO] = jnp.zeros((2, HALO, HALF), BF16)
    queries[:, full:] = jnp.zeros((2, WINDOW, HALF), BF16)
    mixed[...] = jnp.zeros(mixed.shape, F32)
    pairs[...] = jnp.zeros(pairs.shape, BF16)
    low, high = sentence_range(meta, segs, here)
    wait_by_role(meta, *copies, sem_x)
    for copy in weights:
        copy.wait()

    def project(block, _):
        at = pl.ds(pl.multiple_of(block * HALF, HALF), HALF)
        for half in range(2):
            for c in range(2):
                pairs[half, c, at] = dot(memory[at], held[4 * half + 1 + c]).astype(BF16)
        return 0

    lax.fori_loop(low // HALF, (high + HALF - 1) // HALF, project, 0)
    for lo in range(0, here, HALF):
        hat, _ = norm_parts(hidden[lo : lo + HALF])
        normed = (hat * gain[1:2] + bias[1:2]).astype(BF16)
        for half in range(2):
            queries[half, HALO + lo : HALO + lo + HALF] = dot(normed, held[4 * half]).astype(BF16)

    def sentence(low, high, source_low, source_high):
        first = window_of(low)
        source_first = window_of(source_low)
        allowed = allowed_window(
            0, first, jnp.maximum(low, HALO), jnp.minimum(high, full),
            source_first, source_low, source_high, False,
        )
        at = pl.ds(first, WINDOW)
        source_at = pl.ds(source_first, WINDOW)
        for half in range(2):
            mixed[half, at] += attend_window(
                queries[half, at], pairs[half, 0, source_at], pairs[half, 1, source_at], allowed
            )

    each_sentence(meta, segs, here, sentence)
    mix[...] = mixed[:, HALO:full].astype(BF16)
    for lo in range(0, here, HALF):
        at = slice(lo, lo + HALF)
        hidden_two[at] = hidden[at] + out_product([mix[0, at], mix[1, at]], held)


def gelu_both(inner):
    rate = 0.7978845608028654
    square = inner * inner
    bent = jnp.tanh(rate * inner * (1.0 + 0.044715 * square))
    half = 0.5 * (1.0 + bent)
    slope = half + 0.5 * inner * (1.0 - bent * bent) * (rate * (1.0 + 3 * 0.044715 * square))
    return inner * half, slope


def feed_forward(
    meta, hidden_two, cotangent, targets, gain, bias, halt_weight, halt_bias,
    own_in, i1, i2, i3, i4, own_out, o1, o2, o3, o4,
    result_low, hidden_grad, small, keep_in, send_in, keep_out, send_out,
    held_in, held_out, normed, active, slopes, total, out_low, cot, tgt, grads_in, grads_out,
    sem_w, sem_o, sem_x, sem_g,
):
    here = hidden_two.shape[0]
    first = pl.multiple_of(meta[0] * here, here)
    cot_copy = pltpu.make_async_copy(cotangent.at[pl.ds(first, here)], cot, sem_x.at[0])
    tgt_copy = pltpu.make_async_copy(targets.at[pl.ds(first, here)], tgt, sem_x.at[1])
    weights = start_weights(meta, own_in, (i1, i2, i3, i4), held_in, sem_w)
    weights += start_weights(meta, own_out, (o1, o2, o3, o4), held_out, sem_o)
    cot_copy.start()
    tgt_copy.start()
    blocks = [slice(lo, lo + HALF) for lo in range(0, here, HALF)]
    for at in blocks:
        hat, _ = norm_parts(hidden_two[at])
        normed[at] = (hat * gain[2:3] + bias[2:3]).astype(BF16)
        total[at] = hidden_two[at]
    for copy in weights:
        copy.wait()

    def forward(j, _):
        for at in blocks:
            value, slope = gelu_both(dot(normed[at], held_in[j]))
            value = value.astype(BF16)
            active[j, at] = value
            slopes[j, at] = slope
            total[at] += dot(value, held_out[j])
        return 0

    lax.fori_loop(0, 8, forward, 0)
    cot_copy.wait()
    tgt_copy.wait()
    weight_sum = jnp.zeros((1, halt_weight.shape[1]), F32)
    bias_sum = jnp.zeros((1, 1), F32)
    for at in blocks:
        result = total[at]
        result_low[at] = result.astype(BF16)
        logits = jnp.sum(result * halt_weight[...], axis=-1, keepdims=True) + halt_bias[0]
        halt_grad = 1.0 / (1.0 + jnp.exp(-logits)) - tgt[at]
        out_grad = cot[at].astype(F32) + halt_grad * halt_weight[...]
        out_low[at] = out_grad.astype(BF16)
        hidden_grad[at] = out_grad
        total[at] = jnp.zeros((HALF, result.shape[1]), F32)
        weight_sum += jnp.sum(halt_grad * result, axis=0, keepdims=True)
        bias_sum += jnp.sum(halt_grad, axis=0, keepdims=True)

    def backward(j, _):
        inner_grads = []
        for at in blocks:
            inner_grad = (dot_nt(out_low[at], held_out[j]) * slopes[j, at]).astype(BF16)
            inner_grads.append(inner_grad)
            total[at] += dot_nt(inner_grad, held_in[j])
        grads_in[j] = dot_tn(normed[...], jnp.concatenate(inner_grads, axis=0)).astype(BF16)
        grads_out[j] = dot_tn(active[j], out_low[...]).astype(BF16)
        return 0

    lax.fori_loop(0, 8, backward, 0)
    copies = put_grads(meta, grads_in, keep_in, send_in, sem_g)
    copies += put_grads(meta, grads_out, keep_out, send_out, sem_g)
    gain_sum = jnp.zeros_like(weight_sum)
    shift_sum = jnp.zeros_like(weight_sum)
    for at in blocks:
        hat, scale = norm_parts(hidden_two[at])
        grad = total[at]
        hidden_grad[at] += norm_back(grad, hat, scale, gain[2:3])
        gain_sum += jnp.sum(grad * hat, axis=0, keepdims=True)
        shift_sum += jnp.sum(grad, axis=0, keepdims=True)
    small[...] = jnp.concatenate(
        [gain_sum, shift_sum, weight_sum, jnp.broadcast_to(bias_sum, weight_sum.shape)], axis=0
    )
    for copy in copies:
        copy.wait()


def cross_backward(
    meta, segs, rows_ref, other_ref, hidden, upper_grad, mix, queries, pairs, gain, bias,
    own, w1, w2, w3, w4,
    lower_grad, memory_grad, small, keep, send,
    held, memory, mix_grads, q_grad, pair_grads, pair_sums, grads, sem_w, sem_x, sem_g,
):
    here, width = hidden.shape
    full = here + HALO
    copies = memory_copies(rows_ref, other_ref, memory)
    copy_by_role(meta, *copies, sem_x)
    weights = start_weights(meta, own, (w1, w2, w3, w4), held, sem_w)
    mix_grads[:, 0:HALO] = jnp.zeros((2, HALO, HALF), BF16)
    mix_grads[:, full:] = jnp.zeros((2, WINDOW, HALF), BF16)
    q_grad[...] = jnp.zeros(q_grad.shape, F32)
    pair_grads[...] = jnp.zeros(pair_grads.shape, F32)
    pair_sums[...] = jnp.zeros(pair_sums.shape, F32)
    memory_grad[...] = jnp.zeros(memory_grad.shape, BF16)
    source_low, source_high = sentence_range(meta, segs, here)
    for copy in weights:
        copy.wait()
    out_grads(upper_grad[...].astype(BF16), held, [mix[0], mix[1]], mix_grads, grads, HALO)

    def sentence(low, high, source_low, source_high):
        first = window_of(low)
        source_first = window_of(source_low)
        allowed = allowed_window(
            1, first, jnp.maximum(low, HALO), jnp.minimum(high, full),
            source_first, source_low, source_high, False,
        )
        at = pl.ds(first, WINDOW)
        source_at = pl.ds(source_first, WINDOW)
        for half in range(2):
            dq, dk, dv = attend_window_back(
                queries[half, at], pairs[half, 0, source_at], pairs[half, 1, source_at],
                mix_grads[half, at], allowed,
            )
            q_grad[half, at] += dq
            pair_grads[half, 0, source_at] += dk
            pair_grads[half, 1, source_at] += dv

    each_sentence(meta, segs, here, sentence)
    wait_by_role(meta, *copies, sem_x)

    def project(block, _):
        at = pl.ds(pl.multiple_of(block * HALF, HALF), HALF)
        row_grad = jnp.zeros((HALF, width), F32)
        for half in range(2):
            for c in range(2):
                low = pair_grads[half, c, at].astype(BF16)
                row_grad += dot_nt(low, held[4 * half + 1 + c])
                pair_sums[half, c] += dot_tn(memory[at], low)
        memory_grad[at] = row_grad.astype(BF16)
        return 0

    lax.fori_loop(source_low // HALF, (source_high + HALF - 1) // HALF, project, 0)
    for half in range(2):
        for c in range(2):
            grads[4 * half + 1 + c] = pair_sums[half, c].astype(BF16)
    gain_sum = jnp.zeros((1, width), F32)
    shift_sum = jnp.zeros((1, width), F32)
    normed = []
    q_low = [q_grad[half, HALO:full].astype(BF16) for half in range(2)]
    for lo in range(0, here, HALF):
        at = slice(lo, lo + HALF)
        hat, scale = norm_parts(hidden[at])
        normed.append((hat * gain[1:2] + bias[1:2]).astype(BF16))
        grad = dot_nt(q_low[0][at], held[0]) + dot_nt(q_low[1][at], held[4])
        lower_grad[at] = upper_grad[at] + norm_back(grad, hat, scale, gain[1:2])
        gain_sum += jnp.sum(grad * hat, axis=0, keepdims=True)
        shift_sum += jnp.sum(grad, axis=0, keepdims=True)
    normed = jnp.concatenate(normed, axis=0)
    for half in range(2):
        grads[4 * half] = dot_tn(normed, q_low[half]).astype(BF16)
    put = put_grads(meta, grads, keep, send, sem_g)
    small[...] = jnp.concatenate([gain_sum, shift_sum], axis=0)
    for copy in put:
        copy.wait()


def self_backward(
    meta, segs, rows_ref, other_ref, upper_grad, mix, qkv, gain, bias, own, w1, w2, w3, w4,
    state_grad, halo_grad, small, keep, send,
    held, states, mix_grads, qkv_grads, grads, sem_w, sem_x, sem_g,
):
    here, width = upper_grad.shape
    full = here + HALO
    state_copies = states_copies(rows_ref, other_ref, states, here)
    copy_by_role(meta, *state_copies, sem_x)
    weights = start_weights(meta, own, (w1, w2, w3, w4), held, sem_w)
    mix_grads[:, 0:HALO] = jnp.zeros((2, HALO, HALF), BF16)
    mix_grads[:, full:] = jnp.zeros((2, WINDOW, HALF), BF16)
    qkv_grads[...] = jnp.zeros(qkv_grads.shape, F32)
    wait_by_role(meta, *state_copies, sem_x)

    @pl.when(meta[0] == 0)
    def _():
        states[0:HALO] = jnp.zeros((HALO, width), BF16)

    for copy in weights:
        copy.wait()
    out_grads(upper_grad[...].astype(BF16), held, [mix[0], mix[1]], mix_grads, grads, HALO)

    def sentence(low, high, _low, _high):
        first = window_of(low)
        allowed = allowed_window(
            1, first, jnp.maximum(low, HALO), jnp.minimum(high, full), first, low, high, True
        )
        at = pl.ds(first, WINDOW)
        for half in range(2):
            back = attend_window_back(
                qkv[half, 0, at], qkv[half, 1, at], qkv[half, 2, at], mix_grads[half, at], allowed
            )
            for c in range(3):
                qkv_grads[half, c, at] += back[c]

    each_sentence(meta, segs, here, sentence)
    gain_sum = jnp.zeros((1, width), F32)
    shift_sum = jnp.zeros((1, width), F32)
    normed = []
    step = full // 2
    for lo in range(0, full, step):
        at = slice(lo, lo + step)
        hat, scale = norm_parts(states[at].astype(F32))
        normed.append((hat * gain[0:1] + bias[0:1]).astype(BF16))
        grad = jnp.zeros((step, width), F32)
        for half in range(2):
            for c in range(3):
                grad += dot_nt(qkv_grads[half, c, at].astype(BF16), held[4 * half + c])
        back = norm_back(grad, hat, scale, gain[0:1])
        if lo == 0:
            halo_grad[...] = back[:HALO]
            state_grad[0 : step - HALO] = upper_grad[0 : step - HALO] + back[HALO:]
        else:
            state_grad[lo - HALO :] = upper_grad[lo - HALO :] + back
        gain_sum += jnp.sum(grad * hat, axis=0, keepdims=True)
        shift_sum += jnp.sum(grad, axis=0, keepdims=True)
    normed = jnp.concatenate(normed, axis=0)
    for half in range(2):
        for c in range(3):
            grads[4 * half + c] = dot_tn(normed, qkv_grads[half, c, 0:full].astype(BF16)).astype(BF16)
    put = put_grads(meta, grads, keep, send, sem_g)
    small[...] = jnp.concatenate([gain_sum, shift_sum], axis=0)
    for copy in put:
        copy.wait()


def unpack(kind, meta, mine, by_x, by_role, by_both, *rest):
    outs, (held, sem) = rest[:-2], rest[-2:]
    rows = mine.shape[1]
    copies = []
    for rel, ref in ((0, mine), (2, by_x), (1, by_role), (3, by_both)):
        for z in range(4):
            first = pl.multiple_of((z ^ meta[2]) * rows, rows)
            copy = pltpu.make_async_copy(
                ref.at[z], held.at[rel ^ meta[1], pl.ds(first, rows)], sem.at[0]
            )
            copy.start()
            copies.append(copy)
    for copy in copies:
        copy.wait()
    if kind == "rows":
        for j in range(4):
            outs[0][j * 4 * rows : (j + 1) * 4 * rows] = held[j].astype(F32)
        return
    if kind == "columns":
        for j in range(4):
            outs[0][:, j * HALF : (j + 1) * HALF] = held[j].astype(F32)
        return
    at = 0
    for out in outs[:-1]:
        for c in range(out.shape[1] // HALF):
            out[:, c * HALF : (c + 1) * HALF] = held[at].astype(F32)
            at += 1
    outs[-1][:, 0:HALF] = held[3, 0:HALF].astype(F32)
    outs[-1][:, HALF:] = held[3, HALF:].astype(F32)


def shape(*dims, dtype=F32):
    return jax.ShapeDtypeStruct(dims, dtype)


def call(body, outs, out_specs, scratch, flops, name, in_specs):
    return pl.pallas_call(
        body,
        out_shape=outs,
        in_specs=in_specs,
        out_specs=out_specs,
        scratch_shapes=scratch,
        name=name,
        compiler_params=pltpu.CompilerParams(vmem_limit_bytes=VMEM_LIMIT),
        cost_estimate=pl.CostEstimate(flops=flops, bytes_accessed=10_000_000, transcendentals=0),
    )


def flip(value, axis, bit=1):
    count = lax.axis_size(axis)
    return lax.ppermute(value, axis, [(i, i ^ bit) for i in range(count)])


def add(a, b):
    return (a.astype(F32) + b.astype(F32)).astype(BF16)


def fetch_other(own, me):
    first = flip(lax.dynamic_index_in_dim(own, me, 0, keepdims=False), "head")
    second = flip(first, "dp", 1)
    return own, first, second, flip(first, "role"), flip(second, "role")


def reduce_sum(keep, send):
    got = flip(send, "role")
    away, near = add(keep[1], got[1]), add(keep[0], got[0])
    got = flip(away, "head")
    away, near = add(near[1], got[1]), add(near[0], got[0])
    got = flip(away, "dp", 1)
    away, near = add(near[2:], got[2:]), add(near[:2], got[:2])
    got = flip(away, "dp", 2)
    away, near = add(near[1], got[1]), add(near[0], got[0])
    total = add(near, flip(away, "dp", 4))
    bit = 8
    while bit < lax.axis_size("dp"):
        total = add(total, flip(total, "dp", bit))
        bit *= 2
    return total


def spread_sum(total):
    beside = flip(total, "dp", 4)
    mine = jnp.stack([total, beside, flip(total, "dp", 2), flip(beside, "dp", 2)])
    by_x = flip(mine, "dp", 1)
    return mine, by_x, flip(mine, "role"), flip(by_x, "role")


def all_sum(value):
    value = value + flip(value, "role")
    value = value + flip(value, "head")
    bit = 1
    while bit < lax.axis_size("dp"):
        value = value + flip(value, "dp", bit)
        bit *= 2
    return value


def shards(
    layer_in,
    lengths,
    cotangent,
    targets,
    self_qkv,
    self_out,
    cross_q,
    cross_kv,
    cross_out,
    ffn_in,
    ffn_out,
    norm_gain,
    norm_bias,
    halt_weight,
    halt_bias,
):
    role, head, place = (lax.axis_index(name) for name in ("role", "head", "dp"))
    target_side = role == 1
    me = 2 * (place & 1) + role
    z_me = (place & 2) + ((place >> 2) & 1)
    meta = jnp.stack([role, me, z_me, head]).astype(jnp.int32)
    rows = layer_in[0]
    row_len, width = rows.shape
    here = row_len // 2
    full = here + HALO

    other_rows = flip(rows, "role")
    lens = lax.dynamic_index_in_dim(lengths[0], head, 0, keepdims=False)
    other_lens = flip(lens, "role")
    segs = jnp.where(target_side, jnp.stack([other_lens, lens]), jnp.stack([lens, other_lens]))

    def halves(out):
        return jnp.concatenate([out[:, :HALF], out[:, HALF:]], axis=0)[None]

    self_own = jnp.concatenate([self_qkv.transpose(1, 0, 2), halves(self_out)], axis=0)
    cross_own = jnp.concatenate(
        [cross_q[None], cross_kv.transpose(1, 0, 2), halves(cross_out)], axis=0
    )
    in_own = ffn_in.reshape(width, 4, HALF).transpose(1, 0, 2)
    out_own = ffn_out.reshape(4, HALF, width)
    self_weights = fetch_other(self_own, me)
    cross_weights = fetch_other(cross_own, me)
    in_weights = fetch_other(in_own, me)
    out_weights = fetch_other(out_own, me)

    weight_specs = [ANY] * 5
    held = pltpu.VMEM((8, width, HALF), BF16)
    weight_sems = pltpu.SemaphoreType.DMA((5,))
    one_sem = pltpu.SemaphoreType.DMA
    dense = 2 * here * width * HALF * 8

    hidden, self_mix, qkv = call(
        self_forward,
        (shape(here, width), shape(2, here, HALF, dtype=BF16), shape(2, 3, full + WINDOW, HALF, dtype=BF16)),
        (VMEM,) * 3,
        [held, pltpu.VMEM((full, width), BF16), pltpu.VMEM((2, full + WINDOW, HALF), F32), weight_sems, one_sem],
        2 * dense,
        "self_forward",
        [SMEM, SMEM, ANY, ANY, VMEM, VMEM] + weight_specs,
    )(meta, segs, rows, other_rows, norm_gain, norm_bias, *self_weights)

    hidden_two, cross_mix, queries, pairs = call(
        cross_forward,
        (
            shape(here, width),
            shape(2, here, HALF, dtype=BF16),
            shape(2, full + WINDOW, HALF, dtype=BF16),
            shape(2, 2, row_len + WINDOW, HALF, dtype=BF16),
        ),
        (VMEM,) * 4,
        [held, pltpu.VMEM((row_len, width), BF16), pltpu.VMEM((2, full + WINDOW, HALF), F32), weight_sems, one_sem],
        2 * dense,
        "cross_forward",
        [SMEM, SMEM, ANY, ANY, VMEM, VMEM, VMEM] + weight_specs,
    )(meta, segs, rows, other_rows, hidden, norm_gain, norm_bias, *cross_weights)

    grad_parts = shape(2, 2, 4, width // 4, HALF, dtype=BF16)
    out_parts = shape(2, 2, 4, HALF // 4, width, dtype=BF16)
    grad_sems = pltpu.SemaphoreType.DMA((1,))
    result_low, two_grad, ffn_small, keep_in, send_in, keep_out, send_out = call(
        feed_forward,
        (shape(here, width, dtype=BF16), shape(here, width), shape(4, width), grad_parts, grad_parts, out_parts, out_parts),
        (VMEM, VMEM, VMEM, ANY, ANY, ANY, ANY),
        [
            held,
            pltpu.VMEM((8, HALF, width), BF16),
            pltpu.VMEM((here, width), BF16),
            pltpu.VMEM((8, here, HALF), BF16),
            pltpu.VMEM((8, here, HALF), F32),
            pltpu.VMEM((here, width), F32),
            pltpu.VMEM((here, width), BF16),
            pltpu.VMEM((here, width), BF16),
            pltpu.VMEM((here, 1), F32),
            pltpu.VMEM((8, width, HALF), BF16),
            pltpu.VMEM((8, HALF, width), BF16),
            weight_sems,
            weight_sems,
            pltpu.SemaphoreType.DMA((2,)),
            grad_sems,
        ],
        6 * dense,
        "feed_forward",
        [SMEM, VMEM, ANY, ANY, VMEM, VMEM, VMEM, SMEM] + weight_specs * 2,
    )(
        meta, hidden_two, cotangent, targets.astype(F32)[:, None], norm_gain, norm_bias,
        halt_weight[None], halt_bias, *in_weights, *out_weights,
    )

    one_grad, memory_part, cross_small, keep_cross, send_cross = call(
        cross_backward,
        (shape(here, width), shape(row_len, width, dtype=BF16), shape(2, width), grad_parts, grad_parts),
        (VMEM, VMEM, VMEM, ANY, ANY),
        [
            held,
            pltpu.VMEM((row_len, width), BF16),
            pltpu.VMEM((2, full + WINDOW, HALF), BF16),
            pltpu.VMEM((2, full + WINDOW, HALF), F32),
            pltpu.VMEM((2, 2, row_len + WINDOW, HALF), F32),
            pltpu.VMEM((2, 2, width, HALF), F32),
            pltpu.VMEM((8, width, HALF), BF16),
            weight_sems,
            one_sem,
            grad_sems,
        ],
        4 * dense,
        "cross_backward",
        [SMEM, SMEM, ANY, ANY] + [VMEM] * 7 + weight_specs,
    )(
        meta, segs, rows, other_rows, hidden, two_grad, cross_mix, queries, pairs, norm_gain, norm_bias,
        *cross_weights,
    )

    state_grad, halo_grad, self_small, keep_self, send_self = call(
        self_backward,
        (shape(here, width), shape(HALO, width), shape(2, width), grad_parts, grad_parts),
        (VMEM, VMEM, VMEM, ANY, ANY),
        [
            held,
            pltpu.VMEM((full, width), BF16),
            pltpu.VMEM((2, full + WINDOW, HALF), BF16),
            pltpu.VMEM((2, 3, full + WINDOW, HALF), F32),
            pltpu.VMEM((8, width, HALF), BF16),
            weight_sems,
            one_sem,
            grad_sems,
        ],
        4 * dense,
        "self_backward",
        [SMEM, SMEM, ANY, ANY] + [VMEM] * 5 + weight_specs,
    )(
        meta, segs, rows, other_rows, one_grad, self_mix, qkv, norm_gain, norm_bias, *self_weights,
    )

    def totals(kind, keep, send, out_shapes):
        pieces = spread_sum(reduce_sum(keep, send))
        rows_each = keep.shape[3]
        return call(
            functools.partial(unpack, kind),
            out_shapes,
            (VMEM,) * len(out_shapes),
            [pltpu.VMEM((4, 4 * rows_each, keep.shape[4]), BF16), pltpu.SemaphoreType.DMA((1,))],
            0,
            "unpack_" + kind,
            [SMEM] + [ANY] * 4,
        )(meta, *pieces)

    (ffn_out_grad,) = totals("rows", keep_out, send_out, (shape(4 * HALF, width),))
    (ffn_in_grad,) = totals("columns", keep_in, send_in, (shape(width, 4 * HALF),))
    cross_q_grad, cross_kv_grad, cross_out_grad = totals(
        "mixed", keep_cross, send_cross, (shape(width, HALF), shape(width, 2 * HALF), shape(HALF, width))
    )
    self_qkv_grad, self_out_grad = totals(
        "mixed", keep_self, send_self, (shape(width, 3 * HALF), shape(HALF, width))
    )

    small = all_sum(
        jnp.concatenate(
            [
                self_small[0:1], cross_small[0:1], ffn_small[0:1],
                self_small[1:2], cross_small[1:2], ffn_small[1:2], ffn_small[2:4],
            ],
            axis=0,
        )
    )

    to_target, to_memory = [(0, 1)], [(1, 0)]
    low_result = lax.ppermute(result_low, "role", to_target)
    low_grad = lax.ppermute(state_grad.astype(BF16), "role", to_target).astype(F32)
    other_memory = lax.ppermute(memory_part, "role", to_memory)
    layer_out = jnp.where(
        target_side, jnp.concatenate([low_result, result_low], axis=0), rows
    )[None]
    halo_rows = jnp.concatenate(
        [jnp.zeros((here - HALO, width), F32), halo_grad, jnp.zeros((here, width), F32)], axis=0
    )
    target_grads = jnp.concatenate([low_grad, state_grad], axis=0) + halo_rows
    memory_grads = memory_part.astype(F32) + other_memory.astype(F32)
    input_grads = jnp.where(target_side, target_grads, memory_grads)[None]
    return (
        layer_out,
        input_grads,
        self_qkv_grad.reshape(width, 3, HALF),
        self_out_grad,
        cross_q_grad,
        cross_kv_grad.reshape(width, 2, HALF),
        cross_out_grad,
        ffn_in_grad,
        ffn_out_grad,
        small[0:3],
        small[3:6],
        small[6],
        small[7, 0:1],
    )


def solution(mesh):
    placed = (
        P("role", ("dp", "head"), None),
        P("role", "dp", None),
        P(("dp", "head"), None),
        P(("dp", "head")),
        P(None, None, "head"),
        P("head", None),
        P(None, "head"),
        P(None, None, "head"),
        P("head", None),
        P(None, "head"),
        P("head", None),
        P(),
        P(),
        P(),
        P(),
    )
    return jax.shard_map(
        shards,
        mesh=mesh,
        in_specs=placed,
        out_specs=(
            P("role", ("dp", "head"), None),
            P("role", ("dp", "head"), None),
            P(None, None, "head"),
            P("head", None),
            P(None, "head"),
            P(None, None, "head"),
            P("head", None),
            P(None, "head"),
            P("head", None),
            P(),
            P(),
            P(),
            P(),
        ),
        check_vma=False,
    )
```

```python
import functools

import jax
import jax.numpy as jnp
from jax import lax
from jax.experimental import pallas as pl
from jax.experimental.pallas import tpu as pltpu
from jax.sharding import PartitionSpec as P

F32 = jnp.float32
BF16 = jnp.bfloat16

HEAD_DIM = 64
HALF = 256
HEADS = HALF // HEAD_DIM
HALO = 128
GROUPS = 2
WINDOW = 128
MASKED = -1e30
VMEM_LIMIT = 32 * 1024 * 1024
ANY = pl.BlockSpec(memory_space=pl.ANY)
VMEM = pl.BlockSpec(memory_space=pltpu.VMEM)
SMEM = pl.BlockSpec(memory_space=pltpu.SMEM)
ARRIVALS = (0, 2, 1, 3)


def dot(a, b):
    return jnp.dot(a, b, preferred_element_type=F32)


def dot_nt(a, b):
    return lax.dot_general(a, b, (((1,), (1,)), ((), ())), preferred_element_type=F32)


def dot_tn(a, b):
    return lax.dot_general(a, b, (((0,), (0,)), ((), ())), preferred_element_type=F32)


def norm_parts(values):
    center = values - jnp.mean(values, axis=-1, keepdims=True)
    spread = jnp.mean(center * center, axis=-1, keepdims=True)
    scale = lax.rsqrt(spread + 1e-05)
    return center * scale, scale


def norm_back(grad, hat, scale, gain):
    grad_hat = grad * gain
    first = jnp.mean(grad_hat, axis=-1, keepdims=True)
    second = jnp.mean(grad_hat * hat, axis=-1, keepdims=True)
    return scale * (grad_hat - first - hat * second)


def start_weights(meta, own, arrived, held, sem):
    copies = [pltpu.make_async_copy(own, held.at[pl.ds(0, 4)], sem.at[0])]
    for at, (ref, flip) in enumerate(zip(arrived, ARRIVALS)):
        copies.append(pltpu.make_async_copy(ref, held.at[4 + (meta[1] ^ flip)], sem.at[1 + at]))
    for copy in copies:
        copy.start()
    return copies


def put_grads(meta, grads, keep, send, sem):
    rows = keep.shape[3]
    copies = []
    for half in range(2):
        for rel in range(4):
            at = 4 * half + (rel ^ meta[1])
            for part in range(grads.shape[1] // rows):
                target = (send if rel & 1 else keep).at[part, half, rel >> 1]
                copy = pltpu.make_async_copy(
                    grads.at[at, pl.ds(part * rows, rows)], target, sem.at[0]
                )
                copy.start()
                copies.append(copy)
    return copies


def sentence_range(meta, segs, rows_here):
    first_row = meta[0] * rows_here

    def step(c, carry):
        target, source, low, high = carry
        target_end = target + segs[1, c]
        source_end = source + segs[0, c]
        mine = (target_end > first_row) & (target < first_row + rows_here)
        low = jnp.where(mine, jnp.minimum(low, source), low)
        high = jnp.where(mine, jnp.maximum(high, source_end), high)
        return target_end, source_end, low, high

    zero = jnp.int32(0)
    _, _, low, high = lax.fori_loop(0, segs.shape[1] - 2, step, (zero, zero, jnp.int32(1 << 20), zero))
    return low, high


def each_group(meta, segs, plan, rows_here, cross, compute, store):
    first_row = meta[0] * rows_here
    last_row = first_row + rows_here
    shift = HALO - first_row

    def step(c, carry):
        t0, s0, done, count = carry
        t1, s1 = t0 + segs[1, c], s0 + segs[0, c]
        t2, s2 = t1 + segs[1, c + 1], s1 + segs[0, c + 1]
        t3, s3 = t2 + segs[1, c + 2], s2 + segs[0, c + 2]
        target_end, source_end = window_of(t0) + WINDOW, window_of(s0) + WINDOW
        two = (t2 <= target_end) & (t1 < last_row)
        three = two & (t3 <= target_end) & (t2 < last_row)
        if cross:
            two = two & (s2 <= source_end)
            three = three & (s3 <= source_end) & two
        t2, s2 = jnp.where(two, t2, t1), jnp.where(two, s2, s1)
        t3, s3 = jnp.where(three, t3, t2), jnp.where(three, s3, s2)
        here = (c >= done) & (t1 > first_row) & (t0 < last_row)
        for at, bound in enumerate((t0, t1, t2, t3)):
            plan[at, count] = bound + shift
        for at, bound in enumerate((s0, s1, s2, s3)):
            plan[4 + at, count] = bound
        size = 1 + two.astype(jnp.int32) + three.astype(jnp.int32)
        return t1, s1, jnp.where(here, c + size, done), count + here.astype(jnp.int32)

    zero = jnp.int32(0)
    count = lax.fori_loop(0, segs.shape[1] - 2, step, (zero, zero, zero, zero))[3]
    for g in range(GROUPS):
        for at in range(8):
            plan[at, count + g] = 0

    def some(i, _):
        bounds = [
            (
                [plan[at, i * GROUPS + g] for at in range(4)],
                [plan[4 + at, i * GROUPS + g] for at in range(4)],
            )
            for g in range(GROUPS)
        ]
        results = [compute(*each) for each in bounds]
        for each, result in zip(bounds, results):
            store(*each, result)
        return 0

    lax.fori_loop(0, (count + GROUPS - 1) // GROUPS, some, 0)


def window_of(start):
    return pl.multiple_of((start // 16) * 16, 16)


def spread_lanes(block):
    lanes = lax.broadcasted_iota(jnp.int32, (1, HALF), 1) // HEAD_DIM
    return jnp.concatenate(
        [jnp.where(lanes == h, block, jnp.zeros_like(block)) for h in range(HEADS)], axis=0
    )


def spread_rows(block):
    none = jnp.zeros((HEAD_DIM, block.shape[1]), block.dtype)
    return jnp.concatenate(
        [
            jnp.concatenate(
                [block[g * HEAD_DIM : (g + 1) * HEAD_DIM] if g == h else none for g in range(HEADS)],
                axis=0,
            )
            for h in range(HEADS)
        ],
        axis=1,
    )


def join_rows(spread):
    columns = spread.shape[1] // HEADS
    return jnp.concatenate(
        [
            spread[h * HEAD_DIM : (h + 1) * HEAD_DIM, h * columns : (h + 1) * columns]
            for h in range(HEADS)
        ],
        axis=0,
    )


def window_mask(q_first, q_bounds, k_first, k_bounds, q_low, q_high, causal):
    q = lax.broadcasted_iota(jnp.int32, (1, WINDOW), 1) + q_first
    k = lax.broadcasted_iota(jnp.int32, (WINDOW, WINDOW), 0) + k_first
    q_id = sum((q >= bound).astype(jnp.int32) for bound in q_bounds)
    k_id = sum((k >= bound).astype(jnp.int32) for bound in k_bounds)
    allowed = k_id == q_id
    if causal:
        allowed = allowed & (k <= q)
    valid = (q >= jnp.maximum(q_bounds[0], q_low)) & (q < jnp.minimum(q_bounds[3], q_high))
    return jnp.concatenate([allowed] * HEADS, axis=1), jnp.concatenate([valid] * HEADS, axis=1)


def window_weights(k, q_rows, mask):
    allowed, valid = mask
    scores = jnp.where(allowed, dot(k, q_rows), MASKED)
    weights = jnp.exp(scores - jnp.max(scores, axis=0, keepdims=True))
    inverse = jnp.where(valid, 1.0 / jnp.sum(weights, axis=0, keepdims=True), 0.0)
    return weights * inverse


def attend_window(q, k, v, mask):
    q_rows = spread_rows((q * jnp.asarray(HEAD_DIM**-0.5, BF16)).T)
    probabilities = window_weights(k, q_rows, mask).astype(BF16)
    return join_rows(dot(v.T, probabilities)).T.astype(BF16)


def attend_window_back(q, k, v, grad, mask):
    scale = HEAD_DIM**-0.5
    q = q * jnp.asarray(scale, BF16)
    probabilities = window_weights(k, spread_rows(q.T), mask)
    prob_grad = dot(v, spread_rows(grad.T))
    inner = jnp.sum(probabilities * prob_grad, axis=0, keepdims=True)
    score_grad = (probabilities * (prob_grad - inner)).astype(BF16)
    q_grad = (join_rows(dot(k.T, score_grad)) * scale).T
    k_grad = dot(score_grad, spread_lanes(q))
    v_grad = dot(probabilities.astype(BF16), spread_lanes(grad))
    return q_grad.astype(BF16), k_grad.astype(BF16), v_grad.astype(BF16)


def out_product(mixes, held):
    left = sum(dot(mix, held[4 * half + 3, 0:HALF]) for half, mix in enumerate(mixes))
    right = sum(dot(mix, held[4 * half + 3, HALF:]) for half, mix in enumerate(mixes))
    return jnp.concatenate([left, right], axis=1)


def out_grads(grad_low, held, mixes, mix_grads, grads, first):
    rows = grad_low.shape[0]
    for half in range(2):
        at = 4 * half + 3
        for lo in range(0, rows, HALF):
            block = grad_low[lo : lo + HALF]
            mix_grad = dot_nt(block[:, :HALF], held[at, 0:HALF]) + dot_nt(
                block[:, HALF:], held[at, HALF:]
            )
            mix_grads[half, first + lo : first + lo + HALF] = mix_grad.astype(BF16)
        mix = mixes[half]
        grads[half, 0:HALF] = dot_tn(mix, grad_low[:, :HALF]).astype(BF16)
        grads[half, HALF:] = dot_tn(mix, grad_low[:, HALF:]).astype(BF16)


def copy_by_role(meta, pairs_zero, pairs_one, sem):
    @pl.when(meta[0] == 0)
    def _():
        for source, target in pairs_zero:
            pltpu.make_async_copy(source, target, sem).start()

    @pl.when(meta[0] == 1)
    def _():
        for source, target in pairs_one:
            pltpu.make_async_copy(source, target, sem).start()


def wait_by_role(meta, pairs_zero, pairs_one, sem):
    @pl.when(meta[0] == 0)
    def _():
        for source, target in pairs_zero:
            pltpu.make_async_copy(source, target, sem).wait()

    @pl.when(meta[0] == 1)
    def _():
        for source, target in pairs_one:
            pltpu.make_async_copy(source, target, sem).wait()


def states_copies(rows_ref, other_ref, held, here):
    zero = [(other_ref.at[pl.ds(0, here)], held.at[pl.ds(HALO, here)])]
    one = [(rows_ref.at[pl.ds(here - HALO, here + HALO)], held.at[pl.ds(0, here + HALO)])]
    return zero, one


def self_forward(
    meta, segs, rows_ref, other_ref, gain, bias, own, w1, w2, w3, w4,
    hidden, mix, qkv, plan, held, states, sem_w, sem_x,
):
    here = hidden.shape[0]
    full = here + HALO
    state_copies = states_copies(rows_ref, other_ref, states, here)
    copy_by_role(meta, *state_copies, sem_x)
    weights = start_weights(meta, own, (w1, w2, w3, w4), held, sem_w)
    qkv[:, :, full:] = jnp.zeros((2, 3, WINDOW, HALF), BF16)
    mix[...] = jnp.zeros(mix.shape, BF16)
    wait_by_role(meta, *state_copies, sem_x)

    @pl.when(meta[0] == 0)
    def _():
        states[0:HALO] = jnp.zeros((HALO, states.shape[1]), BF16)

    for copy in weights:
        copy.wait()
    step = full // 2
    for lo in range(0, full, step):
        hat, _ = norm_parts(states[lo : lo + step].astype(F32))
        normed = (hat * gain[0:1] + bias[0:1]).astype(BF16)
        for half in range(2):
            for c in range(3):
                qkv[half, c, lo : lo + step] = dot(normed, held[4 * half + c]).astype(BF16)

    def group(bounds, _):
        first = window_of(bounds[0])
        mask = window_mask(first, bounds, first, bounds, HALO, full, True)
        at = pl.ds(first, WINDOW)
        return [attend_window(qkv[half, 0, at], qkv[half, 1, at], qkv[half, 2, at], mask) for half in range(2)]

    def store(bounds, _, result):
        at = pl.ds(window_of(bounds[0]), WINDOW)
        for half in range(2):
            mix[half, at] += result[half]

    each_group(meta, segs, plan, here, False, group, store)
    for lo in range(HALO, full, HALF):
        at = slice(lo, lo + HALF)
        hidden[lo - HALO : lo - HALO + HALF] = states[at].astype(F32) + out_product(
            [mix[0, at], mix[1, at]], held
        )


def memory_copies(rows_ref, other_ref, held):
    return [(rows_ref, held)], [(other_ref, held)]


def cross_forward(
    meta, segs, rows_ref, other_ref, hidden, gain, bias, own, w1, w2, w3, w4,
    hidden_two, mix, queries, pairs, plan, held, memory, sem_w, sem_x,
):
    here = hidden.shape[0]
    full = here + HALO
    copies = memory_copies(rows_ref, other_ref, memory)
    copy_by_role(meta, *copies, sem_x)
    weights = start_weights(meta, own, (w1, w2, w3, w4), held, sem_w)
    queries[:, 0:HALO] = jnp.zeros((2, HALO, HALF), BF16)
    queries[:, full:] = jnp.zeros((2, WINDOW, HALF), BF16)
    mix[...] = jnp.zeros(mix.shape, BF16)
    pairs[...] = jnp.zeros(pairs.shape, BF16)
    low, high = sentence_range(meta, segs, here)
    wait_by_role(meta, *copies, sem_x)
    for copy in weights:
        copy.wait()

    def project(block, _):
        at = pl.ds(pl.multiple_of(block * HALF, HALF), HALF)
        for half in range(2):
            for c in range(2):
                pairs[half, c, at] = dot(memory[at], held[4 * half + 1 + c]).astype(BF16)
        return 0

    lax.fori_loop(low // HALF, (high + HALF - 1) // HALF, project, 0)
    for lo in range(0, here, HALF):
        hat, _ = norm_parts(hidden[lo : lo + HALF])
        normed = (hat * gain[1:2] + bias[1:2]).astype(BF16)
        for half in range(2):
            queries[half, HALO + lo : HALO + lo + HALF] = dot(normed, held[4 * half]).astype(BF16)

    def group(bounds, source_bounds):
        first = window_of(bounds[0])
        source_first = window_of(source_bounds[0])
        mask = window_mask(first, bounds, source_first, source_bounds, HALO, full, False)
        at = pl.ds(first, WINDOW)
        source_at = pl.ds(source_first, WINDOW)
        return [
            attend_window(queries[half, at], pairs[half, 0, source_at], pairs[half, 1, source_at], mask)
            for half in range(2)
        ]

    def store(bounds, _, result):
        at = pl.ds(window_of(bounds[0]), WINDOW)
        for half in range(2):
            mix[half, at] += result[half]

    each_group(meta, segs, plan, here, True, group, store)
    for lo in range(0, here, HALF):
        at = slice(lo, lo + HALF)
        mix_at = slice(HALO + lo, HALO + lo + HALF)
        hidden_two[at] = hidden[at] + out_product([mix[0, mix_at], mix[1, mix_at]], held)


def gelu_both(inner):
    rate = 0.7978845608028654
    square = inner * inner
    bent = jnp.tanh(rate * inner * (1.0 + 0.044715 * square))
    half = 0.5 * (1.0 + bent)
    slope = half + 0.5 * inner * (1.0 - bent * bent) * (rate * (1.0 + 3 * 0.044715 * square))
    return inner * half, slope


def feed_forward(
    meta, hidden_two, cotangent, targets, gain, bias, halt_weight, halt_bias,
    own_in, i1, i2, i3, i4, own_out, o1, o2, o3, o4,
    result_low, hidden_grad, small, keep, send,
    held_in, held_out, normed, active, slopes, total, out_low, cot, tgt, grads_in, grads_out,
    sem_w, sem_o, sem_x, sem_g,
):
    here = hidden_two.shape[0]
    first = pl.multiple_of(meta[0] * here, here)
    cot_copy = pltpu.make_async_copy(cotangent.at[pl.ds(first, here)], cot, sem_x.at[0])
    tgt_copy = pltpu.make_async_copy(targets.at[pl.ds(first, here)], tgt, sem_x.at[1])
    weights = start_weights(meta, own_in, (i1, i2, i3, i4), held_in, sem_w)
    weights += start_weights(meta, own_out, (o1, o2, o3, o4), held_out, sem_o)
    cot_copy.start()
    tgt_copy.start()
    blocks = [slice(lo, lo + HALF) for lo in range(0, here, HALF)]
    for at in blocks:
        hat, _ = norm_parts(hidden_two[at])
        normed[at] = (hat * gain[2:3] + bias[2:3]).astype(BF16)
        total[at] = hidden_two[at]
    for copy in weights:
        copy.wait()

    def forward(j, _):
        for at in blocks:
            value, slope = gelu_both(dot(normed[at], held_in[j]))
            value = value.astype(BF16)
            active[j, at] = value
            slopes[j, at] = slope
            total[at] += dot(value, held_out[j])
        return 0

    lax.fori_loop(0, 8, forward, 0)
    cot_copy.wait()
    tgt_copy.wait()
    weight_sum = jnp.zeros((1, halt_weight.shape[1]), F32)
    bias_sum = jnp.zeros((1, 1), F32)
    for at in blocks:
        result = total[at]
        result_low[at] = result.astype(BF16)
        logits = jnp.sum(result * halt_weight[...], axis=-1, keepdims=True) + halt_bias[0]
        halt_grad = 1.0 / (1.0 + jnp.exp(-logits)) - tgt[at]
        out_grad = cot[at].astype(F32) + halt_grad * halt_weight[...]
        out_low[at] = out_grad.astype(BF16)
        hidden_grad[at] = out_grad
        total[at] = jnp.zeros((HALF, result.shape[1]), F32)
        weight_sum += jnp.sum(halt_grad * result, axis=0, keepdims=True)
        bias_sum += jnp.sum(halt_grad, axis=0, keepdims=True)

    def backward(j, _):
        inner_grads = []
        for at in blocks:
            inner_grad = (dot_nt(out_low[at], held_out[j]) * slopes[j, at]).astype(BF16)
            inner_grads.append(inner_grad)
            total[at] += dot_nt(inner_grad, held_in[j])
        grads_in[j] = dot_tn(normed[...], jnp.concatenate(inner_grads, axis=0)).astype(BF16)
        grads_out[j, 0:HALF] = dot_tn(active[j], out_low[:, :HALF]).astype(BF16)
        grads_out[j, HALF:] = dot_tn(active[j], out_low[:, HALF:]).astype(BF16)
        return 0

    lax.fori_loop(0, 8, backward, 0)
    copies = put_grads(meta, grads_in, keep.at[pl.ds(0, 1)], send.at[pl.ds(0, 1)], sem_g)
    copies += put_grads(meta, grads_out, keep.at[pl.ds(1, 1)], send.at[pl.ds(1, 1)], sem_g)
    gain_sum = jnp.zeros_like(weight_sum)
    shift_sum = jnp.zeros_like(weight_sum)
    for at in blocks:
        hat, scale = norm_parts(hidden_two[at])
        grad = total[at]
        hidden_grad[at] += norm_back(grad, hat, scale, gain[2:3])
        gain_sum += jnp.sum(grad * hat, axis=0, keepdims=True)
        shift_sum += jnp.sum(grad, axis=0, keepdims=True)
    small[...] = jnp.concatenate(
        [gain_sum, shift_sum, weight_sum, jnp.broadcast_to(bias_sum, weight_sum.shape)], axis=0
    )
    for copy in copies:
        copy.wait()


def cross_backward(
    meta, segs, upper_grad, mix, queries, pairs, own, w1, w2, w3, w4,
    q_grad, pair_grads, grads, plan, held, mix_grads, sem_w,
):
    here = upper_grad.shape[0]
    full = here + HALO
    weights = start_weights(meta, own, (w1, w2, w3, w4), held, sem_w)
    mix_grads[:, 0:HALO] = jnp.zeros((2, HALO, HALF), BF16)
    mix_grads[:, full:] = jnp.zeros((2, WINDOW, HALF), BF16)
    q_grad[...] = jnp.zeros(q_grad.shape, BF16)
    pair_grads[...] = jnp.zeros(pair_grads.shape, BF16)
    for copy in weights:
        copy.wait()
    out_grads(upper_grad[...].astype(BF16), held, [mix[0, HALO:full], mix[1, HALO:full]], mix_grads, grads, HALO)

    def group(bounds, source_bounds):
        first = window_of(bounds[0])
        source_first = window_of(source_bounds[0])
        mask = window_mask(first, bounds, source_first, source_bounds, HALO, full, False)
        at = pl.ds(first, WINDOW)
        source_at = pl.ds(source_first, WINDOW)
        return [
            attend_window_back(
                queries[half, at], pairs[half, 0, source_at], pairs[half, 1, source_at],
                mix_grads[half, at], mask,
            )
            for half in range(2)
        ]

    def store(bounds, source_bounds, result):
        at = pl.ds(window_of(bounds[0]), WINDOW)
        source_at = pl.ds(window_of(source_bounds[0]), WINDOW)
        for half, (dq, dk, dv) in enumerate(result):
            q_grad[half, at] += dq
            pair_grads[half, 0, source_at] += dk
            pair_grads[half, 1, source_at] += dv

    each_group(meta, segs, plan, here, True, group, store)


def cross_products(
    meta, segs, rows_ref, other_ref, hidden, upper_grad, q_grad, pair_grads, out_grad, gain, bias,
    own, w1, w2, w3, w4,
    lower_grad, memory_grad, small, keep, send,
    held, memory, pair_sums, grads, sem_w, sem_x, sem_g,
):
    here, width = hidden.shape
    full = here + HALO
    copies = memory_copies(rows_ref, other_ref, memory)
    copy_by_role(meta, *copies, sem_x)
    weights = start_weights(meta, own, (w1, w2, w3, w4), held, sem_w)
    pair_sums[...] = jnp.zeros(pair_sums.shape, F32)
    memory_grad[...] = jnp.zeros(memory_grad.shape, BF16)
    source_low, source_high = sentence_range(meta, segs, here)
    for half in range(2):
        grads[4 * half + 3] = out_grad[half]
    for copy in weights:
        copy.wait()
    wait_by_role(meta, *copies, sem_x)

    def project(block, _):
        at = pl.ds(pl.multiple_of(block * HALF, HALF), HALF)
        row_grad = jnp.zeros((HALF, width), F32)
        for half in range(2):
            for c in range(2):
                low = pair_grads[half, c, at]
                row_grad += dot_nt(low, held[4 * half + 1 + c])
                pair_sums[half, c] += dot_tn(memory[at], low)
        memory_grad[at] = row_grad.astype(BF16)
        return 0

    lax.fori_loop(source_low // HALF, (source_high + HALF - 1) // HALF, project, 0)
    for half in range(2):
        for c in range(2):
            grads[4 * half + 1 + c] = pair_sums[half, c].astype(BF16)
    gain_sum = jnp.zeros((1, width), F32)
    shift_sum = jnp.zeros((1, width), F32)
    normed = []
    q_low = [q_grad[half, HALO:full] for half in range(2)]
    for lo in range(0, here, HALF):
        at = slice(lo, lo + HALF)
        hat, scale = norm_parts(hidden[at])
        normed.append((hat * gain[1:2] + bias[1:2]).astype(BF16))
        grad = dot_nt(q_low[0][at], held[0]) + dot_nt(q_low[1][at], held[4])
        lower_grad[at] = upper_grad[at] + norm_back(grad, hat, scale, gain[1:2])
        gain_sum += jnp.sum(grad * hat, axis=0, keepdims=True)
        shift_sum += jnp.sum(grad, axis=0, keepdims=True)
    normed = jnp.concatenate(normed, axis=0)
    for half in range(2):
        grads[4 * half] = dot_tn(normed, q_low[half]).astype(BF16)
    put = put_grads(meta, grads, keep, send, sem_g)
    small[...] = jnp.concatenate([gain_sum, shift_sum], axis=0)
    for copy in put:
        copy.wait()


def self_backward(
    meta, segs, upper_grad, mix, qkv, own, w1, w2, w3, w4,
    qkv_grads, grads, plan, held, mix_grads, sem_w,
):
    here = upper_grad.shape[0]
    full = here + HALO
    weights = start_weights(meta, own, (w1, w2, w3, w4), held, sem_w)
    mix_grads[:, 0:HALO] = jnp.zeros((2, HALO, HALF), BF16)
    mix_grads[:, full:] = jnp.zeros((2, WINDOW, HALF), BF16)
    qkv_grads[...] = jnp.zeros(qkv_grads.shape, BF16)
    for copy in weights:
        copy.wait()
    out_grads(upper_grad[...].astype(BF16), held, [mix[0, HALO:full], mix[1, HALO:full]], mix_grads, grads, HALO)

    def group(bounds, _):
        first = window_of(bounds[0])
        mask = window_mask(first, bounds, first, bounds, HALO, full, True)
        at = pl.ds(first, WINDOW)
        return [
            attend_window_back(
                qkv[half, 0, at], qkv[half, 1, at], qkv[half, 2, at], mix_grads[half, at], mask
            )
            for half in range(2)
        ]

    def store(bounds, _, result):
        at = pl.ds(window_of(bounds[0]), WINDOW)
        for half in range(2):
            for c in range(3):
                qkv_grads[half, c, at] += result[half][c]

    each_group(meta, segs, plan, here, False, group, store)


def self_products(
    meta, rows_ref, other_ref, upper_grad, qkv_grads, out_grad, gain, bias, own, w1, w2, w3, w4,
    state_grad, halo_grad, small, keep, send,
    held, states, grads, sem_w, sem_x, sem_g,
):
    here, width = upper_grad.shape
    full = here + HALO
    state_copies = states_copies(rows_ref, other_ref, states, here)
    copy_by_role(meta, *state_copies, sem_x)
    weights = start_weights(meta, own, (w1, w2, w3, w4), held, sem_w)
    for half in range(2):
        grads[4 * half + 3] = out_grad[half]
    wait_by_role(meta, *state_copies, sem_x)

    @pl.when(meta[0] == 0)
    def _():
        states[0:HALO] = jnp.zeros((HALO, width), BF16)

    for copy in weights:
        copy.wait()
    gain_sum = jnp.zeros((1, width), F32)
    shift_sum = jnp.zeros((1, width), F32)
    normed = []
    step = full // 2
    for lo in range(0, full, step):
        at = slice(lo, lo + step)
        hat, scale = norm_parts(states[at].astype(F32))
        normed.append((hat * gain[0:1] + bias[0:1]).astype(BF16))
        grad = jnp.zeros((step, width), F32)
        for half in range(2):
            for c in range(3):
                grad += dot_nt(qkv_grads[half, c, at], held[4 * half + c])
        back = norm_back(grad, hat, scale, gain[0:1])
        if lo == 0:
            halo_grad[...] = back[:HALO]
            state_grad[0 : step - HALO] = upper_grad[0 : step - HALO] + back[HALO:]
        else:
            state_grad[lo - HALO :] = upper_grad[lo - HALO :] + back
        gain_sum += jnp.sum(grad * hat, axis=0, keepdims=True)
        shift_sum += jnp.sum(grad, axis=0, keepdims=True)
    normed = jnp.concatenate(normed, axis=0)
    for half in range(2):
        for c in range(3):
            grads[4 * half + c] = dot_tn(normed, qkv_grads[half, c, 0:full]).astype(BF16)
    put = put_grads(meta, grads, keep, send, sem_g)
    small[...] = jnp.concatenate([gain_sum, shift_sum], axis=0)
    for copy in put:
        copy.wait()


def unpack(kind, meta, mine, by_x, by_role, by_both, *rest):
    outs, (held, sem) = rest[:-2], rest[-2:]
    rows = mine.shape[1]
    copies = []
    for rel, ref in ((0, mine), (2, by_x), (1, by_role), (3, by_both)):
        for part in range(2):
            if kind == "ffn":
                target = held.at[part, rel ^ meta[1]]
            else:
                target = held.at[0, rel ^ meta[1], pl.ds(part * rows, rows)]
            copy = pltpu.make_async_copy(ref.at[part], target, sem.at[0])
            copy.start()
            copies.append(copy)
    for copy in copies:
        copy.wait()
    if kind == "ffn":
        grad_in, grad_out = outs
        for j in range(4):
            at = slice(j * HALF, (j + 1) * HALF)
            grad_in[:, at] = held[0, j].astype(F32)
            grad_out[at, 0:HALF] = held[1, j, 0:HALF].astype(F32)
            grad_out[at, HALF:] = held[1, j, HALF:].astype(F32)
        return
    at = 0
    for out in outs[:-1]:
        for c in range(out.shape[1] // HALF):
            out[:, c * HALF : (c + 1) * HALF] = held[0, at].astype(F32)
            at += 1
    outs[-1][:, 0:HALF] = held[0, 3, 0:HALF].astype(F32)
    outs[-1][:, HALF:] = held[0, 3, HALF:].astype(F32)


def shape(*dims, dtype=F32):
    return jax.ShapeDtypeStruct(dims, dtype)


def near(*dims, dtype=F32):
    return pltpu.VMEM(dims, dtype)


def held_near(*values):
    return [pltpu.with_memory_space_constraint(value, pltpu.VMEM) for value in values]


def call(body, outs, out_specs, scratch, flops, name, in_specs):
    return pl.pallas_call(
        body,
        out_shape=outs,
        in_specs=in_specs,
        out_specs=out_specs,
        scratch_shapes=scratch,
        name=name,
        compiler_params=pltpu.CompilerParams(vmem_limit_bytes=VMEM_LIMIT),
        cost_estimate=pl.CostEstimate(flops=flops, bytes_accessed=10_000_000, transcendentals=0),
    )


def flip(value, axis, bit=1):
    count = lax.axis_size(axis)
    return lax.ppermute(value, axis, [(i, i ^ bit) for i in range(count)])


def add(a, b):
    return (a.astype(F32) + b.astype(F32)).astype(BF16)


def fetch_other(own, me):
    first = flip(lax.dynamic_index_in_dim(own, me, 0, keepdims=False), "head")
    second = flip(first, "dp", 1)
    return own, first, second, flip(first, "role"), flip(second, "role")


def after(value, *events):
    return lax.optimization_barrier((value, events))[0]


class Order:
    def __init__(self):
        self.last = ()

    def __call__(self, step, *values):
        values, _ = lax.optimization_barrier((values, self.last))
        result = step(*values)
        self.last = (jax.tree.leaves(result)[-1],)
        return result


class Sum:
    def __init__(self, keep, send):
        self.keep, self.got = keep, flip(send, "role")

    def cores(self, keep, got):
        return add(keep[0, 0], got[0, 0]), add(keep[0, 1], got[0, 1]), add(keep[1, :, 0], got[1, :, 0]), add(
            keep[1, :, 1], got[1, :, 1]
        )

    def begin(self, order):
        one, away_one, two, away_two = order(self.cores, self.keep, self.got)
        self.keep = one, two
        self.got = flip(away_one, "head"), flip(away_two, "dp", 1)

    def first(self, order):
        def halve(one, two, got_one, got_two):
            return add(one[0], got_one[0]), add(one[1], got_one[1]), add(two[0], got_two[0]), add(two[1], got_two[1])

        one, away_one, two, away_two = order(halve, *self.keep, *self.got)
        self.keep = one, two
        self.got = flip(away_one, "dp", 1), flip(away_two, "head")

    def plain(self, order, bits):
        def both(one, two, got_one, got_two):
            return add(one, got_one), add(two, got_two)

        one, two = order(both, *self.keep, *self.got)
        self.keep = one, two
        self.got = flip(one, "dp", bits[0]), flip(two, "dp", bits[1])

    def second(self, order):
        self.plain(order, (2, 4))

    def third(self, order):
        self.plain(order, (4, 2))

    def last(self, order):
        bit = 8
        while bit < lax.axis_size("dp"):
            self.plain(order, (bit, bit))
            bit *= 2

        def both(one, two, got_one, got_two):
            return jnp.stack([add(one, got_one), add(two, got_two)])

        self.mine = order(both, *self.keep, *self.got)
        self.by_x = flip(self.mine, "dp", 1)

    def pieces(self):
        return self.mine, self.by_x, flip(self.mine, "role"), flip(self.by_x, "role")


class SmallSum:
    def __init__(self, value):
        count = lax.axis_size("dp")
        self.steps = [("role", 1), ("head", 1)] + [("dp", 1 << at) for at in range(count.bit_length() - 1)]
        self.value, self.got = value, flip(value, *self.steps.pop(0))

    def step(self, order):
        self.value = order(lambda value, got: value + got, self.value, self.got)
        self.got = flip(self.value, *self.steps.pop(0)) if self.steps else jnp.zeros_like(self.value)

    def total(self):
        value = self.value + self.got
        for axis, bit in self.steps:
            value = value + flip(value, axis, bit)
        return value


def shards(
    layer_in,
    lengths,
    cotangent,
    targets,
    self_qkv,
    self_out,
    cross_q,
    cross_kv,
    cross_out,
    ffn_in,
    ffn_out,
    norm_gain,
    norm_bias,
    halt_weight,
    halt_bias,
):
    role, head, place = (lax.axis_index(name) for name in ("role", "head", "dp"))
    target_side = role == 1
    me = 2 * (place & 1) + role
    meta = jnp.stack([role, me]).astype(jnp.int32)
    rows = layer_in[0]
    row_len, width = rows.shape
    here = row_len // 2
    full = here + HALO

    other_rows = flip(rows, "role")
    lens = lax.dynamic_index_in_dim(lengths[0], head, 0, keepdims=False)
    other_lens = flip(lens, "role")
    segs = jnp.where(target_side, jnp.stack([other_lens, lens]), jnp.stack([lens, other_lens]))
    segs = jnp.pad(segs, ((0, 0), (0, 2)))

    def halves(out):
        return jnp.concatenate([out[:, :HALF], out[:, HALF:]], axis=0)[None]

    self_own = jnp.concatenate([self_qkv.transpose(1, 0, 2), halves(self_out)], axis=0)
    cross_own = jnp.concatenate(
        [cross_q[None], cross_kv.transpose(1, 0, 2), halves(cross_out)], axis=0
    )
    in_own = ffn_in.reshape(width, 4, HALF).transpose(1, 0, 2)
    out_own = ffn_out.reshape(4, HALF, width)
    self_weights = fetch_other(self_own, me)
    cross_weights = fetch_other(cross_own, me)
    in_weights = fetch_other(in_own, me)
    out_weights = fetch_other(out_own, me)

    weight_specs = [ANY] * 5
    held = pltpu.VMEM((8, width, HALF), BF16)
    plan = pltpu.SMEM((8, 40), jnp.int32)
    weight_sems = pltpu.SemaphoreType.DMA((5,))
    one_sem = pltpu.SemaphoreType.DMA
    dense = 2 * here * width * HALF * 8

    hidden, self_mix, qkv = call(
        self_forward,
        (near(here, width), near(2, full + WINDOW, HALF, dtype=BF16), near(2, 3, full + WINDOW, HALF, dtype=BF16)),
        (VMEM,) * 3,
        [plan, held, pltpu.VMEM((full, width), BF16), weight_sems, one_sem],
        2 * dense,
        "self_forward",
        [SMEM, SMEM, ANY, ANY, VMEM, VMEM] + weight_specs,
    )(meta, segs, rows, other_rows, norm_gain, norm_bias, *self_weights)

    hidden_two, cross_mix, queries, pairs = call(
        cross_forward,
        (
            near(here, width),
            near(2, full + WINDOW, HALF, dtype=BF16),
            near(2, full + WINDOW, HALF, dtype=BF16),
            near(2, 2, row_len + WINDOW, HALF, dtype=BF16),
        ),
        (VMEM,) * 4,
        [plan, held, pltpu.VMEM((row_len, width), BF16), weight_sems, one_sem],
        2 * dense,
        "cross_forward",
        [SMEM, SMEM, ANY, ANY, VMEM, VMEM, VMEM] + weight_specs,
    )(meta, segs, rows, other_rows, *held_near(hidden), norm_gain, norm_bias, *cross_weights)

    grad_parts = shape(2, 2, 2, width // 2, HALF, dtype=BF16)
    ffn_parts = shape(2, 2, 2, width, HALF, dtype=BF16)
    grad_sems = pltpu.SemaphoreType.DMA((1,))
    result_low, two_grad, ffn_small, keep_ffn, send_ffn = call(
        feed_forward,
        (shape(here, width, dtype=BF16), near(here, width), shape(4, width), ffn_parts, ffn_parts),
        (VMEM, VMEM, VMEM, ANY, ANY),
        [
            held,
            pltpu.VMEM((8, HALF, width), BF16),
            pltpu.VMEM((here, width), BF16),
            pltpu.VMEM((8, here, HALF), BF16),
            pltpu.VMEM((8, here, HALF), F32),
            pltpu.VMEM((here, width), F32),
            pltpu.VMEM((here, width), BF16),
            pltpu.VMEM((here, width), BF16),
            pltpu.VMEM((here, 1), F32),
            pltpu.VMEM((8, width, HALF), BF16),
            pltpu.VMEM((8, width, HALF), BF16),
            weight_sems,
            weight_sems,
            pltpu.SemaphoreType.DMA((2,)),
            grad_sems,
        ],
        6 * dense,
        "feed_forward",
        [SMEM, VMEM, ANY, ANY, VMEM, VMEM, VMEM, SMEM] + weight_specs * 2,
    )(
        meta, *held_near(hidden_two), cotangent, targets.astype(F32)[:, None], norm_gain, norm_bias,
        halt_weight[None], halt_bias, *in_weights, *out_weights,
    )

    query_grad, pair_grads, cross_out_part = call(
        cross_backward,
        (
            near(2, full + WINDOW, HALF, dtype=BF16),
            near(2, 2, row_len + WINDOW, HALF, dtype=BF16),
            near(2, width, HALF, dtype=BF16),
        ),
        (VMEM,) * 3,
        [plan, held, pltpu.VMEM((2, full + WINDOW, HALF), BF16), weight_sems],
        2 * dense,
        "cross_backward",
        [SMEM, SMEM] + [VMEM] * 4 + weight_specs,
    )(meta, segs, *held_near(two_grad, cross_mix, queries, pairs), *cross_weights)

    order = Order()
    ffn_sum = Sum(keep_ffn, send_ffn)
    ffn_sum.begin(order)
    one_grad, memory_part, cross_small, keep_cross, send_cross = call(
        cross_products,
        (near(here, width), shape(row_len, width, dtype=BF16), shape(2, width), grad_parts, grad_parts),
        (VMEM, VMEM, VMEM, ANY, ANY),
        [
            held,
            pltpu.VMEM((row_len, width), BF16),
            pltpu.VMEM((2, 2, width, HALF), F32),
            pltpu.VMEM((8, width, HALF), BF16),
            weight_sems,
            one_sem,
            grad_sems,
        ],
        4 * dense,
        "cross_products",
        [SMEM, SMEM, ANY, ANY] + [VMEM] * 7 + weight_specs,
    )(
        after(meta, *order.last), segs, rows, other_rows,
        *held_near(hidden, two_grad, query_grad, pair_grads, cross_out_part), norm_gain, norm_bias, *cross_weights,
    )

    qkv_grads, self_out_part = call(
        self_backward,
        (near(2, 3, full + WINDOW, HALF, dtype=BF16), near(2, width, HALF, dtype=BF16)),
        (VMEM,) * 2,
        [plan, held, pltpu.VMEM((2, full + WINDOW, HALF), BF16), weight_sems],
        2 * dense,
        "self_backward",
        [SMEM, SMEM] + [VMEM] * 3 + weight_specs,
    )(meta, segs, *held_near(one_grad, self_mix, qkv), *self_weights)

    cross_sum = Sum(keep_cross, send_cross)
    ffn_sum.first(order)
    cross_sum.begin(order)
    state_grad, halo_grad, self_small, keep_self, send_self = call(
        self_products,
        (shape(here, width), shape(HALO, width), shape(2, width), grad_parts, grad_parts),
        (VMEM, VMEM, VMEM, ANY, ANY),
        [held, pltpu.VMEM((full, width), BF16), pltpu.VMEM((8, width, HALF), BF16), weight_sems, one_sem, grad_sems],
        4 * dense,
        "self_products",
        [SMEM, ANY, ANY] + [VMEM] * 5 + weight_specs,
    )(
        after(meta, *order.last), rows, other_rows, *held_near(one_grad, qkv_grads, self_out_part),
        norm_gain, norm_bias, *self_weights,
    )

    order.last = (self_small,)
    self_sum = Sum(keep_self, send_self)
    small = SmallSum(
        jnp.concatenate(
            [
                self_small[0:1], cross_small[0:1], ffn_small[0:1],
                self_small[1:2], cross_small[1:2], ffn_small[1:2], ffn_small[2:4],
            ],
            axis=0,
        )
    )
    to_target, to_memory = [(0, 1)], [(1, 0)]
    low_result = lax.ppermute(result_low, "role", to_target)
    other_memory = lax.ppermute(memory_part, "role", to_memory)
    low_grad = lax.ppermute(state_grad.astype(BF16), "role", to_target)
    ffn_sum.second(order)
    self_sum.begin(order)
    cross_sum.first(order)
    small.step(order)
    cross_sum.second(order)
    self_sum.first(order)
    small.step(order)
    ffn_sum.third(order)
    self_sum.second(order)
    small.step(order)
    cross_sum.third(order)
    ffn_sum.last(order)
    self_sum.third(order)
    cross_sum.last(order)
    small.step(order)
    ffn_pieces = order(lambda *_: ffn_sum.pieces(), ffn_sum.by_x)
    self_sum.last(order)
    small.step(order)
    cross_pieces = order(lambda *_: cross_sum.pieces(), cross_sum.by_x)

    def totals(kind, pieces, out_shapes):
        parts, rows_each, columns = pieces[0].shape
        held_shape = (2, 4, rows_each, columns) if kind == "ffn" else (1, 4, 2 * rows_each, columns)
        return call(
            functools.partial(unpack, kind),
            out_shapes,
            (VMEM,) * len(out_shapes),
            [pltpu.VMEM(held_shape, BF16), pltpu.SemaphoreType.DMA((1,))],
            0,
            "unpack_" + kind,
            [SMEM] + [ANY] * 4,
        )(meta, *pieces)

    ffn_in_grad, ffn_out_grad = totals("ffn", ffn_pieces, (shape(width, 4 * HALF), shape(4 * HALF, width)))
    cross_q_grad, cross_kv_grad, cross_out_grad = totals(
        "cross", cross_pieces, (shape(width, HALF), shape(width, 2 * HALF), shape(HALF, width))
    )
    self_qkv_grad, self_out_grad = totals(
        "self", self_sum.pieces(), (shape(width, 3 * HALF), shape(HALF, width))
    )
    small = small.total()
    low_grad = low_grad.astype(F32)
    layer_out = jnp.where(
        target_side, jnp.concatenate([low_result, result_low], axis=0), rows
    )[None]
    halo_rows = jnp.concatenate(
        [jnp.zeros((here - HALO, width), F32), halo_grad, jnp.zeros((here, width), F32)], axis=0
    )
    target_grads = jnp.concatenate([low_grad, state_grad], axis=0) + halo_rows
    memory_grads = memory_part.astype(F32) + other_memory.astype(F32)
    input_grads = jnp.where(target_side, target_grads, memory_grads)[None]
    return (
        layer_out,
        input_grads,
        self_qkv_grad.reshape(width, 3, HALF),
        self_out_grad,
        cross_q_grad,
        cross_kv_grad.reshape(width, 2, HALF),
        cross_out_grad,
        ffn_in_grad,
        ffn_out_grad,
        small[0:3],
        small[3:6],
        small[6],
        small[7, 0:1],
    )


def solution(mesh):
    placed = (
        P("role", ("dp", "head"), None),
        P("role", "dp", None),
        P(("dp", "head"), None),
        P(("dp", "head")),
        P(None, None, "head"),
        P("head", None),
        P(None, "head"),
        P(None, None, "head"),
        P("head", None),
        P(None, "head"),
        P("head", None),
        P(),
        P(),
        P(),
        P(),
    )
    return jax.shard_map(
        shards,
        mesh=mesh,
        in_specs=placed,
        out_specs=(
            P("role", ("dp", "head"), None),
            P("role", ("dp", "head"), None),
            P(None, None, "head"),
            P("head", None),
            P(None, "head"),
            P(None, None, "head"),
            P("head", None),
            P(None, "head"),
            P("head", None),
            P(),
            P(),
            P(),
            P(),
        ),
        check_vma=False,
    )
```

```python
import functools

import jax
import jax.numpy as jnp
from jax import lax
from jax.experimental import pallas as pl
from jax.experimental.pallas import tpu as pltpu
from jax.sharding import PartitionSpec as P

F32 = jnp.float32
BF16 = jnp.bfloat16

HEAD_DIM = 64
HALF = 256
HEADS = HALF // HEAD_DIM
HALO = 128
GROUPS = 3
WINDOW = 128
MASKED = -1e30
VMEM_LIMIT = 40 << 20
WEIGHT = 1.2e9
ANY = pl.BlockSpec(memory_space=pl.ANY)
VMEM = pl.BlockSpec(memory_space=pltpu.VMEM)
SMEM = pl.BlockSpec(memory_space=pltpu.SMEM)
ARRIVALS = (0, 2, 1, 3)
FFN_ROUTES = [("head", "x"), ("x", "head")]
CROSS_ROUTES = [("x", "head")]
SELF_ROUTES = [("head", "x"), ("x", "head")]
HEAVY = 8
PIECES = 4


def dot(a, b):
    return jnp.dot(a, b, preferred_element_type=F32)


def dot_nt(a, b):
    return lax.dot_general(a, b, (((1,), (1,)), ((), ())), preferred_element_type=F32)


def dot_tn(a, b):
    return lax.dot_general(a, b, (((0,), (0,)), ((), ())), preferred_element_type=F32)


def norm_parts(values):
    center = values - jnp.mean(values, axis=-1, keepdims=True)
    spread = jnp.mean(center * center, axis=-1, keepdims=True)
    scale = lax.rsqrt(spread + 1e-05)
    return center * scale, scale


def norm_back(grad, hat, scale, gain):
    grad_hat = grad * gain
    first = jnp.mean(grad_hat, axis=-1, keepdims=True)
    second = jnp.mean(grad_hat * hat, axis=-1, keepdims=True)
    return scale * (grad_hat - first - hat * second)


class Load:
    def __init__(self, source, target, sem):
        self.target, self.copies = target, [pltpu.make_async_copy(source, target, sem)]
        self.copies[0].start()

    def __call__(self):
        wait(self.copies)
        self.copies = []
        return self.target


class Store:
    def __init__(self, ref, target, sem):
        self.ref, self.copy, self.sent = ref, pltpu.make_async_copy(ref, target, sem), False

    def send(self):
        if not self.sent:
            self.copy.start()
        self.sent = True


def start(copies):
    for copy in copies:
        copy.start()
    return copies


def wait(copies):
    for copy in copies:
        copy.wait()


def cut_self(meta, matrices, out, piece, sem):
    wait(start(row_copies(meta[1], matrices, out, piece.ref, 0, sem)))


def row_copies(which, matrices, out, piece, first, sem):
    count, rows = matrices.shape[0], piece.shape[1]
    low = pl.multiple_of(which * rows, rows)
    out_low = pl.multiple_of((which & 1) * rows, rows)
    out_left = pl.multiple_of((which >> 1) * HALF, HALF)
    return [
        pltpu.make_async_copy(matrices.at[:, pl.ds(low, rows)], piece.at[pl.ds(first, count)], sem.at[0]),
        pltpu.make_async_copy(out.at[pl.ds(out_low, rows), pl.ds(out_left, HALF)], piece.at[3], sem.at[1]),
    ]


def cut_rest(meta, q, pair, out, ffn_in, ffn_out, cross_piece, in_piece, out_piece, sem):
    cross_piece, in_piece, out_piece = cross_piece.ref, in_piece.ref, out_piece.ref
    rows = cross_piece.shape[1]
    low = pl.multiple_of(meta[2] * rows, rows)
    copies = row_copies(meta[2], pair, out, cross_piece, 1, sem)
    copies.append(pltpu.make_async_copy(q.at[pl.ds(low, rows)], cross_piece.at[0], sem.at[2]))
    low = pl.multiple_of(meta[1] * rows, rows)
    for j in range(4):
        source = ffn_in.at[pl.ds(low, rows), pl.ds(j * HALF, HALF)]
        copies.append(pltpu.make_async_copy(source, in_piece.at[j], sem.at[3]))
    low = pl.multiple_of(meta[2] * HALF, HALF)
    copies.append(pltpu.make_async_copy(ffn_out.at[pl.ds(low, HALF)], out_piece, sem.at[4]))
    wait(start(copies))


def start_out_own(out, held, sem):
    return start(
        [
            pltpu.make_async_copy(out.at[:, pl.ds(c * HALF, HALF)], held.at[pl.ds(c * HALF, HALF)], sem.at[c])
            for c in range(2)
        ]
    )


def start_other(place, arrived, first, held, sem):
    rows, count = arrived[0].shape[1], held.shape[0]
    copies = []
    for at, (ref, flip) in enumerate(zip(arrived, ARRIVALS)):
        low = pl.multiple_of((place ^ flip) * rows, rows)
        source = ref.at[pl.ds(first, count)]
        copies.append(pltpu.make_async_copy(source, held.at[:, pl.ds(low, rows)], sem.at[2 + at]))
    return start(copies)


def start_in(meta, own, arrived, held, sem):
    copies = [
        pltpu.make_async_copy(own.at[:, pl.ds(j * HALF, HALF)], held.at[j], sem.at[0]) for j in range(4)
    ]
    return start(copies) + start_other(meta[1], arrived, 0, held.at[pl.ds(4, 4)], sem)


def start_out(meta, own, arrived, held, sem):
    copies = [
        pltpu.make_async_copy(own.at[pl.ds(j * HALF, HALF)], held.at[j], sem.at[0]) for j in range(4)
    ]
    for at, (ref, flip) in enumerate(zip(arrived, ARRIVALS)):
        copies.append(pltpu.make_async_copy(ref, held.at[4 + (meta[2] ^ flip)], sem.at[2 + at]))
    return start(copies)


def put_grads(meta, grads, keep, send, sem, x_first=False):
    _, _, count, rows, _ = keep.shape
    copies = []
    for half in range(2):
        for rel in range(PIECES):
            first = pl.multiple_of((rel ^ meta[1]) * rows, rows)
            source = grads.at[pl.ds(half * count, count), pl.ds(first, rows)]
            at = (rel >> 1, half) if x_first else (half, rel >> 1)
            target = (send if rel & 1 else keep).at[at]
            copy = pltpu.make_async_copy(source, target, sem.at[0])
            copy.start()
            copies.append(copy)
    return copies


def sentence_range(meta, segs, rows_here):
    first_row = meta[0] * rows_here

    def step(c, carry):
        target, source, low, high = carry
        target_end = target + segs[1, c]
        source_end = source + segs[0, c]
        mine = (target_end > first_row) & (target < first_row + rows_here)
        low = jnp.where(mine, jnp.minimum(low, source), low)
        high = jnp.where(mine, jnp.maximum(high, source_end), high)
        return target_end, source_end, low, high

    zero = jnp.int32(0)
    _, _, low, high = lax.fori_loop(0, segs.shape[1] - 2, step, (zero, zero, jnp.int32(1 << 20), zero))
    return low, high


def each_group(meta, segs, plan, rows_here, cross, together, windows, compute, store):
    first_row = meta[0] * rows_here
    last_row = first_row + rows_here
    shift = HALO - first_row

    def step(c, carry):
        t0, s0, done, count = carry
        t1, s1 = t0 + segs[1, c], s0 + segs[0, c]
        t2, s2 = t1 + segs[1, c + 1], s1 + segs[0, c + 1]
        t3, s3 = t2 + segs[1, c + 2], s2 + segs[0, c + 2]
        target_end, source_end = window_of(t0) + WINDOW, window_of(s0) + WINDOW
        two = (t2 <= target_end) & (t1 < last_row)
        three = two & (t3 <= target_end) & (t2 < last_row)
        if cross:
            two = two & (s2 <= source_end)
            three = three & (s3 <= source_end) & two
        t2, s2 = jnp.where(two, t2, t1), jnp.where(two, s2, s1)
        t3, s3 = jnp.where(three, t3, t2), jnp.where(three, s3, s2)
        here = (c >= done) & (t1 > first_row) & (t0 < last_row)
        for at, bound in enumerate((t0, t1, t2, t3)):
            plan[at, count] = bound + shift
        for at, bound in enumerate((s0, s1, s2, s3)):
            plan[4 + at, count] = bound
        size = 1 + two.astype(jnp.int32) + three.astype(jnp.int32)
        return t1, s1, jnp.where(here, c + size, done), count + here.astype(jnp.int32)

    zero = jnp.int32(0)
    count = lax.fori_loop(0, segs.shape[1] - 2, step, (zero, zero, zero, zero))[3]
    for g in range(together):
        for at in range(8):
            plan[at, count + g] = 0

    def some(i, _):
        bounds = [
            (
                [plan[at, i * together + g] for at in range(4)],
                [plan[4 + at, i * together + g] for at in range(4)],
            )
            for g in range(together)
        ]
        operands = [windows(*each) for each in bounds]
        results = iter(compute([window for each in operands for window in each]))
        for each, windows_of_it in zip(bounds, operands):
            store(*each, [next(results) for _ in windows_of_it])
        return 0

    lax.fori_loop(0, (count + together - 1) // together, some, 0)


def window_of(start):
    return pl.multiple_of((start // 16) * 16, 16)


def spread_lanes(block):
    lanes = lax.broadcasted_iota(jnp.int32, (1, HALF), 1) // HEAD_DIM
    return jnp.concatenate(
        [jnp.where(lanes == h, block, jnp.zeros_like(block)) for h in range(HEADS)], axis=0
    )


def spread_rows(block):
    none = jnp.zeros((HEAD_DIM, block.shape[1]), block.dtype)
    return jnp.concatenate(
        [
            jnp.concatenate(
                [block[g * HEAD_DIM : (g + 1) * HEAD_DIM] if g == h else none for g in range(HEADS)],
                axis=0,
            )
            for h in range(HEADS)
        ],
        axis=1,
    )


def by_head(rows, spread):
    columns = spread.shape[1] // HEADS
    return jnp.concatenate(
        [
            dot(rows[h * HEAD_DIM : (h + 1) * HEAD_DIM], spread[:, h * columns : (h + 1) * columns])
            for h in range(HEADS)
        ],
        axis=0,
    )


def window_mask(q_first, q_bounds, k_first, k_bounds, q_low, q_high, causal):
    q = lax.broadcasted_iota(jnp.int32, (1, WINDOW), 1) + q_first
    k = lax.broadcasted_iota(jnp.int32, (WINDOW, WINDOW), 0) + k_first
    q_id = sum((q >= bound).astype(jnp.int32) for bound in q_bounds)
    k_id = sum((k >= bound).astype(jnp.int32) for bound in k_bounds)
    allowed = k_id == q_id
    if causal:
        allowed = allowed & (k <= q)
    valid = (q >= jnp.maximum(q_bounds[0], q_low)) & (q < jnp.minimum(q_bounds[3], q_high))
    return jnp.concatenate([allowed] * HEADS, axis=1), jnp.concatenate([valid] * HEADS, axis=1)


def window_weights(scores, masks):
    scores = [jnp.where(allowed, each, MASKED) for each, (allowed, _) in zip(scores, masks)]
    weights = [jnp.exp(each - jnp.max(each, axis=0, keepdims=True)) for each in scores]
    inverses = [
        jnp.where(valid, 1.0 / jnp.sum(each, axis=0, keepdims=True), 0.0)
        for each, (_, valid) in zip(weights, masks)
    ]
    return [each * inverse for each, inverse in zip(weights, inverses)]


def attend_windows(windows):
    qs, ks, vs, masks = zip(*windows)
    q_rows = [spread_rows((q * jnp.asarray(HEAD_DIM**-0.5, BF16)).T) for q in qs]
    scores = [dot(k, q) for k, q in zip(ks, q_rows)]
    probabilities = [each.astype(BF16) for each in window_weights(scores, masks)]
    mixes = [by_head(v.T, each) for v, each in zip(vs, probabilities)]
    return [mix.astype(BF16).T for mix in mixes]


def attend_windows_back(windows):
    qs, ks, vs, grads, masks = zip(*windows)
    scale = HEAD_DIM**-0.5
    qs = [q * jnp.asarray(scale, BF16) for q in qs]
    scores = [dot(k, spread_rows(q.T)) for k, q in zip(ks, qs)]
    prob_grads = [dot(v, spread_rows(grad.T)) for v, grad in zip(vs, grads)]
    probabilities = window_weights(scores, masks)
    inners = [
        jnp.sum(each * grad, axis=0, keepdims=True) for each, grad in zip(probabilities, prob_grads)
    ]
    score_grads = [
        (each * (grad - inner)).astype(BF16)
        for each, grad, inner in zip(probabilities, prob_grads, inners)
    ]
    v_grads = [
        dot(each.astype(BF16), spread_lanes(grad)) for each, grad in zip(probabilities, grads)
    ]
    q_grads = [by_head(k.T, each) for k, each in zip(ks, score_grads)]
    k_grads = [dot(each, spread_lanes(q)) for each, q in zip(score_grads, qs)]
    q_grads = [(each * scale).astype(BF16).T for each in q_grads]
    return [(q, k.astype(BF16), v.astype(BF16)) for q, k, v in zip(q_grads, k_grads, v_grads)]


def out_product(mixes, outs):
    left = sum(dot(mix, out[0:HALF]) for mix, out in zip(mixes, outs))
    right = sum(dot(mix, out[HALF:]) for mix, out in zip(mixes, outs))
    return jnp.concatenate([left, right], axis=1)


def out_mix_grads(grad_low, outs, mix_grads, first):
    rows = grad_low.shape[0]
    for half in range(2):
        for lo in range(0, rows, HALF):
            block = grad_low[lo : lo + HALF]
            mix_grad = dot_nt(block[:, :HALF], outs[half, 0:HALF]) + dot_nt(block[:, HALF:], outs[half, HALF:])
            mix_grads[half, first + lo : first + lo + HALF] = mix_grad.astype(BF16)


def out_weight_grads(grad_low, mixes, grads):
    for half, mix in enumerate(mixes):
        grads[half, 0:HALF] = dot_tn(mix, grad_low[:, :HALF]).astype(BF16)
        grads[half, HALF:] = dot_tn(mix, grad_low[:, HALF:]).astype(BF16)


def copy_by_role(meta, pairs_zero, pairs_one, sem):
    @pl.when(meta[0] == 0)
    def _():
        for source, target in pairs_zero:
            pltpu.make_async_copy(source, target, sem).start()

    @pl.when(meta[0] == 1)
    def _():
        for source, target in pairs_one:
            pltpu.make_async_copy(source, target, sem).start()


def wait_by_role(meta, pairs_zero, pairs_one, sem):
    @pl.when(meta[0] == 0)
    def _():
        for source, target in pairs_zero:
            pltpu.make_async_copy(source, target, sem).wait()

    @pl.when(meta[0] == 1)
    def _():
        for source, target in pairs_one:
            pltpu.make_async_copy(source, target, sem).wait()


def states_copies(rows_ref, other_ref, held, here):
    zero = [(other_ref.at[pl.ds(0, here)], held.at[pl.ds(HALO, here)])]
    one = [(rows_ref.at[pl.ds(here - HALO, here + HALO)], held.at[pl.ds(0, here + HALO)])]
    return zero, one


def self_attention(meta, segs, plan, here, qkvs, mixes):
    full = here + HALO
    for mix in mixes:
        mix[...] = jnp.zeros(mix.shape, BF16)

    def group(bounds, _):
        first = window_of(bounds[0])
        mask = window_mask(first, bounds, first, bounds, HALO, full, True)
        at = pl.ds(first, WINDOW)
        return [(qkv[0, at], qkv[1, at], qkv[2, at], mask) for qkv in qkvs]

    def store(bounds, _, result):
        at = pl.ds(window_of(bounds[0]), WINDOW)
        for mix, each in zip(mixes, result):
            mix[at] += each

    together = 2 * GROUPS // len(qkvs)
    each_group(meta, segs, plan, here, False, together, group, attend_windows, store)


def self_project(normed, held, qkv):
    full = normed.shape[0]
    qkv[:, full:] = jnp.zeros((3, WINDOW, HALF), BF16)
    for c in range(3):
        qkv[c, 0:full] = dot(normed[...], held[c]).astype(BF16)


def self_forward(
    meta, segs, rows_ref, other_ref, gain, bias, own, own_out, w1, w2, w3, w4,
    hidden, normed, qkv, mix, plan, states, held, outs, sem_w, sem_x,
):
    full = states.shape[0]
    here = full - HALO
    state_copies = states_copies(rows_ref, other_ref, states, here)
    copy_by_role(meta, *state_copies, sem_x)
    weights = start_other(meta[1], (w1, w2, w3, w4), 0, held, sem_w)
    weights += start_out_own(own_out, outs, sem_w)
    mix.ref[...] = jnp.zeros(mix.ref.shape, BF16)
    wait_by_role(meta, *state_copies, sem_x)

    @pl.when(meta[0] == 0)
    def _():
        states[0:HALO] = jnp.zeros((HALO, states.shape[1]), BF16)

    for lo in range(0, full, HALO):
        hat, _ = norm_parts(states[lo : lo + HALO].astype(F32))
        normed.ref[lo : lo + HALO] = (hat * gain[0:1] + bias[0:1]).astype(BF16)
    normed.send()
    own = own()
    wait(weights)
    qkv.ref[:, :, full:] = jnp.zeros((2, 3, WINDOW, HALF), BF16)
    for half, matrices in enumerate((own, held)):
        for c in range(3):
            qkv.ref[half, c, 0:full] = dot(normed.ref[...], matrices[c]).astype(BF16)
    qkv.send()

    def group(bounds, _):
        first = window_of(bounds[0])
        mask = window_mask(first, bounds, first, bounds, HALO, full, True)
        at = pl.ds(first, WINDOW)
        return [(qkv.ref[half, 0, at], qkv.ref[half, 1, at], qkv.ref[half, 2, at], mask) for half in range(2)]

    def store(bounds, _, result):
        at = pl.ds(window_of(bounds[0]), WINDOW)
        for half in range(2):
            mix.ref[half, at] += result[half]

    each_group(meta, segs, plan, here, False, GROUPS, group, attend_windows, store)
    mix.send()
    for lo in range(HALO, full, HALF):
        at = slice(lo, lo + HALF)
        hidden[lo - HALO : lo - HALO + HALF] = states[at].astype(F32) + out_product(
            [mix.ref[0, at], mix.ref[1, at]], [outs, held[3]]
        )


def blocks_do(low, high, pairs, target, sem, act):
    def one(block, _):
        at = pl.ds(pl.multiple_of(block * HALF, HALF), HALF)
        act(pltpu.make_async_copy(pairs.at[:, :, at], target.at[:, :, at], sem))
        return 0

    lax.fori_loop(low // HALF, (high + HALF - 1) // HALF, one, 0)


def zero_after(high, pairs):
    end = pl.multiple_of(((high + HALF - 1) // HALF) * HALF, HALF)
    pairs[:, :, pl.ds(end, WINDOW)] = jnp.zeros((2, 2, WINDOW, HALF), BF16)


def memory_copies(rows_ref, other_ref, held):
    return [(rows_ref, held)], [(other_ref, held)]


def cross_forward(
    meta, segs, rows_ref, other_ref, hidden, gain, bias, own_q, own_pair, own_out, w1, w2, w3, w4,
    hidden_two, hidden_far, normed, mix, queries, pairs_far, plan, pairs, memory, held, outs, sem_w, sem_x, sem_h,
):
    here = hidden_two.shape[0]
    hidden_copy = pltpu.make_async_copy(hidden, hidden_far, sem_h.at[0])
    hidden_copy.start()
    full = here + HALO
    copies = memory_copies(rows_ref, other_ref, memory)
    copy_by_role(meta, *copies, sem_x)
    weights = start_other(meta[2], (w1, w2, w3, w4), 0, held, sem_w)
    weights += start_out_own(own_out, outs, sem_w)
    queries.ref[:, 0:HALO] = jnp.zeros((2, HALO, HALF), BF16)
    queries.ref[:, full:] = jnp.zeros((2, WINDOW, HALF), BF16)
    mix.ref[...] = jnp.zeros(mix.ref.shape, BF16)
    low, high = sentence_range(meta, segs, here)
    zero_after(high, pairs)
    for lo in range(0, here, HALF):
        at = slice(lo, lo + HALF)
        hat, _ = norm_parts(hidden[at])
        normed.ref[at] = (hat * gain[1:2] + bias[1:2]).astype(BF16)
    normed.send()
    own_q, own_pair = own_q(), own_pair()
    wait(weights)
    for half, matrix in enumerate((own_q, held.at[0])):
        queries.ref[half, HALO:full] = dot(normed.ref[...], matrix[...]).astype(BF16)
    queries.send()
    wait_by_role(meta, *copies, sem_x)

    def project(block, _):
        at = pl.ds(pl.multiple_of(block * HALF, HALF), HALF)
        for c in range(2):
            pairs[0, c, at] = dot(memory[at], own_pair[c]).astype(BF16)
            pairs[1, c, at] = dot(memory[at], held[1 + c]).astype(BF16)
        return 0

    lax.fori_loop(low // HALF, (high + HALF - 1) // HALF, project, 0)
    blocks_do(low, high, pairs, pairs_far, sem_h.at[1], lambda copy: copy.start())

    def group(bounds, source_bounds):
        first = window_of(bounds[0])
        source_first = window_of(source_bounds[0])
        mask = window_mask(first, bounds, source_first, source_bounds, HALO, full, False)
        at = pl.ds(first, WINDOW)
        source_at = pl.ds(source_first, WINDOW)
        return [
            (queries.ref[half, at], pairs[half, 0, source_at], pairs[half, 1, source_at], mask)
            for half in range(2)
        ]

    def store(bounds, _, result):
        at = pl.ds(window_of(bounds[0]), WINDOW)
        for half in range(2):
            mix.ref[half, at] += result[half]

    each_group(meta, segs, plan, here, True, GROUPS, group, attend_windows, store)
    mix.send()
    for lo in range(0, here, HALF):
        at = slice(lo, lo + HALF)
        mix_at = slice(HALO + lo, HALO + lo + HALF)
        hidden_two[at] = hidden[at] + out_product([mix.ref[0, mix_at], mix.ref[1, mix_at]], [outs, held[3]])
    hidden_copy.wait()
    blocks_do(low, high, pairs, pairs_far, sem_h.at[1], lambda copy: copy.wait())


def gelu_both(inner):
    rate = 0.7978845608028654
    square = inner * inner
    bent = jnp.tanh(rate * inner * (1.0 + 0.044715 * square))
    half = 0.5 * (1.0 + bent)
    slope = half + 0.5 * inner * (1.0 - bent * bent) * (rate * (1.0 + 3 * 0.044715 * square))
    return inner * half, slope


def column(values, role, at):
    lanes = lax.broadcasted_iota(jnp.int32, (WINDOW, WINDOW), 1)
    own = lax.broadcasted_iota(jnp.int32, (WINDOW, WINDOW), 0) == lanes
    blocks = []
    for block in range(at.start // WINDOW, at.stop // WINDOW):
        row = values[role, block : block + 1]
        blocks.append(jnp.sum(jnp.where(own, row, 0.0), axis=1, keepdims=True))
    return jnp.concatenate(blocks, axis=0)


def feed_forward(
    meta, hidden_two, cotangent, targets, gain, bias, halt_weight, halt_bias,
    own_in, i1, i2, i3, i4, own_out, o1, o2, o3, o4,
    result_low, hidden_grad, small, keep, send,
    held_in, held_out, normed, active, slopes, total, out_low, cot, grads, sem_w, sem_o, sem_x, sem_g,
):
    here, width = total.shape
    first = pl.multiple_of(meta[0] * here, here)
    cot_copy = pltpu.make_async_copy(cotangent.at[pl.ds(first, here)], cot, sem_x.at[0])
    weights = start_in(meta, own_in, (i1, i2, i3, i4), held_in, sem_w)
    weights += start_out(meta, own_out, (o1, o2, o3, o4), held_out, sem_o)
    cot_copy.start()
    blocks = [slice(lo, lo + HALF) for lo in range(0, here, HALF)]
    for at in blocks:
        hat, _ = norm_parts(hidden_two[at])
        normed[at] = (hat * gain[2:3] + bias[2:3]).astype(BF16)
        total[at] = hidden_two[at]
    wait(weights)

    def forward(pair, _):
        js = (2 * pair, 2 * pair + 1)
        for at in blocks:
            inners = [dot(normed[at], held_in[j]) for j in js]
            both = [gelu_both(inner) for inner in inners]
            values = [value.astype(BF16) for value, _ in both]
            for j, value, (_, slope) in zip(js, values, both):
                active[j, at] = value
                slopes[j, at] = slope
            total[at] += sum(dot(value, held_out[j]) for j, value in zip(js, values))
        return 0

    lax.fori_loop(0, 4, forward, 0)
    cot_copy.wait()
    weight_sum = jnp.zeros((1, width), F32)
    bias_sum = jnp.zeros((1, 1), F32)
    for at in blocks:
        result = total[at]
        result_low.ref[at] = result.astype(BF16)
        logits = jnp.sum(result * halt_weight[...], axis=-1, keepdims=True) + halt_bias[0]
        halt_grad = 1.0 / (1.0 + jnp.exp(-logits)) - column(targets, meta[0], at)
        out_grad = cot[at].astype(F32) + halt_grad * halt_weight[...]
        out_low[at] = out_grad.astype(BF16)
        hidden_grad[at] = out_grad
        total[at] = jnp.zeros((HALF, width), F32)
        weight_sum += jnp.sum(halt_grad * result, axis=0, keepdims=True)
        bias_sum += jnp.sum(halt_grad, axis=0, keepdims=True)
    result_low.send()

    def backward(j, _):
        inner_grads = []
        for at in blocks:
            inner_grad = (dot_nt(out_low[at], held_out[j]) * slopes[j, at]).astype(BF16)
            inner_grads.append(inner_grad)
            total[at] += dot_nt(inner_grad, held_in[j])
        half, block = j // 4, j % 4
        grads[8 * half + block] = dot_tn(normed[...], jnp.concatenate(inner_grads, axis=0)).astype(BF16)
        grads[8 * half + 4 + block, 0:HALF] = dot_tn(active[j], out_low[:, :HALF]).astype(BF16)
        grads[8 * half + 4 + block, HALF:] = dot_tn(active[j], out_low[:, HALF:]).astype(BF16)
        return 0

    lax.fori_loop(0, 8, backward, 0)
    copies = put_grads(meta, grads, keep, send, sem_g)
    gain_sum = jnp.zeros_like(weight_sum)
    shift_sum = jnp.zeros_like(weight_sum)
    for at in blocks:
        hat, scale = norm_parts(hidden_two[at])
        grad = total[at]
        hidden_grad[at] += norm_back(grad, hat, scale, gain[2:3])
        gain_sum += jnp.sum(grad * hat, axis=0, keepdims=True)
        shift_sum += jnp.sum(grad, axis=0, keepdims=True)
    small[...] = jnp.concatenate(
        [gain_sum, shift_sum, weight_sum, jnp.broadcast_to(bias_sum, weight_sum.shape)], axis=0
    )
    wait(copies)


def out_backward(
    meta, upper_grad, mix, own_out, w1, w2, w3, w4, mix_grads, out_part, upper_far, outs, sem_w, sem_h, *, place
):
    full = mix_grads.shape[1] - WINDOW
    weights = start_other(meta[place], (w1, w2, w3, w4), 3, outs.at[pl.ds(1, 1)], sem_w)
    weights += start_out_own(own_out, outs.at[0], sem_w)
    upper_copy = pltpu.make_async_copy(upper_grad, upper_far, sem_h.at[0])
    upper_copy.start()
    mix_grads[:, 0:HALO] = jnp.zeros((2, HALO, HALF), BF16)
    mix_grads[:, full:] = jnp.zeros((2, WINDOW, HALF), BF16)
    grad_low = upper_grad[...].astype(BF16)
    wait(weights)
    out_mix_grads(grad_low, outs, mix_grads, HALO)
    mix = mix()
    out_weight_grads(grad_low, [mix[0, HALO:full], mix[1, HALO:full]], out_part.ref)
    upper_copy.wait()


def cross_backward(meta, segs, mix_grads, queries, pairs_far, q_grad, pair_grads, plan, pairs, sem_h):
    full = mix_grads.shape[1] - WINDOW
    here = full - HALO
    low, high = sentence_range(meta, segs, here)
    blocks_do(low, high, pairs_far, pairs, sem_h.at[0], lambda copy: copy.start())
    q_grad[...] = jnp.zeros(q_grad.shape, BF16)
    pair_grads[...] = jnp.zeros(pair_grads.shape, BF16)
    zero_after(high, pairs)
    queries = queries()
    blocks_do(low, high, pairs_far, pairs, sem_h.at[0], lambda copy: copy.wait())

    def group(bounds, source_bounds):
        first = window_of(bounds[0])
        source_first = window_of(source_bounds[0])
        mask = window_mask(first, bounds, source_first, source_bounds, HALO, full, False)
        at = pl.ds(first, WINDOW)
        source_at = pl.ds(source_first, WINDOW)
        return [
            (
                queries[half, at], pairs[half, 0, source_at], pairs[half, 1, source_at],
                mix_grads[half, at], mask,
            )
            for half in range(2)
        ]

    def store(bounds, source_bounds, result):
        at = pl.ds(window_of(bounds[0]), WINDOW)
        source_at = pl.ds(window_of(source_bounds[0]), WINDOW)
        for half, (dq, dk, dv) in enumerate(result):
            q_grad[half, at] += dq
            pair_grads[half, 0, source_at] += dk
            pair_grads[half, 1, source_at] += dv

    each_group(meta, segs, plan, here, True, GROUPS, group, attend_windows_back, store)


def cross_products(
    meta, segs, rows_ref, other_ref, hidden, normed, upper_grad, q_grad, pair_grads, out_part, own_q, own_pair,
    w1, w2, w3, w4, gain,
    lower_grad, memory_grad, small, keep, send, memory, pair_sums, grads, held, sem_w, sem_x, sem_g,
):
    here, width = lower_grad.shape
    full = here + HALO
    weights = start_other(meta[2], (w1, w2, w3, w4), 0, held, sem_w)
    copies = memory_copies(rows_ref, other_ref, memory)
    copy_by_role(meta, *copies, sem_x)
    pair_sums[...] = jnp.zeros(pair_sums.shape, F32)
    memory_grad.ref[...] = jnp.zeros(memory_grad.ref.shape, BF16)
    source_low, source_high = sentence_range(meta, segs, here)
    parts = start(
        [pltpu.make_async_copy(out_part.at[half], grads.at[4 * half + 3], sem_g.at[0]) for half in range(2)]
    )
    gain_sum = jnp.zeros((1, width), F32)
    shift_sum = jnp.zeros((1, width), F32)
    own_q, own_pair = own_q(), own_pair()
    wait(weights)
    wait_by_role(meta, *copies, sem_x)

    def project(block, _):
        at = pl.ds(pl.multiple_of(block * HALF, HALF), HALF)
        row_grad = jnp.zeros((HALF, width), F32)
        for half in range(2):
            for c in range(2):
                low = pair_grads[half, c, at]
                row_grad += dot_nt(low, held[1 + c] if half else own_pair[c])
                pair_sums[half, c] += dot_tn(memory[at], low)
        memory_grad.ref[at] = row_grad.astype(BF16)
        return 0

    lax.fori_loop(source_low // HALF, (source_high + HALF - 1) // HALF, project, 0)
    memory_grad.send()
    for half in range(2):
        for c in range(2):
            grads[4 * half + 1 + c] = pair_sums[half, c].astype(BF16)
    normed = normed()
    for half in range(2):
        grads[4 * half] = dot_tn(normed[...], q_grad[half, HALO:full]).astype(BF16)
    wait(parts)
    put = put_grads(meta, grads, keep, send, sem_g, x_first=True)
    hidden, upper_grad = hidden(), upper_grad()
    for lo in range(0, here, HALF):
        at = slice(lo, lo + HALF)
        q_at = slice(HALO + lo, HALO + lo + HALF)
        hat, scale = norm_parts(hidden[at])
        grad = dot_nt(q_grad[0, q_at], own_q[...]) + dot_nt(q_grad[1, q_at], held[0])
        lower_grad[at] = upper_grad[at] + norm_back(grad, hat, scale, gain[1:2])
        gain_sum += jnp.sum(grad * hat, axis=0, keepdims=True)
        shift_sum += jnp.sum(grad, axis=0, keepdims=True)
    small[...] = jnp.concatenate([gain_sum, shift_sum], axis=0)
    wait(put)


def self_backward(meta, segs, mix_grads, qkv, qkv_grads, plan):
    full = mix_grads.shape[1] - WINDOW
    here = full - HALO
    qkv_grads[...] = jnp.zeros(qkv_grads.shape, BF16)
    qkv = qkv()

    def group(bounds, _):
        first = window_of(bounds[0])
        mask = window_mask(first, bounds, first, bounds, HALO, full, True)
        at = pl.ds(first, WINDOW)
        return [
            (qkv[half, 0, at], qkv[half, 1, at], qkv[half, 2, at], mix_grads[half, at], mask)
            for half in range(2)
        ]

    def store(bounds, _, result):
        at = pl.ds(window_of(bounds[0]), WINDOW)
        for half in range(2):
            for c in range(3):
                qkv_grads[half, c, at] += result[half][c]

    each_group(meta, segs, plan, here, False, GROUPS, group, attend_windows_back, store)


def self_products(meta, normed, qkv_grads, out_part, keep, send, grads_far, grads, sem_g, sem_h):
    grads_copy = pltpu.make_async_copy(qkv_grads, grads_far, sem_h.at[0])
    grads_copy.start()
    parts = start(
        [pltpu.make_async_copy(out_part.at[half], grads.at[4 * half + 3], sem_g.at[0]) for half in range(2)]
    )
    normed = normed()
    full = normed.shape[0]
    for half in range(2):
        for c in range(3):
            grads[4 * half + c] = dot_tn(normed[...], qkv_grads[half, c, 0:full]).astype(BF16)
    wait(parts)
    wait(put_grads(meta, grads, keep, send, sem_g))
    grads_copy.wait()


def states_backward(
    meta, rows_ref, other_ref, upper_grad, qkv_grads, own, w1, w2, w3, w4, gain,
    state_grad, state_low, halo_grad, small, states, held, sem_w, sem_x,
):
    full, width = states.shape
    here = full - HALO
    weights = start_other(meta[1], (w1, w2, w3, w4), 0, held, sem_w)
    state_copies = states_copies(rows_ref, other_ref, states, here)
    copy_by_role(meta, *state_copies, sem_x)
    gain_sum = jnp.zeros((1, width), F32)
    shift_sum = jnp.zeros((1, width), F32)
    wait_by_role(meta, *state_copies, sem_x)

    @pl.when(meta[0] == 0)
    def _():
        states[0:HALO] = jnp.zeros((HALO, width), BF16)

    upper_grad, qkv_grads, own = upper_grad(), qkv_grads(), own()
    wait(weights)
    for lo in range(0, full, HALO):
        at = slice(lo, lo + HALO)
        hat, scale = norm_parts(states[at].astype(F32))
        grad = sum(
            dot_nt(qkv_grads[half, c, at], matrices[c])
            for half, matrices in enumerate((own, held))
            for c in range(3)
        )
        back = norm_back(grad, hat, scale, gain[0:1])
        if lo == 0:
            halo_grad.ref[...] = back
        else:
            back += upper_grad[lo - HALO : lo]
            state_grad.ref[lo - HALO : lo] = back
            state_low.ref[lo - HALO : lo] = back.astype(BF16)
        gain_sum += jnp.sum(grad * hat, axis=0, keepdims=True)
        shift_sum += jnp.sum(grad, axis=0, keepdims=True)
    small[...] = jnp.concatenate([gain_sum, shift_sum], axis=0)


def finish_rows(
    meta, rows, low_result, result, low_grad, grad, halo_grad, memory_part, other_memory,
    layer_out, input_grads, parts, halo, sem,
):
    here = result.shape[0]
    low, high = pl.ds(0, here), pl.ds(here, here)

    @pl.when(meta[0] == 0)
    def _():
        copies = [(rows, layer_out.ref), (memory_part, parts.at[0]), (other_memory, parts.at[1])]
        wait(start([pltpu.make_async_copy(*copy, sem) for copy in copies]))
        input_grads.ref[...] = parts[0].astype(F32) + parts[1].astype(F32)

    @pl.when(meta[0] == 1)
    def _():
        copies = [
            (low_result, layer_out.ref.at[low]),
            (result, layer_out.ref.at[high]),
            (low_grad, parts.at[0, low]),
            (grad, input_grads.ref.at[high]),
            (halo_grad, halo),
        ]
        wait(start([pltpu.make_async_copy(*copy, sem) for copy in copies]))
        input_grads.ref[0:here] = parts[0, 0:here].astype(F32)
        input_grads.ref[here - HALO : here] += halo[...]


def unpack(kind, meta, mine, by_x, by_role, by_both, *rest):
    outs, (held, sem) = rest[:-2], rest[-2:]
    rows = mine.shape[1]
    copies = []
    for rel, ref in ((0, mine), (2, by_x), (1, by_role), (3, by_both)):
        first = pl.multiple_of((rel ^ meta[1]) * rows, rows)
        copy = pltpu.make_async_copy(ref, held.at[:, pl.ds(first, rows)], sem.at[0])
        copy.start()
        copies.append(copy)
    for copy in copies:
        copy.wait()
    if kind == "ffn":
        grad_in, grad_out = outs
        for j in range(4):
            at = slice(j * HALF, (j + 1) * HALF)
            grad_in[:, at] = held[j].astype(F32)
            grad_out[at, 0:HALF] = held[4 + j, 0:HALF].astype(F32)
            grad_out[at, HALF:] = held[4 + j, HALF:].astype(F32)
        return
    if kind == "cross":
        outs[0][...] = held[0].astype(F32)
        for c in range(2):
            outs[1][:, c] = held[1 + c].astype(F32)
    else:
        outs[0][...] = held[0:3].astype(F32)
    outs[-1][:, 0:HALF] = held[3, 0:HALF].astype(F32)
    outs[-1][:, HALF:] = held[3, HALF:].astype(F32)


def shape(*dims, dtype=F32):
    return jax.ShapeDtypeStruct(dims, dtype)


def far(*dims, dtype=F32):
    return pltpu.HBM(dims, dtype)


def near(*dims, dtype=F32):
    return pltpu.VMEM(dims, dtype)


class Put:
    def __init__(self, *dims, dtype=F32):
        self.shape = far(*dims, dtype=dtype)
        self.scratch = pltpu.VMEM(dims, dtype)


class Get:
    def __init__(self, value):
        self.value = value
        self.scratch = pltpu.VMEM(value.shape, value.dtype)


class Here:
    def __init__(self, value):
        self.value = value


class Any:
    def __init__(self, value):
        self.value = value


class Far:
    def __init__(self, value):
        self.value = value


def call(body, ins, outs, scratch, weight):
    smem, others = ins
    operands = list(smem) + list(others)
    values, in_specs = list(smem), [SMEM] * len(smem)
    for other in others:
        if isinstance(other, (Get, Far)):
            values.append(pltpu.with_memory_space_constraint(other.value, pltpu.HBM))
            in_specs.append(ANY)
        elif isinstance(other, Any):
            values.append(other.value)
            in_specs.append(ANY)
        elif isinstance(other, Here):
            values.append(pltpu.with_memory_space_constraint(other.value, pltpu.VMEM))
            in_specs.append(VMEM)
        else:
            values.append(other)
            in_specs.append(VMEM)
    moved = [at for at, each in enumerate(operands) if isinstance(each, Get)]
    put = [at for at, each in enumerate(outs) if isinstance(each, Put)]

    def inner(*refs):
        in_refs, refs = list(refs[: len(values)]), refs[len(values) :]
        out_refs, refs = list(refs[: len(outs)]), refs[len(outs) :]
        moved_refs, refs = refs[: len(moved)], refs[len(moved) :]
        put_refs, refs = refs[: len(put)], refs[len(put) :]
        sems, refs = refs[0], refs[1:]
        for i, at in enumerate(moved):
            in_refs[at] = Load(in_refs[at], moved_refs[i], sems.at[i])
        for i, at in enumerate(put):
            out_refs[at] = Store(put_refs[i], out_refs[at], sems.at[len(moved) + i])
        body(*in_refs, *out_refs, *refs)
        for at in moved:
            in_refs[at]()
        for at in put:
            out_refs[at].send()
        wait([out_refs[at].copy for at in put])

    return pl.pallas_call(
        inner,
        out_shape=[out.shape if isinstance(out, Put) else out for out in outs],
        in_specs=in_specs,
        out_specs=[ANY if isinstance(out, Put) or getattr(out, "memory_space", None) is pltpu.HBM else VMEM for out in outs],
        scratch_shapes=[operands[at].scratch for at in moved]
        + [outs[at].scratch for at in put]
        + [pltpu.SemaphoreType.DMA((len(moved) + len(put) + 1,))]
        + list(scratch),
        name=getattr(body, "__name__", "out_backward"),
        compiler_params=pltpu.CompilerParams(vmem_limit_bytes=VMEM_LIMIT),
        cost_estimate=pl.CostEstimate(flops=int(weight * WEIGHT), bytes_accessed=0, transcendentals=0),
    )(*values)


def flip(value, axis, bit=1):
    count = lax.axis_size(axis)
    return lax.ppermute(value, axis, [(i, i ^ bit) for i in range(count)])


def add(a, b):
    return (a.astype(F32) + b.astype(F32)).astype(BF16)


def after(value, *events):
    return lax.optimization_barrier((value, events))[0]


class Order:
    def __init__(self, meta):
        self.meta = meta
        self.last = ()

    def now(self):
        return after(self.meta, *self.last)

    def __call__(self, weight, *jobs):
        operands = [value for job in jobs for value in job[0]]
        shapes = [each for job in jobs for each in job[1]]

        def sums(meta, *refs):
            ins, outs = list(refs[: len(operands)]), list(refs[len(operands) :])
            for values, results, body, _ in jobs:
                body(meta, ins[: len(values)], outs[: len(results)])
                ins, outs = ins[len(values) :], outs[len(results) :]

        results = list(
            pl.pallas_call(
                sums,
                out_shape=shapes,
                in_specs=[SMEM] + [VMEM] * len(operands),
                out_specs=[VMEM] * len(shapes),
                name="sums",
                compiler_params=pltpu.CompilerParams(vmem_limit_bytes=VMEM_LIMIT),
                cost_estimate=pl.CostEstimate(flops=int(weight * WEIGHT), bytes_accessed=0, transcendentals=0),
            )(self.now(), *operands)
        )
        self.last = tuple(results)
        for _, each, _, take in jobs:
            take(results[: len(each)])
            results = results[len(each) :]


class Sum:
    def __init__(self, keep, send, routes):
        self.routes = routes
        self.near, self.got = [keep], [flip(send, "role")]

    def job(self, shapes, body, take):
        count = len(self.near)
        return (
            [*self.near, *self.got],
            [jax.ShapeDtypeStruct(each, BF16) for each in shapes],
            lambda meta, ins, outs: body(meta, ins[:count], ins[count:], outs),
            take,
        )

    def pass_on(self, stage):
        def take(parts):
            self.near = parts[0::2]
            self.got = [step(away, route[stage]) for away, route in zip(parts[1::2], self.routes)]

        return take

    def begin(self):
        count = len(self.routes)
        _, _, matrices, rows, columns = self.near[0].shape
        share = matrices // count

        def body(meta, near, got, outs):
            for at, route in enumerate(self.routes):
                mine = pl.ds(at * share, share)
                for which in range(2):
                    place = (slice(None), which, mine) if route[0] == "x" and count > 1 else (which, slice(None), mine)
                    outs[2 * at + which][...] = add(near[0][place], got[0][place])

        return self.job([(2, share, rows, columns)] * (2 * count), body, self.pass_on(0))

    def second(self):
        def body(meta, near, got, outs):
            for at in range(len(near)):
                for which in range(2):
                    outs[2 * at + which][...] = add(near[at][which], got[at][which])

        return self.job([self.near[0].shape[1:]] * (2 * len(self.near)), body, self.pass_on(1))

    def halve(self):
        count = len(self.near)
        matrices, rows, columns = self.near[0].shape
        half = count * matrices // 2

        def body(meta, near, got, outs):
            upper = meta[2] >> 1
            for out, which in zip(outs, (upper, 1 - upper)):
                if count == 1:
                    at = pl.ds(which * half, half)
                    out[...] = add(near[0][at], got[0][at])
                else:
                    both = [add(mine[...], theirs[...]) for mine, theirs in zip(near, got)]
                    out[...] = jnp.where(which == 1, both[1], both[0])

        def take(parts):
            self.near, self.got = [parts[0]], [flip(parts[1], "dp", 2)]

        return self.job([(half, rows, columns)] * 2, body, take)

    def plain(self, bit):
        def body(meta, near, got, outs):
            outs[0][...] = add(near[0][...], got[0][...])

        def take(parts):
            self.near, self.got = parts, [flip(parts[0], "dp", bit)]

        return self.job([self.near[0].shape], body, take)

    def whole(self):
        return self.plain(4)

    def back(self, order):
        bit = 8
        while bit < lax.axis_size("dp"):
            order(1, self.plain(bit))
            bit *= 2
        return self.plain(2)

    def last(self):
        half, rows, columns = self.near[0].shape

        def body(meta, near, got, outs):
            upper = meta[2] >> 1
            outs[0][pl.ds(upper * half, half)] = near[0][...]
            outs[0][pl.ds((1 - upper) * half, half)] = got[0][...]

        def take(parts):
            self.mine = parts[0]
            self.by_x = flip(self.mine, "dp", 1)

        return self.job([(2 * half, rows, columns)], body, take)

    def pieces(self):
        return self.mine, self.by_x, flip(self.mine, "role"), flip(self.by_x, "role")


def step(value, route):
    if route == "head":
        return flip(value, "head")
    return flip(value, "dp", 1)


class SmallSum:
    def __init__(self, value):
        count = lax.axis_size("dp")
        self.steps = [("role", 1), ("head", 1)] + [("dp", 1 << at) for at in range(count.bit_length() - 1)]
        self.value, self.got = value, flip(value, *self.steps.pop(0))

    def step(self):
        def body(meta, ins, outs):
            outs[0][...] = ins[0][...] + ins[1][...]

        def take(parts):
            self.value = parts[0]
            self.got = flip(self.value, *self.steps.pop(0)) if self.steps else None

        return [self.value, self.got], [jax.ShapeDtypeStruct(self.value.shape, F32)], body, take

    def total(self):
        while self.got is not None:
            self.value = self.value + self.got
            self.got = flip(self.value, *self.steps.pop(0)) if self.steps else None
        return self.value


def shards(
    layer_in,
    lengths,
    cotangent,
    targets,
    self_qkv,
    self_out,
    cross_q,
    cross_kv,
    cross_out,
    ffn_in,
    ffn_out,
    norm_gain,
    norm_bias,
    halt_weight,
    halt_bias,
):
    role, head, place = (lax.axis_index(name) for name in ("role", "head", "dp"))
    target_side = role == 1
    me = 2 * (place & 1) + role
    me_z = (place & 2) + role
    meta = jnp.stack([role, me, me_z]).astype(jnp.int32)

    rows = layer_in[0]
    row_len, width = rows.shape
    here = row_len // 2
    full = here + HALO

    other_rows = flip(rows, "role")
    lens = lax.dynamic_index_in_dim(lengths[0], head, 0, keepdims=False)
    other_lens = flip(lens, "role")
    segs = jnp.where(target_side, jnp.stack([other_lens, lens]), jnp.stack([lens, other_lens]))
    segs = jnp.pad(segs, ((0, 0), (0, 2)))

    self_own, cross_own = self_qkv.transpose(1, 0, 2), cross_kv.transpose(1, 0, 2)
    piece_shape = Put(4, width // PIECES, HALF, dtype=BF16)
    (self_piece,) = call(
        cut_self, ([meta], [Far(self_own), Far(self_out)]), [piece_shape], [pltpu.SemaphoreType.DMA((2,))], 1
    )
    cross_piece, in_piece, out_own_piece = call(
        cut_rest,
        ([meta], [Far(cross_q), Far(cross_own), Far(cross_out), Far(ffn_in), Far(ffn_out)]),
        [piece_shape, piece_shape, Put(HALF, width, dtype=BF16)],
        [pltpu.SemaphoreType.DMA((5,))],
        1,
    )
    self_first, cross_first, in_first, out_first = (
        flip(piece, "head") for piece in (self_piece, cross_piece, in_piece, out_own_piece)
    )

    plan = pltpu.SMEM((8, 40), jnp.int32)
    weight_sems = pltpu.SemaphoreType.DMA((6,))
    one_sem = pltpu.SemaphoreType.DMA
    grad_sems = pltpu.SemaphoreType.DMA((1,))
    states_held = pltpu.VMEM((full, width), BF16)
    memory_held = pltpu.VMEM((row_len, width), BF16)
    out_held = pltpu.VMEM((width, HALF), BF16)
    mix_grads = pltpu.VMEM((2, full + WINDOW, HALF), BF16)

    def heads(*dims):
        return Put(*dims, full + WINDOW, HALF, dtype=BF16)

    def matrices(count):
        return pltpu.VMEM((count, width, HALF), BF16)

    pair_shape = (2, 2, row_len + WINDOW, HALF)

    both_rows = Far(rows), Far(other_rows)

    self_first = after(self_first, cross_piece, other_lens)
    self_second = flip(self_first, "dp", 1)
    cross_second = flip(cross_first, "dp", 2)
    in_second = flip(in_first, "dp", 1)
    self_weights = [self_first, self_second, flip(self_first, "role"), flip(self_second, "role")]
    self_pieces = [Far(piece) for piece in self_weights]
    hidden, normed_one, qkv, self_mix = call(
        self_forward,
        (
            [after(meta, cross_first, in_first), segs],
            [*both_rows, norm_gain, norm_bias, Get(self_own), Far(self_out), *self_pieces],
        ),
        [near(here, width), Put(full, width, dtype=BF16), heads(2, 3), heads(2)],
        [plan, states_held, matrices(4), out_held, weight_sems, one_sem],
        11,
    )

    cross_second = after(cross_second, normed_one)
    cross_weights = [cross_first, cross_second, flip(cross_first, "role"), flip(cross_second, "role")]
    cross_pieces = [Far(piece) for piece in cross_weights]
    out_first = after(out_first, normed_one)
    out_second = flip(out_first, "dp", 2)
    hidden_two, hidden_far, normed_two, cross_mix, queries, pairs = call(
        cross_forward,
        (
            [meta, segs],
            [
                *both_rows, Here(hidden), norm_gain, norm_bias, Get(cross_q), Get(cross_own), Far(cross_out),
                *cross_pieces,
            ],
        ),
        [near(here, width), far(here, width), Put(here, width, dtype=BF16), heads(2), heads(2), far(*pair_shape, dtype=BF16)],
        [
            plan, pltpu.VMEM(pair_shape, BF16), memory_held, matrices(4), out_held, weight_sems, one_sem,
            pltpu.SemaphoreType.DMA((2,)),
        ],
        12,
    )

    in_second, out_second = after((in_second, out_second), normed_two)
    in_weights = in_first, in_second, flip(in_first, "role"), flip(in_second, "role")
    out_weights = out_first, out_second, flip(out_first, "role"), flip(out_second, "role")
    ffn_parts = far(2, 2, 8, width // PIECES, HALF, dtype=BF16)
    grad_parts = far(2, 2, 4, width // PIECES, HALF, dtype=BF16)
    result_low, two_grad, ffn_small, keep_ffn, send_ffn = call(
        feed_forward,
        (
            [meta],
            [
                Here(hidden_two), Far(cotangent), targets.astype(F32).reshape(2, here // WINDOW, WINDOW),
                norm_gain, norm_bias, halt_weight[None], halt_bias, Far(ffn_in), *map(Far, in_weights),
                Far(ffn_out), *map(Far, out_weights),
            ],
        ),
        [Put(here, width, dtype=BF16), near(here, width), shape(4, width), ffn_parts, ffn_parts],
        [
            matrices(8),
            pltpu.VMEM((8, HALF, width), BF16),
            pltpu.VMEM((here, width), BF16),
            pltpu.VMEM((8, here, HALF), BF16),
            pltpu.VMEM((8, here, HALF), F32),
            pltpu.VMEM((here, width), F32),
            pltpu.VMEM((here, width), BF16),
            pltpu.VMEM((here, width), BF16),
            matrices(16),
            weight_sems,
            weight_sems,
            pltpu.SemaphoreType.DMA((1,)),
            grad_sems,
        ],
        24,
    )

    mix_grads_shape = near(2, full + WINDOW, HALF, dtype=BF16)
    out_scratch = [matrices(2), weight_sems, grad_sems]
    cross_mix_grads, cross_out_part, two_far = call(
        functools.partial(out_backward, place=2),
        ([meta], [Here(two_grad), Get(cross_mix), Far(cross_out), *cross_pieces]),
        [mix_grads_shape, Put(2, width, HALF, dtype=BF16), far(here, width)],
        out_scratch,
        4,
    )

    order = Order(meta)
    ffn_sum = Sum(keep_ffn, send_ffn, FFN_ROUTES)
    order(1, ffn_sum.begin())
    query_grad, pair_grads = call(
        cross_backward,
        ([order.now(), segs], [Here(cross_mix_grads), Get(queries), Far(pairs)]),
        [near(2, full + WINDOW, HALF, dtype=BF16), near(*pair_shape, dtype=BF16)],
        [plan, pltpu.VMEM(pair_shape, BF16), grad_sems],
        9,
    )
    one_grad, memory_part, cross_small, keep_cross, send_cross = call(
        cross_products,
        (
            [meta, segs],
            [
                *both_rows, Get(hidden_far), Get(normed_two), Get(two_far), Here(query_grad), Here(pair_grads),
                Far(cross_out_part), Get(cross_q), Get(cross_own), *cross_pieces, norm_gain,
            ],
        ),
        [near(here, width), Put(row_len, width, dtype=BF16), shape(2, width), grad_parts, grad_parts],
        [
            memory_held,
            pltpu.VMEM((2, 2, width, HALF), F32),
            matrices(8),
            matrices(3),
            weight_sems,
            one_sem,
            grad_sems,
        ],
        8,
    )

    cross_sum = Sum(keep_cross, send_cross, CROSS_ROUTES)
    order(1, ffn_sum.second())
    self_mix_grads, self_out_part, one_far = call(
        functools.partial(out_backward, place=1),
        ([order.now()], [Here(one_grad), Get(self_mix), Far(self_out), *self_pieces]),
        [mix_grads_shape, Put(2, width, HALF, dtype=BF16), far(here, width)],
        out_scratch,
        4,
    )
    order(1, cross_sum.begin(), ffn_sum.halve())
    (qkv_grads,) = call(
        self_backward,
        ([order.now(), segs], [Here(self_mix_grads), Get(qkv)]),
        [near(2, 3, full + WINDOW, HALF, dtype=BF16)],
        [plan],
        9,
    )
    order(1, ffn_sum.whole(), cross_sum.second())
    keep_self, send_self, qkv_grads_far = call(
        self_products,
        ([order.now()], [Get(normed_one), Here(qkv_grads), Far(self_out_part)]),
        [grad_parts, grad_parts, far(2, 3, full + WINDOW, HALF, dtype=BF16)],
        [matrices(8), grad_sems, grad_sems],
        6,
    )
    self_sum = Sum(keep_self, send_self, SELF_ROUTES)
    to_target, to_memory = [(0, 1)], [(1, 0)]
    order.last = (keep_self,)
    order(1, self_sum.begin(), cross_sum.halve())
    state_grad, state_low, halo_grad, self_small = call(
        states_backward,
        (
            [order.now()],
            [*both_rows, Get(one_far), Get(qkv_grads_far), Get(self_own), *self_pieces, norm_gain],
        ),
        [Put(here, width), Put(here, width, dtype=BF16), Put(HALO, width), shape(2, width)],
        [states_held, matrices(3), weight_sems, one_sem],
        9,
    )
    order.last = (self_small,)
    small = SmallSum(
        jnp.concatenate(
            [
                self_small[0:1], cross_small[0:1], ffn_small[0:1],
                self_small[1:2], cross_small[1:2], ffn_small[1:2], ffn_small[2:4],
            ],
            axis=0,
        )
    )
    low_result, low_grad = lax.ppermute((result_low, state_low), "role", to_target)
    other_memory = lax.ppermute(memory_part, "role", to_memory)
    order(1, self_sum.second(), cross_sum.whole(), ffn_sum.back(order), small.step())
    order(1, self_sum.halve(), ffn_sum.last(), small.step())
    layer_out, input_grads = call(
        finish_rows,
        (
            [order.now()],
            [Any(each) for each in (rows, low_result, result_low, low_grad, state_grad, halo_grad, memory_part, other_memory)],
        ),
        [Put(row_len, width, dtype=BF16), Put(row_len, width)],
        [pltpu.VMEM((2, row_len, width), BF16), pltpu.VMEM((HALO, width), F32), one_sem],
        HEAVY,
    )
    order.last = (layer_out,)
    order(1, self_sum.whole(), cross_sum.back(order), small.step())

    def totals(kind, pieces, out_shapes):
        count, rows_each, columns = pieces[0].shape
        results = pl.pallas_call(
            functools.partial(unpack, kind),
            out_shape=out_shapes,
            in_specs=[SMEM] + [ANY] * 4,
            out_specs=[VMEM] * len(out_shapes),
            scratch_shapes=[
                pltpu.VMEM((count, PIECES * rows_each, columns), BF16),
                pltpu.SemaphoreType.DMA((1,)),
            ],
            name="unpack_" + kind,
            compiler_params=pltpu.CompilerParams(vmem_limit_bytes=24 << 20),
            cost_estimate=pl.CostEstimate(flops=int(HEAVY * WEIGHT), bytes_accessed=0, transcendentals=0),
        )(order.now(), *pieces)
        order.last = (results[-1],)
        return results

    ffn_in_grad, ffn_out_grad = totals(
        "ffn", ffn_sum.pieces(), (shape(width, 4 * HALF), shape(4 * HALF, width))
    )
    order(1, self_sum.back(order), cross_sum.last(), small.step())
    order(1, self_sum.last(), small.step())
    cross_q_grad, cross_kv_grad, cross_out_grad = totals(
        "cross", cross_sum.pieces(), (shape(width, HALF), shape(width, 2, HALF), shape(HALF, width))
    )
    self_qkv_grad, self_out_grad = totals(
        "self", self_sum.pieces(), (shape(3, width, HALF), shape(HALF, width))
    )
    small = small.total()
    return (
        layer_out[None],
        input_grads[None],
        self_qkv_grad.transpose(1, 0, 2),
        self_out_grad,
        cross_q_grad,
        cross_kv_grad,
        cross_out_grad,
        ffn_in_grad,
        ffn_out_grad,
        small[0:3],
        small[3:6],
        small[6],
        small[7, 0:1],
    )


def solution(mesh):
    placed = (
        P("role", ("dp", "head"), None),
        P("role", "dp", None),
        P(("dp", "head"), None),
        P(("dp", "head")),
        P(None, None, "head"),
        P("head", None),
        P(None, "head"),
        P(None, None, "head"),
        P("head", None),
        P(None, "head"),
        P("head", None),
        P(),
        P(),
        P(),
        P(),
    )
    return jax.shard_map(
        shards,
        mesh=mesh,
        in_specs=placed,
        out_specs=(
            P("role", ("dp", "head"), None),
            P("role", ("dp", "head"), None),
            P(None, None, "head"),
            P("head", None),
            P(None, "head"),
            P(None, None, "head"),
            P("head", None),
            P(None, "head"),
            P("head", None),
            P(),
            P(),
            P(),
            P(),
        ),
        check_vma=False,
    )
```

```python
import functools
import math

import jax
import jax.numpy as jnp
from jax import lax
from jax.experimental import pallas as pl
from jax.experimental.pallas import tpu as pltpu
from jax.sharding import PartitionSpec as P

F32 = jnp.float32
BF16 = jnp.bfloat16

HEAD_DIM = 64
HALF = 256
HEADS = HALF // HEAD_DIM
HALO = 128
GROUPS = 3
WINDOW = 128
MASKED = -1e30
SPARE = 8
WEIGHT = 1.2e9
ANY = pl.BlockSpec(memory_space=pl.ANY)
VMEM = pl.BlockSpec(memory_space=pltpu.VMEM)
SMEM = pl.BlockSpec(memory_space=pltpu.SMEM)
ARRIVALS = (0, 2, 1, 3)
FFN_ROUTES = [("head", "x"), ("x", "head")]
CROSS_ROUTES = [("x", "head")]
SELF_ROUTES = [("head", "x"), ("x", "head")]
HEAVY = 8
PIECES = 4


def dot(a, b):
    return jnp.dot(a, b, preferred_element_type=F32)


def dot_nt(a, b):
    return lax.dot_general(a, b, (((1,), (1,)), ((), ())), preferred_element_type=F32)


def dot_tn(a, b):
    return lax.dot_general(a, b, (((0,), (0,)), ((), ())), preferred_element_type=F32)


def norm_parts(values):
    center = values - jnp.mean(values, axis=-1, keepdims=True)
    spread = jnp.mean(center * center, axis=-1, keepdims=True)
    scale = lax.rsqrt(spread + 1e-05)
    return center * scale, scale


def norm_back(grad, hat, scale, gain):
    grad_hat = grad * gain
    first = jnp.mean(grad_hat, axis=-1, keepdims=True)
    second = jnp.mean(grad_hat * hat, axis=-1, keepdims=True)
    return scale * (grad_hat - first - hat * second)


class Load:
    def __init__(self, source, target, sem):
        self.target, self.copy = target, pltpu.make_async_copy(source, target, sem)
        self.gone = self.come = False

    def go(self):
        if not self.gone:
            self.copy.start()
        self.gone = True

    def __call__(self):
        self.go()
        if not self.come:
            self.copy.wait()
        self.come = True
        return self.target


class Store:
    def __init__(self, ref, target, sem):
        self.ref, self.copy, self.sent = ref, pltpu.make_async_copy(ref, target, sem), False

    def send(self):
        if not self.sent:
            self.copy.start()
        self.sent = True


def start(copies):
    for copy in copies:
        copy.start()
    return copies


def wait(copies):
    for copy in copies:
        copy.wait()


def cut_self(meta, matrices, out, piece, sem):
    wait(start(row_copies(meta[1], matrices, out, piece.ref, 0, sem)))


def row_copies(which, matrices, out, piece, first, sem):
    count, rows = matrices.shape[0], piece.shape[1]
    low = pl.multiple_of(which * rows, rows)
    out_low = pl.multiple_of((which & 1) * rows, rows)
    out_left = pl.multiple_of((which >> 1) * HALF, HALF)
    return [
        pltpu.make_async_copy(matrices.at[:, pl.ds(low, rows)], piece.at[pl.ds(first, count)], sem.at[0]),
        pltpu.make_async_copy(out.at[pl.ds(out_low, rows), pl.ds(out_left, HALF)], piece.at[3], sem.at[1]),
    ]


def cut_rest(meta, q, pair, out, ffn_in, ffn_out, cross_piece, in_piece, out_piece, sem):
    cross_piece, in_piece, out_piece = cross_piece.ref, in_piece.ref, out_piece.ref
    rows = cross_piece.shape[1]
    low = pl.multiple_of(meta[2] * rows, rows)
    copies = row_copies(meta[2], pair, out, cross_piece, 1, sem)
    copies.append(pltpu.make_async_copy(q.at[pl.ds(low, rows)], cross_piece.at[0], sem.at[2]))
    low = pl.multiple_of(meta[1] * rows, rows)
    for j in range(4):
        source = ffn_in.at[pl.ds(low, rows), pl.ds(j * HALF, HALF)]
        copies.append(pltpu.make_async_copy(source, in_piece.at[j], sem.at[3]))
    low = pl.multiple_of(meta[2] * HALF, HALF)
    copies.append(pltpu.make_async_copy(ffn_out.at[pl.ds(low, HALF)], out_piece, sem.at[4]))
    wait(start(copies))


def start_out_own(out, held, sem):
    return start(
        [
            pltpu.make_async_copy(out.at[:, pl.ds(c * HALF, HALF)], held.at[pl.ds(c * HALF, HALF)], sem.at[c])
            for c in range(2)
        ]
    )


def start_other(place, arrived, first, held, sem):
    rows, count = arrived[0].shape[1], held.shape[0]
    copies = []
    for at, (ref, flip) in enumerate(zip(arrived, ARRIVALS)):
        low = pl.multiple_of((place ^ flip) * rows, rows)
        source = ref.at[pl.ds(first, count)]
        copies.append(pltpu.make_async_copy(source, held.at[:, pl.ds(low, rows)], sem.at[2 + at]))
    return start(copies)


def start_in(meta, own, arrived, held, sem):
    copies = [
        pltpu.make_async_copy(own.at[:, pl.ds(j * HALF, HALF)], held.at[j], sem.at[0]) for j in range(4)
    ]
    return start(copies) + start_other(meta[1], arrived, 0, held.at[pl.ds(4, 4)], sem)


def start_out(meta, own, arrived, held, sem):
    copies = [
        pltpu.make_async_copy(own.at[pl.ds(j * HALF, HALF)], held.at[j], sem.at[0]) for j in range(4)
    ]
    for at, (ref, flip) in enumerate(zip(arrived, ARRIVALS)):
        copies.append(pltpu.make_async_copy(ref, held.at[4 + (meta[2] ^ flip)], sem.at[2 + at]))
    return start(copies)


def put_half(meta, grads, keep, send, sem, half, x_first=False):
    _, _, count, rows, _ = keep.shape
    copies = []
    for rel in range(PIECES):
        first = pl.multiple_of((rel ^ meta[1]) * rows, rows)
        source = grads.at[pl.ds(half * count, count), pl.ds(first, rows)]
        at = (rel >> 1, half) if x_first else (half, rel >> 1)
        target = (send if rel & 1 else keep).at[at]
        copies.append(pltpu.make_async_copy(source, target, sem.at[0]))
    return start(copies)


def put_grads(meta, grads, keep, send, sem, x_first=False):
    return [copy for half in range(2) for copy in put_half(meta, grads, keep, send, sem, half, x_first)]


def group_sentences(meta, segs, self_plan, cross_plan):
    first_row = meta[0] * meta[3]
    last_row = first_row + meta[3]
    shift = HALO - first_row
    zero = jnp.int32(0)
    for plan, cross in ((self_plan, False), (cross_plan, True)):

        def step(c, carry, plan=plan, cross=cross):
            t0, s0, done, count, low, high = carry
            t1, s1 = t0 + segs[1, c], s0 + segs[0, c]
            t2, s2 = t1 + segs[1, c + 1], s1 + segs[0, c + 1]
            t3, s3 = t2 + segs[1, c + 2], s2 + segs[0, c + 2]
            target_end, source_end = window_of(t0) + WINDOW, window_of(s0) + WINDOW
            two = (t2 <= target_end) & (t1 < last_row)
            three = two & (t3 <= target_end) & (t2 < last_row)
            if cross:
                two = two & (s2 <= source_end)
                three = three & (s3 <= source_end) & two
            t2, s2 = jnp.where(two, t2, t1), jnp.where(two, s2, s1)
            t3, s3 = jnp.where(three, t3, t2), jnp.where(three, s3, s2)
            mine = (t1 > first_row) & (t0 < last_row)
            here = (c >= done) & mine
            for at, bound in enumerate((t0, t1, t2, t3)):
                plan[at, count] = bound + shift
            for at, bound in enumerate((s0, s1, s2, s3)):
                plan[4 + at, count] = bound
            size = 1 + two.astype(jnp.int32) + three.astype(jnp.int32)
            low = jnp.where(mine, jnp.minimum(low, s0), low)
            high = jnp.where(mine, jnp.maximum(high, s1), high)
            return t1, s1, jnp.where(here, c + size, done), count + here.astype(jnp.int32), low, high

        start = (zero, zero, zero, zero, jnp.int32(1 << 20), zero)
        _, _, _, count, low, high = lax.fori_loop(0, segs.shape[1] - 2, step, start)
        for g in range(GROUPS):
            for at in range(8):
                plan[at, count + g] = 0
        plan[8, 0] = count
        plan[8, 1] = low
        plan[8, 2] = high


def each_group(plan, windows, compute, store):
    def some(i, _):
        bounds = [
            (
                [plan[at, i * GROUPS + g] for at in range(4)],
                [plan[4 + at, i * GROUPS + g] for at in range(4)],
            )
            for g in range(GROUPS)
        ]
        operands = [windows(*each) for each in bounds]
        results = iter(compute([window for each in operands for window in each]))
        for each, windows_of_it in zip(bounds, operands):
            store(*each, [next(results) for _ in windows_of_it])
        return 0

    lax.fori_loop(0, (plan[8, 0] + GROUPS - 1) // GROUPS, some, 0)


def window_of(start):
    return pl.multiple_of((start // 16) * 16, 16)


def spread_lanes(block):
    lanes = lax.broadcasted_iota(jnp.int32, (1, HALF), 1) // HEAD_DIM
    return jnp.concatenate(
        [jnp.where(lanes == h, block, jnp.zeros_like(block)) for h in range(HEADS)], axis=0
    )


def spread_rows(block):
    none = jnp.zeros((HEAD_DIM, block.shape[1]), block.dtype)
    return jnp.concatenate(
        [
            jnp.concatenate(
                [block[g * HEAD_DIM : (g + 1) * HEAD_DIM] if g == h else none for g in range(HEADS)],
                axis=0,
            )
            for h in range(HEADS)
        ],
        axis=1,
    )


def by_head(rows, spread):
    columns = spread.shape[1] // HEADS
    return jnp.concatenate(
        [
            dot(rows[h * HEAD_DIM : (h + 1) * HEAD_DIM], spread[:, h * columns : (h + 1) * columns])
            for h in range(HEADS)
        ],
        axis=0,
    )


def window_mask(q_first, q_bounds, k_first, k_bounds, q_low, q_high, causal):
    q = lax.broadcasted_iota(jnp.int32, (1, WINDOW), 1) + q_first
    k = lax.broadcasted_iota(jnp.int32, (WINDOW, WINDOW), 0) + k_first
    q_id = sum((q >= bound).astype(jnp.int32) for bound in q_bounds)
    k_id = sum((k >= bound).astype(jnp.int32) for bound in k_bounds)
    allowed = k_id == q_id
    if causal:
        allowed = allowed & (k <= q)
    valid = (q >= jnp.maximum(q_bounds[0], q_low)) & (q < jnp.minimum(q_bounds[3], q_high))
    return jnp.concatenate([allowed] * HEADS, axis=1), jnp.concatenate([valid] * HEADS, axis=1)


def window_weights(scores, masks):
    scores = [jnp.where(allowed, each, MASKED) for each, (allowed, _) in zip(scores, masks)]
    weights = [jnp.exp(each - jnp.max(each, axis=0, keepdims=True)) for each in scores]
    inverses = [
        jnp.where(valid, 1.0 / jnp.sum(each, axis=0, keepdims=True), 0.0)
        for each, (_, valid) in zip(weights, masks)
    ]
    return [each * inverse for each, inverse in zip(weights, inverses)]


def attend_windows(windows):
    qs, ks, vs, masks = zip(*windows)
    q_rows = [spread_rows((q * jnp.asarray(HEAD_DIM**-0.5, BF16)).T) for q in qs]
    scores = [dot(k, q) for k, q in zip(ks, q_rows)]
    probabilities = [each.astype(BF16) for each in window_weights(scores, masks)]
    mixes = [by_head(v.T, each) for v, each in zip(vs, probabilities)]
    return [mix.astype(BF16).T for mix in mixes]


def attend_windows_back(windows):
    qs, ks, vs, grads, masks = zip(*windows)
    scale = HEAD_DIM**-0.5
    qs = [q * jnp.asarray(scale, BF16) for q in qs]
    scores = [dot(k, spread_rows(q.T)) for k, q in zip(ks, qs)]
    prob_grads = [dot(v, spread_rows(grad.T)) for v, grad in zip(vs, grads)]
    probabilities = window_weights(scores, masks)
    inners = [
        jnp.sum(each * grad, axis=0, keepdims=True) for each, grad in zip(probabilities, prob_grads)
    ]
    score_grads = [
        (each * (grad - inner)).astype(BF16)
        for each, grad, inner in zip(probabilities, prob_grads, inners)
    ]
    v_grads = [
        dot(each.astype(BF16), spread_lanes(grad)) for each, grad in zip(probabilities, grads)
    ]
    q_grads = [by_head(k.T, each) for k, each in zip(ks, score_grads)]
    k_grads = [dot(each, spread_lanes(q)) for each, q in zip(score_grads, qs)]
    q_grads = [(each * scale).astype(BF16).T for each in q_grads]
    return [(q, k.astype(BF16), v.astype(BF16)) for q, k, v in zip(q_grads, k_grads, v_grads)]


def out_product(mixes, outs):
    left = sum(dot(mix, out[0:HALF]) for mix, out in zip(mixes, outs))
    right = sum(dot(mix, out[HALF:]) for mix, out in zip(mixes, outs))
    return jnp.concatenate([left, right], axis=1)


def out_mix_grads(grad_low, outs, mix_grads, first):
    rows = grad_low.shape[0]
    for half in range(2):
        for lo in range(0, rows, HALF):
            block = grad_low[lo : lo + HALF]
            mix_grad = dot_nt(block[:, :HALF], outs[half, 0:HALF]) + dot_nt(block[:, HALF:], outs[half, HALF:])
            mix_grads[half, first + lo : first + lo + HALF] = mix_grad.astype(BF16)


def out_weight_grads(grad_low, mixes, grads):
    for half, mix in enumerate(mixes):
        grads[half, 0:HALF] = dot_tn(mix, grad_low[:, :HALF]).astype(BF16)
        grads[half, HALF:] = dot_tn(mix, grad_low[:, HALF:]).astype(BF16)


def copy_by_role(meta, pairs_zero, pairs_one, sem):
    @pl.when(meta[0] == 0)
    def _():
        for source, target in pairs_zero:
            pltpu.make_async_copy(source, target, sem).start()

    @pl.when(meta[0] == 1)
    def _():
        for source, target in pairs_one:
            pltpu.make_async_copy(source, target, sem).start()


def wait_by_role(meta, pairs_zero, pairs_one, sem):
    @pl.when(meta[0] == 0)
    def _():
        for source, target in pairs_zero:
            pltpu.make_async_copy(source, target, sem).wait()

    @pl.when(meta[0] == 1)
    def _():
        for source, target in pairs_one:
            pltpu.make_async_copy(source, target, sem).wait()


def states_copies(rows_ref, other_ref, held, here):
    zero = [(other_ref.at[pl.ds(0, here)], held.at[pl.ds(HALO, here)])]
    one = [(rows_ref.at[pl.ds(here - HALO, here + HALO)], held.at[pl.ds(0, here + HALO)])]
    return zero, one


def self_attention(meta, segs, plan, here, qkvs, mixes):
    full = here + HALO
    for mix in mixes:
        mix[...] = jnp.zeros(mix.shape, BF16)

    def group(bounds, _):
        first = window_of(bounds[0])
        mask = window_mask(first, bounds, first, bounds, HALO, full, True)
        at = pl.ds(first, WINDOW)
        return [(qkv[0, at], qkv[1, at], qkv[2, at], mask) for qkv in qkvs]

    def store(bounds, _, result):
        at = pl.ds(window_of(bounds[0]), WINDOW)
        for mix, each in zip(mixes, result):
            mix[at] += each

    together = 2 * GROUPS // len(qkvs)
    each_group(meta, segs, plan, here, False, together, group, attend_windows, store)


def self_project(normed, held, qkv):
    full = normed.shape[0]
    qkv[:, full:] = jnp.zeros((3, WINDOW, HALF), BF16)
    for c in range(3):
        qkv[c, 0:full] = dot(normed[...], held[c]).astype(BF16)


def self_forward(
    meta, plan, rows_ref, other_ref, gain, bias, own, own_out, w1, w2, w3, w4,
    hidden, normed, qkv, mix, states, held, outs, sem_w, sem_x,
):
    full = states.shape[0]
    here = full - HALO
    state_copies = states_copies(rows_ref, other_ref, states, here)
    copy_by_role(meta, *state_copies, sem_x)
    weights = start_other(meta[1], (w1, w2, w3, w4), 0, held, sem_w)
    weights += start_out_own(own_out, outs, sem_w)
    mix.ref[...] = jnp.zeros(mix.ref.shape, BF16)
    wait_by_role(meta, *state_copies, sem_x)

    @pl.when(meta[0] == 0)
    def _():
        states[0:HALO] = jnp.zeros((HALO, states.shape[1]), BF16)

    for lo in range(0, full, HALO):
        hat, _ = norm_parts(states[lo : lo + HALO].astype(F32))
        normed.ref[lo : lo + HALO] = (hat * gain[0:1] + bias[0:1]).astype(BF16)
    normed.send()
    own = own()
    wait(weights)
    qkv.ref[:, :, full:] = jnp.zeros((2, 3, WINDOW, HALF), BF16)
    for half, matrices in enumerate((own, held)):
        for c in range(3):
            qkv.ref[half, c, 0:full] = dot(normed.ref[...], matrices[c]).astype(BF16)
    qkv.send()

    def group(bounds, _):
        first = window_of(bounds[0])
        mask = window_mask(first, bounds, first, bounds, HALO, full, True)
        at = pl.ds(first, WINDOW)
        return [(qkv.ref[half, 0, at], qkv.ref[half, 1, at], qkv.ref[half, 2, at], mask) for half in range(2)]

    def store(bounds, _, result):
        at = pl.ds(window_of(bounds[0]), WINDOW)
        for half in range(2):
            mix.ref[half, at] += result[half]

    each_group(plan, group, attend_windows, store)
    mix.send()
    for lo in range(HALO, full, HALF):
        at = slice(lo, lo + HALF)
        hidden[lo - HALO : lo - HALO + HALF] = states[at].astype(F32) + out_product(
            [mix.ref[0, at], mix.ref[1, at]], [outs, held[3]]
        )


def blocks_do(low, high, pairs, target, sem, act):
    def one(block, _):
        at = pl.ds(pl.multiple_of(block * HALF, HALF), HALF)
        act(pltpu.make_async_copy(pairs.at[:, :, at], target.at[:, :, at], sem))
        return 0

    lax.fori_loop(low // HALF, (high + HALF - 1) // HALF, one, 0)


def zero_after(high, pairs):
    end = pl.multiple_of(((high + HALF - 1) // HALF) * HALF, HALF)
    pairs[:, :, pl.ds(end, WINDOW)] = jnp.zeros((2, 2, WINDOW, HALF), BF16)


def memory_copies(rows_ref, other_ref, held):
    return [(rows_ref, held)], [(other_ref, held)]


def cross_forward(
    meta, plan, rows_ref, other_ref, hidden, gain, bias, own_q, own_pair, own_out, w1, w2, w3, w4,
    hidden_two, hidden_far, normed, mix, queries, pairs_far, pairs, memory, held, outs, sem_w, sem_x, sem_h,
):
    here = hidden_two.shape[0]
    hidden_copy = pltpu.make_async_copy(hidden, hidden_far, sem_h.at[0])
    hidden_copy.start()
    full = here + HALO
    copies = memory_copies(rows_ref, other_ref, memory)
    copy_by_role(meta, *copies, sem_x)
    weights = start_other(meta[2], (w1, w2, w3, w4), 0, held, sem_w)
    weights += start_out_own(own_out, outs, sem_w)
    queries.ref[:, 0:HALO] = jnp.zeros((2, HALO, HALF), BF16)
    queries.ref[:, full:] = jnp.zeros((2, WINDOW, HALF), BF16)
    mix.ref[...] = jnp.zeros(mix.ref.shape, BF16)
    low, high = plan[8, 1], plan[8, 2]
    zero_after(high, pairs)
    for lo in range(0, here, HALF):
        at = slice(lo, lo + HALF)
        hat, _ = norm_parts(hidden[at])
        normed.ref[at] = (hat * gain[1:2] + bias[1:2]).astype(BF16)
    normed.send()
    own_q, own_pair = own_q(), own_pair()
    wait(weights)
    for half, matrix in enumerate((own_q, held.at[0])):
        queries.ref[half, HALO:full] = dot(normed.ref[...], matrix[...]).astype(BF16)
    queries.send()
    wait_by_role(meta, *copies, sem_x)

    def project(block, _):
        at = pl.ds(pl.multiple_of(block * HALF, HALF), HALF)
        for c in range(2):
            pairs[0, c, at] = dot(memory[at], own_pair[c]).astype(BF16)
            pairs[1, c, at] = dot(memory[at], held[1 + c]).astype(BF16)
        return 0

    lax.fori_loop(low // HALF, (high + HALF - 1) // HALF, project, 0)
    blocks_do(low, high, pairs, pairs_far, sem_h.at[1], lambda copy: copy.start())

    def group(bounds, source_bounds):
        first = window_of(bounds[0])
        source_first = window_of(source_bounds[0])
        mask = window_mask(first, bounds, source_first, source_bounds, HALO, full, False)
        at = pl.ds(first, WINDOW)
        source_at = pl.ds(source_first, WINDOW)
        return [
            (queries.ref[half, at], pairs[half, 0, source_at], pairs[half, 1, source_at], mask)
            for half in range(2)
        ]

    def store(bounds, _, result):
        at = pl.ds(window_of(bounds[0]), WINDOW)
        for half in range(2):
            mix.ref[half, at] += result[half]

    each_group(plan, group, attend_windows, store)
    mix.send()
    for lo in range(0, here, HALF):
        at = slice(lo, lo + HALF)
        mix_at = slice(HALO + lo, HALO + lo + HALF)
        hidden_two[at] = hidden[at] + out_product([mix.ref[0, mix_at], mix.ref[1, mix_at]], [outs, held[3]])
    hidden_copy.wait()
    blocks_do(low, high, pairs, pairs_far, sem_h.at[1], lambda copy: copy.wait())


def gelu_both(inner):
    rate, cubic = 0.7978845608028654, 0.7978845608028654 * 0.044715
    square = inner * inner
    bent = jnp.tanh(inner * (rate + cubic * square))
    half = 0.5 + 0.5 * bent
    slope = half + inner * (1.0 - bent * bent) * (0.5 * rate + 1.5 * cubic * square)
    return inner * half, slope


def column(values, role, at):
    lanes = lax.broadcasted_iota(jnp.int32, (WINDOW, WINDOW), 1)
    own = lax.broadcasted_iota(jnp.int32, (WINDOW, WINDOW), 0) == lanes
    blocks = []
    for block in range(at.start // WINDOW, at.stop // WINDOW):
        row = values[role, block : block + 1]
        blocks.append(jnp.sum(jnp.where(own, row, 0.0), axis=1, keepdims=True))
    return jnp.concatenate(blocks, axis=0)


def feed_forward(
    meta, hidden_two, cotangent, targets, gain, bias, halt_weight, halt_bias,
    own_in, i1, i2, i3, i4, own_out, o1, o2, o3, o4,
    result_low, hidden_grad, hidden_far, small, keep, send,
    held_in, held_out, normed, active, slopes, total, out_low, cot, grads, sem_w, sem_o, sem_x, sem_g,
):
    here, width = total.shape
    first = pl.multiple_of(meta[0] * here, here)
    cot_copy = pltpu.make_async_copy(cotangent.at[pl.ds(first, here)], cot, sem_x.at[0])
    weights = start_in(meta, own_in, (i1, i2, i3, i4), held_in, sem_w)
    weights += start_out(meta, own_out, (o1, o2, o3, o4), held_out, sem_o)
    cot_copy.start()
    blocks = [slice(lo, lo + HALF) for lo in range(0, here, HALF)]
    for at in blocks:
        hat, _ = norm_parts(hidden_two[at])
        normed[at] = (hat * gain[2:3] + bias[2:3]).astype(BF16)
        total[at] = hidden_two[at]
    wait(weights)

    def forward(pair, _):
        items = [(at, 8 * pair + u) for at in blocks for u in range(8)]
        inner = dot(normed[items[0][0]], held_in[items[0][1]])
        products = []
        for i, (at, j) in enumerate(items):
            coming = dot(normed[items[i + 1][0]], held_in[items[i + 1][1]]) if i + 1 < len(items) else None
            value, slope = gelu_both(inner)
            value = value.astype(BF16)
            active[j, at] = value
            slopes[j, at] = slope
            products.append(dot(value, held_out[j]))
            if len(products) == 8:
                total[at] += sum(products)
                products = []
            inner = coming
        return 0

    lax.fori_loop(0, 1, forward, 0)
    cot_copy.wait()
    weight_sum = jnp.zeros((1, width), F32)
    bias_sum = jnp.zeros((1, 1), F32)
    for at in blocks:
        result = total[at]
        result_low.ref[at] = result.astype(BF16)
        logits = jnp.sum(result * halt_weight[...], axis=-1, keepdims=True) + halt_bias[0]
        halt_grad = 1.0 / (1.0 + jnp.exp(-logits)) - column(targets, meta[0], at)
        out_grad = cot[at].astype(F32) + halt_grad * halt_weight[...]
        out_low[at] = out_grad.astype(BF16)
        hidden_grad[at] = out_grad
        total[at] = jnp.zeros((HALF, width), F32)
        weight_sum += jnp.sum(halt_grad * result, axis=0, keepdims=True)
        bias_sum += jnp.sum(halt_grad, axis=0, keepdims=True)
    result_low.send()

    def backward(i, _):
        js = [4 * i + u for u in range(4)]
        value_grads = [[dot_nt(out_low[at], held_out[j]) for at in blocks] for j in js]
        inner_grads = [
            [(grad * slopes[j, at]).astype(BF16) for grad, at in zip(grads_of_it, blocks)]
            for j, grads_of_it in zip(js, value_grads)
        ]
        for b, at in enumerate(blocks):
            total[at] += sum(dot_nt(each[b], held_in[j]) for j, each in zip(js, inner_grads))
        for j, each in zip(js, inner_grads):
            half, block = j // 4, j % 4
            grads[8 * half + block] = dot_tn(normed[...], jnp.concatenate(each, axis=0)).astype(BF16)
            out_grad = dot_tn(active[j], out_low[...]).astype(BF16)
            grads[8 * half + 4 + block, 0:HALF] = out_grad[:, :HALF]
            grads[8 * half + 4 + block, HALF:] = out_grad[:, HALF:]
        return 0

    lax.fori_loop(0, 4 // 4, backward, 0)
    copies = put_half(meta, grads, keep, send, sem_g, 0)
    lax.fori_loop(4 // 4, 8 // 4, backward, 0)
    copies += put_half(meta, grads, keep, send, sem_g, 1)
    gain_sum = jnp.zeros_like(weight_sum)
    shift_sum = jnp.zeros_like(weight_sum)
    for at in blocks:
        hat, scale = norm_parts(hidden_two[at])
        grad = total[at]
        hidden_grad[at] += norm_back(grad, hat, scale, gain[2:3])
        gain_sum += jnp.sum(grad * hat, axis=0, keepdims=True)
        shift_sum += jnp.sum(grad, axis=0, keepdims=True)
    small[...] = jnp.concatenate(
        [gain_sum, shift_sum, weight_sum, jnp.broadcast_to(bias_sum, weight_sum.shape)], axis=0
    )
    copies += start([pltpu.make_async_copy(hidden_grad, hidden_far, sem_x.at[1])])
    wait(copies)


def out_backward(
    meta, upper_grad, mix, own_out, w1, w2, w3, w4, *rest, place, ahead
):
    sources, (mix_grads, out_part), rest = rest[:ahead], rest[ahead : ahead + 2], rest[ahead + 2 :]
    targets, (outs, sem_w, sem_h) = rest[:ahead], rest[ahead:]
    full = mix_grads.shape[1] - WINDOW
    weights = start_other(meta[place], (w1, w2, w3, w4), 3, outs.at[pl.ds(1, 1)], sem_w)
    weights += start_out_own(own_out, outs.at[0], sem_w)
    mix.go()
    brought = start(
        [pltpu.make_async_copy(*copy, sem_h.at[at]) for at, copy in enumerate(zip(sources, targets))]
    )
    mix_grads[:, 0:HALO] = jnp.zeros((2, HALO, HALF), BF16)
    mix_grads[:, full:] = jnp.zeros((2, WINDOW, HALF), BF16)
    grad_low = upper_grad[...].astype(BF16)
    wait(weights)
    out_mix_grads(grad_low, outs, mix_grads, HALO)
    mix = mix()
    out_weight_grads(grad_low, [mix[0, HALO:full], mix[1, HALO:full]], out_part.ref)
    wait(brought)


def cross_backward(meta, plan, mix_grads, queries, pairs_far, q_grad, pair_grads, pairs, sem_h):
    full = mix_grads.shape[1] - WINDOW
    here = full - HALO
    low, high = plan[8, 1], plan[8, 2]
    blocks_do(low, high, pairs_far, pairs, sem_h.at[0], lambda copy: copy.start())
    q_grad[...] = jnp.zeros(q_grad.shape, BF16)
    pair_grads[...] = jnp.zeros(pair_grads.shape, BF16)
    zero_after(high, pairs)
    blocks_do(low, high, pairs_far, pairs, sem_h.at[0], lambda copy: copy.wait())

    def group(bounds, source_bounds):
        first = window_of(bounds[0])
        source_first = window_of(source_bounds[0])
        mask = window_mask(first, bounds, source_first, source_bounds, HALO, full, False)
        at = pl.ds(first, WINDOW)
        source_at = pl.ds(source_first, WINDOW)
        return [
            (
                queries[half, at], pairs[half, 0, source_at], pairs[half, 1, source_at],
                mix_grads[half, at], mask,
            )
            for half in range(2)
        ]

    def store(bounds, source_bounds, result):
        at = pl.ds(window_of(bounds[0]), WINDOW)
        source_at = pl.ds(window_of(source_bounds[0]), WINDOW)
        for half, (dq, dk, dv) in enumerate(result):
            q_grad[half, at] += dq
            pair_grads[half, 0, source_at] += dk
            pair_grads[half, 1, source_at] += dv

    each_group(plan, group, attend_windows_back, store)


def cross_products(
    meta, plan, rows_ref, other_ref, hidden, normed, upper_grad, q_grad, pair_grads, out_part, own_q, own_pair,
    w1, w2, w3, w4, gain,
    lower_grad, lower_far, memory_grad, small, keep, send, memory, pair_sums, grads, held, sem_w, sem_x, sem_g, sem_h,
):
    here, width = lower_grad.shape
    full = here + HALO
    weights = start_other(meta[2], (w1, w2, w3, w4), 0, held, sem_w)
    copies = memory_copies(rows_ref, other_ref, memory)
    copy_by_role(meta, *copies, sem_x)
    normed.go()
    hidden.go()
    upper_grad.go()
    pair_sums[...] = jnp.zeros(pair_sums.shape, F32)
    memory_grad.ref[...] = jnp.zeros(memory_grad.ref.shape, BF16)
    source_low, source_high = plan[8, 1], plan[8, 2]
    parts = start(
        [pltpu.make_async_copy(out_part.at[half], grads.at[4 * half + 3], sem_g.at[0]) for half in range(2)]
    )
    gain_sum = jnp.zeros((1, width), F32)
    shift_sum = jnp.zeros((1, width), F32)
    own_q, own_pair = own_q(), own_pair()
    wait(weights)
    wait_by_role(meta, *copies, sem_x)

    def project(block, _):
        at = pl.ds(pl.multiple_of(block * HALF, HALF), HALF)
        row_grad = jnp.zeros((HALF, width), F32)
        for half in range(2):
            for c in range(2):
                low = pair_grads[half, c, at]
                row_grad += dot_nt(low, held[1 + c] if half else own_pair[c])
                pair_sums[half, c] += dot_tn(memory[at], low)
        memory_grad.ref[at] = row_grad.astype(BF16)
        return 0

    lax.fori_loop(source_low // HALF, (source_high + HALF - 1) // HALF, project, 0)
    memory_grad.send()
    for half in range(2):
        for c in range(2):
            grads[4 * half + 1 + c] = pair_sums[half, c].astype(BF16)
    normed = normed()
    for half in range(2):
        grads[4 * half] = dot_tn(normed[...], q_grad[half, HALO:full]).astype(BF16)
    wait(parts)
    put = put_grads(meta, grads, keep, send, sem_g, x_first=True)
    hidden, upper_grad = hidden(), upper_grad()
    for lo in range(0, here, HALF):
        at = slice(lo, lo + HALF)
        q_at = slice(HALO + lo, HALO + lo + HALF)
        hat, scale = norm_parts(hidden[at])
        grad = dot_nt(q_grad[0, q_at], own_q[...]) + dot_nt(q_grad[1, q_at], held[0])
        lower_grad[at] = upper_grad[at] + norm_back(grad, hat, scale, gain[1:2])
        gain_sum += jnp.sum(grad * hat, axis=0, keepdims=True)
        shift_sum += jnp.sum(grad, axis=0, keepdims=True)
    small[...] = jnp.concatenate([gain_sum, shift_sum], axis=0)
    put += start([pltpu.make_async_copy(lower_grad, lower_far, sem_h.at[0])])
    wait(put)


def self_backward(meta, plan, mix_grads, qkv, qkv_grads):
    full = mix_grads.shape[1] - WINDOW
    here = full - HALO
    qkv_grads[...] = jnp.zeros(qkv_grads.shape, BF16)

    def group(bounds, _):
        first = window_of(bounds[0])
        mask = window_mask(first, bounds, first, bounds, HALO, full, True)
        at = pl.ds(first, WINDOW)
        return [
            (qkv[half, 0, at], qkv[half, 1, at], qkv[half, 2, at], mix_grads[half, at], mask)
            for half in range(2)
        ]

    def store(bounds, _, result):
        at = pl.ds(window_of(bounds[0]), WINDOW)
        for half in range(2):
            for c in range(3):
                qkv_grads[half, c, at] += result[half][c]

    each_group(plan, group, attend_windows_back, store)


def self_products(
    meta, rows_ref, other_ref, normed, qkv_grads, out_part, upper_grad, own, w1, w2, w3, w4, gain, result, memory_part,
    keep, send, state_grad, swap, halo_grad, small, grads, states, held, sem_g, sem_w, sem_x, sem_s,
):
    full, width = states.shape
    here = full - HALO
    normed.go()
    parts = start(
        [pltpu.make_async_copy(out_part.at[half], grads.at[4 * half + 3], sem_g.at[0]) for half in range(2)]
    )
    weights = start_other(meta[1], (w1, w2, w3, w4), 0, held, sem_w)
    state_copies = states_copies(rows_ref, other_ref, states, here)
    copy_by_role(meta, *state_copies, sem_x)
    swaps = [(result, swap.ref.at[pl.ds(0, here)])], [(memory_part, swap.ref)]
    own.go()
    upper_grad.go()
    copy_by_role(meta, *swaps, sem_s)
    normed = normed()
    for half in range(2):
        for c in range(3):
            grads[4 * half + c] = dot_tn(normed[...], qkv_grads[half, c, 0:full]).astype(BF16)
    wait(parts)
    put = put_grads(meta, grads, keep, send, sem_g)
    wait_by_role(meta, *state_copies, sem_x)

    @pl.when(meta[0] == 0)
    def _():
        states[0:HALO] = jnp.zeros((HALO, width), BF16)

    own, upper_grad = own(), upper_grad()
    wait(weights)
    gain_sum = jnp.zeros((1, width), F32)
    shift_sum = jnp.zeros((1, width), F32)
    step = full // 2
    for lo in range(0, full, step):
        at = slice(lo, lo + step)
        hat, scale = norm_parts(states[at].astype(F32))
        grad = sum(
            dot_nt(qkv_grads[half, c, at], matrices[c])
            for half, matrices in enumerate((own, held))
            for c in range(3)
        )
        back = norm_back(grad, hat, scale, gain[0:1])
        if lo == 0:
            halo_grad.ref[...] = back[:HALO]
            back = back[HALO:]
        first = max(lo, HALO) - HALO
        at = slice(first, lo + step - HALO)
        back += upper_grad[at]
        state_grad.ref[at] = back

        @pl.when(meta[0] == 0)
        def _(low=back.astype(BF16), at=slice(here + at.start, here + at.stop)):
            swap.ref[at] = low

        gain_sum += jnp.sum(grad * hat, axis=0, keepdims=True)
        shift_sum += jnp.sum(grad, axis=0, keepdims=True)
    small[...] = jnp.concatenate([gain_sum, shift_sum], axis=0)
    wait_by_role(meta, *swaps, sem_s)
    wait(put)


def finish_rows(
    meta, rows, result, grad, halo_grad, memory_part, swapped, layer_out, input_grads, parts, halo, sem,
):
    here = result.shape[0]
    low, high = pl.ds(0, here), pl.ds(here, here)

    @pl.when(meta[0] == 0)
    def _():
        copies = [(rows, layer_out.ref), (memory_part, parts.at[0]), (swapped, parts.at[1])]
        wait(start([pltpu.make_async_copy(*copy, sem) for copy in copies]))
        input_grads.ref[...] = parts[0].astype(F32) + parts[1].astype(F32)

    @pl.when(meta[0] == 1)
    def _():
        copies = [
            (swapped.at[low], layer_out.ref.at[low]),
            (result, layer_out.ref.at[high]),
            (swapped.at[high], parts.at[0, low]),
            (grad, input_grads.ref.at[high]),
            (halo_grad, halo),
        ]
        wait(start([pltpu.make_async_copy(*copy, sem) for copy in copies]))
        input_grads.ref[0:here] = parts[0, 0:here].astype(F32)
        input_grads.ref[here - HALO : here] += halo[...]


def unpack(kind, meta, mine, by_x, by_role, by_both, *rest):
    outs, (held, sem) = rest[:-2], rest[-2:]
    rows = mine.shape[1]
    copies = []
    for rel, ref in ((0, mine), (2, by_x), (1, by_role), (3, by_both)):
        first = pl.multiple_of((rel ^ meta[1]) * rows, rows)
        copy = pltpu.make_async_copy(ref, held.at[:, pl.ds(first, rows)], sem.at[0])
        copy.start()
        copies.append(copy)
    for copy in copies:
        copy.wait()
    if kind == "ffn":
        grad_in, grad_out = outs
        for j in range(4):
            at = slice(j * HALF, (j + 1) * HALF)
            grad_in[:, at] = held[j].astype(F32)
            grad_out[at, 0:HALF] = held[4 + j, 0:HALF].astype(F32)
            grad_out[at, HALF:] = held[4 + j, HALF:].astype(F32)
        return
    if kind == "cross":
        small, (gain, shift, weight, bias), outs = outs[0], outs[4:], outs[1:4]
        gain[...], shift[...] = small[0:3], small[3:6]
        weight[...], bias[...] = small[6:7], small[7:8, 0:1]
        outs[0][...] = held[0].astype(F32)
        for c in range(2):
            outs[1][:, c] = held[1 + c].astype(F32)
    else:
        outs[0][...] = held[0:3].astype(F32)
    outs[-1][:, 0:HALF] = held[3, 0:HALF].astype(F32)
    outs[-1][:, HALF:] = held[3, HALF:].astype(F32)


def shape(*dims, dtype=F32):
    return jax.ShapeDtypeStruct(dims, dtype)


def far(*dims, dtype=F32):
    return pltpu.HBM(dims, dtype)


def near(*dims, dtype=F32):
    return pltpu.VMEM(dims, dtype)


def room(shapes, spare):
    return sum(math.prod(each.shape) * jnp.dtype(each.dtype).itemsize for each in shapes) + (spare << 20)


class Put:
    def __init__(self, *dims, dtype=F32):
        self.shape = far(*dims, dtype=dtype)
        self.scratch = pltpu.VMEM(dims, dtype)


class Get:
    def __init__(self, value, late=False):
        self.value = value
        self.late = late
        self.scratch = pltpu.VMEM(value.shape, value.dtype)


class Here:
    def __init__(self, value):
        self.value = value


class Any:
    def __init__(self, value):
        self.value = value


class Far:
    def __init__(self, value):
        self.value = value


def call(body, ins, outs, scratch, weight):
    smem, others = ins
    operands = list(smem) + list(others)
    values, in_specs = list(smem), [SMEM] * len(smem)
    for other in others:
        if isinstance(other, (Get, Far)):
            values.append(pltpu.with_memory_space_constraint(other.value, pltpu.HBM))
            in_specs.append(ANY)
        elif isinstance(other, Any):
            values.append(other.value)
            in_specs.append(ANY)
        elif isinstance(other, Here):
            values.append(pltpu.with_memory_space_constraint(other.value, pltpu.VMEM))
            in_specs.append(VMEM)
        else:
            values.append(other)
            in_specs.append(VMEM)
    moved = [at for at, each in enumerate(operands) if isinstance(each, Get)]
    put = [at for at, each in enumerate(outs) if isinstance(each, Put)]

    def inner(*refs):
        in_refs, refs = list(refs[: len(values)]), refs[len(values) :]
        out_refs, refs = list(refs[: len(outs)]), refs[len(outs) :]
        moved_refs, refs = refs[: len(moved)], refs[len(moved) :]
        put_refs, refs = refs[: len(put)], refs[len(put) :]
        sems, refs = refs[0], refs[1:]
        for i, at in enumerate(moved):
            in_refs[at] = Load(in_refs[at], moved_refs[i], sems.at[i])
            if not operands[at].late:
                in_refs[at].go()
        for i, at in enumerate(put):
            out_refs[at] = Store(put_refs[i], out_refs[at], sems.at[len(moved) + i])
        body(*in_refs, *out_refs, *refs)
        for at in moved:
            in_refs[at]()
        for at in put:
            out_refs[at].send()
        wait([out_refs[at].copy for at in put])

    in_vmem = [operands[at].scratch for at in moved] + [outs[at].scratch for at in put]
    in_vmem += [each for each in scratch if getattr(each, "memory_space", None) is pltpu.VMEM]
    in_vmem += [value for value, spec in zip(values, in_specs) if spec is VMEM]
    in_vmem += [out for out in outs if not isinstance(out, Put) and getattr(out, "memory_space", None) is not pltpu.HBM]
    return pl.pallas_call(
        inner,
        out_shape=[out.shape if isinstance(out, Put) else out for out in outs],
        in_specs=in_specs,
        out_specs=[ANY if isinstance(out, Put) or getattr(out, "memory_space", None) is pltpu.HBM else VMEM for out in outs],
        scratch_shapes=[operands[at].scratch for at in moved]
        + [outs[at].scratch for at in put]
        + [pltpu.SemaphoreType.DMA((len(moved) + len(put) + 1,))]
        + list(scratch),
        name=getattr(body, "__name__", "out_backward"),
        compiler_params=pltpu.CompilerParams(vmem_limit_bytes=room(in_vmem, SPARE)),
        cost_estimate=pl.CostEstimate(flops=int(weight * WEIGHT), bytes_accessed=0, transcendentals=0),
    )(*values)


def flip(value, axis, bit=1):
    count = lax.axis_size(axis)
    return lax.ppermute(value, axis, [(i, i ^ bit) for i in range(count)])


def add(a, b):
    return (a.astype(F32) + b.astype(F32)).astype(BF16)


def after(value, *events):
    return lax.optimization_barrier((value, events))[0]


class Order:
    def __init__(self, meta):
        self.meta = meta
        self.last = ()

    def now(self):
        return after(self.meta, *self.last)

    def __call__(self, weight, *jobs):
        operands = [value for job in jobs for value in job[0]]
        shapes = [each for job in jobs for each in job[1]]

        def sums(meta, *refs):
            ins, outs = list(refs[: len(operands)]), list(refs[len(operands) :])
            for values, results, body, _ in jobs:
                body(meta, ins[: len(values)], outs[: len(results)])
                ins, outs = ins[len(values) :], outs[len(results) :]

        results = list(
            pl.pallas_call(
                sums,
                out_shape=shapes,
                in_specs=[SMEM] + [VMEM] * len(operands),
                out_specs=[VMEM] * len(shapes),
                name="sums",
                compiler_params=pltpu.CompilerParams(vmem_limit_bytes=room(operands + shapes, 4)),
                cost_estimate=pl.CostEstimate(flops=int(weight * WEIGHT), bytes_accessed=0, transcendentals=0),
            )(self.now(), *operands)
        )
        self.last = tuple(results)
        for _, each, _, take in jobs:
            take(results[: len(each)])
            results = results[len(each) :]


class Sum:
    def __init__(self, keep, send, routes):
        self.routes = routes
        self.near, self.got = [keep], [flip(send, "role")]

    def job(self, shapes, body, take):
        count = len(self.near)
        return (
            [*self.near, *self.got],
            [jax.ShapeDtypeStruct(each, BF16) if isinstance(each, tuple) else each for each in shapes],
            lambda meta, ins, outs: body(meta, ins[:count], ins[count:], outs),
            take,
        )

    def pass_on(self, stage, far_near=False):
        def take(parts):
            self.near = parts[0::2]
            if far_near:
                self.near = [pltpu.with_memory_space_constraint(each, pltpu.HBM) for each in self.near]
            self.got = [step(away, route[stage]) for away, route in zip(parts[1::2], self.routes)]

        return take

    def begin(self, far_near=False):
        count = len(self.routes)
        _, _, matrices, rows, columns = self.near[0].shape
        share = matrices // count

        def body(meta, near, got, outs):
            for at, route in enumerate(self.routes):
                mine = pl.ds(at * share, share)
                for which in range(2):
                    place = (slice(None), which, mine) if route[0] == "x" and count > 1 else (which, slice(None), mine)
                    outs[2 * at + which][...] = add(near[0][place], got[0][place])

        shapes = [jax.ShapeDtypeStruct((2, share, rows, columns), BF16)] * (2 * count)
        if far_near:
            shapes[0::2] = [far(2, share, rows, columns, dtype=BF16)] * count
        return self.job(shapes, body, self.pass_on(0, far_near))

    def second(self):
        def body(meta, near, got, outs):
            for at in range(len(near)):
                for which in range(2):
                    outs[2 * at + which][...] = add(near[at][which], got[at][which])

        return self.job([self.near[0].shape[1:]] * (2 * len(self.near)), body, self.pass_on(1))

    def halve(self):
        count = len(self.near)
        matrices, rows, columns = self.near[0].shape
        half = count * matrices // 2

        def body(meta, near, got, outs):
            upper = meta[2] >> 1
            for out, which in zip(outs, (upper, 1 - upper)):
                if count == 1:
                    at = pl.ds(which * half, half)
                    out[...] = add(near[0][at], got[0][at])
                else:
                    both = [add(mine[...], theirs[...]) for mine, theirs in zip(near, got)]
                    out[...] = jnp.where(which == 1, both[1], both[0])

        def take(parts):
            self.near, self.got = [parts[0]], [flip(parts[1], "dp", 2)]

        return self.job([(half, rows, columns)] * 2, body, take)

    def plain(self, bit):
        def body(meta, near, got, outs):
            outs[0][...] = add(near[0][...], got[0][...])

        def take(parts):
            self.near, self.got = parts, [flip(parts[0], "dp", bit)]

        return self.job([self.near[0].shape], body, take)

    def whole(self):
        return self.plain(4)

    def back(self, order):
        bit = 8
        while bit < lax.axis_size("dp"):
            order(1, self.plain(bit))
            bit *= 2
        return self.plain(2)

    def last(self):
        half, rows, columns = self.near[0].shape

        def body(meta, near, got, outs):
            upper = meta[2] >> 1
            outs[0][pl.ds(upper * half, half)] = near[0][...]
            outs[0][pl.ds((1 - upper) * half, half)] = got[0][...]

        def take(parts):
            self.mine = parts[0]
            self.by_x = flip(self.mine, "dp", 1)

        return self.job([(2 * half, rows, columns)], body, take)

    def pieces(self, order):
        by_x = after(self.by_x, *order.last)
        return self.mine, by_x, flip(self.mine, "role"), flip(by_x, "role")


def step(value, route):
    if route == "head":
        return flip(value, "head")
    return flip(value, "dp", 1)


class SmallSum:
    def __init__(self, value):
        count = lax.axis_size("dp")
        self.steps = [("role", 1), ("head", 1)] + [("dp", 1 << at) for at in range(count.bit_length() - 1)]
        self.value, self.got = value, flip(value, *self.steps.pop(0))

    def step(self):
        def body(meta, ins, outs):
            outs[0][...] = ins[0][...] + ins[1][...]

        def take(parts):
            self.value = parts[0]
            self.got = flip(self.value, *self.steps.pop(0)) if self.steps else None

        return [self.value, self.got], [jax.ShapeDtypeStruct(self.value.shape, F32)], body, take

    def total(self):
        while self.got is not None:
            self.value = self.value + self.got
            self.got = flip(self.value, *self.steps.pop(0)) if self.steps else None
        return self.value


def shards(
    layer_in,
    lengths,
    cotangent,
    targets,
    self_qkv,
    self_out,
    cross_q,
    cross_kv,
    cross_out,
    ffn_in,
    ffn_out,
    norm_gain,
    norm_bias,
    halt_weight,
    halt_bias,
):
    role, head, place = (lax.axis_index(name) for name in ("role", "head", "dp"))
    target_side = role == 1
    me = 2 * (place & 1) + role
    me_z = (place & 2) + role
    meta = jnp.stack([role, me, me_z, layer_in.shape[1] // 2]).astype(jnp.int32)

    rows = layer_in[0]
    row_len, width = rows.shape
    here = row_len // 2
    full = here + HALO

    other_rows = flip(rows, "role")
    lens = lax.dynamic_index_in_dim(lengths[0], head, 0, keepdims=False)
    other_lens = flip(lens, "role")
    segs = jnp.where(target_side, jnp.stack([other_lens, lens]), jnp.stack([lens, other_lens]))
    segs = jnp.pad(segs, ((0, 0), (0, 2)))

    self_own, cross_own = self_qkv.transpose(1, 0, 2), cross_kv.transpose(1, 0, 2)
    piece_shape = Put(4, width // PIECES, HALF, dtype=BF16)
    (self_piece,) = call(
        cut_self, ([meta], [Far(self_own), Far(self_out)]), [piece_shape], [pltpu.SemaphoreType.DMA((2,))], 1
    )
    cross_piece, in_piece, out_own_piece = call(
        cut_rest,
        ([meta], [Far(cross_q), Far(cross_own), Far(cross_out), Far(ffn_in), Far(ffn_out)]),
        [piece_shape, piece_shape, Put(HALF, width, dtype=BF16)],
        [pltpu.SemaphoreType.DMA((5,))],
        1,
    )
    self_first, cross_first, in_first, out_first = (
        flip(piece, "head") for piece in (self_piece, cross_piece, in_piece, out_own_piece)
    )

    weight_sems = pltpu.SemaphoreType.DMA((6,))
    one_sem = pltpu.SemaphoreType.DMA
    grad_sems = pltpu.SemaphoreType.DMA((1,))
    states_held = pltpu.VMEM((full, width), BF16)
    memory_held = pltpu.VMEM((row_len, width), BF16)
    out_held = pltpu.VMEM((width, HALF), BF16)
    mix_grads = pltpu.VMEM((2, full + WINDOW, HALF), BF16)

    def heads(*dims):
        return Put(*dims, full + WINDOW, HALF, dtype=BF16)

    def matrices(count):
        return pltpu.VMEM((count, width, HALF), BF16)

    pair_shape = (2, 2, row_len + WINDOW, HALF)

    both_rows = Any(rows), Any(other_rows)

    self_plan, cross_plan = pl.pallas_call(
        group_sentences,
        out_shape=[jax.ShapeDtypeStruct((9, 40), jnp.int32)] * 2,
        in_specs=[SMEM] * 2,
        out_specs=[SMEM] * 2,
        name="group_sentences",
        cost_estimate=pl.CostEstimate(flops=int(HEAVY * WEIGHT), bytes_accessed=0, transcendentals=0),
    )(after(meta, cross_piece, self_first), segs)
    self_second = flip(self_first, "dp", 1)
    cross_second = flip(cross_first, "dp", 2)
    in_second = flip(in_first, "dp", 1)
    self_second = after(self_second, self_plan)
    self_weights = [self_first, self_second, flip(self_first, "role"), flip(self_second, "role")]
    self_pieces = [Any(piece) for piece in self_weights]
    hidden, normed_one, qkv, self_mix = call(
        self_forward,
        (
            [after(meta, cross_first, in_first), self_plan],
            [*both_rows, norm_gain, norm_bias, Get(self_own), Far(self_out), *self_pieces],
        ),
        [near(here, width), Put(full, width, dtype=BF16), heads(2, 3), heads(2)],
        [states_held, matrices(4), out_held, weight_sems, one_sem],
        11,
    )

    cross_second = after(cross_second, normed_one)
    cross_weights = [cross_first, cross_second, flip(cross_first, "role"), flip(cross_second, "role")]
    cross_pieces = [Any(piece) for piece in cross_weights]
    out_first = after(out_first, normed_one)
    out_second = flip(out_first, "dp", 2)
    hidden_two, hidden_far, normed_two, cross_mix, queries, pairs = call(
        cross_forward,
        (
            [meta, cross_plan],
            [
                *both_rows, Here(hidden), norm_gain, norm_bias, Get(cross_q), Get(cross_own), Far(cross_out),
                *cross_pieces,
            ],
        ),
        [near(here, width), far(here, width), Put(here, width, dtype=BF16), heads(2), heads(2), far(*pair_shape, dtype=BF16)],
        [
            pltpu.VMEM(pair_shape, BF16), memory_held, matrices(4), out_held, weight_sems, one_sem,
            pltpu.SemaphoreType.DMA((2,)),
        ],
        12,
    )

    in_second, out_second = after((in_second, out_second), normed_two)
    in_weights = in_first, in_second, flip(in_first, "role"), flip(in_second, "role")
    out_weights = out_first, out_second, flip(out_first, "role"), flip(out_second, "role")
    ffn_parts = far(2, 2, 8, width // PIECES, HALF, dtype=BF16)
    grad_parts = far(2, 2, 4, width // PIECES, HALF, dtype=BF16)
    result_low, two_grad, two_far, ffn_small, keep_ffn, send_ffn = call(
        feed_forward,
        (
            [meta],
            [
                Here(hidden_two), Far(cotangent), targets.astype(F32).reshape(2, here // WINDOW, WINDOW),
                norm_gain, norm_bias, halt_weight[None], halt_bias, Far(ffn_in), *map(Far, in_weights),
                Far(ffn_out), *map(Far, out_weights),
            ],
        ),
        [Put(here, width, dtype=BF16), near(here, width), far(here, width), shape(4, width), ffn_parts, ffn_parts],
        [
            matrices(8),
            pltpu.VMEM((8, HALF, width), BF16),
            pltpu.VMEM((here, width), BF16),
            pltpu.VMEM((8, here, HALF), BF16),
            pltpu.VMEM((8, here, HALF), F32),
            pltpu.VMEM((here, width), F32),
            pltpu.VMEM((here, width), BF16),
            pltpu.VMEM((here, width), BF16),
            matrices(16),
            weight_sems,
            weight_sems,
            pltpu.SemaphoreType.DMA((2,)),
            grad_sems,
        ],
        17,
    )

    mix_grads_shape = near(2, full + WINDOW, HALF, dtype=BF16)
    out_scratch = [matrices(2), weight_sems, grad_sems]
    cross_mix_grads, cross_out_part, queries = call(
        functools.partial(out_backward, place=2, ahead=1),
        ([meta], [Here(two_grad), Get(cross_mix, late=True), Far(cross_out), *cross_pieces, Far(queries)]),
        [mix_grads_shape, Put(2, width, HALF, dtype=BF16), near(2, full + WINDOW, HALF, dtype=BF16)],
        out_scratch,
        4,
    )

    def totals(kind, pieces, out_shapes, *more):
        count, rows_each, columns = pieces[0].shape
        results = pl.pallas_call(
            functools.partial(unpack, kind),
            out_shape=out_shapes,
            in_specs=[SMEM] + [ANY] * 4 + [VMEM] * len(more),
            out_specs=[VMEM] * len(out_shapes),
            scratch_shapes=[
                pltpu.VMEM((count, PIECES * rows_each, columns), BF16),
                pltpu.SemaphoreType.DMA((1,)),
            ],
            name="unpack_" + kind,
            compiler_params=pltpu.CompilerParams(vmem_limit_bytes=room([*out_shapes, pieces[0]], 6)),
            cost_estimate=pl.CostEstimate(flops=1000, bytes_accessed=0, transcendentals=0),
        )(order.now(), *pieces, *more)
        order.last = (results[0],)
        return results

    order = Order(meta)
    ffn_sum = Sum(keep_ffn, send_ffn, FFN_ROUTES)
    order(1, ffn_sum.begin())
    query_grad, pair_grads = call(
        cross_backward,
        ([order.now(), cross_plan], [Here(cross_mix_grads), Here(queries), Far(pairs)]),
        [near(2, full + WINDOW, HALF, dtype=BF16), near(*pair_shape, dtype=BF16)],
        [pltpu.VMEM(pair_shape, BF16), grad_sems],
        9,
    )
    one_grad, one_far, memory_part, cross_small, keep_cross, send_cross = call(
        cross_products,
        (
            [meta, cross_plan],
            [
                *both_rows, Get(hidden_far, late=True), Get(normed_two, late=True), Get(two_far, late=True), Here(query_grad), Here(pair_grads),
                Far(cross_out_part), Get(cross_q), Get(cross_own), *cross_pieces, norm_gain,
            ],
        ),
        [near(here, width), far(here, width), Put(row_len, width, dtype=BF16), shape(2, width), grad_parts, grad_parts],
        [
            memory_held,
            pltpu.VMEM((2, 2, width, HALF), F32),
            matrices(8),
            matrices(3),
            weight_sems,
            one_sem,
            grad_sems,
            grad_sems,
        ],
        8,
    )

    cross_sum = Sum(keep_cross, send_cross, CROSS_ROUTES)
    order(1, ffn_sum.second())
    self_mix_grads, self_out_part, qkv = call(
        functools.partial(out_backward, place=1, ahead=1),
        ([order.now()], [Here(one_grad), Get(self_mix, late=True), Far(self_out), *self_pieces, Far(qkv)]),
        [mix_grads_shape, Put(2, width, HALF, dtype=BF16), near(2, 3, full + WINDOW, HALF, dtype=BF16)],
        out_scratch,
        4,
    )
    order(1, cross_sum.begin(), ffn_sum.halve())
    (qkv_grads,) = call(
        self_backward,
        ([order.now(), self_plan], [Here(self_mix_grads), Here(qkv)]),
        [near(2, 3, full + WINDOW, HALF, dtype=BF16)],
        [],
        9,
    )
    order(1, ffn_sum.whole(), cross_sum.second())
    keep_self, send_self, state_grad, swap, halo_grad, self_small = call(
        self_products,
        (
            [order.now()],
            [
                *both_rows, Get(normed_one, late=True), Here(qkv_grads), Far(self_out_part), Get(one_far, late=True), Get(self_own, late=True),
                *self_pieces, norm_gain, Far(result_low), Far(memory_part),
            ],
        ),
        [
            grad_parts,
            grad_parts,
            Put(here, width),
            Put(row_len, width, dtype=BF16),
            Put(HALO, width),
            shape(2, width),
        ],
        [matrices(8), states_held, matrices(3), grad_sems, weight_sems, one_sem, one_sem],
        11,
    )
    self_sum = Sum(keep_self, send_self, SELF_ROUTES)
    order.last = (keep_self,)
    order(HEAVY, cross_sum.halve(), ffn_sum.back(order))
    order(1, self_sum.begin(far_near=True))
    self_small = after(self_small, *order.last)
    small = SmallSum(
        jnp.concatenate(
            [
                self_small[0:1], cross_small[0:1], ffn_small[0:1],
                self_small[1:2], cross_small[1:2], ffn_small[1:2], ffn_small[2:4],
            ],
            axis=0,
        )
    )
    swapped = flip(after(swap, *order.last), "role")
    order(HEAVY, cross_sum.whole())
    order(1, self_sum.second(), small.step())
    order(1, self_sum.halve(), cross_sum.back(order), ffn_sum.last(), small.step())
    order(1, self_sum.whole(), small.step())
    layer_out, input_grads = call(
        finish_rows,
        (
            [order.now()],
            [Any(each) for each in (rows, result_low, state_grad, halo_grad, memory_part, swapped)],
        ),
        [Put(row_len, width, dtype=BF16), Put(row_len, width)],
        [pltpu.VMEM((2, row_len, width), BF16), pltpu.VMEM((HALO, width), F32), one_sem],
        HEAVY,
    )
    order.last = (layer_out,)
    order(1, cross_sum.last())
    order(1, self_sum.back(order), small.step())
    ffn_in_grad, ffn_out_grad = totals(
        "ffn", ffn_sum.pieces(order), (shape(width, 4 * HALF), shape(4 * HALF, width))
    )
    order(1, self_sum.last(), small.step())
    cross_q_grad, cross_kv_grad, cross_out_grad, *small = totals(
        "cross",
        cross_sum.pieces(order),
        (
            shape(width, HALF), shape(width, 2, HALF), shape(HALF, width),
            shape(3, width), shape(3, width), shape(1, width), shape(1, 1),
        ),
        small.total(),
    )
    self_qkv_grad, self_out_grad = totals(
        "self", self_sum.pieces(order), (shape(3, width, HALF), shape(HALF, width))
    )
    return (
        layer_out[None],
        input_grads[None],
        self_qkv_grad.transpose(1, 0, 2),
        self_out_grad,
        cross_q_grad,
        cross_kv_grad,
        cross_out_grad,
        ffn_in_grad,
        ffn_out_grad,
        small[0],
        small[1],
        small[2][0],
        small[3][0],
    )


def solution(mesh):
    placed = (
        P("role", ("dp", "head"), None),
        P("role", "dp", None),
        P(("dp", "head"), None),
        P(("dp", "head")),
        P(None, None, "head"),
        P("head", None),
        P(None, "head"),
        P(None, None, "head"),
        P("head", None),
        P(None, "head"),
        P("head", None),
        P(),
        P(),
        P(),
        P(),
    )
    return jax.shard_map(
        shards,
        mesh=mesh,
        in_specs=placed,
        out_specs=(
            P("role", ("dp", "head"), None),
            P("role", ("dp", "head"), None),
            P(None, None, "head"),
            P("head", None),
            P(None, "head"),
            P(None, None, "head"),
            P("head", None),
            P(None, "head"),
            P("head", None),
            P(),
            P(),
            P(),
            P(),
        ),
        check_vma=False,
    )
```

```python
import functools
import math

import jax
import jax.numpy as jnp
from jax import lax
from jax.experimental import pallas as pl
from jax.experimental.pallas import tpu as pltpu
from jax.sharding import PartitionSpec as P

F32 = jnp.float32
BF16 = jnp.bfloat16

HEAD_DIM = 64
HALF = 256
HEADS = HALF // HEAD_DIM
HALO = 128
GROUPS = 3
WINDOW = 128
MASKED = -1e30
SPARE = 8
WEIGHT = 1.2e9
ANY = pl.BlockSpec(memory_space=pl.ANY)
VMEM = pl.BlockSpec(memory_space=pltpu.VMEM)
SMEM = pl.BlockSpec(memory_space=pltpu.SMEM)
ARRIVALS = (0, 2, 1, 3)
FFN_ROUTES = [("head", "x"), ("x", "head")]
CROSS_ROUTES = [("x", "head")]
SELF_ROUTES = [("head", "x"), ("x", "head")]
HEAVY = 8
PIECES = 4


def dot(a, b):
    return jnp.dot(a, b, preferred_element_type=F32)


def dot_nt(a, b):
    return lax.dot_general(a, b, (((1,), (1,)), ((), ())), preferred_element_type=F32)


def dot_tn(a, b):
    return lax.dot_general(a, b, (((0,), (0,)), ((), ())), preferred_element_type=F32)


def norm_parts(values):
    center = values - jnp.mean(values, axis=-1, keepdims=True)
    spread = jnp.mean(center * center, axis=-1, keepdims=True)
    scale = lax.rsqrt(spread + 1e-05)
    return center * scale, scale


def norm_back(grad, hat, scale, gain):
    grad_hat = grad * gain
    first = jnp.mean(grad_hat, axis=-1, keepdims=True)
    second = jnp.mean(grad_hat * hat, axis=-1, keepdims=True)
    return scale * (grad_hat - first - hat * second)


class Load:
    def __init__(self, source, target, sem):
        self.target, self.copy = target, pltpu.make_async_copy(source, target, sem)
        self.gone = self.come = False

    def go(self):
        if not self.gone:
            self.copy.start()
        self.gone = True

    def __call__(self):
        self.go()
        if not self.come:
            self.copy.wait()
        self.come = True
        return self.target


class Store:
    def __init__(self, ref, target, sem):
        self.ref, self.target, self.sem, self.copies = ref, target, sem, []

    def send(self, at=None):
        if at is None:
            copy = pltpu.make_async_copy(self.ref, self.target, self.sem)
        else:
            at = pl.ds(at.start, at.stop - at.start)
            copy = pltpu.make_async_copy(self.ref.at[at], self.target.at[at], self.sem)
        copy.start()
        self.copies.append(copy)

    def end(self):
        if not self.copies:
            self.send()
        wait(self.copies)


def start(copies):
    for copy in copies:
        copy.start()
    return copies


def wait(copies):
    for copy in copies:
        copy.wait()


def cut_self(meta, matrices, out, piece, sem):
    wait(start(row_copies(meta[1], matrices, out, piece.ref, 0, sem)))


def row_copies(which, matrices, out, piece, first, sem):
    count, rows = matrices.shape[0], piece.shape[1]
    low = pl.multiple_of(which * rows, rows)
    out_low = pl.multiple_of((which & 1) * rows, rows)
    out_left = pl.multiple_of((which >> 1) * HALF, HALF)
    return [
        pltpu.make_async_copy(matrices.at[:, pl.ds(low, rows)], piece.at[pl.ds(first, count)], sem.at[0]),
        pltpu.make_async_copy(out.at[pl.ds(out_low, rows), pl.ds(out_left, HALF)], piece.at[3], sem.at[1]),
    ]


def cut_rest(meta, q, pair, out, ffn_in, ffn_out, cross_piece, in_piece, out_piece, sem):
    cross_piece, in_piece, out_piece = cross_piece.ref, in_piece.ref, out_piece.ref
    rows = cross_piece.shape[1]
    low = pl.multiple_of(meta[2] * rows, rows)
    copies = row_copies(meta[2], pair, out, cross_piece, 1, sem)
    copies.append(pltpu.make_async_copy(q.at[pl.ds(low, rows)], cross_piece.at[0], sem.at[2]))
    low = pl.multiple_of(meta[1] * rows, rows)
    for j in range(4):
        source = ffn_in.at[pl.ds(low, rows), pl.ds(j * HALF, HALF)]
        copies.append(pltpu.make_async_copy(source, in_piece.at[j], sem.at[3]))
    low = pl.multiple_of(meta[2] * HALF, HALF)
    copies.append(pltpu.make_async_copy(ffn_out.at[pl.ds(low, HALF)], out_piece, sem.at[4]))
    wait(start(copies))


def start_out_own(out, held, sem):
    return start(
        [
            pltpu.make_async_copy(out.at[:, pl.ds(c * HALF, HALF)], held.at[pl.ds(c * HALF, HALF)], sem.at[c])
            for c in range(2)
        ]
    )


def start_other(place, arrived, first, held, sem):
    rows, count = arrived[0].shape[1], held.shape[0]
    copies = []
    for at, (ref, flip) in enumerate(zip(arrived, ARRIVALS)):
        low = pl.multiple_of((place ^ flip) * rows, rows)
        source = ref.at[pl.ds(first, count)]
        copies.append(pltpu.make_async_copy(source, held.at[:, pl.ds(low, rows)], sem.at[2 + at]))
    return start(copies)


def start_in(meta, own, arrived, held, sem):
    copies = [
        pltpu.make_async_copy(own.at[:, pl.ds(j * HALF, HALF)], held.at[j], sem.at[0]) for j in range(4)
    ]
    return start(copies) + start_other(meta[1], arrived, 0, held.at[pl.ds(4, 4)], sem)


def start_out(meta, own, arrived, held, sem):
    copies = [
        pltpu.make_async_copy(own.at[pl.ds(j * HALF, HALF)], held.at[j], sem.at[0]) for j in range(4)
    ]
    for at, (ref, flip) in enumerate(zip(arrived, ARRIVALS)):
        copies.append(pltpu.make_async_copy(ref, held.at[4 + (meta[2] ^ flip)], sem.at[2 + at]))
    return start(copies)


def put_half(meta, grads, keep, send, sem, half, x_first=False):
    _, _, count, rows, _ = keep.shape
    copies = []
    for rel in range(PIECES):
        first = pl.multiple_of((rel ^ meta[1]) * rows, rows)
        source = grads.at[pl.ds(half * count, count), pl.ds(first, rows)]
        at = (rel >> 1, half) if x_first else (half, rel >> 1)
        target = (send if rel & 1 else keep).at[at]
        copies.append(pltpu.make_async_copy(source, target, sem.at[0]))
    return start(copies)


def put_grads(meta, grads, keep, send, sem, x_first=False):
    return [copy for half in range(2) for copy in put_half(meta, grads, keep, send, sem, half, x_first)]


def group_sentences(meta, segs, self_plan, cross_plan):
    first_row = meta[0] * meta[3]
    last_row = first_row + meta[3]
    shift = HALO - first_row
    zero = jnp.int32(0)
    for plan, cross in ((self_plan, False), (cross_plan, True)):

        def step(c, carry, plan=plan, cross=cross):
            t0, s0, done, count, low, high = carry
            t1, s1 = t0 + segs[1, c], s0 + segs[0, c]
            t2, s2 = t1 + segs[1, c + 1], s1 + segs[0, c + 1]
            t3, s3 = t2 + segs[1, c + 2], s2 + segs[0, c + 2]
            target_end, source_end = window_of(t0) + WINDOW, window_of(s0) + WINDOW
            two = (t2 <= target_end) & (t1 < last_row)
            three = two & (t3 <= target_end) & (t2 < last_row)
            if cross:
                two = two & (s2 <= source_end)
                three = three & (s3 <= source_end) & two
            t2, s2 = jnp.where(two, t2, t1), jnp.where(two, s2, s1)
            t3, s3 = jnp.where(three, t3, t2), jnp.where(three, s3, s2)
            mine = (t1 > first_row) & (t0 < last_row)
            here = (c >= done) & mine
            for at, bound in enumerate((t0, t1, t2, t3)):
                plan[at, count] = bound + shift
            for at, bound in enumerate((s0, s1, s2, s3)):
                plan[4 + at, count] = bound
            size = 1 + two.astype(jnp.int32) + three.astype(jnp.int32)
            low = jnp.where(mine, jnp.minimum(low, s0), low)
            high = jnp.where(mine, jnp.maximum(high, s1), high)
            return t1, s1, jnp.where(here, c + size, done), count + here.astype(jnp.int32), low, high

        start = (zero, zero, zero, zero, jnp.int32(1 << 20), zero)
        _, _, _, count, low, high = lax.fori_loop(0, segs.shape[1] - 2, step, start)
        for g in range(GROUPS):
            for at in range(8):
                plan[at, count + g] = 0
        plan[8, 0] = count
        plan[8, 1] = low
        plan[8, 2] = high


def each_group(plan, windows, compute, store):
    def work(first, count):
        bounds = [
            ([plan[at, first + g] for at in range(4)], [plan[4 + at, first + g] for at in range(4)])
            for g in range(count)
        ]
        operands = [windows(*each) for each in bounds]
        results = iter(compute([window for each in operands for window in each]))
        for each, windows_of_it in zip(bounds, operands):
            store(*each, [next(results) for _ in windows_of_it])

    def some(i, _):
        work(i * GROUPS, GROUPS)
        return 0

    def one(i, _):
        work(i, 1)
        return 0

    count = plan[8, 0]
    together = count // GROUPS
    lax.fori_loop(0, together, some, 0)
    lax.fori_loop(together * GROUPS, count, one, 0)


def window_of(start):
    return pl.multiple_of((start // 16) * 16, 16)


def spread_lanes(block):
    lanes = lax.broadcasted_iota(jnp.int32, (1, HALF), 1) // HEAD_DIM
    return jnp.concatenate(
        [jnp.where(lanes == h, block, jnp.zeros_like(block)) for h in range(HEADS)], axis=0
    )


def spread_rows(block):
    none = jnp.zeros((HEAD_DIM, block.shape[1]), block.dtype)
    return jnp.concatenate(
        [
            jnp.concatenate(
                [block[g * HEAD_DIM : (g + 1) * HEAD_DIM] if g == h else none for g in range(HEADS)],
                axis=0,
            )
            for h in range(HEADS)
        ],
        axis=1,
    )


def by_head(rows, spread):
    columns = spread.shape[1] // HEADS
    return jnp.concatenate(
        [
            dot(rows[h * HEAD_DIM : (h + 1) * HEAD_DIM], spread[:, h * columns : (h + 1) * columns])
            for h in range(HEADS)
        ],
        axis=0,
    )


def window_mask(q_first, q_bounds, k_first, k_bounds, q_low, q_high, causal):
    q = lax.broadcasted_iota(jnp.int32, (1, WINDOW), 1) + q_first
    k = lax.broadcasted_iota(jnp.int32, (WINDOW, WINDOW), 0) + k_first
    q_id = sum((q >= bound).astype(jnp.int32) for bound in q_bounds)
    k_id = sum((k >= bound).astype(jnp.int32) for bound in k_bounds)
    allowed = k_id == q_id
    if causal:
        allowed = allowed & (k <= q)
    valid = (q >= jnp.maximum(q_bounds[0], q_low)) & (q < jnp.minimum(q_bounds[3], q_high))
    return jnp.concatenate([allowed] * HEADS, axis=1), jnp.concatenate([valid] * HEADS, axis=1)


def window_weights(scores, masks):
    scores = [jnp.where(allowed, each, MASKED) for each, (allowed, _) in zip(scores, masks)]
    weights = [jnp.exp(each - jnp.max(each, axis=0, keepdims=True)) for each in scores]
    inverses = [
        jnp.where(valid, 1.0 / jnp.sum(each, axis=0, keepdims=True), 0.0)
        for each, (_, valid) in zip(weights, masks)
    ]
    return [each * inverse for each, inverse in zip(weights, inverses)]


def attend_windows(windows):
    qs, ks, vs, masks = zip(*windows)
    q_rows = [spread_rows((q * jnp.asarray(HEAD_DIM**-0.5, BF16)).T) for q in qs]
    scores = [dot(k, q) for k, q in zip(ks, q_rows)]
    probabilities = [each.astype(BF16) for each in window_weights(scores, masks)]
    mixes = [by_head(v.T, each) for v, each in zip(vs, probabilities)]
    return [mix.astype(BF16).T for mix in mixes]


def attend_windows_back(windows):
    qs, ks, vs, grads, masks = zip(*windows)
    scale = HEAD_DIM**-0.5
    qs = [q * jnp.asarray(scale, BF16) for q in qs]
    scores = [dot(k, spread_rows(q.T)) for k, q in zip(ks, qs)]
    prob_grads = [dot(v, spread_rows(grad.T)) for v, grad in zip(vs, grads)]
    probabilities = window_weights(scores, masks)
    inners = [
        jnp.sum(each * grad, axis=0, keepdims=True) for each, grad in zip(probabilities, prob_grads)
    ]
    score_grads = [
        (each * (grad - inner)).astype(BF16)
        for each, grad, inner in zip(probabilities, prob_grads, inners)
    ]
    v_grads = [
        dot(each.astype(BF16), spread_lanes(grad)) for each, grad in zip(probabilities, grads)
    ]
    q_grads = [by_head(k.T, each) for k, each in zip(ks, score_grads)]
    k_grads = [dot(each, spread_lanes(q)) for each, q in zip(score_grads, qs)]
    q_grads = [(each * scale).astype(BF16).T for each in q_grads]
    return [(q, k.astype(BF16), v.astype(BF16)) for q, k, v in zip(q_grads, k_grads, v_grads)]


def out_product(mixes, outs):
    left = sum(dot(mix, out[0:HALF]) for mix, out in zip(mixes, outs))
    right = sum(dot(mix, out[HALF:]) for mix, out in zip(mixes, outs))
    return jnp.concatenate([left, right], axis=1)


def out_mix_grads(grad_low, outs, mix_grads, first):
    rows = grad_low.shape[0]
    for half in range(2):
        for lo in range(0, rows, HALF):
            block = grad_low[lo : lo + HALF]
            mix_grad = dot_nt(block[:, :HALF], outs[half, 0:HALF]) + dot_nt(block[:, HALF:], outs[half, HALF:])
            mix_grads[half, first + lo : first + lo + HALF] = mix_grad.astype(BF16)


def out_weight_grads(grad_low, mixes, grads):
    for half, mix in enumerate(mixes):
        grads[half, 0:HALF] = dot_tn(mix, grad_low[:, :HALF]).astype(BF16)
        grads[half, HALF:] = dot_tn(mix, grad_low[:, HALF:]).astype(BF16)


def copy_by_role(meta, pairs_zero, pairs_one, sem):
    @pl.when(meta[0] == 0)
    def _():
        for source, target in pairs_zero:
            pltpu.make_async_copy(source, target, sem).start()

    @pl.when(meta[0] == 1)
    def _():
        for source, target in pairs_one:
            pltpu.make_async_copy(source, target, sem).start()


def wait_by_role(meta, pairs_zero, pairs_one, sem):
    @pl.when(meta[0] == 0)
    def _():
        for source, target in pairs_zero:
            pltpu.make_async_copy(source, target, sem).wait()

    @pl.when(meta[0] == 1)
    def _():
        for source, target in pairs_one:
            pltpu.make_async_copy(source, target, sem).wait()


def states_copies(rows_ref, other_ref, held, here):
    zero = [(other_ref.at[pl.ds(0, here)], held.at[pl.ds(HALO, here)])]
    one = [(rows_ref.at[pl.ds(here - HALO, here + HALO)], held.at[pl.ds(0, here + HALO)])]
    return zero, one


def self_attention(meta, segs, plan, here, qkvs, mixes):
    full = here + HALO
    for mix in mixes:
        mix[...] = jnp.zeros(mix.shape, BF16)

    def group(bounds, _):
        first = window_of(bounds[0])
        mask = window_mask(first, bounds, first, bounds, HALO, full, True)
        at = pl.ds(first, WINDOW)
        return [(qkv[0, at], qkv[1, at], qkv[2, at], mask) for qkv in qkvs]

    def store(bounds, _, result):
        at = pl.ds(window_of(bounds[0]), WINDOW)
        for mix, each in zip(mixes, result):
            mix[at] += each

    together = 2 * GROUPS // len(qkvs)
    each_group(meta, segs, plan, here, False, together, group, attend_windows, store)


def self_project(normed, held, qkv):
    full = normed.shape[0]
    qkv[:, full:] = jnp.zeros((3, WINDOW, HALF), BF16)
    for c in range(3):
        qkv[c, 0:full] = dot(normed[...], held[c]).astype(BF16)


def self_forward(
    meta, plan, rows_ref, other_ref, gain, bias, own, own_out, w1, w2, w3, w4,
    hidden, normed, qkv, mix, states, held, outs, sem_w, sem_x,
):
    full = states.shape[0]
    here = full - HALO
    state_copies = states_copies(rows_ref, other_ref, states, here)
    copy_by_role(meta, *state_copies, sem_x)
    weights = start_other(meta[1], (w1, w2, w3, w4), 0, held, sem_w)
    weights += start_out_own(own_out, outs, sem_w)
    mix.ref[...] = jnp.zeros(mix.ref.shape, BF16)
    wait_by_role(meta, *state_copies, sem_x)

    @pl.when(meta[0] == 0)
    def _():
        states[0:HALO] = jnp.zeros((HALO, states.shape[1]), BF16)

    for lo in range(0, full, HALO):
        hat, _ = norm_parts(states[lo : lo + HALO].astype(F32))
        normed.ref[lo : lo + HALO] = (hat * gain[0:1] + bias[0:1]).astype(BF16)
    normed.send()
    own = own()
    wait(weights)
    qkv.ref[:, :, full:] = jnp.zeros((2, 3, WINDOW, HALF), BF16)
    for half, matrices in enumerate((own, held)):
        for c in range(3):
            qkv.ref[half, c, 0:full] = dot(normed.ref[...], matrices[c]).astype(BF16)
    qkv.send()

    def group(bounds, _):
        first = window_of(bounds[0])
        mask = window_mask(first, bounds, first, bounds, HALO, full, True)
        at = pl.ds(first, WINDOW)
        return [(qkv.ref[half, 0, at], qkv.ref[half, 1, at], qkv.ref[half, 2, at], mask) for half in range(2)]

    def store(bounds, _, result):
        at = pl.ds(window_of(bounds[0]), WINDOW)
        for half in range(2):
            mix.ref[half, at] += result[half]

    each_group(plan, group, attend_windows, store)
    mix.send()
    for lo in range(HALO, full, HALF):
        at = slice(lo, lo + HALF)
        hidden[lo - HALO : lo - HALO + HALF] = states[at].astype(F32) + out_product(
            [mix.ref[0, at], mix.ref[1, at]], [outs, held[3]]
        )


def blocks_do(low, high, pairs, target, sem, act):
    def one(block, _):
        at = pl.ds(pl.multiple_of(block * HALF, HALF), HALF)
        act(pltpu.make_async_copy(pairs.at[:, :, at], target.at[:, :, at], sem))
        return 0

    lax.fori_loop(low // HALF, (high + HALF - 1) // HALF, one, 0)


def zero_after(high, pairs):
    end = pl.multiple_of(((high + HALF - 1) // HALF) * HALF, HALF)
    pairs[:, :, pl.ds(end, WINDOW)] = jnp.zeros((2, 2, WINDOW, HALF), BF16)


def memory_copies(rows_ref, other_ref, held):
    return [(rows_ref, held)], [(other_ref, held)]


def cross_forward(
    meta, plan, rows_ref, other_ref, hidden, gain, bias, own_q, own_pair, own_out, w1, w2, w3, w4,
    hidden_two, hidden_far, normed, mix, queries, pairs_far, pairs, memory, held, outs, sem_w, sem_x, sem_h,
):
    here = hidden_two.ref.shape[0]
    hidden_copy = pltpu.make_async_copy(hidden, hidden_far, sem_h.at[0])
    hidden_copy.start()
    full = here + HALO
    copies = memory_copies(rows_ref, other_ref, memory)
    copy_by_role(meta, *copies, sem_x)
    weights = start_other(meta[2], (w1, w2, w3, w4), 0, held, sem_w)
    weights += start_out_own(own_out, outs, sem_w)
    queries.ref[:, 0:HALO] = jnp.zeros((2, HALO, HALF), BF16)
    queries.ref[:, full:] = jnp.zeros((2, WINDOW, HALF), BF16)
    mix.ref[...] = jnp.zeros(mix.ref.shape, BF16)
    low, high = plan[8, 1], plan[8, 2]
    zero_after(high, pairs)
    for lo in range(0, here, HALF):
        at = slice(lo, lo + HALF)
        hat, _ = norm_parts(hidden[at])
        normed.ref[at] = (hat * gain[1:2] + bias[1:2]).astype(BF16)
    normed.send()
    own_q, own_pair = own_q(), own_pair()
    wait(weights)
    for half, matrix in enumerate((own_q, held.at[0])):
        queries.ref[half, HALO:full] = dot(normed.ref[...], matrix[...]).astype(BF16)
    queries.send()
    wait_by_role(meta, *copies, sem_x)

    def project(block, _):
        at = pl.ds(pl.multiple_of(block * HALF, HALF), HALF)
        for c in range(2):
            pairs[0, c, at] = dot(memory[at], own_pair[c]).astype(BF16)
            pairs[1, c, at] = dot(memory[at], held[1 + c]).astype(BF16)
        return 0

    lax.fori_loop(low // HALF, (high + HALF - 1) // HALF, project, 0)
    blocks_do(low, high, pairs, pairs_far, sem_h.at[1], lambda copy: copy.start())

    def group(bounds, source_bounds):
        first = window_of(bounds[0])
        source_first = window_of(source_bounds[0])
        mask = window_mask(first, bounds, source_first, source_bounds, HALO, full, False)
        at = pl.ds(first, WINDOW)
        source_at = pl.ds(source_first, WINDOW)
        return [
            (queries.ref[half, at], pairs[half, 0, source_at], pairs[half, 1, source_at], mask)
            for half in range(2)
        ]

    def store(bounds, _, result):
        at = pl.ds(window_of(bounds[0]), WINDOW)
        for half in range(2):
            mix.ref[half, at] += result[half]

    each_group(plan, group, attend_windows, store)
    mix.send()
    for lo in range(0, here, HALF):
        at = slice(lo, lo + HALF)
        mix_at = slice(HALO + lo, HALO + lo + HALF)
        hidden_two.ref[at] = hidden[at] + out_product([mix.ref[0, mix_at], mix.ref[1, mix_at]], [outs, held[3]])
        hidden_two.send(at)
    hidden_copy.wait()
    blocks_do(low, high, pairs, pairs_far, sem_h.at[1], lambda copy: copy.wait())


def gelu_both(inner):
    rate, cubic = 0.7978845608028654, 0.7978845608028654 * 0.044715
    square = inner * inner
    bent = jnp.tanh(inner * (rate + cubic * square))
    half = 0.5 + 0.5 * bent
    slope = half + inner * (1.0 - bent * bent) * (0.5 * rate + 1.5 * cubic * square)
    return inner * half, slope


def column(values, role, at):
    lanes = lax.broadcasted_iota(jnp.int32, (WINDOW, WINDOW), 1)
    own = lax.broadcasted_iota(jnp.int32, (WINDOW, WINDOW), 0) == lanes
    blocks = []
    for block in range(at.start // WINDOW, at.stop // WINDOW):
        row = values[role, block : block + 1]
        blocks.append(jnp.sum(jnp.where(own, row, 0.0), axis=1, keepdims=True))
    return jnp.concatenate(blocks, axis=0)


def feed_forward(
    meta, hidden_two, cotangent, targets, gain, bias, halt_weight, halt_bias,
    own_in, i1, i2, i3, i4, own_out, o1, o2, o3, o4,
    result_low, hidden_grad, hidden_far, small, keep, send,
    held_in, held_out, normed, active, slopes, total, out_low, cot, grads, sem_w, sem_o, sem_x, sem_g,
):
    here, width = total.shape
    first = pl.multiple_of(meta[0] * here, here)
    cot_copy = pltpu.make_async_copy(cotangent.at[pl.ds(first, here)], cot, sem_x.at[0])
    weights = start_in(meta, own_in, (i1, i2, i3, i4), held_in, sem_w)
    weights += start_out(meta, own_out, (o1, o2, o3, o4), held_out, sem_o)
    cot_copy.start()
    hidden_two = hidden_two()
    blocks = [slice(lo, lo + HALF) for lo in range(0, here, HALF)]
    for at in blocks:
        hat, _ = norm_parts(hidden_two[at])
        normed[at] = (hat * gain[2:3] + bias[2:3]).astype(BF16)
        total[at] = hidden_two[at]
    wait(weights)

    def forward(pair, _):
        items = [(at, 8 * pair + u) for at in blocks for u in range(8)]
        inner = dot(normed[items[0][0]], held_in[items[0][1]])
        products = []
        for i, (at, j) in enumerate(items):
            coming = dot(normed[items[i + 1][0]], held_in[items[i + 1][1]]) if i + 1 < len(items) else None
            value, slope = gelu_both(inner)
            value = value.astype(BF16)
            active[j, at] = value
            slopes[j, at] = slope
            products.append(dot(value, held_out[j]))
            if len(products) == 8:
                total[at] += sum(products)
                products = []
            inner = coming
        return 0

    lax.fori_loop(0, 1, forward, 0)
    cot_copy.wait()
    weight_sum = jnp.zeros((1, width), F32)
    bias_sum = jnp.zeros((1, 1), F32)
    for at in blocks:
        result = total[at]
        result_low.ref[at] = result.astype(BF16)
        logits = jnp.sum(result * halt_weight[...], axis=-1, keepdims=True) + halt_bias[0]
        halt_grad = 1.0 / (1.0 + jnp.exp(-logits)) - column(targets, meta[0], at)
        out_grad = cot[at].astype(F32) + halt_grad * halt_weight[...]
        out_low[at] = out_grad.astype(BF16)
        hidden_grad[at] = out_grad
        total[at] = jnp.zeros((HALF, width), F32)
        weight_sum += jnp.sum(halt_grad * result, axis=0, keepdims=True)
        bias_sum += jnp.sum(halt_grad, axis=0, keepdims=True)
    result_low.send()

    def backward(i, _):
        js = [4 * i + u for u in range(4)]
        value_grads = [[dot_nt(out_low[at], held_out[j]) for at in blocks] for j in js]
        inner_grads = [
            [(grad * slopes[j, at]).astype(BF16) for grad, at in zip(grads_of_it, blocks)]
            for j, grads_of_it in zip(js, value_grads)
        ]
        for b, at in enumerate(blocks):
            total[at] += sum(dot_nt(each[b], held_in[j]) for j, each in zip(js, inner_grads))
        for j, each in zip(js, inner_grads):
            half, block = j // 4, j % 4
            grads[8 * half + block] = dot_tn(normed[...], jnp.concatenate(each, axis=0)).astype(BF16)
            out_grad = dot_tn(active[j], out_low[...]).astype(BF16)
            grads[8 * half + 4 + block, 0:HALF] = out_grad[:, :HALF]
            grads[8 * half + 4 + block, HALF:] = out_grad[:, HALF:]
        return 0

    lax.fori_loop(0, 4 // 4, backward, 0)
    copies = put_half(meta, grads, keep, send, sem_g, 0)
    lax.fori_loop(4 // 4, 8 // 4, backward, 0)
    copies += put_half(meta, grads, keep, send, sem_g, 1)
    gain_sum = jnp.zeros_like(weight_sum)
    shift_sum = jnp.zeros_like(weight_sum)
    for at in blocks:
        hat, scale = norm_parts(hidden_two[at])
        grad = total[at]
        hidden_grad[at] += norm_back(grad, hat, scale, gain[2:3])
        gain_sum += jnp.sum(grad * hat, axis=0, keepdims=True)
        shift_sum += jnp.sum(grad, axis=0, keepdims=True)
    small[...] = jnp.concatenate(
        [gain_sum, shift_sum, weight_sum, jnp.broadcast_to(bias_sum, weight_sum.shape)], axis=0
    )
    copies += start([pltpu.make_async_copy(hidden_grad, hidden_far, sem_x.at[1])])
    wait(copies)


def out_backward(
    meta, upper_grad, mix, own_out, w1, w2, w3, w4, *rest, place, ahead
):
    sources, (mix_grads, out_part), rest = rest[:ahead], rest[ahead : ahead + 2], rest[ahead + 2 :]
    targets, (outs, sem_w, sem_h) = rest[:ahead], rest[ahead:]
    full = mix_grads.shape[1] - WINDOW
    weights = start_other(meta[place], (w1, w2, w3, w4), 3, outs.at[pl.ds(1, 1)], sem_w)
    weights += start_out_own(own_out, outs.at[0], sem_w)
    mix.go()
    brought = start(
        [pltpu.make_async_copy(*copy, sem_h.at[at]) for at, copy in enumerate(zip(sources, targets))]
    )
    mix_grads[:, 0:HALO] = jnp.zeros((2, HALO, HALF), BF16)
    mix_grads[:, full:] = jnp.zeros((2, WINDOW, HALF), BF16)
    grad_low = upper_grad[...].astype(BF16)
    wait(weights)
    out_mix_grads(grad_low, outs, mix_grads, HALO)
    mix = mix()
    out_weight_grads(grad_low, [mix[0, HALO:full], mix[1, HALO:full]], out_part.ref)
    wait(brought)


def cross_backward(meta, plan, mix_grads, queries, pairs_far, q_grad, pair_grads, pairs, sem_h):
    full = mix_grads.shape[1] - WINDOW
    here = full - HALO
    low, high = plan[8, 1], plan[8, 2]
    blocks_do(low, high, pairs_far, pairs, sem_h.at[0], lambda copy: copy.start())
    q_grad[...] = jnp.zeros(q_grad.shape, BF16)
    pair_grads[...] = jnp.zeros(pair_grads.shape, BF16)
    zero_after(high, pairs)
    blocks_do(low, high, pairs_far, pairs, sem_h.at[0], lambda copy: copy.wait())

    def group(bounds, source_bounds):
        first = window_of(bounds[0])
        source_first = window_of(source_bounds[0])
        mask = window_mask(first, bounds, source_first, source_bounds, HALO, full, False)
        at = pl.ds(first, WINDOW)
        source_at = pl.ds(source_first, WINDOW)
        return [
            (
                queries[half, at], pairs[half, 0, source_at], pairs[half, 1, source_at],
                mix_grads[half, at], mask,
            )
            for half in range(2)
        ]

    def store(bounds, source_bounds, result):
        at = pl.ds(window_of(bounds[0]), WINDOW)
        source_at = pl.ds(window_of(source_bounds[0]), WINDOW)
        for half, (dq, dk, dv) in enumerate(result):
            q_grad[half, at] += dq
            pair_grads[half, 0, source_at] += dk
            pair_grads[half, 1, source_at] += dv

    each_group(plan, group, attend_windows_back, store)


def cross_products(
    meta, plan, rows_ref, other_ref, hidden, normed, upper_grad, q_grad, pair_grads, out_part, own_q, own_pair,
    w1, w2, w3, w4, gain,
    lower_grad, lower_far, memory_grad, small, keep, send, memory, pair_sums, grads, held, sem_w, sem_x, sem_g, sem_h,
):
    here, width = lower_grad.shape
    full = here + HALO
    weights = start_other(meta[2], (w1, w2, w3, w4), 0, held, sem_w)
    copies = memory_copies(rows_ref, other_ref, memory)
    copy_by_role(meta, *copies, sem_x)
    normed.go()
    hidden.go()
    upper_grad.go()
    pair_sums[...] = jnp.zeros(pair_sums.shape, F32)
    memory_grad.ref[...] = jnp.zeros(memory_grad.ref.shape, BF16)
    source_low, source_high = plan[8, 1], plan[8, 2]
    parts = start(
        [pltpu.make_async_copy(out_part.at[half], grads.at[4 * half + 3], sem_g.at[0]) for half in range(2)]
    )
    gain_sum = jnp.zeros((1, width), F32)
    shift_sum = jnp.zeros((1, width), F32)
    own_q, own_pair = own_q(), own_pair()
    wait(weights)
    wait_by_role(meta, *copies, sem_x)

    def project(block, _):
        at = pl.ds(pl.multiple_of(block * HALF, HALF), HALF)
        row_grad = jnp.zeros((HALF, width), F32)
        for half in range(2):
            for c in range(2):
                low = pair_grads[half, c, at]
                row_grad += dot_nt(low, held[1 + c] if half else own_pair[c])
                pair_sums[half, c] += dot_tn(memory[at], low)
        memory_grad.ref[at] = row_grad.astype(BF16)
        return 0

    lax.fori_loop(source_low // HALF, (source_high + HALF - 1) // HALF, project, 0)
    memory_grad.send()
    for half in range(2):
        for c in range(2):
            grads[4 * half + 1 + c] = pair_sums[half, c].astype(BF16)
    normed = normed()
    for half in range(2):
        grads[4 * half] = dot_tn(normed[...], q_grad[half, HALO:full]).astype(BF16)
    wait(parts)
    put = put_grads(meta, grads, keep, send, sem_g, x_first=True)
    hidden, upper_grad = hidden(), upper_grad()
    for lo in range(0, here, HALF):
        at = slice(lo, lo + HALF)
        q_at = slice(HALO + lo, HALO + lo + HALF)
        hat, scale = norm_parts(hidden[at])
        grad = dot_nt(q_grad[0, q_at], own_q[...]) + dot_nt(q_grad[1, q_at], held[0])
        lower_grad[at] = upper_grad[at] + norm_back(grad, hat, scale, gain[1:2])
        gain_sum += jnp.sum(grad * hat, axis=0, keepdims=True)
        shift_sum += jnp.sum(grad, axis=0, keepdims=True)
    small[...] = jnp.concatenate([gain_sum, shift_sum], axis=0)
    put += start([pltpu.make_async_copy(lower_grad, lower_far, sem_h.at[0])])
    wait(put)


def self_backward(meta, plan, mix_grads, qkv, qkv_grads):
    full = mix_grads.shape[1] - WINDOW
    here = full - HALO
    qkv_grads[...] = jnp.zeros(qkv_grads.shape, BF16)

    def group(bounds, _):
        first = window_of(bounds[0])
        mask = window_mask(first, bounds, first, bounds, HALO, full, True)
        at = pl.ds(first, WINDOW)
        return [
            (qkv[half, 0, at], qkv[half, 1, at], qkv[half, 2, at], mix_grads[half, at], mask)
            for half in range(2)
        ]

    def store(bounds, _, result):
        at = pl.ds(window_of(bounds[0]), WINDOW)
        for half in range(2):
            for c in range(3):
                qkv_grads[half, c, at] += result[half][c]

    each_group(plan, group, attend_windows_back, store)


def self_products(
    meta, rows_ref, other_ref, normed, qkv_grads, out_part, upper_grad, own, w1, w2, w3, w4, gain, result, memory_part,
    keep, send, state_grad, swap, halo_grad, small, grads, states, held, sem_g, sem_w, sem_x, sem_s,
):
    full, width = states.shape
    here = full - HALO
    normed.go()
    parts = start(
        [pltpu.make_async_copy(out_part.at[half], grads.at[4 * half + 3], sem_g.at[0]) for half in range(2)]
    )
    weights = start_other(meta[1], (w1, w2, w3, w4), 0, held, sem_w)
    state_copies = states_copies(rows_ref, other_ref, states, here)
    copy_by_role(meta, *state_copies, sem_x)
    swaps = [(result, swap.ref.at[pl.ds(0, here)])], [(memory_part, swap.ref)]
    own.go()
    upper_grad.go()
    copy_by_role(meta, *swaps, sem_s)
    normed = normed()
    for half in range(2):
        for c in range(3):
            grads[4 * half + c] = dot_tn(normed[...], qkv_grads[half, c, 0:full]).astype(BF16)
    wait(parts)
    put = put_grads(meta, grads, keep, send, sem_g)
    wait_by_role(meta, *state_copies, sem_x)

    @pl.when(meta[0] == 0)
    def _():
        states[0:HALO] = jnp.zeros((HALO, width), BF16)

    own, upper_grad = own(), upper_grad()
    wait(weights)
    gain_sum = jnp.zeros((1, width), F32)
    shift_sum = jnp.zeros((1, width), F32)
    step = full // 2
    for lo in range(0, full, step):
        at = slice(lo, lo + step)
        hat, scale = norm_parts(states[at].astype(F32))
        grad = sum(
            dot_nt(qkv_grads[half, c, at], matrices[c])
            for half, matrices in enumerate((own, held))
            for c in range(3)
        )
        back = norm_back(grad, hat, scale, gain[0:1])
        if lo == 0:
            halo_grad.ref[...] = back[:HALO]
            back = back[HALO:]
        first = max(lo, HALO) - HALO
        at = slice(first, lo + step - HALO)
        back += upper_grad[at]
        state_grad.ref[at] = back

        @pl.when(meta[0] == 0)
        def _(low=back.astype(BF16), at=slice(here + at.start, here + at.stop)):
            swap.ref[at] = low

        gain_sum += jnp.sum(grad * hat, axis=0, keepdims=True)
        shift_sum += jnp.sum(grad, axis=0, keepdims=True)
    small[...] = jnp.concatenate([gain_sum, shift_sum], axis=0)
    wait_by_role(meta, *swaps, sem_s)
    wait(put)


def finish_rows(
    meta, rows, result, grad, halo_grad, memory_part, swapped, layer_out, input_grads, parts, halo, sem,
):
    here = result.shape[0]
    low, high = pl.ds(0, here), pl.ds(here, here)

    @pl.when(meta[0] == 0)
    def _():
        copies = [(rows, layer_out.ref), (memory_part, parts.at[0]), (swapped, parts.at[1])]
        wait(start([pltpu.make_async_copy(*copy, sem) for copy in copies]))
        input_grads.ref[...] = parts[0].astype(F32) + parts[1].astype(F32)

    @pl.when(meta[0] == 1)
    def _():
        copies = [
            (swapped.at[low], layer_out.ref.at[low]),
            (result, layer_out.ref.at[high]),
            (swapped.at[high], parts.at[0, low]),
            (grad, input_grads.ref.at[high]),
            (halo_grad, halo),
        ]
        wait(start([pltpu.make_async_copy(*copy, sem) for copy in copies]))
        input_grads.ref[0:here] = parts[0, 0:here].astype(F32)
        input_grads.ref[here - HALO : here] += halo[...]


OUTPUTS = {"ffn": 2, "cross": 7, "self": 2}


def unpack(kinds, meta, *refs):
    pieces, refs = refs[: 4 * len(kinds)], refs[4 * len(kinds) :]
    if "cross" in kinds:
        small, refs = refs[0], refs[1:]
    count = sum(OUTPUTS[kind] for kind in kinds)
    outs, held, sem = refs[:count], refs[count:-1], refs[-1]
    copies = []
    for at in range(len(kinds)):
        rows = pieces[4 * at].shape[1]
        came = zip((0, 2, 1, 3), pieces[4 * at : 4 * at + 4])
        firsts = [(pl.multiple_of((rel ^ meta[1]) * rows, rows), ref) for rel, ref in came]
        copies.append(
            start(
                [
                    pltpu.make_async_copy(ref, held[at].at[:, pl.ds(first, rows)], sem.at[at])
                    for first, ref in firsts
                ]
            )
        )
    for kind, grads, arrived in zip(kinds, held, copies):
        outs, rest = outs[: OUTPUTS[kind]], outs[OUTPUTS[kind] :]
        wait(arrived)
        if kind == "ffn":
            grad_in, grad_out = outs
            for j in range(4):
                at = slice(j * HALF, (j + 1) * HALF)
                grad_in[:, at] = grads[j].astype(F32)
                grad_out[at, 0:HALF] = grads[4 + j, 0:HALF].astype(F32)
                grad_out[at, HALF:] = grads[4 + j, HALF:].astype(F32)
        else:
            if kind == "cross":
                gain, shift, weight, bias = outs[3:]
                gain[...], shift[...] = small[0:3], small[3:6]
                weight[...], bias[...] = small[6:7], small[7:8, 0:1]
                outs[0][...] = grads[0].astype(F32)
                for c in range(2):
                    outs[1][:, c] = grads[1 + c].astype(F32)
                out = outs[2]
            else:
                outs[0][...] = grads[0:3].astype(F32)
                out = outs[1]
            out[:, 0:HALF] = grads[3, 0:HALF].astype(F32)
            out[:, HALF:] = grads[3, HALF:].astype(F32)
        outs = rest


def shape(*dims, dtype=F32):
    return jax.ShapeDtypeStruct(dims, dtype)


def far(*dims, dtype=F32):
    return pltpu.HBM(dims, dtype)


def near(*dims, dtype=F32):
    return pltpu.VMEM(dims, dtype)


def room(shapes, spare):
    return sum(math.prod(each.shape) * jnp.dtype(each.dtype).itemsize for each in shapes) + (spare << 20)


class Put:
    def __init__(self, *dims, dtype=F32):
        self.shape = far(*dims, dtype=dtype)
        self.scratch = pltpu.VMEM(dims, dtype)


class Get:
    def __init__(self, value, late=False):
        self.value = value
        self.late = late
        self.scratch = pltpu.VMEM(value.shape, value.dtype)


class Here:
    def __init__(self, value):
        self.value = value


class Any:
    def __init__(self, value):
        self.value = value


class Far:
    def __init__(self, value):
        self.value = value


def call(body, ins, outs, scratch, weight):
    smem, others = ins
    operands = list(smem) + list(others)
    values, in_specs = list(smem), [SMEM] * len(smem)
    for other in others:
        if isinstance(other, (Get, Far)):
            values.append(pltpu.with_memory_space_constraint(other.value, pltpu.HBM))
            in_specs.append(ANY)
        elif isinstance(other, Any):
            values.append(other.value)
            in_specs.append(ANY)
        elif isinstance(other, Here):
            values.append(pltpu.with_memory_space_constraint(other.value, pltpu.VMEM))
            in_specs.append(VMEM)
        else:
            values.append(other)
            in_specs.append(VMEM)
    moved = [at for at, each in enumerate(operands) if isinstance(each, Get)]
    put = [at for at, each in enumerate(outs) if isinstance(each, Put)]

    def inner(*refs):
        in_refs, refs = list(refs[: len(values)]), refs[len(values) :]
        out_refs, refs = list(refs[: len(outs)]), refs[len(outs) :]
        moved_refs, refs = refs[: len(moved)], refs[len(moved) :]
        put_refs, refs = refs[: len(put)], refs[len(put) :]
        sems, refs = refs[0], refs[1:]
        for i, at in enumerate(moved):
            in_refs[at] = Load(in_refs[at], moved_refs[i], sems.at[i])
            if not operands[at].late:
                in_refs[at].go()
        for i, at in enumerate(put):
            out_refs[at] = Store(put_refs[i], out_refs[at], sems.at[len(moved) + i])
        body(*in_refs, *out_refs, *refs)
        for at in moved:
            in_refs[at]()
        for at in put:
            if not out_refs[at].copies:
                out_refs[at].send()
        for at in put:
            out_refs[at].end()

    in_vmem = [operands[at].scratch for at in moved] + [outs[at].scratch for at in put]
    in_vmem += [each for each in scratch if getattr(each, "memory_space", None) is pltpu.VMEM]
    in_vmem += [value for value, spec in zip(values, in_specs) if spec is VMEM]
    in_vmem += [out for out in outs if not isinstance(out, Put) and getattr(out, "memory_space", None) is not pltpu.HBM]
    return pl.pallas_call(
        inner,
        out_shape=[out.shape if isinstance(out, Put) else out for out in outs],
        in_specs=in_specs,
        out_specs=[ANY if isinstance(out, Put) or getattr(out, "memory_space", None) is pltpu.HBM else VMEM for out in outs],
        scratch_shapes=[operands[at].scratch for at in moved]
        + [outs[at].scratch for at in put]
        + [pltpu.SemaphoreType.DMA((len(moved) + len(put) + 1,))]
        + list(scratch),
        name=getattr(body, "__name__", "out_backward"),
        compiler_params=pltpu.CompilerParams(vmem_limit_bytes=room(in_vmem, SPARE)),
        cost_estimate=pl.CostEstimate(flops=int(weight * WEIGHT), bytes_accessed=0, transcendentals=0),
    )(*values)


def flip(value, axis, bit=1):
    count = lax.axis_size(axis)
    return lax.ppermute(value, axis, [(i, i ^ bit) for i in range(count)])


def add(a, b):
    return (a.astype(F32) + b.astype(F32)).astype(BF16)


def after(value, *events):
    return lax.optimization_barrier((value, events))[0]


class Order:
    def __init__(self, meta):
        self.meta = meta
        self.last = ()

    def now(self):
        return after(self.meta, *self.last)

    def __call__(self, weight, *jobs):
        operands = [value for job in jobs for value in job[0]]
        shapes = [each for job in jobs for each in job[1]]

        def sums(meta, *refs):
            ins, outs = list(refs[: len(operands)]), list(refs[len(operands) :])
            for values, results, body, _ in jobs:
                body(meta, ins[: len(values)], outs[: len(results)])
                ins, outs = ins[len(values) :], outs[len(results) :]

        results = list(
            pl.pallas_call(
                sums,
                out_shape=shapes,
                in_specs=[SMEM] + [VMEM] * len(operands),
                out_specs=[VMEM] * len(shapes),
                name="sums",
                compiler_params=pltpu.CompilerParams(vmem_limit_bytes=room(operands + shapes, 4)),
                cost_estimate=pl.CostEstimate(flops=int(weight * WEIGHT), bytes_accessed=0, transcendentals=0),
            )(self.now(), *operands)
        )
        self.last = tuple(results)
        for _, each, _, take in jobs:
            take(results[: len(each)])
            results = results[len(each) :]


class Sum:
    def __init__(self, keep, send, routes):
        self.routes = routes
        self.near, self.got = [keep], [flip(send, "role")]

    def job(self, shapes, body, take):
        count = len(self.near)
        return (
            [*self.near, *self.got],
            [jax.ShapeDtypeStruct(each, BF16) if isinstance(each, tuple) else each for each in shapes],
            lambda meta, ins, outs: body(meta, ins[:count], ins[count:], outs),
            take,
        )

    def pass_on(self, stage, far_near=False):
        def take(parts):
            self.near = parts[0::2]
            if far_near:
                self.near = [pltpu.with_memory_space_constraint(each, pltpu.HBM) for each in self.near]
            self.got = [step(away, route[stage]) for away, route in zip(parts[1::2], self.routes)]

        return take

    def begin(self, far_near=False):
        count = len(self.routes)
        _, _, matrices, rows, columns = self.near[0].shape
        share = matrices // count

        def body(meta, near, got, outs):
            for at, route in enumerate(self.routes):
                mine = pl.ds(at * share, share)
                for which in range(2):
                    place = (slice(None), which, mine) if route[0] == "x" and count > 1 else (which, slice(None), mine)
                    outs[2 * at + which][...] = add(near[0][place], got[0][place])

        shapes = [jax.ShapeDtypeStruct((2, share, rows, columns), BF16)] * (2 * count)
        if far_near:
            shapes[0::2] = [far(2, share, rows, columns, dtype=BF16)] * count
        return self.job(shapes, body, self.pass_on(0, far_near))

    def second(self):
        def body(meta, near, got, outs):
            for at in range(len(near)):
                for which in range(2):
                    outs[2 * at + which][...] = add(near[at][which], got[at][which])

        return self.job([self.near[0].shape[1:]] * (2 * len(self.near)), body, self.pass_on(1))

    def halve(self):
        count = len(self.near)
        matrices, rows, columns = self.near[0].shape
        half = count * matrices // 2

        def body(meta, near, got, outs):
            upper = meta[2] >> 1
            for out, which in zip(outs, (upper, 1 - upper)):
                if count == 1:
                    at = pl.ds(which * half, half)
                    out[...] = add(near[0][at], got[0][at])
                else:
                    both = [add(mine[...], theirs[...]) for mine, theirs in zip(near, got)]
                    out[...] = jnp.where(which == 1, both[1], both[0])

        def take(parts):
            self.near, self.got = [parts[0]], [flip(parts[1], "dp", 2)]

        return self.job([(half, rows, columns)] * 2, body, take)

    def plain(self, bit):
        def body(meta, near, got, outs):
            outs[0][...] = add(near[0][...], got[0][...])

        def take(parts):
            self.near, self.got = parts, [flip(parts[0], "dp", bit)]

        return self.job([self.near[0].shape], body, take)

    def whole(self):
        return self.plain(4)

    def back(self, order):
        bit = 8
        while bit < lax.axis_size("dp"):
            order(1, self.plain(bit))
            bit *= 2
        return self.plain(2)

    def last(self):
        half, rows, columns = self.near[0].shape

        def body(meta, near, got, outs):
            upper = meta[2] >> 1
            outs[0][pl.ds(upper * half, half)] = near[0][...]
            outs[0][pl.ds((1 - upper) * half, half)] = got[0][...]

        def take(parts):
            self.mine = parts[0]
            self.by_x = flip(self.mine, "dp", 1)

        return self.job([(2 * half, rows, columns)], body, take)

    def pieces(self, order):
        by_x = after(self.by_x, *order.last)
        return self.mine, by_x, flip(self.mine, "role"), flip(by_x, "role")


def step(value, route):
    if route == "head":
        return flip(value, "head")
    return flip(value, "dp", 1)


class SmallSum:
    def __init__(self, value):
        count = lax.axis_size("dp")
        self.steps = [("role", 1), ("head", 1)] + [("dp", 1 << at) for at in range(count.bit_length() - 1)]
        self.value, self.got = value, flip(value, *self.steps.pop(0))

    def step(self):
        def body(meta, ins, outs):
            outs[0][...] = ins[0][...] + ins[1][...]

        def take(parts):
            self.value = parts[0]
            self.got = flip(self.value, *self.steps.pop(0)) if self.steps else None

        return [self.value, self.got], [jax.ShapeDtypeStruct(self.value.shape, F32)], body, take

    def total(self):
        while self.got is not None:
            self.value = self.value + self.got
            self.got = flip(self.value, *self.steps.pop(0)) if self.steps else None
        return self.value


def shards(
    layer_in,
    lengths,
    cotangent,
    targets,
    self_qkv,
    self_out,
    cross_q,
    cross_kv,
    cross_out,
    ffn_in,
    ffn_out,
    norm_gain,
    norm_bias,
    halt_weight,
    halt_bias,
):
    role, head, place = (lax.axis_index(name) for name in ("role", "head", "dp"))
    target_side = role == 1
    me = 2 * (place & 1) + role
    me_z = (place & 2) + role
    meta = jnp.stack([role, me, me_z, layer_in.shape[1] // 2]).astype(jnp.int32)

    rows = layer_in[0]
    row_len, width = rows.shape
    here = row_len // 2
    full = here + HALO

    other_rows = flip(rows, "role")
    lens = lax.dynamic_index_in_dim(lengths[0], head, 0, keepdims=False)
    other_lens = flip(lens, "role")
    segs = jnp.where(target_side, jnp.stack([other_lens, lens]), jnp.stack([lens, other_lens]))
    segs = jnp.pad(segs, ((0, 0), (0, 2)))

    self_own, cross_own = self_qkv.transpose(1, 0, 2), cross_kv.transpose(1, 0, 2)
    piece_shape = Put(4, width // PIECES, HALF, dtype=BF16)
    (self_piece,) = call(
        cut_self, ([meta], [Far(self_own), Far(self_out)]), [piece_shape], [pltpu.SemaphoreType.DMA((2,))], 1
    )
    cross_piece, in_piece, out_own_piece = call(
        cut_rest,
        ([meta], [Far(cross_q), Far(cross_own), Far(cross_out), Far(ffn_in), Far(ffn_out)]),
        [piece_shape, piece_shape, Put(HALF, width, dtype=BF16)],
        [pltpu.SemaphoreType.DMA((5,))],
        1,
    )
    self_first, cross_first, in_first, out_first = (
        flip(piece, "head") for piece in (self_piece, cross_piece, in_piece, out_own_piece)
    )

    weight_sems = pltpu.SemaphoreType.DMA((6,))
    one_sem = pltpu.SemaphoreType.DMA
    grad_sems = pltpu.SemaphoreType.DMA((1,))
    states_held = pltpu.VMEM((full, width), BF16)
    memory_held = pltpu.VMEM((row_len, width), BF16)
    out_held = pltpu.VMEM((width, HALF), BF16)
    mix_grads = pltpu.VMEM((2, full + WINDOW, HALF), BF16)

    def heads(*dims):
        return Put(*dims, full + WINDOW, HALF, dtype=BF16)

    def matrices(count):
        return pltpu.VMEM((count, width, HALF), BF16)

    pair_shape = (2, 2, row_len + WINDOW, HALF)

    both_rows = Any(rows), Any(other_rows)

    self_plan, cross_plan = pl.pallas_call(
        group_sentences,
        out_shape=[jax.ShapeDtypeStruct((9, 40), jnp.int32)] * 2,
        in_specs=[SMEM] * 2,
        out_specs=[SMEM] * 2,
        name="group_sentences",
        cost_estimate=pl.CostEstimate(flops=int(HEAVY * WEIGHT), bytes_accessed=0, transcendentals=0),
    )(after(meta, cross_piece, self_first), segs)
    self_second = flip(self_first, "dp", 1)
    cross_second = flip(cross_first, "dp", 2)
    in_second = flip(in_first, "dp", 1)
    self_second = after(self_second, self_plan)
    self_weights = [self_first, self_second, flip(self_first, "role"), flip(self_second, "role")]
    self_pieces = [Any(piece) for piece in self_weights]
    hidden, normed_one, qkv, self_mix = call(
        self_forward,
        (
            [after(meta, cross_first), self_plan],
            [*both_rows, norm_gain, norm_bias, Get(self_own), Far(self_out), *self_pieces],
        ),
        [near(here, width), Put(full, width, dtype=BF16), heads(2, 3), heads(2)],
        [states_held, matrices(4), out_held, weight_sems, one_sem],
        11,
    )

    cross_second = after(cross_second, normed_one)
    cross_weights = [cross_first, cross_second, flip(cross_first, "role"), flip(cross_second, "role")]
    cross_pieces = [Any(piece) for piece in cross_weights]
    out_first = after(out_first, normed_one)
    out_second = flip(out_first, "dp", 2)
    hidden_two, hidden_far, normed_two, cross_mix, queries, pairs = call(
        cross_forward,
        (
            [meta, cross_plan],
            [
                *both_rows, Here(hidden), norm_gain, norm_bias, Get(cross_q), Get(cross_own), Far(cross_out),
                *cross_pieces,
            ],
        ),
        [Put(here, width), far(here, width), Put(here, width, dtype=BF16), heads(2), heads(2), far(*pair_shape, dtype=BF16)],
        [
            pltpu.VMEM(pair_shape, BF16), memory_held, matrices(4), out_held, weight_sems, one_sem,
            pltpu.SemaphoreType.DMA((2,)),
        ],
        12,
    )

    in_second, out_second = after((in_second, out_second), normed_two)
    in_weights = in_first, in_second, flip(in_first, "role"), flip(in_second, "role")
    out_weights = out_first, out_second, flip(out_first, "role"), flip(out_second, "role")
    ffn_parts = far(2, 2, 8, width // PIECES, HALF, dtype=BF16)
    grad_parts = far(2, 2, 4, width // PIECES, HALF, dtype=BF16)
    result_low, two_grad, two_far, ffn_small, keep_ffn, send_ffn = call(
        feed_forward,
        (
            [meta],
            [
                Get(hidden_two), Far(cotangent), targets.astype(F32).reshape(2, here // WINDOW, WINDOW),
                norm_gain, norm_bias, halt_weight[None], halt_bias, Far(ffn_in), *map(Far, in_weights),
                Far(ffn_out), *map(Far, out_weights),
            ],
        ),
        [Put(here, width, dtype=BF16), near(here, width), far(here, width), shape(4, width), ffn_parts, ffn_parts],
        [
            matrices(8),
            pltpu.VMEM((8, HALF, width), BF16),
            pltpu.VMEM((here, width), BF16),
            pltpu.VMEM((8, here, HALF), BF16),
            pltpu.VMEM((8, here, HALF), F32),
            pltpu.VMEM((here, width), F32),
            pltpu.VMEM((here, width), BF16),
            pltpu.VMEM((here, width), BF16),
            matrices(16),
            weight_sems,
            weight_sems,
            pltpu.SemaphoreType.DMA((2,)),
            grad_sems,
        ],
        17,
    )

    mix_grads_shape = near(2, full + WINDOW, HALF, dtype=BF16)
    out_scratch = [matrices(2), weight_sems, grad_sems]
    cross_mix_grads, cross_out_part, queries = call(
        functools.partial(out_backward, place=2, ahead=1),
        ([meta], [Here(two_grad), Get(cross_mix, late=True), Far(cross_out), *cross_pieces, Far(queries)]),
        [mix_grads_shape, Put(2, width, HALF, dtype=BF16), near(2, full + WINDOW, HALF, dtype=BF16)],
        out_scratch,
        4,
    )

    def totals(kinds, pieces, out_shapes, *more):
        scratch = [pltpu.VMEM((each[0].shape[0], width, HALF), BF16) for each in pieces]
        results = pl.pallas_call(
            functools.partial(unpack, kinds),
            out_shape=out_shapes,
            in_specs=[SMEM] + [ANY] * (4 * len(kinds)) + [VMEM] * len(more),
            out_specs=[VMEM] * len(out_shapes),
            scratch_shapes=scratch + [pltpu.SemaphoreType.DMA((len(kinds),))],
            name="unpack_" + kinds[0],
            compiler_params=pltpu.CompilerParams(vmem_limit_bytes=room([*out_shapes, *scratch], 6)),
            cost_estimate=pl.CostEstimate(flops=1000, bytes_accessed=0, transcendentals=0),
        )(order.now(), *[piece for each in pieces for piece in each], *more)
        order.last = (results[0],)
        return results

    order = Order(meta)
    ffn_sum = Sum(keep_ffn, send_ffn, FFN_ROUTES)
    order(1, ffn_sum.begin())
    query_grad, pair_grads = call(
        cross_backward,
        ([order.now(), cross_plan], [Here(cross_mix_grads), Here(queries), Far(pairs)]),
        [near(2, full + WINDOW, HALF, dtype=BF16), near(*pair_shape, dtype=BF16)],
        [pltpu.VMEM(pair_shape, BF16), grad_sems],
        9,
    )
    one_grad, one_far, memory_part, cross_small, keep_cross, send_cross = call(
        cross_products,
        (
            [meta, cross_plan],
            [
                *both_rows, Get(hidden_far, late=True), Get(normed_two, late=True), Get(two_far, late=True), Here(query_grad), Here(pair_grads),
                Far(cross_out_part), Get(cross_q), Get(cross_own), *cross_pieces, norm_gain,
            ],
        ),
        [near(here, width), far(here, width), Put(row_len, width, dtype=BF16), shape(2, width), grad_parts, grad_parts],
        [
            memory_held,
            pltpu.VMEM((2, 2, width, HALF), F32),
            matrices(8),
            matrices(3),
            weight_sems,
            one_sem,
            grad_sems,
            grad_sems,
        ],
        8,
    )

    cross_sum = Sum(keep_cross, send_cross, CROSS_ROUTES)
    order(1, ffn_sum.second())
    self_mix_grads, self_out_part, qkv = call(
        functools.partial(out_backward, place=1, ahead=1),
        ([order.now()], [Here(one_grad), Get(self_mix, late=True), Far(self_out), *self_pieces, Far(qkv)]),
        [mix_grads_shape, Put(2, width, HALF, dtype=BF16), near(2, 3, full + WINDOW, HALF, dtype=BF16)],
        out_scratch,
        4,
    )
    order(1, cross_sum.begin())
    order(1, ffn_sum.halve())
    (qkv_grads,) = call(
        self_backward,
        ([order.now(), self_plan], [Here(self_mix_grads), Here(qkv)]),
        [near(2, 3, full + WINDOW, HALF, dtype=BF16)],
        [],
        9,
    )
    order(1, ffn_sum.whole(), cross_sum.second())
    keep_self, send_self, state_grad, swap, halo_grad, self_small = call(
        self_products,
        (
            [order.now()],
            [
                *both_rows, Get(normed_one, late=True), Here(qkv_grads), Far(self_out_part), Get(one_far, late=True), Get(self_own, late=True),
                *self_pieces, norm_gain, Far(result_low), Far(memory_part),
            ],
        ),
        [
            grad_parts,
            grad_parts,
            Put(here, width),
            Put(row_len, width, dtype=BF16),
            Put(HALO, width),
            shape(2, width),
        ],
        [matrices(8), states_held, matrices(3), grad_sems, weight_sems, one_sem, one_sem],
        11,
    )
    self_sum = Sum(keep_self, send_self, SELF_ROUTES)
    order.last = (keep_self,)
    order(HEAVY, cross_sum.halve(), ffn_sum.back(order))
    order(1, self_sum.begin(far_near=True))
    self_small = after(self_small, *order.last)
    small = SmallSum(
        jnp.concatenate(
            [
                self_small[0:1], cross_small[0:1], ffn_small[0:1],
                self_small[1:2], cross_small[1:2], ffn_small[1:2], ffn_small[2:4],
            ],
            axis=0,
        )
    )
    swapped = flip(after(swap, *order.last), "role")
    order(HEAVY, cross_sum.whole())
    order(1, self_sum.second(), small.step())
    order(1, self_sum.halve(), cross_sum.back(order), ffn_sum.last(), small.step())
    order(1, self_sum.whole(), small.step())
    layer_out, input_grads = call(
        finish_rows,
        (
            [order.now()],
            [Any(each) for each in (rows, result_low, state_grad, halo_grad, memory_part, swapped)],
        ),
        [Put(row_len, width, dtype=BF16), Put(row_len, width)],
        [pltpu.VMEM((2, row_len, width), BF16), pltpu.VMEM((HALO, width), F32), one_sem],
        HEAVY,
    )
    order.last = (layer_out,)
    order(1, cross_sum.last(), small.step())
    order(1, self_sum.back(order))
    order.last = (*order.last, cross_sum.by_x)
    order(1, self_sum.last(), small.step())
    ffn_in_grad, ffn_out_grad, cross_q_grad, cross_kv_grad, cross_out_grad, *small = totals(
        ("ffn", "cross"),
        (ffn_sum.pieces(order), cross_sum.pieces(order)),
        (
            shape(width, 4 * HALF), shape(4 * HALF, width),
            shape(width, HALF), shape(width, 2, HALF), shape(HALF, width),
            shape(3, width), shape(3, width), shape(1, width), shape(1, 1),
        ),
        small.total(),
    )
    self_qkv_grad, self_out_grad = totals(
        ("self",), (self_sum.pieces(order),), (shape(3, width, HALF), shape(HALF, width))
    )
    return (
        layer_out[None],
        input_grads[None],
        self_qkv_grad.transpose(1, 0, 2),
        self_out_grad,
        cross_q_grad,
        cross_kv_grad,
        cross_out_grad,
        ffn_in_grad,
        ffn_out_grad,
        small[0],
        small[1],
        small[2][0],
        small[3][0],
    )


def solution(mesh):
    placed = (
        P("role", ("dp", "head"), None),
        P("role", "dp", None),
        P(("dp", "head"), None),
        P(("dp", "head")),
        P(None, None, "head"),
        P("head", None),
        P(None, "head"),
        P(None, None, "head"),
        P("head", None),
        P(None, "head"),
        P("head", None),
        P(),
        P(),
        P(),
        P(),
    )
    return jax.shard_map(
        shards,
        mesh=mesh,
        in_specs=placed,
        out_specs=(
            P("role", ("dp", "head"), None),
            P("role", ("dp", "head"), None),
            P(None, None, "head"),
            P("head", None),
            P(None, "head"),
            P(None, None, "head"),
            P("head", None),
            P(None, "head"),
            P("head", None),
            P(),
            P(),
            P(),
            P(),
        ),
        check_vma=False,
    )
```

```python
import functools
import math

import jax
import jax.numpy as jnp
from jax import lax
from jax.experimental import pallas as pl
from jax.experimental.pallas import tpu as pltpu
from jax.sharding import PartitionSpec as P

F32 = jnp.float32
BF16 = jnp.bfloat16

HEAD_DIM = 64
HALF = 256
HEADS = HALF // HEAD_DIM
HALO = 128
GROUPS = 3
WINDOW = 128
MASKED = -1e30
SPARE = 8
WEIGHT = 1.2e9
ANY = pl.BlockSpec(memory_space=pl.ANY)
VMEM = pl.BlockSpec(memory_space=pltpu.VMEM)
SMEM = pl.BlockSpec(memory_space=pltpu.SMEM)
ARRIVALS = (0, 2, 1, 3)
FFN_ROUTES = [("head", "x"), ("x", "head")]
CROSS_ROUTES = [("x", "head")]
SELF_ROUTES = [("head", "x"), ("x", "head")]
HEAVY = 24
PIECES = 4


def dot(a, b):
    return jnp.dot(a, b, preferred_element_type=F32)


def dot_nt(a, b):
    return lax.dot_general(a, b, (((1,), (1,)), ((), ())), preferred_element_type=F32)


def dot_tn(a, b):
    return lax.dot_general(a, b, (((0,), (0,)), ((), ())), preferred_element_type=F32)


def norm_parts(values):
    center = values - jnp.mean(values, axis=-1, keepdims=True)
    spread = jnp.mean(center * center, axis=-1, keepdims=True)
    scale = lax.rsqrt(spread + 1e-05)
    return center * scale, scale


def norm_back(grad, hat, scale, gain):
    grad_hat = grad * gain
    first = jnp.mean(grad_hat, axis=-1, keepdims=True)
    second = jnp.mean(grad_hat * hat, axis=-1, keepdims=True)
    return scale * (grad_hat - first - hat * second)


class Load:
    def __init__(self, source, target, sem):
        self.target, self.copy = target, pltpu.make_async_copy(source, target, sem)
        self.gone = self.come = False

    def go(self):
        if not self.gone:
            self.copy.start()
        self.gone = True

    def __call__(self):
        self.go()
        if not self.come:
            self.copy.wait()
        self.come = True
        return self.target


class Store:
    def __init__(self, ref, target, sem):
        self.ref, self.target, self.sem, self.copies = ref, target, sem, []

    def send(self, at=None):
        if at is None:
            copy = pltpu.make_async_copy(self.ref, self.target, self.sem)
        else:
            at = pl.ds(at.start, at.stop - at.start)
            copy = pltpu.make_async_copy(self.ref.at[at], self.target.at[at], self.sem)
        copy.start()
        self.copies.append(copy)

    def end(self):
        if not self.copies:
            self.send()
        wait(self.copies)


def start(copies):
    for copy in copies:
        copy.start()
    return copies


def wait(copies):
    for copy in copies:
        copy.wait()


def cut_self(meta, matrices, out, piece, sem):
    wait(start(row_copies(meta[1], matrices, out, piece.ref, 0, sem)))


def row_copies(which, matrices, out, piece, first, sem):
    count, rows = matrices.shape[0], piece.shape[1]
    low = pl.multiple_of(which * rows, rows)
    out_low = pl.multiple_of((which & 1) * rows, rows)
    out_left = pl.multiple_of((which >> 1) * HALF, HALF)
    return [
        pltpu.make_async_copy(matrices.at[:, pl.ds(low, rows)], piece.at[pl.ds(first, count)], sem.at[0]),
        pltpu.make_async_copy(out.at[pl.ds(out_low, rows), pl.ds(out_left, HALF)], piece.at[3], sem.at[1]),
    ]


def cut_rest(meta, q, pair, out, ffn_in, ffn_out, cross_piece, in_piece, out_piece, sem):
    cross_piece, in_piece, out_piece = cross_piece.ref, in_piece.ref, out_piece.ref
    rows = cross_piece.shape[1]
    low = pl.multiple_of(meta[2] * rows, rows)
    copies = row_copies(meta[2], pair, out, cross_piece, 1, sem)
    copies.append(pltpu.make_async_copy(q.at[pl.ds(low, rows)], cross_piece.at[0], sem.at[2]))
    low = pl.multiple_of(meta[1] * rows, rows)
    for j in range(4):
        source = ffn_in.at[pl.ds(low, rows), pl.ds(j * HALF, HALF)]
        copies.append(pltpu.make_async_copy(source, in_piece.at[j], sem.at[3]))
    low = pl.multiple_of(meta[2] * HALF, HALF)
    copies.append(pltpu.make_async_copy(ffn_out.at[pl.ds(low, HALF)], out_piece, sem.at[4]))
    wait(start(copies))


def start_out_own(out, held, sem):
    return start(
        [
            pltpu.make_async_copy(out.at[:, pl.ds(c * HALF, HALF)], held.at[pl.ds(c * HALF, HALF)], sem.at[c])
            for c in range(2)
        ]
    )


def start_other(place, arrived, first, held, sem):
    rows, count = arrived[0].shape[1], held.shape[0]
    copies = []
    for at, (ref, flip) in enumerate(zip(arrived, ARRIVALS)):
        low = pl.multiple_of((place ^ flip) * rows, rows)
        source = ref.at[pl.ds(first, count)]
        copies.append(pltpu.make_async_copy(source, held.at[:, pl.ds(low, rows)], sem.at[2 + at]))
    return start(copies)


def start_in(meta, own, arrived, held, sem):
    copies = [
        pltpu.make_async_copy(own.at[:, pl.ds(j * HALF, HALF)], held.at[j], sem.at[0]) for j in range(4)
    ]
    return start(copies) + start_other(meta[1], arrived, 0, held.at[pl.ds(4, 4)], sem)


def start_out(meta, own, arrived, held, sem):
    copies = [
        pltpu.make_async_copy(own.at[pl.ds(j * HALF, HALF)], held.at[j], sem.at[0]) for j in range(4)
    ]
    for at, (ref, flip) in enumerate(zip(arrived, ARRIVALS)):
        copies.append(pltpu.make_async_copy(ref, held.at[4 + (meta[2] ^ flip)], sem.at[2 + at]))
    return start(copies)


def put_half(meta, grads, keep, send, sem, half, x_first=False):
    _, _, count, rows, _ = keep.shape
    copies = []
    for rel in range(PIECES):
        first = pl.multiple_of((rel ^ meta[1]) * rows, rows)
        source = grads.at[pl.ds(half * count, count), pl.ds(first, rows)]
        at = (rel >> 1, half) if x_first else (half, rel >> 1)
        target = (send if rel & 1 else keep).at[at]
        copies.append(pltpu.make_async_copy(source, target, sem.at[0]))
    return start(copies)


def put_grads(meta, grads, keep, send, sem, x_first=False):
    return [copy for half in range(2) for copy in put_half(meta, grads, keep, send, sem, half, x_first)]


def group_sentences(meta, segs, self_plan, cross_plan):
    first_row = meta[0] * meta[3]
    last_row = first_row + meta[3]
    shift = HALO - first_row
    zero = jnp.int32(0)
    for plan, cross in ((self_plan, False), (cross_plan, True)):

        def step(c, carry, plan=plan, cross=cross):
            t0, s0, done, count, low, high = carry
            t1, s1 = t0 + segs[1, c], s0 + segs[0, c]
            t2, s2 = t1 + segs[1, c + 1], s1 + segs[0, c + 1]
            t3, s3 = t2 + segs[1, c + 2], s2 + segs[0, c + 2]
            target_end, source_end = window_of(t0) + WINDOW, window_of(s0) + WINDOW
            two = (t2 <= target_end) & (t1 < last_row)
            three = two & (t3 <= target_end) & (t2 < last_row)
            if cross:
                two = two & (s2 <= source_end)
                three = three & (s3 <= source_end) & two
            t2, s2 = jnp.where(two, t2, t1), jnp.where(two, s2, s1)
            t3, s3 = jnp.where(three, t3, t2), jnp.where(three, s3, s2)
            mine = (t1 > first_row) & (t0 < last_row)
            here = (c >= done) & mine
            for at, bound in enumerate((t0, t1, t2, t3)):
                plan[at, count] = bound + shift
            for at, bound in enumerate((s0, s1, s2, s3)):
                plan[4 + at, count] = bound
            size = 1 + two.astype(jnp.int32) + three.astype(jnp.int32)
            low = jnp.where(mine, jnp.minimum(low, s0), low)
            high = jnp.where(mine, jnp.maximum(high, s1), high)
            return t1, s1, jnp.where(here, c + size, done), count + here.astype(jnp.int32), low, high

        start = (zero, zero, zero, zero, jnp.int32(1 << 20), zero)
        _, _, _, count, low, high = lax.fori_loop(0, segs.shape[1] - 2, step, start)
        for g in range(GROUPS):
            for at in range(8):
                plan[at, count + g] = 0
        plan[8, 0] = count
        plan[8, 1] = low
        plan[8, 2] = high


def each_group(plan, windows, compute, store):
    def work(first, count):
        bounds = [
            ([plan[at, first + g] for at in range(4)], [plan[4 + at, first + g] for at in range(4)])
            for g in range(count)
        ]
        operands = [windows(*each) for each in bounds]
        results = iter(compute([window for each in operands for window in each]))
        for each, windows_of_it in zip(bounds, operands):
            store(*each, [next(results) for _ in windows_of_it])

    def some(i, _):
        work(i * GROUPS, GROUPS)
        return 0

    def one(i, _):
        work(i, 1)
        return 0

    count = plan[8, 0]
    together = count // GROUPS
    lax.fori_loop(0, together, some, 0)
    lax.fori_loop(together * GROUPS, count, one, 0)


def window_of(start):
    return pl.multiple_of((start // 16) * 16, 16)


def spread_lanes(block):
    lanes = lax.broadcasted_iota(jnp.int32, (1, HALF), 1) // HEAD_DIM
    return jnp.concatenate(
        [jnp.where(lanes == h, block, jnp.zeros_like(block)) for h in range(HEADS)], axis=0
    )


def spread_rows(block):
    none = jnp.zeros((HEAD_DIM, block.shape[1]), block.dtype)
    return jnp.concatenate(
        [
            jnp.concatenate(
                [block[g * HEAD_DIM : (g + 1) * HEAD_DIM] if g == h else none for g in range(HEADS)],
                axis=0,
            )
            for h in range(HEADS)
        ],
        axis=1,
    )


def by_head(rows, spread):
    columns = spread.shape[1] // HEADS
    return jnp.concatenate(
        [
            dot(rows[h * HEAD_DIM : (h + 1) * HEAD_DIM], spread[:, h * columns : (h + 1) * columns])
            for h in range(HEADS)
        ],
        axis=0,
    )


def window_mask(q_first, q_bounds, k_first, k_bounds, q_low, q_high, causal):
    q = lax.broadcasted_iota(jnp.int32, (1, WINDOW), 1) + q_first
    k = lax.broadcasted_iota(jnp.int32, (WINDOW, WINDOW), 0) + k_first
    q_id = sum((q >= bound).astype(jnp.int32) for bound in q_bounds)
    k_id = sum((k >= bound).astype(jnp.int32) for bound in k_bounds)
    allowed = k_id == q_id
    if causal:
        allowed = allowed & (k <= q)
    valid = (q >= jnp.maximum(q_bounds[0], q_low)) & (q < jnp.minimum(q_bounds[3], q_high))
    return jnp.concatenate([allowed] * HEADS, axis=1), jnp.concatenate([valid] * HEADS, axis=1)


def window_weights(scores, masks):
    scores = [jnp.where(allowed, each, MASKED) for each, (allowed, _) in zip(scores, masks)]
    weights = [jnp.exp(each - jnp.max(each, axis=0, keepdims=True)) for each in scores]
    inverses = [
        jnp.where(valid, 1.0 / jnp.sum(each, axis=0, keepdims=True), 0.0)
        for each, (_, valid) in zip(weights, masks)
    ]
    return [each * inverse for each, inverse in zip(weights, inverses)]


def attend_windows(windows):
    qs, ks, vs, masks = zip(*windows)
    q_rows = [spread_rows((q * jnp.asarray(HEAD_DIM**-0.5, BF16)).T) for q in qs]
    scores = [dot(k, q) for k, q in zip(ks, q_rows)]
    probabilities = [each.astype(BF16) for each in window_weights(scores, masks)]
    mixes = [by_head(v.T, each) for v, each in zip(vs, probabilities)]
    return [mix.astype(BF16).T for mix in mixes]


def attend_windows_back(windows):
    qs, ks, vs, grads, masks = zip(*windows)
    scale = HEAD_DIM**-0.5
    qs = [q * jnp.asarray(scale, BF16) for q in qs]
    scores = [dot(k, spread_rows(q.T)) for k, q in zip(ks, qs)]
    prob_grads = [dot(v, spread_rows(grad.T)) for v, grad in zip(vs, grads)]
    probabilities = window_weights(scores, masks)
    inners = [
        jnp.sum(each * grad, axis=0, keepdims=True) for each, grad in zip(probabilities, prob_grads)
    ]
    score_grads = [
        (each * (grad - inner)).astype(BF16)
        for each, grad, inner in zip(probabilities, prob_grads, inners)
    ]
    v_grads = [
        dot(each.astype(BF16), spread_lanes(grad)) for each, grad in zip(probabilities, grads)
    ]
    q_grads = [by_head(k.T, each) for k, each in zip(ks, score_grads)]
    k_grads = [dot(each, spread_lanes(q)) for each, q in zip(score_grads, qs)]
    q_grads = [(each * scale).astype(BF16).T for each in q_grads]
    return [(q, k.astype(BF16), v.astype(BF16)) for q, k, v in zip(q_grads, k_grads, v_grads)]


def out_product(mixes, outs):
    left = sum(dot(mix, out[0:HALF]) for mix, out in zip(mixes, outs))
    right = sum(dot(mix, out[HALF:]) for mix, out in zip(mixes, outs))
    return jnp.concatenate([left, right], axis=1)


def out_mix_grads(grad_low, outs, mix_grads, first):
    rows = grad_low.shape[0]
    for half in range(2):
        for lo in range(0, rows, HALF):
            block = grad_low[lo : lo + HALF]
            mix_grad = dot_nt(block[:, :HALF], outs[half, 0:HALF]) + dot_nt(block[:, HALF:], outs[half, HALF:])
            mix_grads[half, first + lo : first + lo + HALF] = mix_grad.astype(BF16)


def out_weight_grads(grad_low, mixes, grads):
    for half, mix in enumerate(mixes):
        grads[half, 0:HALF] = dot_tn(mix, grad_low[:, :HALF]).astype(BF16)
        grads[half, HALF:] = dot_tn(mix, grad_low[:, HALF:]).astype(BF16)


def copy_by_role(meta, pairs_zero, pairs_one, sem):
    @pl.when(meta[0] == 0)
    def _():
        for source, target in pairs_zero:
            pltpu.make_async_copy(source, target, sem).start()

    @pl.when(meta[0] == 1)
    def _():
        for source, target in pairs_one:
            pltpu.make_async_copy(source, target, sem).start()


def wait_by_role(meta, pairs_zero, pairs_one, sem):
    @pl.when(meta[0] == 0)
    def _():
        for source, target in pairs_zero:
            pltpu.make_async_copy(source, target, sem).wait()

    @pl.when(meta[0] == 1)
    def _():
        for source, target in pairs_one:
            pltpu.make_async_copy(source, target, sem).wait()


def states_copies(rows_ref, other_ref, held, here):
    zero = [(other_ref.at[pl.ds(0, here)], held.at[pl.ds(HALO, here)])]
    one = [(rows_ref.at[pl.ds(here - HALO, here + HALO)], held.at[pl.ds(0, here + HALO)])]
    return zero, one


def self_attention(meta, segs, plan, here, qkvs, mixes):
    full = here + HALO
    for mix in mixes:
        mix[...] = jnp.zeros(mix.shape, BF16)

    def group(bounds, _):
        first = window_of(bounds[0])
        mask = window_mask(first, bounds, first, bounds, HALO, full, True)
        at = pl.ds(first, WINDOW)
        return [(qkv[0, at], qkv[1, at], qkv[2, at], mask) for qkv in qkvs]

    def store(bounds, _, result):
        at = pl.ds(window_of(bounds[0]), WINDOW)
        for mix, each in zip(mixes, result):
            mix[at] += each

    together = 2 * GROUPS // len(qkvs)
    each_group(meta, segs, plan, here, False, together, group, attend_windows, store)


def self_project(normed, held, qkv):
    full = normed.shape[0]
    qkv[:, full:] = jnp.zeros((3, WINDOW, HALF), BF16)
    for c in range(3):
        qkv[c, 0:full] = dot(normed[...], held[c]).astype(BF16)


def self_forward(
    meta, plan, rows_ref, other_ref, gain, bias, own, own_out, w1, w2, w3, w4,
    hidden, normed, qkv, mix, states, held, outs, sem_w, sem_x,
):
    full = states.shape[0]
    here = full - HALO
    state_copies = states_copies(rows_ref, other_ref, states, here)
    copy_by_role(meta, *state_copies, sem_x)
    weights = start_other(meta[1], (w1, w2, w3, w4), 0, held, sem_w)
    weights += start_out_own(own_out, outs, sem_w)
    mix.ref[...] = jnp.zeros(mix.ref.shape, BF16)
    wait_by_role(meta, *state_copies, sem_x)

    @pl.when(meta[0] == 0)
    def _():
        states[0:HALO] = jnp.zeros((HALO, states.shape[1]), BF16)

    for lo in range(0, full, HALO):
        hat, _ = norm_parts(states[lo : lo + HALO].astype(F32))
        normed.ref[lo : lo + HALO] = (hat * gain[0:1] + bias[0:1]).astype(BF16)
    normed.send()
    own = own()
    wait(weights)
    qkv.ref[:, :, full:] = jnp.zeros((2, 3, WINDOW, HALF), BF16)
    for half, matrices in enumerate((own, held)):
        for c in range(3):
            qkv.ref[half, c, 0:full] = dot(normed.ref[...], matrices[c]).astype(BF16)
    qkv.send()

    def group(bounds, _):
        first = window_of(bounds[0])
        mask = window_mask(first, bounds, first, bounds, HALO, full, True)
        at = pl.ds(first, WINDOW)
        return [(qkv.ref[half, 0, at], qkv.ref[half, 1, at], qkv.ref[half, 2, at], mask) for half in range(2)]

    def store(bounds, _, result):
        at = pl.ds(window_of(bounds[0]), WINDOW)
        for half in range(2):
            mix.ref[half, at] += result[half]

    each_group(plan, group, attend_windows, store)
    mix.send()
    for lo in range(HALO, full, HALF):
        at = slice(lo, lo + HALF)
        hidden[lo - HALO : lo - HALO + HALF] = states[at].astype(F32) + out_product(
            [mix.ref[0, at], mix.ref[1, at]], [outs, held[3]]
        )


def blocks_do(low, high, pairs, target, sem, act):
    def one(block, _):
        at = pl.ds(pl.multiple_of(block * HALF, HALF), HALF)
        act(pltpu.make_async_copy(pairs.at[:, :, at], target.at[:, :, at], sem))
        return 0

    lax.fori_loop(low // HALF, (high + HALF - 1) // HALF, one, 0)


def zero_after(high, pairs):
    end = pl.multiple_of(((high + HALF - 1) // HALF) * HALF, HALF)
    pairs[:, :, pl.ds(end, WINDOW)] = jnp.zeros((2, 2, WINDOW, HALF), BF16)


def memory_copies(rows_ref, other_ref, held):
    return [(rows_ref, held)], [(other_ref, held)]


def cross_forward(
    meta, plan, rows_ref, other_ref, hidden, gain, bias, own_q, own_pair, own_out, w1, w2, w3, w4,
    hidden_two, hidden_far, normed, mix, queries, pairs_far, pairs, memory, held, outs, sem_w, sem_x, sem_h,
):
    here = hidden_two.ref.shape[0]
    hidden_copy = pltpu.make_async_copy(hidden, hidden_far, sem_h.at[0])
    hidden_copy.start()
    full = here + HALO
    copies = memory_copies(rows_ref, other_ref, memory)
    copy_by_role(meta, *copies, sem_x)
    weights = start_other(meta[2], (w1, w2, w3, w4), 0, held, sem_w)
    weights += start_out_own(own_out, outs, sem_w)
    queries.ref[:, 0:HALO] = jnp.zeros((2, HALO, HALF), BF16)
    queries.ref[:, full:] = jnp.zeros((2, WINDOW, HALF), BF16)
    mix.ref[...] = jnp.zeros(mix.ref.shape, BF16)
    low, high = plan[8, 1], plan[8, 2]
    zero_after(high, pairs)
    for lo in range(0, here, HALF):
        at = slice(lo, lo + HALF)
        hat, _ = norm_parts(hidden[at])
        normed.ref[at] = (hat * gain[1:2] + bias[1:2]).astype(BF16)
    normed.send()
    own_q, own_pair = own_q(), own_pair()
    wait(weights)
    for half, matrix in enumerate((own_q, held.at[0])):
        queries.ref[half, HALO:full] = dot(normed.ref[...], matrix[...]).astype(BF16)
    queries.send()
    wait_by_role(meta, *copies, sem_x)

    def project(block, _):
        at = pl.ds(pl.multiple_of(block * HALF, HALF), HALF)
        for c in range(2):
            pairs[0, c, at] = dot(memory[at], own_pair[c]).astype(BF16)
            pairs[1, c, at] = dot(memory[at], held[1 + c]).astype(BF16)
        return 0

    lax.fori_loop(low // HALF, (high + HALF - 1) // HALF, project, 0)
    blocks_do(low, high, pairs, pairs_far, sem_h.at[1], lambda copy: copy.start())

    def group(bounds, source_bounds):
        first = window_of(bounds[0])
        source_first = window_of(source_bounds[0])
        mask = window_mask(first, bounds, source_first, source_bounds, HALO, full, False)
        at = pl.ds(first, WINDOW)
        source_at = pl.ds(source_first, WINDOW)
        return [
            (queries.ref[half, at], pairs[half, 0, source_at], pairs[half, 1, source_at], mask)
            for half in range(2)
        ]

    def store(bounds, _, result):
        at = pl.ds(window_of(bounds[0]), WINDOW)
        for half in range(2):
            mix.ref[half, at] += result[half]

    each_group(plan, group, attend_windows, store)
    mix.send()
    for lo in range(0, here, HALF):
        at = slice(lo, lo + HALF)
        mix_at = slice(HALO + lo, HALO + lo + HALF)
        hidden_two.ref[at] = hidden[at] + out_product([mix.ref[0, mix_at], mix.ref[1, mix_at]], [outs, held[3]])
        hidden_two.send(at)
    hidden_copy.wait()
    blocks_do(low, high, pairs, pairs_far, sem_h.at[1], lambda copy: copy.wait())


def gelu_both(inner):
    rate, cubic = 0.7978845608028654, 0.7978845608028654 * 0.044715
    square = inner * inner
    bent = jnp.tanh(inner * (rate + cubic * square))
    half = 0.5 + 0.5 * bent
    slope = half + inner * (1.0 - bent * bent) * (0.5 * rate + 1.5 * cubic * square)
    return inner * half, slope


def column(values, role, at):
    lanes = lax.broadcasted_iota(jnp.int32, (WINDOW, WINDOW), 1)
    own = lax.broadcasted_iota(jnp.int32, (WINDOW, WINDOW), 0) == lanes
    blocks = []
    for block in range(at.start // WINDOW, at.stop // WINDOW):
        row = values[role, block : block + 1]
        blocks.append(jnp.sum(jnp.where(own, row, 0.0), axis=1, keepdims=True))
    return jnp.concatenate(blocks, axis=0)


def feed_forward(
    meta, hidden_two, cotangent, targets, gain, bias, halt_weight, halt_bias,
    own_in, i1, i2, i3, i4, own_out, o1, o2, o3, o4,
    result_low, hidden_grad, hidden_far, small, keep, send,
    held_in, held_out, normed, active, slopes, total, out_low, cot, grads, sem_w, sem_o, sem_x, sem_g,
):
    here, width = total.shape
    first = pl.multiple_of(meta[0] * here, here)
    cot_copy = pltpu.make_async_copy(cotangent.at[pl.ds(first, here)], cot, sem_x.at[0])
    weights = start_in(meta, own_in, (i1, i2, i3, i4), held_in, sem_w)
    weights += start_out(meta, own_out, (o1, o2, o3, o4), held_out, sem_o)
    cot_copy.start()
    hidden_two = hidden_two()
    blocks = [slice(lo, lo + HALF) for lo in range(0, here, HALF)]
    for at in blocks:
        hat, _ = norm_parts(hidden_two[at])
        normed[at] = (hat * gain[2:3] + bias[2:3]).astype(BF16)
        total[at] = hidden_two[at]
    wait(weights)

    def forward(pair, _):
        items = [(at, 8 * pair + u) for at in blocks for u in range(8)]
        inner = dot(normed[items[0][0]], held_in[items[0][1]])
        products = []
        for i, (at, j) in enumerate(items):
            coming = dot(normed[items[i + 1][0]], held_in[items[i + 1][1]]) if i + 1 < len(items) else None
            value, slope = gelu_both(inner)
            value = value.astype(BF16)
            active[j, at] = value
            slopes[j, at] = slope
            products.append(dot(value, held_out[j]))
            if len(products) == 8:
                total[at] += sum(products)
                products = []
            inner = coming
        return 0

    lax.fori_loop(0, 1, forward, 0)
    cot_copy.wait()
    weight_sum = jnp.zeros((1, width), F32)
    bias_sum = jnp.zeros((1, 1), F32)
    for at in blocks:
        result = total[at]
        result_low.ref[at] = result.astype(BF16)
        logits = jnp.sum(result * halt_weight[...], axis=-1, keepdims=True) + halt_bias[0]
        halt_grad = 1.0 / (1.0 + jnp.exp(-logits)) - column(targets, meta[0], at)
        out_grad = cot[at].astype(F32) + halt_grad * halt_weight[...]
        out_low[at] = out_grad.astype(BF16)
        hidden_grad[at] = out_grad
        total[at] = jnp.zeros((HALF, width), F32)
        weight_sum += jnp.sum(halt_grad * result, axis=0, keepdims=True)
        bias_sum += jnp.sum(halt_grad, axis=0, keepdims=True)
    result_low.send()

    def backward(i, _):
        js = [4 * i + u for u in range(4)]
        value_grads = [[dot_nt(out_low[at], held_out[j]) for at in blocks] for j in js]
        inner_grads = [
            [(grad * slopes[j, at]).astype(BF16) for grad, at in zip(grads_of_it, blocks)]
            for j, grads_of_it in zip(js, value_grads)
        ]
        for b, at in enumerate(blocks):
            total[at] += sum(dot_nt(each[b], held_in[j]) for j, each in zip(js, inner_grads))
        for j, each in zip(js, inner_grads):
            half, block = j // 4, j % 4
            grads[8 * half + block] = dot_tn(normed[...], jnp.concatenate(each, axis=0)).astype(BF16)
            out_grad = dot_tn(active[j], out_low[...]).astype(BF16)
            grads[8 * half + 4 + block, 0:HALF] = out_grad[:, :HALF]
            grads[8 * half + 4 + block, HALF:] = out_grad[:, HALF:]
        return 0

    lax.fori_loop(0, 4 // 4, backward, 0)
    copies = put_half(meta, grads, keep, send, sem_g, 0)
    lax.fori_loop(4 // 4, 8 // 4, backward, 0)
    copies += put_half(meta, grads, keep, send, sem_g, 1)
    gain_sum = jnp.zeros_like(weight_sum)
    shift_sum = jnp.zeros_like(weight_sum)
    for at in blocks:
        hat, scale = norm_parts(hidden_two[at])
        grad = total[at]
        hidden_grad[at] += norm_back(grad, hat, scale, gain[2:3])
        gain_sum += jnp.sum(grad * hat, axis=0, keepdims=True)
        shift_sum += jnp.sum(grad, axis=0, keepdims=True)
    small[...] = jnp.concatenate(
        [gain_sum, shift_sum, weight_sum, jnp.broadcast_to(bias_sum, weight_sum.shape)], axis=0
    )
    copies += start([pltpu.make_async_copy(hidden_grad, hidden_far, sem_x.at[1])])
    wait(copies)


def out_backward(
    meta, upper_grad, mix, own_out, w1, w2, w3, w4, *rest, place, ahead
):
    sources, (mix_grads, out_part), rest = rest[:ahead], rest[ahead : ahead + 2], rest[ahead + 2 :]
    targets, (outs, sem_w, sem_h) = rest[:ahead], rest[ahead:]
    full = mix_grads.shape[1] - WINDOW
    weights = start_other(meta[place], (w1, w2, w3, w4), 3, outs.at[pl.ds(1, 1)], sem_w)
    weights += start_out_own(own_out, outs.at[0], sem_w)
    mix.go()
    brought = start(
        [pltpu.make_async_copy(*copy, sem_h.at[at]) for at, copy in enumerate(zip(sources, targets))]
    )
    mix_grads[:, 0:HALO] = jnp.zeros((2, HALO, HALF), BF16)
    mix_grads[:, full:] = jnp.zeros((2, WINDOW, HALF), BF16)
    grad_low = upper_grad[...].astype(BF16)
    wait(weights)
    out_mix_grads(grad_low, outs, mix_grads, HALO)
    mix = mix()
    out_weight_grads(grad_low, [mix[0, HALO:full], mix[1, HALO:full]], out_part.ref)
    wait(brought)


def cross_backward(meta, plan, mix_grads, queries, pairs_far, q_grad, pair_grads, pairs, sem_h):
    full = mix_grads.shape[1] - WINDOW
    here = full - HALO
    low, high = plan[8, 1], plan[8, 2]
    blocks_do(low, high, pairs_far, pairs, sem_h.at[0], lambda copy: copy.start())
    q_grad[...] = jnp.zeros(q_grad.shape, BF16)
    pair_grads[...] = jnp.zeros(pair_grads.shape, BF16)
    zero_after(high, pairs)
    blocks_do(low, high, pairs_far, pairs, sem_h.at[0], lambda copy: copy.wait())

    def group(bounds, source_bounds):
        first = window_of(bounds[0])
        source_first = window_of(source_bounds[0])
        mask = window_mask(first, bounds, source_first, source_bounds, HALO, full, False)
        at = pl.ds(first, WINDOW)
        source_at = pl.ds(source_first, WINDOW)
        return [
            (
                queries[half, at], pairs[half, 0, source_at], pairs[half, 1, source_at],
                mix_grads[half, at], mask,
            )
            for half in range(2)
        ]

    def store(bounds, source_bounds, result):
        at = pl.ds(window_of(bounds[0]), WINDOW)
        source_at = pl.ds(window_of(source_bounds[0]), WINDOW)
        for half, (dq, dk, dv) in enumerate(result):
            q_grad[half, at] += dq
            pair_grads[half, 0, source_at] += dk
            pair_grads[half, 1, source_at] += dv

    each_group(plan, group, attend_windows_back, store)


def cross_products(
    meta, plan, rows_ref, other_ref, hidden, normed, upper_grad, q_grad, pair_grads, out_part, own_q, own_pair,
    w1, w2, w3, w4, gain,
    lower_grad, lower_far, memory_grad, small, keep, send, memory, pair_sums, grads, held, sem_w, sem_x, sem_g, sem_h,
):
    here, width = lower_grad.shape
    full = here + HALO
    weights = start_other(meta[2], (w1, w2, w3, w4), 0, held, sem_w)
    copies = memory_copies(rows_ref, other_ref, memory)
    copy_by_role(meta, *copies, sem_x)
    normed.go()
    hidden.go()
    upper_grad.go()
    pair_sums[...] = jnp.zeros(pair_sums.shape, F32)
    memory_grad.ref[...] = jnp.zeros(memory_grad.ref.shape, BF16)
    source_low, source_high = plan[8, 1], plan[8, 2]
    parts = start(
        [pltpu.make_async_copy(out_part.at[half], grads.at[4 * half + 3], sem_g.at[0]) for half in range(2)]
    )
    gain_sum = jnp.zeros((1, width), F32)
    shift_sum = jnp.zeros((1, width), F32)
    own_q, own_pair = own_q(), own_pair()
    wait(weights)
    wait_by_role(meta, *copies, sem_x)

    def project(block, _):
        at = pl.ds(pl.multiple_of(block * HALF, HALF), HALF)
        row_grad = jnp.zeros((HALF, width), F32)
        for half in range(2):
            for c in range(2):
                low = pair_grads[half, c, at]
                row_grad += dot_nt(low, held[1 + c] if half else own_pair[c])
                pair_sums[half, c] += dot_tn(memory[at], low)
        memory_grad.ref[at] = row_grad.astype(BF16)
        return 0

    lax.fori_loop(source_low // HALF, (source_high + HALF - 1) // HALF, project, 0)
    memory_grad.send()
    for half in range(2):
        for c in range(2):
            grads[4 * half + 1 + c] = pair_sums[half, c].astype(BF16)
    normed = normed()
    for half in range(2):
        grads[4 * half] = dot_tn(normed[...], q_grad[half, HALO:full]).astype(BF16)
    wait(parts)
    put = put_grads(meta, grads, keep, send, sem_g, x_first=True)
    hidden, upper_grad = hidden(), upper_grad()
    for lo in range(0, here, HALF):
        at = slice(lo, lo + HALF)
        q_at = slice(HALO + lo, HALO + lo + HALF)
        hat, scale = norm_parts(hidden[at])
        grad = dot_nt(q_grad[0, q_at], own_q[...]) + dot_nt(q_grad[1, q_at], held[0])
        lower_grad[at] = upper_grad[at] + norm_back(grad, hat, scale, gain[1:2])
        gain_sum += jnp.sum(grad * hat, axis=0, keepdims=True)
        shift_sum += jnp.sum(grad, axis=0, keepdims=True)
    small[...] = jnp.concatenate([gain_sum, shift_sum], axis=0)
    put += start([pltpu.make_async_copy(lower_grad, lower_far, sem_h.at[0])])
    wait(put)


def self_backward(meta, plan, mix_grads, qkv, qkv_grads):
    full = mix_grads.shape[1] - WINDOW
    here = full - HALO
    qkv_grads[...] = jnp.zeros(qkv_grads.shape, BF16)

    def group(bounds, _):
        first = window_of(bounds[0])
        mask = window_mask(first, bounds, first, bounds, HALO, full, True)
        at = pl.ds(first, WINDOW)
        return [
            (qkv[half, 0, at], qkv[half, 1, at], qkv[half, 2, at], mix_grads[half, at], mask)
            for half in range(2)
        ]

    def store(bounds, _, result):
        at = pl.ds(window_of(bounds[0]), WINDOW)
        for half in range(2):
            for c in range(3):
                qkv_grads[half, c, at] += result[half][c]

    each_group(plan, group, attend_windows_back, store)


def self_products(
    meta, rows_ref, other_ref, normed, qkv_grads, out_part, upper_grad, own, w1, w2, w3, w4, gain, result, memory_part,
    keep, send, state_grad, swap, halo_grad, small, grads, states, held, sem_g, sem_w, sem_x, sem_s,
):
    full, width = states.shape
    here = full - HALO
    normed.go()
    parts = start(
        [pltpu.make_async_copy(out_part.at[half], grads.at[4 * half + 3], sem_g.at[0]) for half in range(2)]
    )
    weights = start_other(meta[1], (w1, w2, w3, w4), 0, held, sem_w)
    state_copies = states_copies(rows_ref, other_ref, states, here)
    copy_by_role(meta, *state_copies, sem_x)
    swaps = [(result, swap.ref.at[pl.ds(0, here)])], [(memory_part, swap.ref)]
    own.go()
    upper_grad.go()
    copy_by_role(meta, *swaps, sem_s)
    normed = normed()
    for half in range(2):
        for c in range(3):
            grads[4 * half + c] = dot_tn(normed[...], qkv_grads[half, c, 0:full]).astype(BF16)
    wait(parts)
    put = put_grads(meta, grads, keep, send, sem_g)
    wait_by_role(meta, *state_copies, sem_x)

    @pl.when(meta[0] == 0)
    def _():
        states[0:HALO] = jnp.zeros((HALO, width), BF16)

    own, upper_grad = own(), upper_grad()
    wait(weights)
    gain_sum = jnp.zeros((1, width), F32)
    shift_sum = jnp.zeros((1, width), F32)
    step = full // 2
    for lo in range(0, full, step):
        at = slice(lo, lo + step)
        hat, scale = norm_parts(states[at].astype(F32))
        grad = sum(
            dot_nt(qkv_grads[half, c, at], matrices[c])
            for half, matrices in enumerate((own, held))
            for c in range(3)
        )
        back = norm_back(grad, hat, scale, gain[0:1])
        if lo == 0:
            halo_grad.ref[...] = back[:HALO]
            back = back[HALO:]
        first = max(lo, HALO) - HALO
        at = slice(first, lo + step - HALO)
        back += upper_grad[at]
        state_grad.ref[at] = back

        @pl.when(meta[0] == 0)
        def _(low=back.astype(BF16), at=slice(here + at.start, here + at.stop)):
            swap.ref[at] = low

        gain_sum += jnp.sum(grad * hat, axis=0, keepdims=True)
        shift_sum += jnp.sum(grad, axis=0, keepdims=True)
    small[...] = jnp.concatenate([gain_sum, shift_sum], axis=0)
    wait_by_role(meta, *swaps, sem_s)
    wait(put)


def finish_rows(
    meta, rows, result, grad, halo_grad, memory_part, swapped, layer_out, input_grads, parts, halo, sem,
):
    here = result.shape[0]
    low, high = pl.ds(0, here), pl.ds(here, here)

    @pl.when(meta[0] == 0)
    def _():
        copies = [(rows, layer_out.ref), (memory_part, parts.at[0]), (swapped, parts.at[1])]
        wait(start([pltpu.make_async_copy(*copy, sem) for copy in copies]))
        input_grads.ref[...] = parts[0].astype(F32) + parts[1].astype(F32)

    @pl.when(meta[0] == 1)
    def _():
        copies = [
            (swapped.at[low], layer_out.ref.at[low]),
            (result, layer_out.ref.at[high]),
            (swapped.at[high], parts.at[0, low]),
            (grad, input_grads.ref.at[high]),
            (halo_grad, halo),
        ]
        wait(start([pltpu.make_async_copy(*copy, sem) for copy in copies]))
        input_grads.ref[0:here] = parts[0, 0:here].astype(F32)
        input_grads.ref[here - HALO : here] += halo[...]


OUTPUTS = {"ffn": 2, "cross": 7, "self": 2}


def unpack(kinds, meta, *refs):
    pieces, refs = refs[: 4 * len(kinds)], refs[4 * len(kinds) :]
    if "cross" in kinds:
        small, refs = refs[0], refs[1:]
    count = sum(OUTPUTS[kind] for kind in kinds)
    outs, held, sem = refs[:count], refs[count:-1], refs[-1]
    copies = []
    for at in range(len(kinds)):
        rows = pieces[4 * at].shape[1]
        came = zip((0, 2, 1, 3), pieces[4 * at : 4 * at + 4])
        firsts = [(pl.multiple_of((rel ^ meta[1]) * rows, rows), ref) for rel, ref in came]
        copies.append(
            start(
                [
                    pltpu.make_async_copy(ref, held[at].at[:, pl.ds(first, rows)], sem.at[at])
                    for first, ref in firsts
                ]
            )
        )
    for kind, grads, arrived in zip(kinds, held, copies):
        outs, rest = outs[: OUTPUTS[kind]], outs[OUTPUTS[kind] :]
        wait(arrived)
        if kind == "ffn":
            grad_in, grad_out = outs
            for j in range(4):
                at = slice(j * HALF, (j + 1) * HALF)
                grad_in[:, at] = grads[j].astype(F32)
                grad_out[at, 0:HALF] = grads[4 + j, 0:HALF].astype(F32)
                grad_out[at, HALF:] = grads[4 + j, HALF:].astype(F32)
        else:
            if kind == "cross":
                gain, shift, weight, bias = outs[3:]
                gain[...], shift[...] = small[0:3], small[3:6]
                weight[...], bias[...] = small[6:7], small[7:8, 0:1]
                outs[0][...] = grads[0].astype(F32)
                for c in range(2):
                    outs[1][:, c] = grads[1 + c].astype(F32)
                out = outs[2]
            else:
                outs[0][...] = grads[0:3].astype(F32)
                out = outs[1]
            out[:, 0:HALF] = grads[3, 0:HALF].astype(F32)
            out[:, HALF:] = grads[3, HALF:].astype(F32)
        outs = rest


def shape(*dims, dtype=F32):
    return jax.ShapeDtypeStruct(dims, dtype)


def far(*dims, dtype=F32):
    return pltpu.HBM(dims, dtype)


def near(*dims, dtype=F32):
    return pltpu.VMEM(dims, dtype)


def room(shapes, spare):
    return sum(math.prod(each.shape) * jnp.dtype(each.dtype).itemsize for each in shapes) + (spare << 20)


class Put:
    def __init__(self, *dims, dtype=F32):
        self.shape = far(*dims, dtype=dtype)
        self.scratch = pltpu.VMEM(dims, dtype)


class Get:
    def __init__(self, value, late=False):
        self.value = value
        self.late = late
        self.scratch = pltpu.VMEM(value.shape, value.dtype)


class Here:
    def __init__(self, value):
        self.value = value


class Any:
    def __init__(self, value):
        self.value = value


class Far:
    def __init__(self, value):
        self.value = value


def call(body, ins, outs, scratch, weight):
    smem, others = ins
    operands = list(smem) + list(others)
    values, in_specs = list(smem), [SMEM] * len(smem)
    for other in others:
        if isinstance(other, (Get, Far)):
            values.append(pltpu.with_memory_space_constraint(other.value, pltpu.HBM))
            in_specs.append(ANY)
        elif isinstance(other, Any):
            values.append(other.value)
            in_specs.append(ANY)
        elif isinstance(other, Here):
            values.append(pltpu.with_memory_space_constraint(other.value, pltpu.VMEM))
            in_specs.append(VMEM)
        else:
            values.append(other)
            in_specs.append(VMEM)
    moved = [at for at, each in enumerate(operands) if isinstance(each, Get)]
    put = [at for at, each in enumerate(outs) if isinstance(each, Put)]

    def inner(*refs):
        in_refs, refs = list(refs[: len(values)]), refs[len(values) :]
        out_refs, refs = list(refs[: len(outs)]), refs[len(outs) :]
        moved_refs, refs = refs[: len(moved)], refs[len(moved) :]
        put_refs, refs = refs[: len(put)], refs[len(put) :]
        sems, refs = refs[0], refs[1:]
        for i, at in enumerate(moved):
            in_refs[at] = Load(in_refs[at], moved_refs[i], sems.at[i])
            if not operands[at].late:
                in_refs[at].go()
        for i, at in enumerate(put):
            out_refs[at] = Store(put_refs[i], out_refs[at], sems.at[len(moved) + i])
        body(*in_refs, *out_refs, *refs)
        for at in moved:
            in_refs[at]()
        for at in put:
            if not out_refs[at].copies:
                out_refs[at].send()
        for at in put:
            out_refs[at].end()

    in_vmem = [operands[at].scratch for at in moved] + [outs[at].scratch for at in put]
    in_vmem += [each for each in scratch if getattr(each, "memory_space", None) is pltpu.VMEM]
    in_vmem += [value for value, spec in zip(values, in_specs) if spec is VMEM]
    in_vmem += [out for out in outs if not isinstance(out, Put) and getattr(out, "memory_space", None) is not pltpu.HBM]
    return pl.pallas_call(
        inner,
        out_shape=[out.shape if isinstance(out, Put) else out for out in outs],
        in_specs=in_specs,
        out_specs=[ANY if isinstance(out, Put) or getattr(out, "memory_space", None) is pltpu.HBM else VMEM for out in outs],
        scratch_shapes=[operands[at].scratch for at in moved]
        + [outs[at].scratch for at in put]
        + [pltpu.SemaphoreType.DMA((len(moved) + len(put) + 1,))]
        + list(scratch),
        name=getattr(body, "__name__", "out_backward"),
        compiler_params=pltpu.CompilerParams(vmem_limit_bytes=room(in_vmem, SPARE)),
        cost_estimate=pl.CostEstimate(flops=int(weight * WEIGHT), bytes_accessed=0, transcendentals=0),
    )(*values)


def flip(value, axis, bit=1):
    count = lax.axis_size(axis)
    return lax.ppermute(value, axis, [(i, i ^ bit) for i in range(count)])


def add(a, b):
    return (a.astype(F32) + b.astype(F32)).astype(BF16)


def after(value, *events):
    return lax.optimization_barrier((value, events))[0]


class Order:
    def __init__(self, meta):
        self.meta = meta
        self.last = ()

    def now(self):
        return after(self.meta, *self.last)

    def __call__(self, weight, *jobs):
        operands = [value for job in jobs for value in job[0]]
        shapes = [each for job in jobs for each in job[1]]

        def sums(meta, *refs):
            ins, outs = list(refs[: len(operands)]), list(refs[len(operands) :])
            for values, results, body, _ in jobs:
                body(meta, ins[: len(values)], outs[: len(results)])
                ins, outs = ins[len(values) :], outs[len(results) :]

        results = list(
            pl.pallas_call(
                sums,
                out_shape=shapes,
                in_specs=[SMEM] + [VMEM] * len(operands),
                out_specs=[VMEM] * len(shapes),
                name="sums",
                compiler_params=pltpu.CompilerParams(vmem_limit_bytes=room(operands + shapes, 4)),
                cost_estimate=pl.CostEstimate(flops=int(weight * WEIGHT), bytes_accessed=0, transcendentals=0),
            )(self.now(), *operands)
        )
        self.last = tuple(results)
        for _, each, _, take in jobs:
            take(results[: len(each)])
            results = results[len(each) :]


class Sum:
    def __init__(self, keep, send, routes):
        self.routes = routes
        self.near, self.got = [keep], [flip(send, "role")]

    def job(self, shapes, body, take):
        count = len(self.near)
        return (
            [*self.near, *self.got],
            [jax.ShapeDtypeStruct(each, BF16) if isinstance(each, tuple) else each for each in shapes],
            lambda meta, ins, outs: body(meta, ins[:count], ins[count:], outs),
            take,
        )

    def pass_on(self, stage, far_near=False):
        def take(parts):
            self.near = parts[0::2]
            if far_near:
                self.near = [pltpu.with_memory_space_constraint(each, pltpu.HBM) for each in self.near]
            self.got = [step(away, route[stage]) for away, route in zip(parts[1::2], self.routes)]

        return take

    def begin(self, far_near=False):
        count = len(self.routes)
        _, _, matrices, rows, columns = self.near[0].shape
        share = matrices // count

        def body(meta, near, got, outs):
            for at, route in enumerate(self.routes):
                mine = pl.ds(at * share, share)
                for which in range(2):
                    place = (slice(None), which, mine) if route[0] == "x" and count > 1 else (which, slice(None), mine)
                    outs[2 * at + which][...] = add(near[0][place], got[0][place])

        shapes = [jax.ShapeDtypeStruct((2, share, rows, columns), BF16)] * (2 * count)
        if far_near:
            shapes[0::2] = [far(2, share, rows, columns, dtype=BF16)] * count
        return self.job(shapes, body, self.pass_on(0, far_near))

    def second(self):
        def body(meta, near, got, outs):
            for at in range(len(near)):
                for which in range(2):
                    outs[2 * at + which][...] = add(near[at][which], got[at][which])

        return self.job([self.near[0].shape[1:]] * (2 * len(self.near)), body, self.pass_on(1))

    def halve(self):
        count = len(self.near)
        matrices, rows, columns = self.near[0].shape
        half = count * matrices // 2

        def body(meta, near, got, outs):
            upper = meta[2] >> 1
            for out, which in zip(outs, (upper, 1 - upper)):
                if count == 1:
                    at = pl.ds(which * half, half)
                    out[...] = add(near[0][at], got[0][at])
                else:
                    both = [add(mine[...], theirs[...]) for mine, theirs in zip(near, got)]
                    out[...] = jnp.where(which == 1, both[1], both[0])

        def take(parts):
            self.near, self.got = [parts[0]], [flip(parts[1], "dp", 2)]

        return self.job([(half, rows, columns)] * 2, body, take)

    def plain(self, bit):
        def body(meta, near, got, outs):
            outs[0][...] = add(near[0][...], got[0][...])

        def take(parts):
            self.near, self.got = parts, [flip(parts[0], "dp", bit)]

        return self.job([self.near[0].shape], body, take)

    def whole(self):
        return self.plain(4)

    def back(self, order):
        bit = 8
        while bit < lax.axis_size("dp"):
            order(1, self.plain(bit))
            bit *= 2
        return self.plain(2)

    def last(self):
        half, rows, columns = self.near[0].shape

        def body(meta, near, got, outs):
            upper = meta[2] >> 1
            outs[0][pl.ds(upper * half, half)] = near[0][...]
            outs[0][pl.ds((1 - upper) * half, half)] = got[0][...]

        def take(parts):
            self.mine = parts[0]
            self.by_x = flip(self.mine, "dp", 1)

        return self.job([(2 * half, rows, columns)], body, take)

    def pieces(self, order):
        by_x = after(self.by_x, *order.last)
        return self.mine, by_x, flip(self.mine, "role"), flip(by_x, "role")


def step(value, route):
    if route == "head":
        return flip(value, "head")
    return flip(value, "dp", 1)


class SmallSum:
    def __init__(self, value):
        count = lax.axis_size("dp")
        self.steps = [("role", 1), ("head", 1)] + [("dp", 1 << at) for at in range(count.bit_length() - 1)]
        self.value, self.got = value, flip(value, *self.steps.pop(0))

    def step(self):
        def body(meta, ins, outs):
            outs[0][...] = ins[0][...] + ins[1][...]

        def take(parts):
            self.value = parts[0]
            self.got = flip(self.value, *self.steps.pop(0)) if self.steps else None

        return [self.value, self.got], [jax.ShapeDtypeStruct(self.value.shape, F32)], body, take

    def total(self):
        while self.got is not None:
            self.value = self.value + self.got
            self.got = flip(self.value, *self.steps.pop(0)) if self.steps else None
        return self.value


def shards(
    layer_in,
    lengths,
    cotangent,
    targets,
    self_qkv,
    self_out,
    cross_q,
    cross_kv,
    cross_out,
    ffn_in,
    ffn_out,
    norm_gain,
    norm_bias,
    halt_weight,
    halt_bias,
):
    role, head, place = (lax.axis_index(name) for name in ("role", "head", "dp"))
    target_side = role == 1
    me = 2 * (place & 1) + role
    me_z = (place & 2) + role
    meta = jnp.stack([role, me, me_z, layer_in.shape[1] // 2]).astype(jnp.int32)

    rows = layer_in[0]
    row_len, width = rows.shape
    here = row_len // 2
    full = here + HALO

    other_rows = flip(rows, "role")
    lens = lax.dynamic_index_in_dim(lengths[0], head, 0, keepdims=False)
    other_lens = flip(lens, "role")
    segs = jnp.where(target_side, jnp.stack([other_lens, lens]), jnp.stack([lens, other_lens]))
    segs = jnp.pad(segs, ((0, 0), (0, 2)))

    self_own, cross_own = self_qkv.transpose(1, 0, 2), cross_kv.transpose(1, 0, 2)
    piece_shape = Put(4, width // PIECES, HALF, dtype=BF16)
    (self_piece,) = call(
        cut_self, ([meta], [Far(self_own), Far(self_out)]), [piece_shape], [pltpu.SemaphoreType.DMA((2,))], 1
    )
    cross_piece, in_piece, out_own_piece = call(
        cut_rest,
        ([meta], [Far(cross_q), Far(cross_own), Far(cross_out), Far(ffn_in), Far(ffn_out)]),
        [piece_shape, piece_shape, Put(HALF, width, dtype=BF16)],
        [pltpu.SemaphoreType.DMA((5,))],
        1,
    )
    self_first, cross_first, in_first, out_first = (
        flip(piece, "head") for piece in (self_piece, cross_piece, in_piece, out_own_piece)
    )

    weight_sems = pltpu.SemaphoreType.DMA((6,))
    one_sem = pltpu.SemaphoreType.DMA
    grad_sems = pltpu.SemaphoreType.DMA((1,))
    states_held = pltpu.VMEM((full, width), BF16)
    memory_held = pltpu.VMEM((row_len, width), BF16)
    out_held = pltpu.VMEM((width, HALF), BF16)
    mix_grads = pltpu.VMEM((2, full + WINDOW, HALF), BF16)

    def heads(*dims):
        return Put(*dims, full + WINDOW, HALF, dtype=BF16)

    def matrices(count):
        return pltpu.VMEM((count, width, HALF), BF16)

    pair_shape = (2, 2, row_len + WINDOW, HALF)

    both_rows = Any(rows), Any(other_rows)

    self_plan, cross_plan = pl.pallas_call(
        group_sentences,
        out_shape=[jax.ShapeDtypeStruct((9, 40), jnp.int32)] * 2,
        in_specs=[SMEM] * 2,
        out_specs=[SMEM] * 2,
        name="group_sentences",
        cost_estimate=pl.CostEstimate(flops=int(HEAVY * WEIGHT), bytes_accessed=0, transcendentals=0),
    )(after(meta, cross_piece, self_first), segs)
    self_second = flip(self_first, "dp", 1)
    cross_second = flip(cross_first, "dp", 2)
    in_second = flip(in_first, "dp", 1)
    self_second = after(self_second, self_plan)
    self_weights = [self_first, self_second, flip(self_first, "role"), flip(self_second, "role")]
    self_pieces = [Any(piece) for piece in self_weights]
    hidden, normed_one, qkv, self_mix = call(
        self_forward,
        (
            [after(meta, cross_first), self_plan],
            [*both_rows, norm_gain, norm_bias, Get(self_own), Far(self_out), *self_pieces],
        ),
        [near(here, width), Put(full, width, dtype=BF16), heads(2, 3), heads(2)],
        [states_held, matrices(4), out_held, weight_sems, one_sem],
        11,
    )

    cross_second = after(cross_second, normed_one)
    cross_weights = [cross_first, cross_second, flip(cross_first, "role"), flip(cross_second, "role")]
    cross_pieces = [Any(piece) for piece in cross_weights]
    out_first = after(out_first, normed_one)
    out_second = flip(out_first, "dp", 2)
    hidden_two, hidden_far, normed_two, cross_mix, queries, pairs = call(
        cross_forward,
        (
            [meta, cross_plan],
            [
                *both_rows, Here(hidden), norm_gain, norm_bias, Get(cross_q), Get(cross_own), Far(cross_out),
                *cross_pieces,
            ],
        ),
        [Put(here, width), far(here, width), Put(here, width, dtype=BF16), heads(2), heads(2), far(*pair_shape, dtype=BF16)],
        [
            pltpu.VMEM(pair_shape, BF16), memory_held, matrices(4), out_held, weight_sems, one_sem,
            pltpu.SemaphoreType.DMA((2,)),
        ],
        12,
    )

    in_second, out_second = after((in_second, out_second), normed_two)
    in_weights = in_first, in_second, flip(in_first, "role"), flip(in_second, "role")
    out_weights = out_first, out_second, flip(out_first, "role"), flip(out_second, "role")
    ffn_parts = far(2, 2, 8, width // PIECES, HALF, dtype=BF16)
    grad_parts = far(2, 2, 4, width // PIECES, HALF, dtype=BF16)
    result_low, two_grad, two_far, ffn_small, keep_ffn, send_ffn = call(
        feed_forward,
        (
            [meta],
            [
                Get(hidden_two), Far(cotangent), targets.astype(F32).reshape(2, here // WINDOW, WINDOW),
                norm_gain, norm_bias, halt_weight[None], halt_bias, Far(ffn_in), *map(Far, in_weights),
                Far(ffn_out), *map(Far, out_weights),
            ],
        ),
        [Put(here, width, dtype=BF16), near(here, width), far(here, width), shape(4, width), ffn_parts, ffn_parts],
        [
            matrices(8),
            pltpu.VMEM((8, HALF, width), BF16),
            pltpu.VMEM((here, width), BF16),
            pltpu.VMEM((8, here, HALF), BF16),
            pltpu.VMEM((8, here, HALF), F32),
            pltpu.VMEM((here, width), F32),
            pltpu.VMEM((here, width), BF16),
            pltpu.VMEM((here, width), BF16),
            matrices(16),
            weight_sems,
            weight_sems,
            pltpu.SemaphoreType.DMA((2,)),
            grad_sems,
        ],
        17,
    )

    mix_grads_shape = near(2, full + WINDOW, HALF, dtype=BF16)
    out_scratch = [matrices(2), weight_sems, grad_sems]
    cross_mix_grads, cross_out_part, queries = call(
        functools.partial(out_backward, place=2, ahead=1),
        ([meta], [Here(two_grad), Get(cross_mix, late=True), Far(cross_out), *cross_pieces, Far(queries)]),
        [mix_grads_shape, Put(2, width, HALF, dtype=BF16), near(2, full + WINDOW, HALF, dtype=BF16)],
        out_scratch,
        4,
    )

    def totals(kinds, pieces, out_shapes, *more):
        scratch = [pltpu.VMEM((each[0].shape[0], width, HALF), BF16) for each in pieces]
        results = pl.pallas_call(
            functools.partial(unpack, kinds),
            out_shape=out_shapes,
            in_specs=[SMEM] + [ANY] * (4 * len(kinds)) + [VMEM] * len(more),
            out_specs=[VMEM] * len(out_shapes),
            scratch_shapes=scratch + [pltpu.SemaphoreType.DMA((len(kinds),))],
            name="unpack_" + kinds[0],
            compiler_params=pltpu.CompilerParams(vmem_limit_bytes=room([*out_shapes, *scratch], 6)),
            cost_estimate=pl.CostEstimate(flops=1000, bytes_accessed=0, transcendentals=0),
        )(order.now(), *[piece for each in pieces for piece in each], *more)
        order.last = (results[0],)
        return results

    order = Order(meta)
    ffn_sum = Sum(keep_ffn, send_ffn, FFN_ROUTES)
    order(1, ffn_sum.begin())
    query_grad, pair_grads = call(
        cross_backward,
        ([order.now(), cross_plan], [Here(cross_mix_grads), Here(queries), Far(pairs)]),
        [near(2, full + WINDOW, HALF, dtype=BF16), near(*pair_shape, dtype=BF16)],
        [pltpu.VMEM(pair_shape, BF16), grad_sems],
        9,
    )
    one_grad, one_far, memory_part, cross_small, keep_cross, send_cross = call(
        cross_products,
        (
            [meta, cross_plan],
            [
                *both_rows, Get(hidden_far, late=True), Get(normed_two, late=True), Get(two_far, late=True), Here(query_grad), Here(pair_grads),
                Far(cross_out_part), Get(cross_q), Get(cross_own), *cross_pieces, norm_gain,
            ],
        ),
        [near(here, width), far(here, width), Put(row_len, width, dtype=BF16), shape(2, width), grad_parts, grad_parts],
        [
            memory_held,
            pltpu.VMEM((2, 2, width, HALF), F32),
            matrices(8),
            matrices(3),
            weight_sems,
            one_sem,
            grad_sems,
            grad_sems,
        ],
        8,
    )

    cross_sum = Sum(keep_cross, send_cross, CROSS_ROUTES)
    order(1, ffn_sum.second())
    self_mix_grads, self_out_part, qkv = call(
        functools.partial(out_backward, place=1, ahead=1),
        ([order.now()], [Here(one_grad), Get(self_mix, late=True), Far(self_out), *self_pieces, Far(qkv)]),
        [mix_grads_shape, Put(2, width, HALF, dtype=BF16), near(2, 3, full + WINDOW, HALF, dtype=BF16)],
        out_scratch,
        4,
    )
    order(1, cross_sum.begin())
    order(1, ffn_sum.halve())
    (qkv_grads,) = call(
        self_backward,
        ([order.now(), self_plan], [Here(self_mix_grads), Here(qkv)]),
        [near(2, 3, full + WINDOW, HALF, dtype=BF16)],
        [],
        9,
    )
    order(1, ffn_sum.whole(), cross_sum.second())
    keep_self, send_self, state_grad, swap, halo_grad, self_small = call(
        self_products,
        (
            [order.now()],
            [
                *both_rows, Get(normed_one, late=True), Here(qkv_grads), Far(self_out_part), Get(one_far, late=True), Get(self_own, late=True),
                *self_pieces, norm_gain, Far(result_low), Far(memory_part),
            ],
        ),
        [
            grad_parts,
            grad_parts,
            Put(here, width),
            Put(row_len, width, dtype=BF16),
            Put(HALO, width),
            shape(2, width),
        ],
        [matrices(8), states_held, matrices(3), grad_sems, weight_sems, one_sem, one_sem],
        11,
    )
    self_sum = Sum(keep_self, send_self, SELF_ROUTES)
    order.last = (keep_self,)
    order(HEAVY, cross_sum.halve(), ffn_sum.back(order))
    order(1, self_sum.begin(far_near=True))
    self_small = after(self_small, *order.last)
    small = SmallSum(
        jnp.concatenate(
            [
                self_small[0:1], cross_small[0:1], ffn_small[0:1],
                self_small[1:2], cross_small[1:2], ffn_small[1:2], ffn_small[2:4],
            ],
            axis=0,
        )
    )
    swapped = flip(after(swap, *order.last), "role")
    order(HEAVY, cross_sum.whole())
    order(1, self_sum.second(), small.step())
    order(1, self_sum.halve(), cross_sum.back(order), ffn_sum.last(), small.step())
    order(1, self_sum.whole(), small.step())
    layer_out, input_grads = call(
        finish_rows,
        (
            [order.now()],
            [Any(each) for each in (rows, result_low, state_grad, halo_grad, memory_part, swapped)],
        ),
        [Put(row_len, width, dtype=BF16), Put(row_len, width)],
        [pltpu.VMEM((2, row_len, width), BF16), pltpu.VMEM((HALO, width), F32), one_sem],
        HEAVY,
    )
    order.last = (layer_out,)
    order(1, cross_sum.last(), small.step())
    order(1, self_sum.back(order))
    order.last = (*order.last, cross_sum.by_x)
    order(1, self_sum.last(), small.step())
    ffn_in_grad, ffn_out_grad, cross_q_grad, cross_kv_grad, cross_out_grad, *small = totals(
        ("ffn", "cross"),
        (ffn_sum.pieces(order), cross_sum.pieces(order)),
        (
            shape(width, 4 * HALF), shape(4 * HALF, width),
            shape(width, HALF), shape(width, 2, HALF), shape(HALF, width),
            shape(3, width), shape(3, width), shape(1, width), shape(1, 1),
        ),
        small.total(),
    )
    self_qkv_grad, self_out_grad = totals(
        ("self",), (self_sum.pieces(order),), (shape(3, width, HALF), shape(HALF, width))
    )
    return (
        layer_out[None],
        input_grads[None],
        self_qkv_grad.transpose(1, 0, 2),
        self_out_grad,
        cross_q_grad,
        cross_kv_grad,
        cross_out_grad,
        ffn_in_grad,
        ffn_out_grad,
        small[0],
        small[1],
        small[2][0],
        small[3][0],
    )


def solution(mesh):
    placed = (
        P("role", ("dp", "head"), None),
        P("role", "dp", None),
        P(("dp", "head"), None),
        P(("dp", "head")),
        P(None, None, "head"),
        P("head", None),
        P(None, "head"),
        P(None, None, "head"),
        P("head", None),
        P(None, "head"),
        P("head", None),
        P(),
        P(),
        P(),
        P(),
    )
    return jax.shard_map(
        shards,
        mesh=mesh,
        in_specs=placed,
        out_specs=(
            P("role", ("dp", "head"), None),
            P("role", ("dp", "head"), None),
            P(None, None, "head"),
            P("head", None),
            P(None, "head"),
            P(None, None, "head"),
            P("head", None),
            P(None, "head"),
            P("head", None),
            P(),
            P(),
            P(),
            P(),
        ),
        check_vma=False,
    )
```

```python
import functools
import math

import jax
import jax.numpy as jnp
from jax import lax
from jax.experimental import pallas as pl
from jax.experimental.pallas import tpu as pltpu
from jax.sharding import PartitionSpec as P

F32 = jnp.float32
BF16 = jnp.bfloat16

HEAD_DIM = 64
HALF = 256
HEADS = HALF // HEAD_DIM
HALO = 128
GROUPS = 3
WINDOW = 128
MASKED = -1e30
SPARE = 8
WEIGHT = 1.2e9
ANY = pl.BlockSpec(memory_space=pl.ANY)
VMEM = pl.BlockSpec(memory_space=pltpu.VMEM)
SMEM = pl.BlockSpec(memory_space=pltpu.SMEM)
ARRIVALS = (0, 2, 1, 3)
FFN_ROUTES = [("head", "x"), ("x", "head")]
CROSS_ROUTES = [("head", "x"), ("x", "head")]
SELF_ROUTES = [("head", "x"), ("x", "head")]
HEAVY = 24
PIECES = 4


def dot(a, b):
    return jnp.dot(a, b, preferred_element_type=F32)


def dot_nt(a, b):
    return lax.dot_general(a, b, (((1,), (1,)), ((), ())), preferred_element_type=F32)


def dot_tn(a, b):
    return lax.dot_general(a, b, (((0,), (0,)), ((), ())), preferred_element_type=F32)


def norm_parts(values):
    center = values - jnp.mean(values, axis=-1, keepdims=True)
    spread = jnp.mean(center * center, axis=-1, keepdims=True)
    scale = lax.rsqrt(spread + 1e-05)
    return center * scale, scale


def norm_back(grad, hat, scale, gain):
    grad_hat = grad * gain
    first = jnp.mean(grad_hat, axis=-1, keepdims=True)
    second = jnp.mean(grad_hat * hat, axis=-1, keepdims=True)
    return scale * (grad_hat - first - hat * second)


class Load:
    def __init__(self, source, target, sem):
        self.target, self.copy = target, pltpu.make_async_copy(source, target, sem)
        self.gone = self.come = False

    def go(self):
        if not self.gone:
            self.copy.start()
        self.gone = True

    def __call__(self):
        self.go()
        if not self.come:
            self.copy.wait()
        self.come = True
        return self.target


class Store:
    def __init__(self, ref, target, sem):
        self.ref, self.target, self.sem, self.copies = ref, target, sem, []

    def send(self, at=None):
        if at is None:
            copy = pltpu.make_async_copy(self.ref, self.target, self.sem)
        else:
            at = pl.ds(at.start, at.stop - at.start)
            copy = pltpu.make_async_copy(self.ref.at[at], self.target.at[at], self.sem)
        copy.start()
        self.copies.append(copy)

    def end(self):
        if not self.copies:
            self.send()
        wait(self.copies)


def start(copies):
    for copy in copies:
        copy.start()
    return copies


def wait(copies):
    for copy in copies:
        copy.wait()


def cut_self(meta, matrices, out, piece, sem):
    wait(start(row_copies(meta[1], matrices, out, piece.ref, 0, sem)))


def row_copies(which, matrices, out, piece, first, sem):
    count, rows = matrices.shape[0], piece.shape[1]
    low = pl.multiple_of(which * rows, rows)
    out_low = pl.multiple_of((which & 1) * rows, rows)
    out_left = pl.multiple_of((which >> 1) * HALF, HALF)
    return [
        pltpu.make_async_copy(matrices.at[:, pl.ds(low, rows)], piece.at[pl.ds(first, count)], sem.at[0]),
        pltpu.make_async_copy(out.at[pl.ds(out_low, rows), pl.ds(out_left, HALF)], piece.at[3], sem.at[1]),
    ]


def cut_rest(meta, q, pair, out, ffn_in, ffn_out, cross_piece, in_piece, out_piece, sem):
    cross_piece, in_piece, out_piece = cross_piece.ref, in_piece.ref, out_piece.ref
    rows = cross_piece.shape[1]
    low = pl.multiple_of(meta[2] * rows, rows)
    copies = row_copies(meta[2], pair, out, cross_piece, 1, sem)
    copies.append(pltpu.make_async_copy(q.at[pl.ds(low, rows)], cross_piece.at[0], sem.at[2]))
    low = pl.multiple_of(meta[1] * rows, rows)
    for j in range(4):
        source = ffn_in.at[pl.ds(low, rows), pl.ds(j * HALF, HALF)]
        copies.append(pltpu.make_async_copy(source, in_piece.at[j], sem.at[3]))
    low = pl.multiple_of(meta[2] * HALF, HALF)
    copies.append(pltpu.make_async_copy(ffn_out.at[pl.ds(low, HALF)], out_piece, sem.at[4]))
    wait(start(copies))


def start_out_own(out, held, sem):
    return start(
        [
            pltpu.make_async_copy(out.at[:, pl.ds(c * HALF, HALF)], held.at[pl.ds(c * HALF, HALF)], sem.at[c])
            for c in range(2)
        ]
    )


def start_other(place, arrived, first, held, sem):
    rows, count = arrived[0].shape[1], held.shape[0]
    copies = []
    for at, (ref, flip) in enumerate(zip(arrived, ARRIVALS)):
        low = pl.multiple_of((place ^ flip) * rows, rows)
        source = ref.at[pl.ds(first, count)]
        copies.append(pltpu.make_async_copy(source, held.at[:, pl.ds(low, rows)], sem.at[2 + at]))
    return start(copies)


def start_in(meta, own, arrived, held, sem):
    copies = [
        pltpu.make_async_copy(own.at[:, pl.ds(j * HALF, HALF)], held.at[j], sem.at[0]) for j in range(4)
    ]
    return start(copies) + start_other(meta[1], arrived, 0, held.at[pl.ds(4, 4)], sem)


def start_out(meta, own, arrived, held, sem):
    copies = [
        pltpu.make_async_copy(own.at[pl.ds(j * HALF, HALF)], held.at[j], sem.at[0]) for j in range(4)
    ]
    for at, (ref, flip) in enumerate(zip(arrived, ARRIVALS)):
        copies.append(pltpu.make_async_copy(ref, held.at[4 + (meta[2] ^ flip)], sem.at[2 + at]))
    return start(copies)


def put_half(meta, grads, keep, send, sem, half, x_first=False):
    _, _, count, rows, _ = keep.shape
    copies = []
    for rel in range(PIECES):
        first = pl.multiple_of((rel ^ meta[1]) * rows, rows)
        source = grads.at[pl.ds(half * count, count), pl.ds(first, rows)]
        at = (rel >> 1, half) if x_first else (half, rel >> 1)
        target = (send if rel & 1 else keep).at[at]
        copies.append(pltpu.make_async_copy(source, target, sem.at[0]))
    return start(copies)


def put_grads(meta, grads, keep, send, sem, x_first=False):
    return [copy for half in range(2) for copy in put_half(meta, grads, keep, send, sem, half, x_first)]


def group_sentences(meta, segs, self_plan, cross_plan):
    first_row = meta[0] * meta[3]
    last_row = first_row + meta[3]
    shift = HALO - first_row
    zero = jnp.int32(0)
    for plan, cross in ((self_plan, False), (cross_plan, True)):

        def step(c, carry, plan=plan, cross=cross):
            t0, s0, done, count, low, high = carry
            t1, s1 = t0 + segs[1, c], s0 + segs[0, c]
            t2, s2 = t1 + segs[1, c + 1], s1 + segs[0, c + 1]
            t3, s3 = t2 + segs[1, c + 2], s2 + segs[0, c + 2]
            target_end, source_end = window_of(t0) + WINDOW, window_of(s0) + WINDOW
            two = (t2 <= target_end) & (t1 < last_row)
            three = two & (t3 <= target_end) & (t2 < last_row)
            if cross:
                two = two & (s2 <= source_end)
                three = three & (s3 <= source_end) & two
            t2, s2 = jnp.where(two, t2, t1), jnp.where(two, s2, s1)
            t3, s3 = jnp.where(three, t3, t2), jnp.where(three, s3, s2)
            mine = (t1 > first_row) & (t0 < last_row)
            here = (c >= done) & mine
            for at, bound in enumerate((t0, t1, t2, t3)):
                plan[at, count] = bound + shift
            for at, bound in enumerate((s0, s1, s2, s3)):
                plan[4 + at, count] = bound
            size = 1 + two.astype(jnp.int32) + three.astype(jnp.int32)
            low = jnp.where(mine, jnp.minimum(low, s0), low)
            high = jnp.where(mine, jnp.maximum(high, s1), high)
            return t1, s1, jnp.where(here, c + size, done), count + here.astype(jnp.int32), low, high

        start = (zero, zero, zero, zero, jnp.int32(1 << 20), zero)
        _, _, _, count, low, high = lax.fori_loop(0, segs.shape[1] - 2, step, start)
        for g in range(GROUPS):
            for at in range(8):
                plan[at, count + g] = 0
        plan[8, 0] = count
        plan[8, 1] = low
        plan[8, 2] = high


def each_group(plan, windows, compute, store):
    def work(first, count):
        bounds = [
            ([plan[at, first + g] for at in range(4)], [plan[4 + at, first + g] for at in range(4)])
            for g in range(count)
        ]
        operands = [windows(*each) for each in bounds]
        results = iter(compute([window for each in operands for window in each]))
        for each, windows_of_it in zip(bounds, operands):
            store(*each, [next(results) for _ in windows_of_it])

    def some(i, _):
        work(i * GROUPS, GROUPS)
        return 0

    def one(i, _):
        work(i, 1)
        return 0

    count = plan[8, 0]
    together = count // GROUPS
    lax.fori_loop(0, together, some, 0)
    lax.fori_loop(together * GROUPS, count, one, 0)


def window_of(start):
    return pl.multiple_of((start // 16) * 16, 16)


def spread_lanes(block):
    lanes = lax.broadcasted_iota(jnp.int32, (1, HALF), 1) // HEAD_DIM
    return jnp.concatenate(
        [jnp.where(lanes == h, block, jnp.zeros_like(block)) for h in range(HEADS)], axis=0
    )


def spread_rows(block):
    none = jnp.zeros((HEAD_DIM, block.shape[1]), block.dtype)
    return jnp.concatenate(
        [
            jnp.concatenate(
                [block[g * HEAD_DIM : (g + 1) * HEAD_DIM] if g == h else none for g in range(HEADS)],
                axis=0,
            )
            for h in range(HEADS)
        ],
        axis=1,
    )


def by_head(rows, spread):
    columns = spread.shape[1] // HEADS
    return jnp.concatenate(
        [
            dot(rows[h * HEAD_DIM : (h + 1) * HEAD_DIM], spread[:, h * columns : (h + 1) * columns])
            for h in range(HEADS)
        ],
        axis=0,
    )


def window_mask(q_first, q_bounds, k_first, k_bounds, q_low, q_high, causal):
    q = lax.broadcasted_iota(jnp.int32, (1, WINDOW), 1) + q_first
    k = lax.broadcasted_iota(jnp.int32, (WINDOW, WINDOW), 0) + k_first
    q_id = sum((q >= bound).astype(jnp.int32) for bound in q_bounds)
    k_id = sum((k >= bound).astype(jnp.int32) for bound in k_bounds)
    allowed = k_id == q_id
    if causal:
        allowed = allowed & (k <= q)
    valid = (q >= jnp.maximum(q_bounds[0], q_low)) & (q < jnp.minimum(q_bounds[3], q_high))
    return jnp.concatenate([allowed] * HEADS, axis=1), jnp.concatenate([valid] * HEADS, axis=1)


def window_weights(scores, masks):
    scores = [jnp.where(allowed, each, MASKED) for each, (allowed, _) in zip(scores, masks)]
    weights = [jnp.exp(each - jnp.max(each, axis=0, keepdims=True)) for each in scores]
    inverses = [
        jnp.where(valid, 1.0 / jnp.sum(each, axis=0, keepdims=True), 0.0)
        for each, (_, valid) in zip(weights, masks)
    ]
    return [each * inverse for each, inverse in zip(weights, inverses)]


def attend_windows(windows):
    qs, ks, vs, masks = zip(*windows)
    q_rows = [spread_rows((q * jnp.asarray(HEAD_DIM**-0.5, BF16)).T) for q in qs]
    scores = [dot(k, q) for k, q in zip(ks, q_rows)]
    probabilities = [each.astype(BF16) for each in window_weights(scores, masks)]
    mixes = [by_head(v.T, each) for v, each in zip(vs, probabilities)]
    return [mix.astype(BF16).T for mix in mixes]


def attend_windows_back(windows):
    qs, ks, vs, grads, masks = zip(*windows)
    scale = HEAD_DIM**-0.5
    qs = [q * jnp.asarray(scale, BF16) for q in qs]
    scores = [dot(k, spread_rows(q.T)) for k, q in zip(ks, qs)]
    prob_grads = [dot(v, spread_rows(grad.T)) for v, grad in zip(vs, grads)]
    probabilities = window_weights(scores, masks)
    inners = [
        jnp.sum(each * grad, axis=0, keepdims=True) for each, grad in zip(probabilities, prob_grads)
    ]
    score_grads = [
        (each * (grad - inner)).astype(BF16)
        for each, grad, inner in zip(probabilities, prob_grads, inners)
    ]
    v_grads = [
        dot(each.astype(BF16), spread_lanes(grad)) for each, grad in zip(probabilities, grads)
    ]
    q_grads = [by_head(k.T, each) for k, each in zip(ks, score_grads)]
    k_grads = [dot(each, spread_lanes(q)) for each, q in zip(score_grads, qs)]
    q_grads = [(each * scale).astype(BF16).T for each in q_grads]
    return [(q, k.astype(BF16), v.astype(BF16)) for q, k, v in zip(q_grads, k_grads, v_grads)]


def out_product(mixes, outs):
    left = sum(dot(mix, out[0:HALF]) for mix, out in zip(mixes, outs))
    right = sum(dot(mix, out[HALF:]) for mix, out in zip(mixes, outs))
    return jnp.concatenate([left, right], axis=1)


def out_mix_grads(grad_low, outs, mix_grads, first):
    rows = grad_low.shape[0]
    for half in range(2):
        for lo in range(0, rows, HALF):
            block = grad_low[lo : lo + HALF]
            mix_grad = dot_nt(block[:, :HALF], outs[half, 0:HALF]) + dot_nt(block[:, HALF:], outs[half, HALF:])
            mix_grads[half, first + lo : first + lo + HALF] = mix_grad.astype(BF16)


def out_weight_grads(grad_low, mixes, grads):
    for half, mix in enumerate(mixes):
        grads[half, 0:HALF] = dot_tn(mix, grad_low[:, :HALF]).astype(BF16)
        grads[half, HALF:] = dot_tn(mix, grad_low[:, HALF:]).astype(BF16)


def copy_by_role(meta, pairs_zero, pairs_one, sem):
    @pl.when(meta[0] == 0)
    def _():
        for source, target in pairs_zero:
            pltpu.make_async_copy(source, target, sem).start()

    @pl.when(meta[0] == 1)
    def _():
        for source, target in pairs_one:
            pltpu.make_async_copy(source, target, sem).start()


def wait_by_role(meta, pairs_zero, pairs_one, sem):
    @pl.when(meta[0] == 0)
    def _():
        for source, target in pairs_zero:
            pltpu.make_async_copy(source, target, sem).wait()

    @pl.when(meta[0] == 1)
    def _():
        for source, target in pairs_one:
            pltpu.make_async_copy(source, target, sem).wait()


def states_copies(rows_ref, other_ref, held, here):
    zero = [(other_ref.at[pl.ds(0, here)], held.at[pl.ds(HALO, here)])]
    one = [(rows_ref.at[pl.ds(here - HALO, here + HALO)], held.at[pl.ds(0, here + HALO)])]
    return zero, one


def self_attention(meta, segs, plan, here, qkvs, mixes):
    full = here + HALO
    for mix in mixes:
        mix[...] = jnp.zeros(mix.shape, BF16)

    def group(bounds, _):
        first = window_of(bounds[0])
        mask = window_mask(first, bounds, first, bounds, HALO, full, True)
        at = pl.ds(first, WINDOW)
        return [(qkv[0, at], qkv[1, at], qkv[2, at], mask) for qkv in qkvs]

    def store(bounds, _, result):
        at = pl.ds(window_of(bounds[0]), WINDOW)
        for mix, each in zip(mixes, result):
            mix[at] += each

    together = 2 * GROUPS // len(qkvs)
    each_group(meta, segs, plan, here, False, together, group, attend_windows, store)


def self_project(normed, held, qkv):
    full = normed.shape[0]
    qkv[:, full:] = jnp.zeros((3, WINDOW, HALF), BF16)
    for c in range(3):
        qkv[c, 0:full] = dot(normed[...], held[c]).astype(BF16)


def self_forward(
    meta, plan, rows_ref, other_ref, gain, bias, own, own_out, w1, w2, w3, w4,
    hidden, normed, qkv, mix, states, held, outs, sem_w, sem_x,
):
    full = states.shape[0]
    here = full - HALO
    state_copies = states_copies(rows_ref, other_ref, states, here)
    copy_by_role(meta, *state_copies, sem_x)
    weights = start_other(meta[1], (w1, w2, w3, w4), 0, held, sem_w)
    weights += start_out_own(own_out, outs, sem_w)
    mix.ref[...] = jnp.zeros(mix.ref.shape, BF16)
    wait_by_role(meta, *state_copies, sem_x)

    @pl.when(meta[0] == 0)
    def _():
        states[0:HALO] = jnp.zeros((HALO, states.shape[1]), BF16)

    for lo in range(0, full, HALO):
        hat, _ = norm_parts(states[lo : lo + HALO].astype(F32))
        normed.ref[lo : lo + HALO] = (hat * gain[0:1] + bias[0:1]).astype(BF16)
    normed.send()
    own = own()
    wait(weights)
    qkv.ref[:, :, full:] = jnp.zeros((2, 3, WINDOW, HALF), BF16)
    for half, matrices in enumerate((own, held)):
        for c in range(3):
            qkv.ref[half, c, 0:full] = dot(normed.ref[...], matrices[c]).astype(BF16)
    qkv.send()

    def group(bounds, _):
        first = window_of(bounds[0])
        mask = window_mask(first, bounds, first, bounds, HALO, full, True)
        at = pl.ds(first, WINDOW)
        return [(qkv.ref[half, 0, at], qkv.ref[half, 1, at], qkv.ref[half, 2, at], mask) for half in range(2)]

    def store(bounds, _, result):
        at = pl.ds(window_of(bounds[0]), WINDOW)
        for half in range(2):
            mix.ref[half, at] += result[half]

    each_group(plan, group, attend_windows, store)
    mix.send()
    for lo in range(HALO, full, HALF):
        at = slice(lo, lo + HALF)
        hidden[lo - HALO : lo - HALO + HALF] = states[at].astype(F32) + out_product(
            [mix.ref[0, at], mix.ref[1, at]], [outs, held[3]]
        )


def blocks_do(low, high, pairs, target, sem, act):
    def one(block, _):
        at = pl.ds(pl.multiple_of(block * HALF, HALF), HALF)
        act(pltpu.make_async_copy(pairs.at[:, :, at], target.at[:, :, at], sem))
        return 0

    lax.fori_loop(low // HALF, (high + HALF - 1) // HALF, one, 0)


def zero_after(high, pairs):
    end = pl.multiple_of(((high + HALF - 1) // HALF) * HALF, HALF)
    pairs[:, :, pl.ds(end, WINDOW)] = jnp.zeros((2, 2, WINDOW, HALF), BF16)


def memory_copies(rows_ref, other_ref, held):
    return [(rows_ref, held)], [(other_ref, held)]


def cross_forward(
    meta, plan, rows_ref, other_ref, hidden, gain, bias, own_q, own_pair, own_out, w1, w2, w3, w4,
    hidden_two, hidden_far, normed, mix, queries, pairs_far, pairs, memory, held, outs, sem_w, sem_x, sem_h,
):
    here = hidden_two.ref.shape[0]
    hidden_copy = pltpu.make_async_copy(hidden, hidden_far, sem_h.at[0])
    hidden_copy.start()
    full = here + HALO
    copies = memory_copies(rows_ref, other_ref, memory)
    copy_by_role(meta, *copies, sem_x)
    weights = start_other(meta[2], (w1, w2, w3, w4), 0, held, sem_w)
    weights += start_out_own(own_out, outs, sem_w)
    queries.ref[:, 0:HALO] = jnp.zeros((2, HALO, HALF), BF16)
    queries.ref[:, full:] = jnp.zeros((2, WINDOW, HALF), BF16)
    mix.ref[...] = jnp.zeros(mix.ref.shape, BF16)
    low, high = plan[8, 1], plan[8, 2]
    zero_after(high, pairs)
    for lo in range(0, here, HALF):
        at = slice(lo, lo + HALF)
        hat, _ = norm_parts(hidden[at])
        normed.ref[at] = (hat * gain[1:2] + bias[1:2]).astype(BF16)
    normed.send()
    own_q, own_pair = own_q(), own_pair()
    wait(weights)
    for half, matrix in enumerate((own_q, held.at[0])):
        queries.ref[half, HALO:full] = dot(normed.ref[...], matrix[...]).astype(BF16)
    queries.send()
    wait_by_role(meta, *copies, sem_x)

    def project(block, _):
        at = pl.ds(pl.multiple_of(block * HALF, HALF), HALF)
        for c in range(2):
            pairs[0, c, at] = dot(memory[at], own_pair[c]).astype(BF16)
            pairs[1, c, at] = dot(memory[at], held[1 + c]).astype(BF16)
        return 0

    lax.fori_loop(low // HALF, (high + HALF - 1) // HALF, project, 0)
    blocks_do(low, high, pairs, pairs_far, sem_h.at[1], lambda copy: copy.start())

    def group(bounds, source_bounds):
        first = window_of(bounds[0])
        source_first = window_of(source_bounds[0])
        mask = window_mask(first, bounds, source_first, source_bounds, HALO, full, False)
        at = pl.ds(first, WINDOW)
        source_at = pl.ds(source_first, WINDOW)
        return [
            (queries.ref[half, at], pairs[half, 0, source_at], pairs[half, 1, source_at], mask)
            for half in range(2)
        ]

    def store(bounds, _, result):
        at = pl.ds(window_of(bounds[0]), WINDOW)
        for half in range(2):
            mix.ref[half, at] += result[half]

    each_group(plan, group, attend_windows, store)
    mix.send()
    for lo in range(0, here, HALF):
        at = slice(lo, lo + HALF)
        mix_at = slice(HALO + lo, HALO + lo + HALF)
        hidden_two.ref[at] = hidden[at] + out_product([mix.ref[0, mix_at], mix.ref[1, mix_at]], [outs, held[3]])
        hidden_two.send(at)
    hidden_copy.wait()
    blocks_do(low, high, pairs, pairs_far, sem_h.at[1], lambda copy: copy.wait())


def gelu_both(inner):
    rate, cubic = 0.7978845608028654, 0.7978845608028654 * 0.044715
    square = inner * inner
    bent = jnp.tanh(inner * (rate + cubic * square))
    half = 0.5 + 0.5 * bent
    slope = half + inner * (1.0 - bent * bent) * (0.5 * rate + 1.5 * cubic * square)
    return inner * half, slope


def column(values, role, at):
    lanes = lax.broadcasted_iota(jnp.int32, (WINDOW, WINDOW), 1)
    own = lax.broadcasted_iota(jnp.int32, (WINDOW, WINDOW), 0) == lanes
    blocks = []
    for block in range(at.start // WINDOW, at.stop // WINDOW):
        row = values[role, block : block + 1]
        blocks.append(jnp.sum(jnp.where(own, row, 0.0), axis=1, keepdims=True))
    return jnp.concatenate(blocks, axis=0)


def feed_forward(
    meta, hidden_two, cotangent, targets, gain, bias, halt_weight, halt_bias,
    own_in, i1, i2, i3, i4, own_out, o1, o2, o3, o4,
    result_low, hidden_grad, hidden_far, small, keep, send,
    held_in, held_out, normed, active, slopes, total, out_low, cot, grads, sem_w, sem_o, sem_x, sem_g,
):
    here, width = total.shape
    first = pl.multiple_of(meta[0] * here, here)
    cot_copy = pltpu.make_async_copy(cotangent.at[pl.ds(first, here)], cot, sem_x.at[0])
    weights = start_in(meta, own_in, (i1, i2, i3, i4), held_in, sem_w)
    weights += start_out(meta, own_out, (o1, o2, o3, o4), held_out, sem_o)
    cot_copy.start()
    hidden_two = hidden_two()
    blocks = [slice(lo, lo + HALF) for lo in range(0, here, HALF)]
    for at in blocks:
        hat, _ = norm_parts(hidden_two[at])
        normed[at] = (hat * gain[2:3] + bias[2:3]).astype(BF16)
        total[at] = hidden_two[at]
    wait(weights)

    def forward(pair, _):
        items = [(at, 8 * pair + u) for at in blocks for u in range(8)]
        inner = dot(normed[items[0][0]], held_in[items[0][1]])
        products = []
        for i, (at, j) in enumerate(items):
            coming = dot(normed[items[i + 1][0]], held_in[items[i + 1][1]]) if i + 1 < len(items) else None
            value, slope = gelu_both(inner)
            value = value.astype(BF16)
            active[j, at] = value
            slopes[j, at] = slope
            products.append(dot(value, held_out[j]))
            if len(products) == 8:
                total[at] += sum(products)
                products = []
            inner = coming
        return 0

    lax.fori_loop(0, 1, forward, 0)
    cot_copy.wait()
    weight_sum = jnp.zeros((1, width), F32)
    bias_sum = jnp.zeros((1, 1), F32)
    for at in blocks:
        result = total[at]
        result_low.ref[at] = result.astype(BF16)
        logits = jnp.sum(result * halt_weight[...], axis=-1, keepdims=True) + halt_bias[0]
        halt_grad = 1.0 / (1.0 + jnp.exp(-logits)) - column(targets, meta[0], at)
        out_grad = cot[at].astype(F32) + halt_grad * halt_weight[...]
        out_low[at] = out_grad.astype(BF16)
        hidden_grad[at] = out_grad
        total[at] = jnp.zeros((HALF, width), F32)
        weight_sum += jnp.sum(halt_grad * result, axis=0, keepdims=True)
        bias_sum += jnp.sum(halt_grad, axis=0, keepdims=True)
    result_low.send()

    def backward(i, _):
        js = [4 * i + u for u in range(4)]
        value_grads = [[dot_nt(out_low[at], held_out[j]) for at in blocks] for j in js]
        inner_grads = [
            [(grad * slopes[j, at]).astype(BF16) for grad, at in zip(grads_of_it, blocks)]
            for j, grads_of_it in zip(js, value_grads)
        ]
        for b, at in enumerate(blocks):
            total[at] += sum(dot_nt(each[b], held_in[j]) for j, each in zip(js, inner_grads))
        for j, each in zip(js, inner_grads):
            half, block = j // 4, j % 4
            grads[8 * half + block] = dot_tn(normed[...], jnp.concatenate(each, axis=0)).astype(BF16)
            out_grad = dot_tn(active[j], out_low[...]).astype(BF16)
            grads[8 * half + 4 + block, 0:HALF] = out_grad[:, :HALF]
            grads[8 * half + 4 + block, HALF:] = out_grad[:, HALF:]
        return 0

    lax.fori_loop(0, 4 // 4, backward, 0)
    copies = put_half(meta, grads, keep, send, sem_g, 0)
    lax.fori_loop(4 // 4, 8 // 4, backward, 0)
    copies += put_half(meta, grads, keep, send, sem_g, 1)
    gain_sum = jnp.zeros_like(weight_sum)
    shift_sum = jnp.zeros_like(weight_sum)
    for at in blocks:
        hat, scale = norm_parts(hidden_two[at])
        grad = total[at]
        hidden_grad[at] += norm_back(grad, hat, scale, gain[2:3])
        gain_sum += jnp.sum(grad * hat, axis=0, keepdims=True)
        shift_sum += jnp.sum(grad, axis=0, keepdims=True)
    small[...] = jnp.concatenate(
        [gain_sum, shift_sum, weight_sum, jnp.broadcast_to(bias_sum, weight_sum.shape)], axis=0
    )
    copies += start([pltpu.make_async_copy(hidden_grad, hidden_far, sem_x.at[1])])
    wait(copies)


def out_backward(
    meta, upper_grad, mix, own_out, w1, w2, w3, w4, *rest, place, ahead
):
    sources, (mix_grads, out_part), rest = rest[:ahead], rest[ahead : ahead + 2], rest[ahead + 2 :]
    targets, (outs, sem_w, sem_h) = rest[:ahead], rest[ahead:]
    full = mix_grads.shape[1] - WINDOW
    weights = start_other(meta[place], (w1, w2, w3, w4), 3, outs.at[pl.ds(1, 1)], sem_w)
    weights += start_out_own(own_out, outs.at[0], sem_w)
    mix.go()
    brought = start(
        [pltpu.make_async_copy(*copy, sem_h.at[at]) for at, copy in enumerate(zip(sources, targets))]
    )
    mix_grads[:, 0:HALO] = jnp.zeros((2, HALO, HALF), BF16)
    mix_grads[:, full:] = jnp.zeros((2, WINDOW, HALF), BF16)
    grad_low = upper_grad[...].astype(BF16)
    wait(weights)
    out_mix_grads(grad_low, outs, mix_grads, HALO)
    mix = mix()
    out_weight_grads(grad_low, [mix[0, HALO:full], mix[1, HALO:full]], out_part.ref)
    wait(brought)


def cross_backward(meta, plan, mix_grads, queries, pairs_far, q_grad, pair_grads, pairs, sem_h):
    full = mix_grads.shape[1] - WINDOW
    here = full - HALO
    low, high = plan[8, 1], plan[8, 2]
    blocks_do(low, high, pairs_far, pairs, sem_h.at[0], lambda copy: copy.start())
    q_grad[...] = jnp.zeros(q_grad.shape, BF16)
    pair_grads[...] = jnp.zeros(pair_grads.shape, BF16)
    zero_after(high, pairs)
    blocks_do(low, high, pairs_far, pairs, sem_h.at[0], lambda copy: copy.wait())

    def group(bounds, source_bounds):
        first = window_of(bounds[0])
        source_first = window_of(source_bounds[0])
        mask = window_mask(first, bounds, source_first, source_bounds, HALO, full, False)
        at = pl.ds(first, WINDOW)
        source_at = pl.ds(source_first, WINDOW)
        return [
            (
                queries[half, at], pairs[half, 0, source_at], pairs[half, 1, source_at],
                mix_grads[half, at], mask,
            )
            for half in range(2)
        ]

    def store(bounds, source_bounds, result):
        at = pl.ds(window_of(bounds[0]), WINDOW)
        source_at = pl.ds(window_of(source_bounds[0]), WINDOW)
        for half, (dq, dk, dv) in enumerate(result):
            q_grad[half, at] += dq
            pair_grads[half, 0, source_at] += dk
            pair_grads[half, 1, source_at] += dv

    each_group(plan, group, attend_windows_back, store)


def cross_products(
    meta, plan, rows_ref, other_ref, hidden, normed, upper_grad, q_grad, pair_grads, out_part, own_q, own_pair,
    w1, w2, w3, w4, gain,
    lower_grad, lower_far, memory_grad, small, keep, send, memory, pair_sums, grads, held, sem_w, sem_x, sem_g, sem_h,
):
    here, width = lower_grad.shape
    full = here + HALO
    weights = start_other(meta[2], (w1, w2, w3, w4), 0, held, sem_w)
    copies = memory_copies(rows_ref, other_ref, memory)
    copy_by_role(meta, *copies, sem_x)
    normed.go()
    hidden.go()
    upper_grad.go()
    pair_sums[...] = jnp.zeros(pair_sums.shape, F32)
    memory_grad.ref[...] = jnp.zeros(memory_grad.ref.shape, BF16)
    source_low, source_high = plan[8, 1], plan[8, 2]
    parts = start(
        [pltpu.make_async_copy(out_part.at[half], grads.at[4 * half + 3], sem_g.at[0]) for half in range(2)]
    )
    gain_sum = jnp.zeros((1, width), F32)
    shift_sum = jnp.zeros((1, width), F32)
    own_q, own_pair = own_q(), own_pair()
    wait(weights)
    wait_by_role(meta, *copies, sem_x)

    def project(block, _):
        at = pl.ds(pl.multiple_of(block * HALF, HALF), HALF)
        row_grad = jnp.zeros((HALF, width), F32)
        for half in range(2):
            for c in range(2):
                low = pair_grads[half, c, at]
                row_grad += dot_nt(low, held[1 + c] if half else own_pair[c])
                pair_sums[half, c] += dot_tn(memory[at], low)
        memory_grad.ref[at] = row_grad.astype(BF16)
        return 0

    lax.fori_loop(source_low // HALF, (source_high + HALF - 1) // HALF, project, 0)
    memory_grad.send()
    for half in range(2):
        for c in range(2):
            grads[4 * half + 1 + c] = pair_sums[half, c].astype(BF16)
    normed = normed()
    for half in range(2):
        grads[4 * half] = dot_tn(normed[...], q_grad[half, HALO:full]).astype(BF16)
    wait(parts)
    put = put_grads(meta, grads, keep, send, sem_g)
    hidden, upper_grad = hidden(), upper_grad()
    for lo in range(0, here, HALF):
        at = slice(lo, lo + HALF)
        q_at = slice(HALO + lo, HALO + lo + HALF)
        hat, scale = norm_parts(hidden[at])
        grad = dot_nt(q_grad[0, q_at], own_q[...]) + dot_nt(q_grad[1, q_at], held[0])
        lower_grad[at] = upper_grad[at] + norm_back(grad, hat, scale, gain[1:2])
        gain_sum += jnp.sum(grad * hat, axis=0, keepdims=True)
        shift_sum += jnp.sum(grad, axis=0, keepdims=True)
    small[...] = jnp.concatenate([gain_sum, shift_sum], axis=0)
    put += start([pltpu.make_async_copy(lower_grad, lower_far, sem_h.at[0])])
    wait(put)


def self_backward(meta, plan, mix_grads, qkv, qkv_grads):
    full = mix_grads.shape[1] - WINDOW
    here = full - HALO
    qkv_grads[...] = jnp.zeros(qkv_grads.shape, BF16)

    def group(bounds, _):
        first = window_of(bounds[0])
        mask = window_mask(first, bounds, first, bounds, HALO, full, True)
        at = pl.ds(first, WINDOW)
        return [
            (qkv[half, 0, at], qkv[half, 1, at], qkv[half, 2, at], mix_grads[half, at], mask)
            for half in range(2)
        ]

    def store(bounds, _, result):
        at = pl.ds(window_of(bounds[0]), WINDOW)
        for half in range(2):
            for c in range(3):
                qkv_grads[half, c, at] += result[half][c]

    each_group(plan, group, attend_windows_back, store)


def self_products(
    meta, rows_ref, other_ref, normed, qkv_grads, out_part, upper_grad, own, w1, w2, w3, w4, gain, result, memory_part,
    keep, send, state_grad, swap, halo_grad, small, grads, states, held, sem_g, sem_w, sem_x, sem_s,
):
    full, width = states.shape
    here = full - HALO
    normed.go()
    parts = start(
        [pltpu.make_async_copy(out_part.at[half], grads.at[4 * half + 3], sem_g.at[0]) for half in range(2)]
    )
    weights = start_other(meta[1], (w1, w2, w3, w4), 0, held, sem_w)
    state_copies = states_copies(rows_ref, other_ref, states, here)
    copy_by_role(meta, *state_copies, sem_x)
    swaps = [(result, swap.ref.at[pl.ds(0, here)])], [(memory_part, swap.ref)]
    own.go()
    upper_grad.go()
    copy_by_role(meta, *swaps, sem_s)
    normed = normed()
    for half in range(2):
        for c in range(3):
            grads[4 * half + c] = dot_tn(normed[...], qkv_grads[half, c, 0:full]).astype(BF16)
    wait(parts)
    put = put_grads(meta, grads, keep, send, sem_g)
    wait_by_role(meta, *state_copies, sem_x)

    @pl.when(meta[0] == 0)
    def _():
        states[0:HALO] = jnp.zeros((HALO, width), BF16)

    own, upper_grad = own(), upper_grad()
    wait(weights)
    gain_sum = jnp.zeros((1, width), F32)
    shift_sum = jnp.zeros((1, width), F32)
    step = full // 2
    for lo in range(0, full, step):
        at = slice(lo, lo + step)
        hat, scale = norm_parts(states[at].astype(F32))
        grad = sum(
            dot_nt(qkv_grads[half, c, at], matrices[c])
            for half, matrices in enumerate((own, held))
            for c in range(3)
        )
        back = norm_back(grad, hat, scale, gain[0:1])
        if lo == 0:
            halo_grad.ref[...] = back[:HALO]
            back = back[HALO:]
        first = max(lo, HALO) - HALO
        at = slice(first, lo + step - HALO)
        back += upper_grad[at]
        state_grad.ref[at] = back

        @pl.when(meta[0] == 0)
        def _(low=back.astype(BF16), at=slice(here + at.start, here + at.stop)):
            swap.ref[at] = low

        gain_sum += jnp.sum(grad * hat, axis=0, keepdims=True)
        shift_sum += jnp.sum(grad, axis=0, keepdims=True)
    small[...] = jnp.concatenate([gain_sum, shift_sum], axis=0)
    wait_by_role(meta, *swaps, sem_s)
    wait(put)


def finish_rows(
    meta, rows, result, grad, halo_grad, memory_part, swapped, layer_out, input_grads, parts, halo, sem,
):
    here = result.shape[0]
    low, high = pl.ds(0, here), pl.ds(here, here)

    @pl.when(meta[0] == 0)
    def _():
        copies = [(rows, layer_out.ref), (memory_part, parts.at[0]), (swapped, parts.at[1])]
        wait(start([pltpu.make_async_copy(*copy, sem) for copy in copies]))
        input_grads.ref[...] = parts[0].astype(F32) + parts[1].astype(F32)

    @pl.when(meta[0] == 1)
    def _():
        copies = [
            (swapped.at[low], layer_out.ref.at[low]),
            (result, layer_out.ref.at[high]),
            (swapped.at[high], parts.at[0, low]),
            (grad, input_grads.ref.at[high]),
            (halo_grad, halo),
        ]
        wait(start([pltpu.make_async_copy(*copy, sem) for copy in copies]))
        input_grads.ref[0:here] = parts[0, 0:here].astype(F32)
        input_grads.ref[here - HALO : here] += halo[...]


OUTPUTS = {"ffn": 2, "cross": 7, "self": 2}


def unpack(kinds, meta, *refs):
    pieces, refs = refs[: 4 * len(kinds)], refs[4 * len(kinds) :]
    if "cross" in kinds:
        small, refs = refs[0], refs[1:]
    count = sum(OUTPUTS[kind] for kind in kinds)
    outs, held, sem = refs[:count], refs[count:-1], refs[-1]
    copies = []
    for at in range(len(kinds)):
        rows = pieces[4 * at].shape[1]
        came = zip((0, 2, 1, 3), pieces[4 * at : 4 * at + 4])
        firsts = [(pl.multiple_of((rel ^ meta[1]) * rows, rows), ref) for rel, ref in came]
        copies.append(
            start(
                [
                    pltpu.make_async_copy(ref, held[at].at[:, pl.ds(first, rows)], sem.at[at])
                    for first, ref in firsts
                ]
            )
        )
    for kind, grads, arrived in zip(kinds, held, copies):
        outs, rest = outs[: OUTPUTS[kind]], outs[OUTPUTS[kind] :]
        wait(arrived)
        if kind == "ffn":
            grad_in, grad_out = outs
            for j in range(4):
                at = slice(j * HALF, (j + 1) * HALF)
                grad_in[:, at] = grads[j].astype(F32)
                grad_out[at, 0:HALF] = grads[4 + j, 0:HALF].astype(F32)
                grad_out[at, HALF:] = grads[4 + j, HALF:].astype(F32)
        else:
            if kind == "cross":
                gain, shift, weight, bias = outs[3:]
                gain[...], shift[...] = small[0:3], small[3:6]
                weight[...], bias[...] = small[6:7], small[7:8, 0:1]
                outs[0][...] = grads[0].astype(F32)
                for c in range(2):
                    outs[1][:, c] = grads[1 + c].astype(F32)
                out = outs[2]
            else:
                outs[0][...] = grads[0:3].astype(F32)
                out = outs[1]
            out[:, 0:HALF] = grads[3, 0:HALF].astype(F32)
            out[:, HALF:] = grads[3, HALF:].astype(F32)
        outs = rest


def shape(*dims, dtype=F32):
    return jax.ShapeDtypeStruct(dims, dtype)


def far(*dims, dtype=F32):
    return pltpu.HBM(dims, dtype)


def near(*dims, dtype=F32):
    return pltpu.VMEM(dims, dtype)


def room(shapes, spare):
    return sum(math.prod(each.shape) * jnp.dtype(each.dtype).itemsize for each in shapes) + (spare << 20)


class Put:
    def __init__(self, *dims, dtype=F32):
        self.shape = far(*dims, dtype=dtype)
        self.scratch = pltpu.VMEM(dims, dtype)


class Get:
    def __init__(self, value, late=False):
        self.value = value
        self.late = late
        self.scratch = pltpu.VMEM(value.shape, value.dtype)


class Here:
    def __init__(self, value):
        self.value = value


class Any:
    def __init__(self, value):
        self.value = value


class Far:
    def __init__(self, value):
        self.value = value


def call(body, ins, outs, scratch, weight):
    smem, others = ins
    operands = list(smem) + list(others)
    values, in_specs = list(smem), [SMEM] * len(smem)
    for other in others:
        if isinstance(other, (Get, Far)):
            values.append(pltpu.with_memory_space_constraint(other.value, pltpu.HBM))
            in_specs.append(ANY)
        elif isinstance(other, Any):
            values.append(other.value)
            in_specs.append(ANY)
        elif isinstance(other, Here):
            values.append(pltpu.with_memory_space_constraint(other.value, pltpu.VMEM))
            in_specs.append(VMEM)
        else:
            values.append(other)
            in_specs.append(VMEM)
    moved = [at for at, each in enumerate(operands) if isinstance(each, Get)]
    put = [at for at, each in enumerate(outs) if isinstance(each, Put)]

    def inner(*refs):
        in_refs, refs = list(refs[: len(values)]), refs[len(values) :]
        out_refs, refs = list(refs[: len(outs)]), refs[len(outs) :]
        moved_refs, refs = refs[: len(moved)], refs[len(moved) :]
        put_refs, refs = refs[: len(put)], refs[len(put) :]
        sems, refs = refs[0], refs[1:]
        for i, at in enumerate(moved):
            in_refs[at] = Load(in_refs[at], moved_refs[i], sems.at[i])
            if not operands[at].late:
                in_refs[at].go()
        for i, at in enumerate(put):
            out_refs[at] = Store(put_refs[i], out_refs[at], sems.at[len(moved) + i])
        body(*in_refs, *out_refs, *refs)
        for at in moved:
            in_refs[at]()
        for at in put:
            if not out_refs[at].copies:
                out_refs[at].send()
        for at in put:
            out_refs[at].end()

    in_vmem = [operands[at].scratch for at in moved] + [outs[at].scratch for at in put]
    in_vmem += [each for each in scratch if getattr(each, "memory_space", None) is pltpu.VMEM]
    in_vmem += [value for value, spec in zip(values, in_specs) if spec is VMEM]
    in_vmem += [out for out in outs if not isinstance(out, Put) and getattr(out, "memory_space", None) is not pltpu.HBM]
    return pl.pallas_call(
        inner,
        out_shape=[out.shape if isinstance(out, Put) else out for out in outs],
        in_specs=in_specs,
        out_specs=[ANY if isinstance(out, Put) or getattr(out, "memory_space", None) is pltpu.HBM else VMEM for out in outs],
        scratch_shapes=[operands[at].scratch for at in moved]
        + [outs[at].scratch for at in put]
        + [pltpu.SemaphoreType.DMA((len(moved) + len(put) + 1,))]
        + list(scratch),
        name=getattr(body, "__name__", "out_backward"),
        compiler_params=pltpu.CompilerParams(vmem_limit_bytes=room(in_vmem, SPARE)),
        cost_estimate=pl.CostEstimate(flops=int(weight * WEIGHT), bytes_accessed=0, transcendentals=0),
    )(*values)


def flip(value, axis, bit=1):
    count = lax.axis_size(axis)
    return lax.ppermute(value, axis, [(i, i ^ bit) for i in range(count)])


def add(a, b):
    return (a.astype(F32) + b.astype(F32)).astype(BF16)


def after(value, *events):
    return lax.optimization_barrier((value, events))[0]


class Order:
    def __init__(self, meta):
        self.meta = meta
        self.last = ()

    def now(self):
        return after(self.meta, *self.last)

    def __call__(self, weight, *jobs):
        operands = [value for job in jobs for value in job[0]]
        shapes = [each for job in jobs for each in job[1]]

        def sums(meta, *refs):
            ins, outs = list(refs[: len(operands)]), list(refs[len(operands) :])
            for values, results, body, _ in jobs:
                body(meta, ins[: len(values)], outs[: len(results)])
                ins, outs = ins[len(values) :], outs[len(results) :]

        results = list(
            pl.pallas_call(
                sums,
                out_shape=shapes,
                in_specs=[SMEM] + [VMEM] * len(operands),
                out_specs=[VMEM] * len(shapes),
                name="sums",
                compiler_params=pltpu.CompilerParams(vmem_limit_bytes=room(operands + shapes, 4)),
                cost_estimate=pl.CostEstimate(flops=int(weight * WEIGHT), bytes_accessed=0, transcendentals=0),
            )(self.now(), *operands)
        )
        self.last = tuple(results)
        for _, each, _, take in jobs:
            take(results[: len(each)])
            results = results[len(each) :]


class Sum:
    def __init__(self, keep, send, routes):
        self.routes = routes
        self.near, self.got = [keep], [flip(send, "role")]

    def job(self, shapes, body, take):
        count = len(self.near)
        return (
            [*self.near, *self.got],
            [jax.ShapeDtypeStruct(each, BF16) if isinstance(each, tuple) else each for each in shapes],
            lambda meta, ins, outs: body(meta, ins[:count], ins[count:], outs),
            take,
        )

    def pass_on(self, stage, far_near=False):
        def take(parts):
            self.near = parts[0::2]
            if far_near:
                self.near = [pltpu.with_memory_space_constraint(each, pltpu.HBM) for each in self.near]
            self.got = [step(away, route[stage]) for away, route in zip(parts[1::2], self.routes)]

        return take

    def begin(self, far_near=False):
        count = len(self.routes)
        _, _, matrices, rows, columns = self.near[0].shape
        share = matrices // count

        def body(meta, near, got, outs):
            for at, route in enumerate(self.routes):
                mine = pl.ds(at * share, share)
                for which in range(2):
                    place = (slice(None), which, mine) if route[0] == "x" and count > 1 else (which, slice(None), mine)
                    outs[2 * at + which][...] = add(near[0][place], got[0][place])

        shapes = [jax.ShapeDtypeStruct((2, share, rows, columns), BF16)] * (2 * count)
        if far_near:
            shapes[0::2] = [far(2, share, rows, columns, dtype=BF16)] * count
        return self.job(shapes, body, self.pass_on(0, far_near))

    def second(self):
        def body(meta, near, got, outs):
            for at in range(len(near)):
                for which in range(2):
                    outs[2 * at + which][...] = add(near[at][which], got[at][which])

        return self.job([self.near[0].shape[1:]] * (2 * len(self.near)), body, self.pass_on(1))

    def halve(self):
        count = len(self.near)
        matrices, rows, columns = self.near[0].shape
        half = count * matrices // 2

        def body(meta, near, got, outs):
            upper = meta[2] >> 1
            for out, which in zip(outs, (upper, 1 - upper)):
                if count == 1:
                    at = pl.ds(which * half, half)
                    out[...] = add(near[0][at], got[0][at])
                else:
                    both = [add(mine[...], theirs[...]) for mine, theirs in zip(near, got)]
                    out[...] = jnp.where(which == 1, both[1], both[0])

        def take(parts):
            self.near, self.got = [parts[0]], [flip(parts[1], "dp", 2)]

        return self.job([(half, rows, columns)] * 2, body, take)

    def plain(self, bit):
        def body(meta, near, got, outs):
            outs[0][...] = add(near[0][...], got[0][...])

        def take(parts):
            self.near, self.got = parts, [flip(parts[0], "dp", bit)]

        return self.job([self.near[0].shape], body, take)

    def whole(self):
        return self.plain(4)

    def back(self, order):
        bit = 8
        while bit < lax.axis_size("dp"):
            order(1, self.plain(bit))
            bit *= 2
        return self.plain(2)

    def last(self):
        half, rows, columns = self.near[0].shape

        def body(meta, near, got, outs):
            upper = meta[2] >> 1
            outs[0][pl.ds(upper * half, half)] = near[0][...]
            outs[0][pl.ds((1 - upper) * half, half)] = got[0][...]

        def take(parts):
            self.mine = parts[0]
            self.by_x = flip(self.mine, "dp", 1)

        return self.job([(2 * half, rows, columns)], body, take)

    def pieces(self, order):
        by_x = after(self.by_x, *order.last)
        return self.mine, by_x, flip(self.mine, "role"), flip(by_x, "role")


def step(value, route):
    if route == "head":
        return flip(value, "head")
    return flip(value, "dp", 1)


class SmallSum:
    def __init__(self, value):
        count = lax.axis_size("dp")
        self.steps = [("role", 1), ("head", 1)] + [("dp", 1 << at) for at in range(count.bit_length() - 1)]
        self.value, self.got = value, flip(value, *self.steps.pop(0))

    def step(self):
        def body(meta, ins, outs):
            outs[0][...] = ins[0][...] + ins[1][...]

        def take(parts):
            self.value = parts[0]
            self.got = flip(self.value, *self.steps.pop(0)) if self.steps else None

        return [self.value, self.got], [jax.ShapeDtypeStruct(self.value.shape, F32)], body, take

    def total(self):
        while self.got is not None:
            self.value = self.value + self.got
            self.got = flip(self.value, *self.steps.pop(0)) if self.steps else None
        return self.value


def shards(
    layer_in,
    lengths,
    cotangent,
    targets,
    self_qkv,
    self_out,
    cross_q,
    cross_kv,
    cross_out,
    ffn_in,
    ffn_out,
    norm_gain,
    norm_bias,
    halt_weight,
    halt_bias,
):
    role, head, place = (lax.axis_index(name) for name in ("role", "head", "dp"))
    target_side = role == 1
    me = 2 * (place & 1) + role
    me_z = (place & 2) + role
    meta = jnp.stack([role, me, me_z, layer_in.shape[1] // 2]).astype(jnp.int32)

    rows = layer_in[0]
    row_len, width = rows.shape
    here = row_len // 2
    full = here + HALO

    other_rows = flip(rows, "role")
    lens = lax.dynamic_index_in_dim(lengths[0], head, 0, keepdims=False)
    other_lens = flip(lens, "role")
    segs = jnp.where(target_side, jnp.stack([other_lens, lens]), jnp.stack([lens, other_lens]))
    segs = jnp.pad(segs, ((0, 0), (0, 2)))

    self_own, cross_own = self_qkv.transpose(1, 0, 2), cross_kv.transpose(1, 0, 2)
    piece_shape = Put(4, width // PIECES, HALF, dtype=BF16)
    (self_piece,) = call(
        cut_self, ([meta], [Far(self_own), Far(self_out)]), [piece_shape], [pltpu.SemaphoreType.DMA((2,))], 1
    )
    cross_piece, in_piece, out_own_piece = call(
        cut_rest,
        ([meta], [Far(cross_q), Far(cross_own), Far(cross_out), Far(ffn_in), Far(ffn_out)]),
        [piece_shape, piece_shape, Put(HALF, width, dtype=BF16)],
        [pltpu.SemaphoreType.DMA((5,))],
        1,
    )
    self_first, cross_first, in_first, out_first = (
        flip(piece, "head") for piece in (self_piece, cross_piece, in_piece, out_own_piece)
    )

    weight_sems = pltpu.SemaphoreType.DMA((6,))
    one_sem = pltpu.SemaphoreType.DMA
    grad_sems = pltpu.SemaphoreType.DMA((1,))
    states_held = pltpu.VMEM((full, width), BF16)
    memory_held = pltpu.VMEM((row_len, width), BF16)
    out_held = pltpu.VMEM((width, HALF), BF16)
    mix_grads = pltpu.VMEM((2, full + WINDOW, HALF), BF16)

    def heads(*dims):
        return Put(*dims, full + WINDOW, HALF, dtype=BF16)

    def matrices(count):
        return pltpu.VMEM((count, width, HALF), BF16)

    pair_shape = (2, 2, row_len + WINDOW, HALF)

    both_rows = Any(rows), Any(other_rows)

    self_plan, cross_plan = pl.pallas_call(
        group_sentences,
        out_shape=[jax.ShapeDtypeStruct((9, 40), jnp.int32)] * 2,
        in_specs=[SMEM] * 2,
        out_specs=[SMEM] * 2,
        name="group_sentences",
        cost_estimate=pl.CostEstimate(flops=int(HEAVY * WEIGHT), bytes_accessed=0, transcendentals=0),
    )(after(meta, cross_piece, self_first), segs)
    self_second = flip(self_first, "dp", 1)
    cross_second = flip(cross_first, "dp", 2)
    in_second = flip(in_first, "dp", 1)
    self_second = after(self_second, self_plan)
    self_weights = [self_first, self_second, flip(self_first, "role"), flip(self_second, "role")]
    self_pieces = [Any(piece) for piece in self_weights]
    hidden, normed_one, qkv, self_mix = call(
        self_forward,
        (
            [after(meta, cross_first), self_plan],
            [*both_rows, norm_gain, norm_bias, Get(self_own), Far(self_out), *self_pieces],
        ),
        [near(here, width), Put(full, width, dtype=BF16), heads(2, 3), heads(2)],
        [states_held, matrices(4), out_held, weight_sems, one_sem],
        11,
    )

    cross_second = after(cross_second, normed_one)
    cross_weights = [cross_first, cross_second, flip(cross_first, "role"), flip(cross_second, "role")]
    cross_pieces = [Any(piece) for piece in cross_weights]
    out_first = after(out_first, normed_one)
    out_second = flip(out_first, "dp", 2)
    hidden_two, hidden_far, normed_two, cross_mix, queries, pairs = call(
        cross_forward,
        (
            [meta, cross_plan],
            [
                *both_rows, Here(hidden), norm_gain, norm_bias, Get(cross_q), Get(cross_own), Far(cross_out),
                *cross_pieces,
            ],
        ),
        [Put(here, width), far(here, width), Put(here, width, dtype=BF16), heads(2), heads(2), far(*pair_shape, dtype=BF16)],
        [
            pltpu.VMEM(pair_shape, BF16), memory_held, matrices(4), out_held, weight_sems, one_sem,
            pltpu.SemaphoreType.DMA((2,)),
        ],
        12,
    )

    in_second, out_second = after((in_second, out_second), normed_two)
    in_weights = in_first, in_second, flip(in_first, "role"), flip(in_second, "role")
    out_weights = out_first, out_second, flip(out_first, "role"), flip(out_second, "role")
    ffn_parts = far(2, 2, 8, width // PIECES, HALF, dtype=BF16)
    grad_parts = far(2, 2, 4, width // PIECES, HALF, dtype=BF16)
    result_low, two_grad, two_far, ffn_small, keep_ffn, send_ffn = call(
        feed_forward,
        (
            [meta],
            [
                Get(hidden_two), Far(cotangent), targets.astype(F32).reshape(2, here // WINDOW, WINDOW),
                norm_gain, norm_bias, halt_weight[None], halt_bias, Far(ffn_in), *map(Far, in_weights),
                Far(ffn_out), *map(Far, out_weights),
            ],
        ),
        [Put(here, width, dtype=BF16), near(here, width), far(here, width), shape(4, width), ffn_parts, ffn_parts],
        [
            matrices(8),
            pltpu.VMEM((8, HALF, width), BF16),
            pltpu.VMEM((here, width), BF16),
            pltpu.VMEM((8, here, HALF), BF16),
            pltpu.VMEM((8, here, HALF), F32),
            pltpu.VMEM((here, width), F32),
            pltpu.VMEM((here, width), BF16),
            pltpu.VMEM((here, width), BF16),
            matrices(16),
            weight_sems,
            weight_sems,
            pltpu.SemaphoreType.DMA((2,)),
            grad_sems,
        ],
        17,
    )

    mix_grads_shape = near(2, full + WINDOW, HALF, dtype=BF16)
    out_scratch = [matrices(2), weight_sems, grad_sems]
    cross_mix_grads, cross_out_part, queries = call(
        functools.partial(out_backward, place=2, ahead=1),
        ([meta], [Here(two_grad), Get(cross_mix, late=True), Far(cross_out), *cross_pieces, Far(queries)]),
        [mix_grads_shape, Put(2, width, HALF, dtype=BF16), near(2, full + WINDOW, HALF, dtype=BF16)],
        out_scratch,
        4,
    )

    def totals(kinds, pieces, out_shapes, *more):
        scratch = [pltpu.VMEM((each[0].shape[0], width, HALF), BF16) for each in pieces]
        results = pl.pallas_call(
            functools.partial(unpack, kinds),
            out_shape=out_shapes,
            in_specs=[SMEM] + [ANY] * (4 * len(kinds)) + [VMEM] * len(more),
            out_specs=[VMEM] * len(out_shapes),
            scratch_shapes=scratch + [pltpu.SemaphoreType.DMA((len(kinds),))],
            name="unpack_" + kinds[0],
            compiler_params=pltpu.CompilerParams(vmem_limit_bytes=room([*out_shapes, *scratch], 6)),
            cost_estimate=pl.CostEstimate(flops=1000, bytes_accessed=0, transcendentals=0),
        )(order.now(), *[piece for each in pieces for piece in each], *more)
        order.last = (results[0],)
        return results

    order = Order(meta)
    ffn_sum = Sum(keep_ffn, send_ffn, FFN_ROUTES)
    order(1, ffn_sum.begin())
    query_grad, pair_grads = call(
        cross_backward,
        ([order.now(), cross_plan], [Here(cross_mix_grads), Here(queries), Far(pairs)]),
        [near(2, full + WINDOW, HALF, dtype=BF16), near(*pair_shape, dtype=BF16)],
        [pltpu.VMEM(pair_shape, BF16), grad_sems],
        9,
    )
    one_grad, one_far, memory_part, cross_small, keep_cross, send_cross = call(
        cross_products,
        (
            [meta, cross_plan],
            [
                *both_rows, Get(hidden_far, late=True), Get(normed_two, late=True), Get(two_far, late=True), Here(query_grad), Here(pair_grads),
                Far(cross_out_part), Get(cross_q), Get(cross_own), *cross_pieces, norm_gain,
            ],
        ),
        [near(here, width), far(here, width), Put(row_len, width, dtype=BF16), shape(2, width), grad_parts, grad_parts],
        [
            memory_held,
            pltpu.VMEM((2, 2, width, HALF), F32),
            matrices(8),
            matrices(3),
            weight_sems,
            one_sem,
            grad_sems,
            grad_sems,
        ],
        8,
    )

    cross_sum = Sum(keep_cross, send_cross, CROSS_ROUTES)
    order(1, ffn_sum.second())
    self_mix_grads, self_out_part, qkv = call(
        functools.partial(out_backward, place=1, ahead=1),
        ([order.now()], [Here(one_grad), Get(self_mix, late=True), Far(self_out), *self_pieces, Far(qkv)]),
        [mix_grads_shape, Put(2, width, HALF, dtype=BF16), near(2, 3, full + WINDOW, HALF, dtype=BF16)],
        out_scratch,
        4,
    )
    order(1, cross_sum.begin())
    order(1, ffn_sum.halve())
    (qkv_grads,) = call(
        self_backward,
        ([order.now(), self_plan], [Here(self_mix_grads), Here(qkv)]),
        [near(2, 3, full + WINDOW, HALF, dtype=BF16)],
        [],
        9,
    )
    order(1, ffn_sum.whole(), cross_sum.second())
    keep_self, send_self, state_grad, swap, halo_grad, self_small = call(
        self_products,
        (
            [order.now()],
            [
                *both_rows, Get(normed_one, late=True), Here(qkv_grads), Far(self_out_part), Get(one_far, late=True), Get(self_own, late=True),
                *self_pieces, norm_gain, Far(result_low), Far(memory_part),
            ],
        ),
        [
            grad_parts,
            grad_parts,
            Put(here, width),
            Put(row_len, width, dtype=BF16),
            Put(HALO, width),
            shape(2, width),
        ],
        [matrices(8), states_held, matrices(3), grad_sems, weight_sems, one_sem, one_sem],
        11,
    )
    self_sum = Sum(keep_self, send_self, SELF_ROUTES)
    order.last = (keep_self,)
    order(HEAVY, cross_sum.halve(), ffn_sum.back(order))
    order(1, self_sum.begin(far_near=True))
    self_small = after(self_small, *order.last)
    small = SmallSum(
        jnp.concatenate(
            [
                self_small[0:1], cross_small[0:1], ffn_small[0:1],
                self_small[1:2], cross_small[1:2], ffn_small[1:2], ffn_small[2:4],
            ],
            axis=0,
        )
    )
    swapped = flip(after(swap, *order.last), "role")
    order(HEAVY, cross_sum.whole())
    order(1, self_sum.second(), small.step())
    order(1, self_sum.halve(), cross_sum.back(order), ffn_sum.last(), small.step())
    order(1, self_sum.whole(), small.step())
    layer_out, input_grads = call(
        finish_rows,
        (
            [order.now()],
            [Any(each) for each in (rows, result_low, state_grad, halo_grad, memory_part, swapped)],
        ),
        [Put(row_len, width, dtype=BF16), Put(row_len, width)],
        [pltpu.VMEM((2, row_len, width), BF16), pltpu.VMEM((HALO, width), F32), one_sem],
        HEAVY,
    )
    order.last = (layer_out,)
    order(1, cross_sum.last(), small.step())
    order(1, self_sum.back(order))
    order.last = (*order.last, cross_sum.by_x)
    order(1, self_sum.last(), small.step())
    ffn_in_grad, ffn_out_grad, cross_q_grad, cross_kv_grad, cross_out_grad, *small = totals(
        ("ffn", "cross"),
        (ffn_sum.pieces(order), cross_sum.pieces(order)),
        (
            shape(width, 4 * HALF), shape(4 * HALF, width),
            shape(width, HALF), shape(width, 2, HALF), shape(HALF, width),
            shape(3, width), shape(3, width), shape(1, width), shape(1, 1),
        ),
        small.total(),
    )
    self_qkv_grad, self_out_grad = totals(
        ("self",), (self_sum.pieces(order),), (shape(3, width, HALF), shape(HALF, width))
    )
    return (
        layer_out[None],
        input_grads[None],
        self_qkv_grad.transpose(1, 0, 2),
        self_out_grad,
        cross_q_grad,
        cross_kv_grad,
        cross_out_grad,
        ffn_in_grad,
        ffn_out_grad,
        small[0],
        small[1],
        small[2][0],
        small[3][0],
    )


def solution(mesh):
    placed = (
        P("role", ("dp", "head"), None),
        P("role", "dp", None),
        P(("dp", "head"), None),
        P(("dp", "head")),
        P(None, None, "head"),
        P("head", None),
        P(None, "head"),
        P(None, None, "head"),
        P("head", None),
        P(None, "head"),
        P("head", None),
        P(),
        P(),
        P(),
        P(),
    )
    return jax.shard_map(
        shards,
        mesh=mesh,
        in_specs=placed,
        out_specs=(
            P("role", ("dp", "head"), None),
            P("role", ("dp", "head"), None),
            P(None, None, "head"),
            P("head", None),
            P(None, "head"),
            P(None, None, "head"),
            P("head", None),
            P(None, "head"),
            P("head", None),
            P(),
            P(),
            P(),
            P(),
        ),
        check_vma=False,
    )
```
